32 devices in a mesh: section: 2 (over core), img: 4 (over z), row: 4 (over y, x).
Axes of the slice: x: 2, y: 2, z: 4, core: 2. Of those that a mesh axis runs over, the one named last changes fastest.
Arguments:
- input_maps: bfloat16 [8, 4, 32, 32, 192], P(None, 'img', 'row'), may hold values from -6 to 6
- valid_rows: int32 [8, 4], P(None, 'img'), may hold values from 17 to 32, as said below
- valid_cols: int32 [8, 4], P(None, 'img'), may hold values from 17 to 32, as said below
- first_reduce: bfloat16 [192, 512], replicated, may hold values from -0.4375 to 0.4375
- first_reduce_gain: bfloat16 [512], replicated, may hold values from 0.5 to 1.5
- first_reduce_shift: bfloat16 [512], replicated, may hold values from -3 to 3
- first_groups: bfloat16 [9, 8, 64, 64], replicated, may hold values from -0.25 to 0.25
- first_groups_gain: bfloat16 [512], replicated, may hold values from 0.5 to 1.5
- first_groups_shift: bfloat16 [512], replicated, may hold values from -3 to 3
- first_squeeze: bfloat16 [512, 48], replicated, may hold values from -0.75 to 0.75
- first_squeeze_bias: bfloat16 [48], replicated, may hold values from -3 to 3
- first_excite: bfloat16 [48, 512], replicated, may hold values from -1.75 to 1.75
- first_excite_bias: bfloat16 [512], replicated, may hold values from -4 to 4
- first_expand: bfloat16 [512, 512], replicated, may hold values from -0.25 to 0.25
- first_expand_gain: bfloat16 [512], replicated, may hold values from 0.5 to 1.5
- first_expand_shift: bfloat16 [512], replicated, may hold values from -3 to 3
- first_shortcut: bfloat16 [192, 512], replicated, may hold values from -0.4375 to 0.4375
- first_shortcut_gain: bfloat16 [512], replicated, may hold values from 0.5 to 1.5
- first_shortcut_shift: bfloat16 [512], replicated, may hold values from -3 to 3
- second_reduce: bfloat16 [512, 512], replicated, may hold values from -0.25 to 0.25
- second_reduce_gain: bfloat16 [512], replicated, may hold values from 0.5 to 1.5
- second_reduce_shift: bfloat16 [512], replicated, may hold values from -3 to 3
- second_groups: bfloat16 [9, 8, 64, 64], replicated, may hold values from -0.25 to 0.25
- second_groups_gain: bfloat16 [512], replicated, may hold values from 0.5 to 1.5
- second_groups_shift: bfloat16 [512], replicated, may hold values from -3 to 3
- second_squeeze: bfloat16 [512, 128], replicated, may hold values from -0.75 to 0.75
- second_squeeze_bias: bfloat16 [128], replicated, may hold values from -3 to 3
- second_excite: bfloat16 [128, 512], replicated, may hold values from -1 to 1
- second_excite_bias: bfloat16 [512], replicated, may hold values from -4 to 4
- second_expand: bfloat16 [512, 512], replicated, may hold values from -0.25 to 0.25
- second_expand_gain: bfloat16 [512], replicated, may hold values from 0.5 to 1.5
- second_expand_shift: bfloat16 [512], replicated, may hold values from -3 to 3
- output_grad: bfloat16 [8, 4, 16, 16, 512], P(None, 'img', 'row'), may hold values from -6 to 6
Outputs:
- activations: bfloat16 [2, 8, 4, 16, 16, 512], P('section', None, 'img', 'row')
- input_gradient: bfloat16 [8, 4, 32, 32, 192], P(None, 'img', 'row', None, 'section')
- grad_first_reduce: float32 [192, 512], replicated
- grad_first_reduce_gain: float32 [512], replicated
- grad_first_reduce_shift: float32 [512], replicated
- grad_first_groups: float32 [9, 8, 64, 64], replicated
- grad_first_groups_gain: float32 [512], replicated
- grad_first_groups_shift: float32 [512], replicated
- grad_first_squeeze: float32 [512, 48], replicated
- grad_first_squeeze_bias: float32 [48], replicated
- grad_first_excite: float32 [48, 512], replicated
- grad_first_excite_bias: float32 [512], replicated
- grad_first_expand: float32 [512, 512], replicated
- grad_first_expand_gain: float32 [512], replicated
- grad_first_expand_shift: float32 [512], replicated
- grad_first_shortcut: float32 [192, 512], replicated
- grad_first_shortcut_gain: float32 [512], replicated
- grad_first_shortcut_shift: float32 [512], replicated
- grad_second_reduce: float32 [512, 512], replicated
- grad_second_reduce_gain: float32 [512], replicated
- grad_second_reduce_shift: float32 [512], replicated
- grad_second_groups: float32 [9, 8, 64, 64], replicated
- grad_second_groups_gain: float32 [512], replicated
- grad_second_groups_shift: float32 [512], replicated
- grad_second_squeeze: float32 [512, 128], replicated
- grad_second_squeeze_bias: float32 [128], replicated
- grad_second_excite: float32 [128, 512], replicated
- grad_second_excite_bias: float32 [512], replicated
- grad_second_expand: float32 [512, 512], replicated
- grad_second_expand_gain: float32 [512], replicated
- grad_second_expand_shift: float32 [512], replicated
The draws below stay inside these ranges and needn't reach their ends.
Inputs may be any that keep to these rules, and one draw needn't show every extreme that they name: `valid_rows`: in every micro-batch at least one image has all 32 rows valid. `valid_cols`: in every micro-batch at least one image has all 32 columns valid.
All inputs are finite; a program needn't handle non-finite values.
Results may differ from the reference program's by a relative error of at most 0.023.
Values may be sent and summed in bfloat16 or wider, within the bound.
A program may use at most 128 MiB of HBM per device.

```python
import jax
import jax.numpy as jnp
from jax import lax

CIN = 192
COUT = 512
GWIDTH = 64
SQ_ONE = 48
SQ_TWO = 128
GROUPS = 8
HEIGHT = 32
WIDTH = 32
MICRO = 8
NI = 4


def bounded_sizes(key, top):
    draw_key, pick_key = jax.random.split(key)
    sizes = jax.random.randint(draw_key, (MICRO, NI), top // 2 + 1, top + 1)
    chosen = jax.random.randint(pick_key, (MICRO, 1), 0, NI)
    positions = jnp.arange(NI)[None, :]
    return jnp.where(positions == chosen, top, sizes).astype(jnp.int32)


def draw_valid_rows(key, part):
    key = jax.random.fold_in(key, 11)
    return bounded_sizes(key, HEIGHT)


def draw_valid_cols(key, part):
    key = jax.random.fold_in(key, 23)
    return bounded_sizes(key, WIDTH)


def block_scale(rng, shape, cuts, least, largest):
    factor_of, own = 1.0, jax.random.fold_in(rng, 6)
    for axis_at, parts in cuts:
        draws = jnp.exp(jax.random.uniform(jax.random.fold_in(own, axis_at), (parts,), jnp.float32, least / len(cuts), largest / len(cuts)))
        factor_of = factor_of * jnp.repeat(draws, shape[axis_at] // parts).reshape([-1 if axis == axis_at else 1 for axis in range(len(shape))])
    return factor_of


def gaussian(own_key, extent, deviation, bound, shards=(), kind=jnp.bfloat16):
    values = deviation * jax.random.normal(own_key, extent, jnp.float32)
    if shards:
        values = values * block_scale(own_key, extent, shards, -0.22, 0.18)
    return jnp.clip(values, -bound, bound).astype(kind)


def setup_inputs(seed: int = 0) -> dict:
    arg_keys = jax.random.split(jax.random.key(seed), 34)
    return {
        "input_maps": gaussian(arg_keys[0], (MICRO, NI, HEIGHT, WIDTH, CIN), 1.0, 6.0, ((1, 4), (2, 4))),
        "valid_rows": draw_valid_rows(jax.random.fold_in(arg_keys[33], 71), 0),
        "valid_cols": draw_valid_cols(jax.random.fold_in(arg_keys[33], 71), 0),
        "first_reduce": gaussian(arg_keys[3], (CIN, COUT), CIN ** -0.5, 0.4375),
        "first_reduce_gain": jnp.clip(1.0 + 0.1 * jax.random.normal(arg_keys[4], (COUT,), jnp.float32), 0.5, 1.5).astype(jnp.bfloat16),
        "first_reduce_shift": gaussian(arg_keys[5], (COUT,), 0.5, 3.0),
        "first_groups": gaussian(arg_keys[6], (9, GROUPS, GWIDTH, GWIDTH), (9 * GWIDTH) ** -0.5, 0.25),
        "first_groups_gain": jnp.clip(1.0 + 0.1 * jax.random.normal(arg_keys[7], (COUT,), jnp.float32), 0.5, 1.5).astype(jnp.bfloat16),
        "first_groups_shift": gaussian(arg_keys[8], (COUT,), 0.5, 3.0),
        "first_squeeze": gaussian(arg_keys[9], (COUT, SQ_ONE), (COUT // 8) ** -0.5, 0.75),
        "first_squeeze_bias": gaussian(arg_keys[10], (SQ_ONE,), 0.5, 3.0),
        "first_excite": gaussian(arg_keys[11], (SQ_ONE, COUT), (SQ_ONE // 4) ** -0.5, 1.75),
        "first_excite_bias": gaussian(arg_keys[12], (COUT,), 1.0, 4.0),
        "first_expand": gaussian(arg_keys[13], (COUT, COUT), COUT ** -0.5, 0.25),
        "first_expand_gain": jnp.clip(1.0 + 0.1 * jax.random.normal(arg_keys[14], (COUT,), jnp.float32), 0.5, 1.5).astype(jnp.bfloat16),
        "first_expand_shift": gaussian(arg_keys[15], (COUT,), 0.5, 3.0),
        "first_shortcut": gaussian(arg_keys[16], (CIN, COUT), CIN ** -0.5, 0.4375),
        "first_shortcut_gain": jnp.clip(1.0 + 0.1 * jax.random.normal(arg_keys[17], (COUT,), jnp.float32), 0.5, 1.5).astype(jnp.bfloat16),
        "first_shortcut_shift": gaussian(arg_keys[18], (COUT,), 0.5, 3.0),
        "second_reduce": gaussian(arg_keys[19], (COUT, COUT), COUT ** -0.5, 0.25),
        "second_reduce_gain": jnp.clip(1.0 + 0.1 * jax.random.normal(arg_keys[20], (COUT,), jnp.float32), 0.5, 1.5).astype(jnp.bfloat16),
        "second_reduce_shift": gaussian(arg_keys[21], (COUT,), 0.5, 3.0),
        "second_groups": gaussian(arg_keys[22], (9, GROUPS, GWIDTH, GWIDTH), (9 * GWIDTH) ** -0.5, 0.25),
        "second_groups_gain": jnp.clip(1.0 + 0.1 * jax.random.normal(arg_keys[23], (COUT,), jnp.float32), 0.5, 1.5).astype(jnp.bfloat16),
        "second_groups_shift": gaussian(arg_keys[24], (COUT,), 0.5, 3.0),
        "second_squeeze": gaussian(arg_keys[25], (COUT, SQ_TWO), (COUT // 8) ** -0.5, 0.75),
        "second_squeeze_bias": gaussian(arg_keys[26], (SQ_TWO,), 0.5, 3.0),
        "second_excite": gaussian(arg_keys[27], (SQ_TWO, COUT), (SQ_TWO // 4) ** -0.5, 1.0),
        "second_excite_bias": gaussian(arg_keys[28], (COUT,), 1.0, 4.0),
        "second_expand": gaussian(arg_keys[29], (COUT, COUT), COUT ** -0.5, 0.25),
        "second_expand_gain": jnp.clip(1.0 + 0.1 * jax.random.normal(arg_keys[30], (COUT,), jnp.float32), 0.5, 1.5).astype(jnp.bfloat16),
        "second_expand_shift": gaussian(arg_keys[31], (COUT,), 0.5, 3.0),
        "output_grad": gaussian(arg_keys[32], (MICRO, NI, HEIGHT // 2, WIDTH // 2, COUT), 1.0, 6.0, ((1, 4), (2, 4))),
    }


epsilon = 1e-05
highest = lax.Precision.HIGHEST

@jax.custom_vjp
def low(v):
    return lax.optimization_barrier(v.astype(jnp.bfloat16)).astype(jnp.float32)

@jax.custom_vjp
def low_back(v):
    return v

def low_keep(v):
    return (low(v), None)

def low_pass(kept, grad):
    return (grad,)

def back_keep(v):
    return (v, None)

def back_low(kept, grad):
    return (low(grad),)
low.defvjp(low_keep, low_pass)
low_back.defvjp(back_keep, back_low)

def grid_masks(heights, widths):
    row_ids = jnp.arange(HEIGHT, dtype=jnp.int32)
    col_ids = jnp.arange(WIDTH, dtype=jnp.int32)
    full = (row_ids[None, :, None] < heights[:, None, None]) & (col_ids[None, None, :] < widths[:, None, None])
    half_rows = 2 * jnp.arange(HEIGHT // 2, dtype=jnp.int32)
    half_cols = 2 * jnp.arange(WIDTH // 2, dtype=jnp.int32)
    half = (half_rows[None, :, None] < heights[:, None, None]) & (half_cols[None, None, :] < widths[:, None, None])
    return (full.astype(jnp.float32)[..., None], half.astype(jnp.float32)[..., None])

def normalize(field, mask, gain, shift):
    count = jnp.sum(mask)
    mean = lax.optimization_barrier(jnp.sum(field * mask, axis=(0, 1, 2))) / count
    var = lax.optimization_barrier(jnp.sum(field * field * mask, axis=(0, 1, 2))) / count - mean * mean
    return (field - mean) * lax.rsqrt(var + epsilon) * gain + shift

def pointwise(field, weight):
    return jnp.einsum('nhwc,cd->nhwd', field, weight, precision=highest)

def group_conv(field, weight, stride):
    images, rows, cols, width = field.shape
    out_rows, out_cols = (rows // stride, cols // stride)
    groups = weight.shape[1]
    padded = jnp.pad(field, ((0, 0), (1, 1), (1, 1), (0, 0)))
    result = jnp.zeros((images, out_rows, out_cols, groups, width // groups), jnp.float32)
    for position in range(9):
        down, across = (position // 3, position % 3)
        piece = padded[:, down:down + stride * out_rows:stride, across:across + stride * out_cols:stride, :]
        piece = piece.reshape(images, out_rows, out_cols, groups, width // groups)
        result = result + jnp.einsum('npqgc,gcd->npqgd', piece, weight[position], precision=highest)
    return result.reshape(images, out_rows, out_cols, width)

def excite(hidden, mask, squeeze_w, squeeze_bias, excite_w, excite_bias):
    pixels = lax.optimization_barrier(jnp.sum(mask, axis=(1, 2)))
    pooled = lax.optimization_barrier(jnp.sum(hidden, axis=(1, 2))) / pixels
    inner = jax.nn.silu(jnp.dot(pooled, squeeze_w, precision=highest) + squeeze_bias)
    gate = jax.nn.sigmoid(jnp.dot(inner, excite_w, precision=highest) + excite_bias)
    return hidden * gate[:, None, None, :]

def first_block(maps, full, half, weights):
    reduce_w, reduce_gain, reduce_shift, groups_w, groups_gain, groups_shift, squeeze_w, squeeze_bias, excite_w, excite_bias, expand_w, expand_gain, expand_shift, shortcut_w, shortcut_gain, shortcut_shift = weights
    reduced = low_back(pointwise(maps, reduce_w))
    act = low(full * jax.nn.silu(normalize(reduced, full, reduce_gain, reduce_shift)))
    conv = low(low_back(group_conv(act, groups_w, 2)))
    hidden = half * jax.nn.silu(normalize(conv, half, groups_gain, groups_shift))
    gated = low(low_back(excite(hidden, half, squeeze_w, squeeze_bias, excite_w, excite_bias)))
    expanded = low_back(pointwise(gated, expand_w))
    shortcut = low_back(pointwise(maps[:, ::2, ::2, :], shortcut_w))
    summed = normalize(expanded, half, expand_gain, expand_shift) + normalize(shortcut, half, shortcut_gain, shortcut_shift)
    return low(low_back(half * jax.nn.silu(summed)))

def second_block(entry, half, weights):
    reduce_w, reduce_gain, reduce_shift, groups_w, groups_gain, groups_shift, squeeze_w, squeeze_bias, excite_w, excite_bias, expand_w, expand_gain, expand_shift = weights
    reduced = low_back(pointwise(entry, reduce_w))
    act = low(half * jax.nn.silu(normalize(reduced, half, reduce_gain, reduce_shift)))
    conv = low(low_back(group_conv(act, groups_w, 1)))
    hidden = half * jax.nn.silu(normalize(conv, half, groups_gain, groups_shift))
    gated = low(low_back(excite(hidden, half, squeeze_w, squeeze_bias, excite_w, excite_bias)))
    expanded = low_back(pointwise(gated, expand_w))
    return half * jax.nn.silu(normalize(expanded, half, expand_gain, expand_shift) + entry)

def reference(input_maps, valid_rows, valid_cols, first_reduce, first_reduce_gain, first_reduce_shift, first_groups, first_groups_gain, first_groups_shift, first_squeeze, first_squeeze_bias, first_excite, first_excite_bias, first_expand, first_expand_gain, first_expand_shift, first_shortcut, first_shortcut_gain, first_shortcut_shift, second_reduce, second_reduce_gain, second_reduce_shift, second_groups, second_groups_gain, second_groups_shift, second_squeeze, second_squeeze_bias, second_excite, second_excite_bias, second_expand, second_expand_gain, second_expand_shift, output_grad):
    first = tuple((weight.astype(jnp.float32) for weight in (first_reduce, first_reduce_gain, first_reduce_shift, first_groups, first_groups_gain, first_groups_shift, first_squeeze, first_squeeze_bias, first_excite, first_excite_bias, first_expand, first_expand_gain, first_expand_shift, first_shortcut, first_shortcut_gain, first_shortcut_shift)))
    second = tuple((weight.astype(jnp.float32) for weight in (second_reduce, second_reduce_gain, second_reduce_shift, second_groups, second_groups_gain, second_groups_shift, second_squeeze, second_squeeze_bias, second_excite, second_excite_bias, second_expand, second_expand_gain, second_expand_shift)))

    def micro_step(totals, operands):
        image, heights, widths, cotangent = operands
        full, half = grid_masks(heights, widths)

        def forward(first_weights, second_weights, maps):
            entry = first_block(maps, full, half, first_weights)
            return (second_block(entry, half, second_weights), entry)
        output, pull, entry = jax.vjp(forward, first, second, image.astype(jnp.float32), has_aux=True)
        first_grads, second_grads, image_grad = pull(cotangent.astype(jnp.float32))
        totals = jax.tree.map(lambda older, newer: older + newer, totals, (first_grads, second_grads))
        return (totals, (entry.astype(jnp.bfloat16), output.astype(jnp.bfloat16), image_grad.astype(jnp.bfloat16)))
    zeros = jax.tree.map(jnp.zeros_like, (first, second))
    (first_totals, second_totals), (entries, outputs, image_grads) = lax.scan(micro_step, zeros, (input_maps, valid_rows, valid_cols, output_grad))
    activations = jnp.stack([entries, outputs])
    return (activations, image_grads, first_totals[0], first_totals[1], first_totals[2], first_totals[3], first_totals[4], first_totals[5], first_totals[6], first_totals[7], first_totals[8], first_totals[9], first_totals[10], first_totals[11], first_totals[12], first_totals[13], first_totals[14], first_totals[15], second_totals[0], second_totals[1], second_totals[2], second_totals[3], second_totals[4], second_totals[5], second_totals[6], second_totals[7], second_totals[8], second_totals[9], second_totals[10], second_totals[11], second_totals[12])
```

```python
import jax
import jax.numpy as jnp
from jax import lax
from jax.sharding import PartitionSpec as P

epsilon = 1e-05
highest = lax.Precision.HIGHEST
f32 = jnp.float32
bf16 = jnp.bfloat16


def slope(pre):
    sigma = jax.nn.sigmoid(pre)
    return sigma * (1.0 + pre * (1.0 - sigma))


def dot(left, right):
    return jnp.dot(left, right, preferred_element_type=f32)


def dot_nt(left, right):
    return lax.dot_general(left, right, (((1,), (1,)), ((), ())), preferred_element_type=f32)


def dot_tn(left, right):
    return lax.dot_general(left, right, (((0,), (0,)), ((), ())), preferred_element_type=f32)


def block_diagonal(weights):
    taps, groups, width, _ = weights.shape
    four = weights.reshape(taps, groups // 4, 4, width, 1, width)
    eye = jnp.eye(4, dtype=weights.dtype).reshape(1, 1, 4, 1, 4, 1)
    return (four * eye).reshape(taps, groups // 4, 4 * width, 4 * width)


def diagonal_blocks(full, groups):
    taps, halves, wide, _ = full.shape
    width = wide // 4
    parts = full.reshape(taps, halves, 4, width, 4, width)
    picked = jnp.stack([parts[:, :, j, :, j, :] for j in range(4)], axis=2)
    return picked.reshape(taps, groups, width, width)


def moved(field, down, across):
    rows, cols, _ = field.shape
    field = jnp.pad(field, ((1, 1), (1, 1), (0, 0)))
    return field[1 + down : 1 + down + rows, 1 + across : 1 + across + cols]


def apply_groups(taps, blocks):
    halves = []
    for h in range(2):
        total = 0.0
        for t, tap in enumerate(taps):
            total = total + dot(tap[:, 256 * h : 256 * h + 256], blocks[t, h])
        halves.append(total)
    return jnp.concatenate(halves, axis=1)


def groups_grad(taps, gradient):
    return jnp.stack(
        [
            jnp.stack(
                [
                    dot_tn(tap[:, 256 * h : 256 * h + 256], gradient[:, 256 * h : 256 * h + 256])
                    for h in range(2)
                ]
            )
            for tap in taps
        ]
    )


def back_groups(pairs, blocks):
    halves = []
    for h in range(2):
        total = 0.0
        for t, gradient in pairs:
            total = total + dot_nt(gradient[:, 256 * h : 256 * h + 256], blocks[t, h])
        halves.append(total)
    return jnp.concatenate(halves, axis=1)


def forward_norm(fields, masks, total, count, gains, shifts):
    outs = []
    pieces = []
    for field, mask in zip(fields, masks):
        pieces.append(sum(jnp.sum(part * m, axis=0) for part, m in zip(field, mask)))
        pieces.append(sum(jnp.sum(part * part * m, axis=0) for part, m in zip(field, mask)))
    totals = total(jnp.stack(pieces))
    for k, field in enumerate(fields):
        mean = totals[2 * k] / count
        scale = lax.rsqrt(totals[2 * k + 1] / count - mean * mean + epsilon)
        centred = [(part - mean) * scale for part in field]
        outs.append((centred, scale, [c * gains[k] + shifts[k] for c in centred]))
    return outs


def backward_norm(gradients, saved, masks, total, count, gains):
    pieces = []
    for gradient, (centred, scale, _) in zip(gradients, saved):
        pieces.append(sum(jnp.sum(g, axis=0) for g in gradient))
        pieces.append(sum(jnp.sum(g * c, axis=0) for g, c in zip(gradient, centred)))
    totals = total(jnp.stack(pieces))
    results = []
    for k, (gradient, (centred, scale, _)) in enumerate(zip(gradients, saved)):
        results.append(
            [
                (
                    gains[k]
                    * scale
                    * (g - m * (totals[2 * k] + c * totals[2 * k + 1]) / count)
                ).astype(bf16)
                for g, c, m in zip(gradient, centred, masks)
            ]
        )
    return results, pieces


def excite_forward(conv, half, pixels, count, total, weights):
    gain, shift, squeeze_w, squeeze_bias, excite_w, excite_bias = weights
    ((centred, scale, normed),) = forward_norm(((conv,),), ((half,),), total, count, (gain,), (shift,))
    saved = (centred, scale, normed)
    hidden = half * jax.nn.silu(normed[0])
    pooled = jnp.sum(hidden, axis=0, keepdims=True) / pixels
    pre = jnp.dot(pooled, squeeze_w, precision=highest) + squeeze_bias
    inner = jax.nn.silu(pre)
    gate = jax.nn.sigmoid(jnp.dot(inner, excite_w, precision=highest) + excite_bias)
    return (hidden * gate).astype(bf16), (saved, hidden, pooled, pre, inner, gate)


def excite_backward(incoming, kept, half, pixels, count, total, weights):
    gain, shift, squeeze_w, squeeze_bias, excite_w, excite_bias = weights
    saved, hidden, pooled, pre, inner, gate = kept
    incoming = incoming.astype(f32)
    dgate = jnp.sum(incoming * hidden, axis=0, keepdims=True)
    dpre = dgate * gate * (1.0 - gate)
    dsq = jnp.dot(dpre, excite_w.T, precision=highest) * slope(pre)
    dpool = jnp.dot(dsq, squeeze_w.T, precision=highest)
    dhidden = incoming * gate + dpool / pixels
    gradient = dhidden * half * slope(saved[2][0])
    ((dconv,),), parts = backward_norm(((gradient,),), (saved,), (half,), total, count, (gain,))
    grads = (
        parts[1],
        parts[0],
        pooled.T * dsq,
        dsq[0],
        inner.T * dpre,
        dpre[0],
    )
    return dconv, grads


PHASES = ((0, 0), (0, 1), (1, 0), (1, 1))


def local_step(x, rows_valid, cols_valid, cotangent, first, second, total):
    (w1, g1, b1, k1, gg1, gb1, sq1, sqb1, ex1, exb1, e1, eg1, eb1, s1, sg1, sb1) = first
    (w2, g2, b2, k2, gg2, gb2, sq2, sqb2, ex2, exb2, e2, eg2, eb2) = second
    side = x.shape[0] // 2
    cin = x.shape[2]
    width = w1.shape[1]
    pixels_all = side * side
    up = lambda v: v.astype(f32)
    phases = x.reshape(side, 2, side, 2, cin).transpose(1, 3, 0, 2, 4).reshape(4, pixels_all, cin)
    p_id = jnp.arange(side)[:, None]
    q_id = jnp.arange(side)[None, :]
    full = [
        ((2 * p_id + a < rows_valid) & (2 * q_id + b < cols_valid)).astype(f32).reshape(pixels_all, 1)
        for a, b in PHASES
    ]
    half = full[0]
    local_full = (rows_valid * cols_valid).astype(f32)
    pixels = (((rows_valid + 1) // 2) * ((cols_valid + 1) // 2)).astype(f32)
    counts = total(jnp.stack([local_full, pixels]))
    count_full, count = counts[0], counts[1]

    reduced = [dot(phases[k], w1) for k in range(4)]
    (saved_a,) = forward_norm((reduced,), (full,), total, count_full, (up(g1),), (up(b1),))
    act = [
        (m * jax.nn.silu(n)).astype(bf16).reshape(side, side, width)
        for m, n in zip(full, saved_a[2])
    ]
    taps1 = []
    for t in range(9):
        u, v = t // 3, t % 3
        source = act[2 * (u != 1) + (v != 1)]
        taps1.append(
            moved(source, -1 if u == 0 else 0, -1 if v == 0 else 0).reshape(pixels_all, width)
        )
    blocks1 = block_diagonal(k1)
    conv1 = apply_groups(taps1, blocks1).astype(bf16).astype(f32)
    ew1 = (up(gg1), up(gb1), up(sq1), up(sqb1), up(ex1), up(exb1))
    gated1, kept1 = excite_forward(conv1, half, pixels, count, total, ew1)
    expanded1 = dot(gated1, e1)
    shortcut = dot(phases[0], s1)
    saved_e, saved_s = forward_norm(
        ((expanded1,), (shortcut,)),
        ((half,), (half,)),
        total,
        count,
        (up(eg1), up(sg1)),
        (up(eb1), up(sb1)),
    )
    sum1 = saved_e[2][0] + saved_s[2][0]
    entry = (half * jax.nn.silu(sum1)).astype(bf16)

    reduced2 = dot(entry, w2)
    (saved_a2,) = forward_norm(((reduced2,),), ((half,),), total, count, (up(g2),), (up(b2),))
    act2 = (half * jax.nn.silu(saved_a2[2][0])).astype(bf16).reshape(side, side, width)
    taps2 = [moved(act2, t // 3 - 1, t % 3 - 1).reshape(pixels_all, width) for t in range(9)]
    blocks2 = block_diagonal(k2)
    conv2 = apply_groups(taps2, blocks2).astype(bf16).astype(f32)
    ew2 = (up(gg2), up(gb2), up(sq2), up(sqb2), up(ex2), up(exb2))
    gated2, kept2 = excite_forward(conv2, half, pixels, count, total, ew2)
    expanded2 = dot(gated2, e2)
    (saved_e2,) = forward_norm(((expanded2,),), ((half,),), total, count, (up(eg2),), (up(eb2),))
    sum2 = saved_e2[2][0] + up(entry)
    leave = (half * jax.nn.silu(sum2)).astype(bf16)

    dsum2 = up(cotangent) * half * slope(sum2)
    ((dexp2,),), parts_e2 = backward_norm(((dsum2,),), (saved_e2,), (half,), total, count, (up(eg2),))
    de2 = dot_tn(gated2, dexp2)
    dgated2 = dot_nt(dexp2, e2).astype(bf16)
    dconv2, xgrads2 = excite_backward(dgated2, kept2, half, pixels, count, total, ew2)
    dk2 = groups_grad(taps2, dconv2)
    dconv2_3 = dconv2.reshape(side, side, width)
    dact2 = back_groups(
        [
            (t, moved(dconv2_3, 1 - t // 3, 1 - t % 3).reshape(pixels_all, width))
            for t in range(9)
        ],
        blocks2,
    )
    gradient = dact2 * half * slope(saved_a2[2][0])
    ((dred2,),), parts_a2 = backward_norm(((gradient,),), (saved_a2,), (half,), total, count, (up(g2),))
    dw2 = dot_tn(entry, dred2)
    dentry = (dsum2 + dot_nt(dred2, w2)).astype(bf16)

    dsum1 = up(dentry) * half * slope(sum1)
    ((dexp1,), (dshort,)), parts_e1 = backward_norm(
        ((dsum1,), (dsum1,)), (saved_e, saved_s), (half,), total, count, (up(eg1), up(sg1))
    )
    de1 = dot_tn(gated1, dexp1)
    ds1 = dot_tn(phases[0], dshort)
    dgated1 = dot_nt(dexp1, e1).astype(bf16)
    dconv1, xgrads1 = excite_backward(dgated1, kept1, half, pixels, count, total, ew1)
    dk1 = groups_grad(taps1, dconv1)
    dconv1_3 = dconv1.reshape(side, side, width)
    gradient = []
    for k, (a, b) in enumerate(PHASES):
        pairs = []
        for t in range(9):
            u, v = t // 3, t % 3
            if (u != 1) == bool(a) and (v != 1) == bool(b):
                pairs.append(
                    (t, moved(dconv1_3, int(u == 0), int(v == 0)).reshape(pixels_all, width))
                )
        gradient.append(back_groups(pairs, blocks1) * full[k] * slope(saved_a[2][k]))
    (dred1,), parts_a1 = backward_norm((gradient,), (saved_a,), full, total, count_full, (up(g1),))
    dw1 = sum(dot_tn(phases[k], dred1[k]) for k in range(4))
    dx = [dot_nt(dred1[k], w1) for k in range(4)]
    dx[0] = dx[0] + dot_nt(dshort, s1)
    dx = jnp.stack(dx).astype(bf16).reshape(2, 2, side, side, cin)
    dx = dx.transpose(2, 0, 3, 1, 4).reshape(2 * side, 2 * side, cin)
    grads = (
        dw1, parts_a1[1], parts_a1[0], diagonal_blocks(dk1, k1.shape[1]), *xgrads1,
        de1, parts_e1[1], parts_e1[0], ds1, parts_e1[3], parts_e1[2],
        dw2, parts_a2[1], parts_a2[0], diagonal_blocks(dk2, k2.shape[1]), *xgrads2,
        de2, parts_e2[1], parts_e2[0],
    )
    return entry.reshape(side, side, width), leave.reshape(side, side, width), dx, grads


def body(input_maps, valid_rows, valid_cols, *rest):
    weights, output_grad = rest[:-1], rest[-1]
    first, second = weights[:16], weights[16:]
    micro = input_maps.shape[0]
    sections, row_count = lax.axis_size("section"), lax.axis_size("row")
    section, row = lax.axis_index("section"), lax.axis_index("row")
    each = micro // sections
    copies = row_count // each
    mine = section * each + row // copies
    lead = (row % copies == 0).astype(f32)

    def gather(field):
        half = lax.dynamic_slice_in_dim(field, section * each, each, 0)
        half = jnp.repeat(half, copies, axis=0) if copies > 1 else half
        return lax.all_to_all(half, "row", split_axis=0, concat_axis=2, tiled=True)[0, 0]

    def scatter(field):
        rows = field.shape[0] // row_count
        parts = field.reshape((row_count, rows) + field.shape[1:])
        parts = lax.all_to_all(parts, "row", split_axis=0, concat_axis=0, tiled=True)
        return parts[::copies]

    def total(values):
        return lax.psum(values, "img")

    x = gather(input_maps)
    cotangent = gather(output_grad)
    pixels = cotangent.shape[0] * cotangent.shape[1]
    heights = lax.dynamic_index_in_dim(valid_rows, mine, 0, keepdims=False)[0]
    widths = lax.dynamic_index_in_dim(valid_cols, mine, 0, keepdims=False)[0]
    entry, leave, dx, grads = local_step(
        x, heights, widths, cotangent.reshape(pixels, -1), first, second, total
    )
    flat = jnp.concatenate([grad.reshape(-1) for grad in grads]) * lead
    flat = lax.psum(flat, ("section", "img", "row"))
    totals = []
    start = 0
    for weight in weights:
        totals.append(flat[start : start + weight.size].reshape(weight.shape))
        start += weight.size

    leading = section == 0
    swap = [(0, 1), (1, 0)]

    def across(kept, sent):
        kept, sent = scatter(kept), scatter(sent)
        got = lax.ppermute(sent, "section", swap)
        return jnp.where(
            leading, jnp.concatenate([kept, got]), jnp.concatenate([got, kept])
        )[:, None]

    activations = across(jnp.where(leading, entry, leave), jnp.where(leading, leave, entry))
    low, high = jnp.split(dx, 2, axis=-1)
    input_gradient = across(jnp.where(leading, low, high), jnp.where(leading, high, low))
    return (activations[None], input_gradient, *totals)


def solution(mesh):
    tiled = P(None, "img", "row", None, None)
    image = P(None, "img")
    return jax.shard_map(
        body,
        mesh=mesh,
        in_specs=(tiled, image, image) + (P(),) * 29 + (tiled,),
        out_specs=(
            P("section", None, "img", "row", None, None),
            P(None, "img", "row", None, "section"),
        )
        + (P(),) * 29,
        check_vma=False,
    )
```

```python
import functools

import jax
import jax.numpy as jnp
from jax import lax
from jax.experimental import pallas as pl
from jax.experimental.pallas import tpu as pltpu
from jax.sharding import PartitionSpec as P

epsilon = 1e-05
f32 = jnp.float32
bf16 = jnp.bfloat16
MESH = pl.DeviceIdType.MESH
PHASES = ((0, 0), (0, 1), (1, 0), (1, 1))
EXCHANGES = 12
NAMES = (
    "g1", "b1", "gg1", "gb1", "exb1", "eg1", "eb1", "sg1", "sb1", "sqb1",
    "g2", "b2", "gg2", "gb2", "exb2", "eg2", "eb2", "sqb2",
)
VEC = {name: k for k, name in enumerate(NAMES)}
VEC_ROWS = 32


def grad_rows(cin, width, taps, group, sq1, sq2):
    parts = (
        ("e2", width), ("k2", taps * group), ("sq2", sq2), ("ex2", sq2), ("w2", width),
        ("e1", width), ("s1", cin), ("k1", taps * group), ("sq1", sq1), ("ex1", sq1),
        ("w1", cin), ("vec", VEC_ROWS),
    )
    starts, at = {}, 0
    for name, rows in parts:
        starts[name] = at
        at += rows
    return starts, at


def sigmoid(v):
    return 0.5 * jnp.tanh(0.5 * v) + 0.5


def silu(v):
    return v * sigmoid(v)


def slope(v):
    s = sigmoid(v)
    return s * (1.0 + v * (1.0 - s))


def dot(left, right):
    return jnp.dot(left, right, preferred_element_type=f32)


def dot_nt(left, right):
    return lax.dot_general(left, right, (((1,), (1,)), ((), ())), preferred_element_type=f32)


def dot_tn(left, right):
    return lax.dot_general(left, right, (((0,), (0,)), ((), ())), preferred_element_type=f32)


def parts_of(v):
    high = v.astype(bf16).astype(f32)
    return high, v - high


def stacked(rows, width):
    ids = lax.broadcasted_iota(jnp.int32, (16, width), 0)
    total = jnp.zeros((16, width), f32)
    for k, row in enumerate(rows):
        total = jnp.where(ids == k, jnp.broadcast_to(row, (16, width)), total)
    return total.astype(bf16)


def small_dot(row, weight, form):
    out = form(stacked(parts_of(row), row.shape[1]), weight)
    return out[0:1] + out[1:2]


def small_outer(left, right):
    lh, ll = parts_of(left)
    rh, rl = parts_of(right)
    return dot_tn(
        stacked((lh, ll, lh, ll), left.shape[1]), stacked((rh, rh, rl, rl), right.shape[1])
    )


def fold(v):
    return v[0:8] + v[8:16]


def column(acc):
    return jnp.sum(acc, axis=0, keepdims=True)


class Plan:
    def __init__(self, mesh_sizes, args):
        self.S, self.I, self.R = mesh_sizes
        x, og, w1, k1, sq1, sq2 = args
        self.M, _, self.rows, self.cols, self.cin = x
        _, _, self.hrows, self.side, self.width = og
        self.taps, self.groups, self.gw, _ = k1
        self.q1, self.q2 = sq1[1], sq2[1]
        self.each = self.M // self.S
        self.copies = self.R // self.each
        self.pix = self.side * self.side
        self.starts, self.total_rows = grad_rows(
            self.cin, self.width, self.taps, self.gw, self.q1, self.q2
        )


def main_kernel(plan, names, *refs):
    ref = dict(zip(names, refs))
    S, I, R = plan.S, plan.I, plan.R
    side, width, pix, cin = plan.side, plan.width, plan.pix, plan.cin
    half_width = width // 2
    s, i, r = lax.axis_index("section"), lax.axis_index("img"), lax.axis_index("row")
    mine = s * plan.each + r // plan.copies
    waits = []

    barrier = pltpu.get_barrier_semaphore()
    peers = []
    for ds in range(S):
        for dr in range(R):
            if ds or dr:
                peers.append((lax.rem(s + ds, S), i, lax.rem(r + dr, R)))
    for di in range(1, I):
        peers.append((s, lax.rem(i + di, I), r))
    for peer in peers:
        pl.semaphore_signal(barrier, inc=1, device_id=peer, device_id_type=MESH)

    own = []
    for name, rows in (("x", plan.rows), ("og", plan.hrows)):
        copy = pltpu.make_async_copy(
            ref[name].at[mine, 0],
            ref[name + "_in"].at[pl.ds(r * rows, rows)],
            ref[name + "_recv"].at[r],
        )
        copy.start()
        own.append(copy)
    pl.semaphore_wait(barrier, len(peers))
    for name, rows in (("x", plan.rows), ("og", plan.hrows)):
        for d in range(1, R):
            t = lax.rem(r + d, R)
            copy = pltpu.make_async_remote_copy(
                src_ref=ref[name].at[s * plan.each + t // plan.copies, 0],
                dst_ref=ref[name + "_in"].at[pl.ds(r * rows, rows)],
                send_sem=ref[name + "_send"].at[d - 1],
                recv_sem=ref[name + "_recv"].at[r],
                device_id=(s, i, t),
                device_id_type=MESH,
            )
            copy.start()
            waits.append(copy.wait_send)

    def arrived(name, rows, position):
        own[position].wait()
        for d in range(1, R):
            t = lax.rem(r + d, R)
            there = ref[name + "_in"].at[pl.ds(t * rows, rows)]
            pltpu.make_async_remote_copy(
                src_ref=there,
                dst_ref=there,
                send_sem=ref[name + "_send"].at[d - 1],
                recv_sem=ref[name + "_recv"].at[t],
                device_id=(s, i, t),
                device_id_type=MESH,
            ).wait_recv()

    st = ref["st"]

    def stats_copy(k, d, slot):
        return pltpu.make_async_remote_copy(
            src_ref=st.at[k, slot],
            dst_ref=st.at[k, slot],
            send_sem=ref["st_send"].at[k, d - 1],
            recv_sem=ref["st_recv"].at[k, slot],
            device_id=(s, lax.rem(i + d, I), r),
            device_id_type=MESH,
        )

    def post(k, rows):
        ids = lax.broadcasted_iota(jnp.int32, (8, width), 0)
        value = jnp.zeros((8, width), f32)
        for j, row in enumerate(rows):
            value = jnp.where(ids == j, jnp.broadcast_to(row, (8, width)), value)
        st[k, i] = value
        for d in range(1, I):
            stats_copy(k, d, i).start()

    def fetch(k):
        for d in range(1, I):
            stats_copy(k, d, i).wait_send()
            stats_copy(k, d, lax.rem(i + d, I)).wait_recv()
        value = st[k, 0]
        for j in range(1, I):
            value = value + st[k, j]
        return value

    vec = ref["vec"]

    def vector(name):
        return vec[VEC[name] : VEC[name] + 1]

    vr, vc = ref["vr"][mine, 0], ref["vc"][mine, 0]
    q_ids = lax.broadcasted_iota(jnp.int32, (side, width), 0)
    first_col, last_col = q_ids == 0, q_ids == side - 1
    cm = ref["cm"]
    for b in range(2):
        cm[b] = (2 * q_ids + b < vc).astype(f32)

    def mask_row(a, b, p):
        return cm[b] * (2 * p + a < vr).astype(f32)

    row_count = jnp.full((1, width), vr * vc, jnp.int32).astype(f32)
    half_count = jnp.full((1, width), ((vr + 1) // 2) * ((vc + 1) // 2), jnp.int32).astype(f32)

    def over_rows(step, *accs):
        init = tuple(jnp.zeros((8, width), f32) for _ in range(accs[0] if accs else 0))

        def run(p, carry):
            out = step(p)
            if not carry:
                return carry
            return tuple(c + fold(o) for c, o in zip(carry, out))

        return tuple(column(c) for c in lax.fori_loop(0, side, run, init, unroll=2))

    def full_dot(out, left, weight, form=dot):
        wide = out.shape[-1]
        step = min(256, wide)
        for h in range(wide // step):
            cut = slice(h * step, h * step + step)
            w = weight[:, cut] if form is dot else weight[cut, :]
            out[:, :, cut] = form(left, w).reshape(side, side, step).astype(out.dtype)

    def flat(value):
        return value.reshape(pix, value.shape[-1])

    def lines(ref_, start=0):
        return flat(ref_[start : start + side])

    G = ref["grads"]
    lead = None if plan.copies == 1 else (lax.rem(r, plan.copies) == 0).astype(f32)

    def put(name, value, offset=0):
        if lead is not None:
            value = value * lead
        at = plan.starts[name] + offset
        G[at : at + value.shape[0], : value.shape[1]] = value.astype(bf16)

    vec_grads = {}

    gw = plan.gw
    wide = 4 * gw
    spread = (
        lax.rem(lax.broadcasted_iota(jnp.int32, (gw, wide), 1), gw)
        == lax.broadcasted_iota(jnp.int32, (gw, wide), 0)
    ).astype(f32).astype(bf16)
    on_diagonal = (
        lax.rem(lax.broadcasted_iota(jnp.int32, (width, wide), 0) // gw, 4)
        == lax.broadcasted_iota(jnp.int32, (width, wide), 1) // gw
    )

    def blocks(kernel_ref, out):
        def run(t, carry):
            rep = dot(kernel_ref[t].reshape(width, gw), spread)
            rep = jnp.where(on_diagonal, rep, 0.0).astype(bf16)
            for h in range(width // wide):
                out[t, h] = rep[h * wide : (h + 1) * wide]
            return carry

        lax.fori_loop(0, plan.taps, run, 0)

    def groups_grad(name, taps, turned):
        lane = lax.broadcasted_iota(jnp.int32, (gw, wide), 1) // gw
        for t, (var, start) in enumerate(taps):
            for h in range(width // wide):
                cut = slice(h * wide, (h + 1) * wide)
                res = dot(turned[h], flat(var[start : start + side, :, cut]))
                out = res[0:gw]
                for j in range(1, 4):
                    out = jnp.where(lane == j, res[j * gw : (j + 1) * gw], out)
                if lead is not None:
                    out = out * lead
                at = plan.starts[name] + t * gw
                G[at : at + gw, cut] = out.astype(bf16)

    blocks(ref["k1"], ref["bd1"])
    band = pix // plan.cols
    bhalf = band // 2
    out_id = lax.broadcasted_iota(jnp.int32, (pix, pix), 0)
    in_id = lax.broadcasted_iota(jnp.int32, (pix, pix), 1)

    def source(o):
        quarter = o // (bhalf * side)
        down = lax.rem(o, bhalf * side) // side
        return (2 * down + quarter // 2) * plan.cols + 2 * lax.rem(o, side) + lax.rem(quarter, 2)

    ref["sort"][...] = (source(out_id) == in_id).astype(f32).astype(bf16)
    ref["unsort"][...] = (source(in_id) == out_id).astype(f32).astype(bf16)

    xp, R1 = ref["xp"], ref["R1"]
    arrived("x", plan.rows, 0)
    for k in range(2 * side // band):
        block = ref["x_in"][k * band : (k + 1) * band].reshape(pix, cin)
        block = dot(ref["sort"][...], block).astype(bf16)
        for ab in range(4):
            piece = block[ab * bhalf * side : (ab + 1) * bhalf * side]
            xp[ab, k * bhalf : (k + 1) * bhalf] = piece.reshape(bhalf, side, cin)
    sums = []
    for ab, (a, b) in enumerate(PHASES):
        full_dot(R1.at[ab], flat(xp[ab]), ref["w1"])

        def step(p, ab=ab, a=a, b=b):
            v = R1[ab, p]
            mv = v * mask_row(a, b, p)
            return mv, mv * v

        sums.append(over_rows(step, 2))
    post(0, [sum(x[0] for x in sums), sum(x[1] for x in sums), row_count, half_count])
    SC = ref["SC"]
    full_dot(SC, flat(xp[0]), ref["s1"])

    def moments(field):
        def step(p):
            v = field[p].astype(f32)
            mv = v * mask_row(0, 0, p)
            return mv, mv * v

        return over_rows(step, 2)

    short_sums = moments(SC)

    def coefficients(first, second, inverse, gain, shift):
        mean = first * inverse
        scale = lax.rsqrt(second * inverse - mean * mean + epsilon)
        a = scale * gain
        return a, shift - mean * a, scale, -mean * scale

    tot = fetch(0)
    inv_full, inv_half = 1.0 / tot[2:3], 1.0 / tot[3:4]
    n1 = coefficients(tot[0:1], tot[1:2], inv_full, vector("g1"), vector("b1"))

    va = ref["va"]
    va[3:6, 0:1] = jnp.zeros((3, 1, side, width), bf16)

    def shifted(v, edge, amount):
        return jnp.where(edge, 0.0, pltpu.roll(v, amount, 0))

    for ab, (a, b) in enumerate(PHASES):

        def step(p, ab=ab, a=a, b=b):
            v = mask_row(a, b, p) * silu(R1[ab, p] * n1[0] + n1[1])
            slot = (0, 1, 3, 4)[ab]
            va[slot, p + a] = v.astype(bf16)
            if b:
                va[slot + 1, p + a] = shifted(v, first_col, 1).astype(bf16)

        over_rows(step)
    taps1 = []
    for t in range(9):
        u, v = t // 3, t % 3
        slot = (0, 1, 3, 4)[2 * (u != 1) + (v != 1)] + (v == 0)
        taps1.append((va.at[slot], 1 if u == 2 else 0))

    def convolve(taps, weights, out):
        for h in range(width // wide):
            cut = slice(h * wide, (h + 1) * wide)
            acc = None
            for t, (var, start) in enumerate(taps):
                term = dot(flat(var[start : start + side, :, cut]), weights[t, h])
                acc = term if acc is None else acc + term
            out[:, :, cut] = acc.astype(bf16).reshape(side, side, wide)

    c1 = ref["c1"]
    convolve(taps1, ref["bd1"], c1)
    post(1, [*moments(c1), *short_sums])
    blocks(ref["k2"], ref["bd2"])
    tot = fetch(1)
    nc1 = coefficients(tot[0:1], tot[1:2], inv_half, vector("gg1"), vector("gb1"))
    ns = coefficients(tot[2:3], tot[3:4], inv_half, vector("sg1"), vector("sb1"))

    def excite(conv, norm, hidden, gated, sq, sqb, ex, exb):
        def step(p):
            v = mask_row(0, 0, p) * silu(conv[p].astype(f32) * norm[0] + norm[1])
            hidden[p] = v
            return (v,)

        (total,) = over_rows(step, 1)
        pooled = total / half_count
        pre = small_dot(pooled, sq[...], dot) + sqb
        inner = silu(pre)
        gate = sigmoid(small_dot(inner, ex[...], dot) + exb)

        def step_two(p):
            gated[p] = (hidden[p] * gate).astype(bf16)

        over_rows(step_two)
        return pooled, pre, inner, gate

    H1, ga1 = ref["H1"], ref["ga1"]
    kept1 = excite(
        c1, nc1, H1, ga1, ref["sq1"], vector("sqb1")[:, : plan.q1], ref["ex1"], vector("exb1")
    )
    E1 = ref["E1"]
    full_dot(E1, lines(ga1), ref["e1"])
    post(2, moments(E1))
    tot = fetch(2)
    ne = coefficients(tot[0:1], tot[1:2], inv_half, vector("eg1"), vector("eb1"))
    ent = ref["ent"]

    def step(p):
        v = E1[p] * ne[0] + SC[p] * ns[0] + (ne[1] + ns[1])
        ent[p] = (mask_row(0, 0, p) * silu(v)).astype(bf16)

    over_rows(step)

    def send_out(source, out, rows, target, base):
        for k in range(R // plan.copies):
            t = lax.rem(r + plan.copies * k, R)
            there = ref[out].at[0, mine, 0] if out == "act" else ref[out].at[mine, 0]
            here = source.at[pl.ds(t * rows, rows)]
            copy = pltpu.make_async_remote_copy(
                src_ref=here,
                dst_ref=there,
                send_sem=ref[out + "_send"].at[target, k],
                recv_sem=ref[out + "_recv"].at[mine],
                device_id=(target, i, t),
                device_id_type=MESH,
            )
            if k:
                copy.start()
                waits.append(copy.wait_send)
            else:
                local = pltpu.make_async_copy(here, there, ref[out + "_recv"].at[mine])

                @pl.when(s == target)
                def _():
                    local.start()

                @pl.when(s != target)
                def _():
                    copy.start()

                def finish(copy=copy):
                    @pl.when(s != target)
                    def _():
                        copy.wait_send()

                waits.append(finish)

    send_out(ent, "act", plan.hrows, 0, 0)

    R2 = ref["R2"]
    full_dot(R2, lines(ent), ref["w2"])
    post(3, moments(R2))
    tot = fetch(3)
    n2 = coefficients(tot[0:1], tot[1:2], inv_half, vector("g2"), vector("b2"))
    vb = ref["vb"]
    vb[:, 0:1] = jnp.zeros((3, 1, side, width), bf16)
    vb[:, side + 1 :] = jnp.zeros((3, 1, side, width), bf16)

    def three(out, p, v):
        out[0, p + 1] = shifted(v, first_col, 1).astype(bf16)
        out[1, p + 1] = v.astype(bf16)
        out[2, p + 1] = shifted(v, last_col, side - 1).astype(bf16)

    def step(p):
        three(vb, p, mask_row(0, 0, p) * silu(R2[p] * n2[0] + n2[1]))

    over_rows(step)
    taps2 = [(vb.at[t % 3], t // 3) for t in range(9)]
    c2 = ref["c2"]
    convolve(taps2, ref["bd2"], c2)
    post(4, moments(c2))
    tot = fetch(4)
    nc2 = coefficients(tot[0:1], tot[1:2], inv_half, vector("gg2"), vector("gb2"))
    H2, ga2 = ref["H2"], ref["ga2"]
    kept2 = excite(
        c2, nc2, H2, ga2, ref["sq2"], vector("sqb2")[:, : plan.q2], ref["ex2"], vector("exb2")
    )
    E2 = ref["E2"]
    full_dot(E2, lines(ga2), ref["e2"])
    post(5, moments(E2))
    arrived("og", plan.hrows, 1)
    tot = fetch(5)
    ne2 = coefficients(tot[0:1], tot[1:2], inv_half, vector("eg2"), vector("eb2"))
    leave, D, og = ref["leave"], ref["D"], ref["og_in"]

    def step(p):
        e = E2[p]
        v = e * ne2[0] + ne2[1] + ent[p].astype(f32)
        sg = sigmoid(v)
        m = mask_row(0, 0, p)
        leave[p] = (m * v * sg).astype(bf16)
        g = og[p].astype(f32) * m * (sg * (1.0 + v * (1.0 - sg)))
        D[p] = g
        return g, g * (e * ne2[2] + ne2[3])

    parts = over_rows(step, 2)
    vec_grads["eb2"], vec_grads["eg2"] = parts
    post(6, parts)
    send_out(leave, "act", plan.hrows, 1, 0)

    def back_rule(sums, inverse, gain, norm):
        a = gain * norm[2]
        k0 = a * (sums[0] + norm[3] * sums[1]) * inverse
        return a, k0, a * norm[2] * sums[1] * inverse

    def back_excite(dg, kept, hidden, conv, norm, sq, ex, out):
        pooled, pre, inner, gate = kept

        def step(p):
            return (dg[p].astype(f32) * hidden[p],)

        (dgate,) = over_rows(step, 1)
        dpre = dgate * gate * (1.0 - gate)
        dsq = small_dot(dpre, ex[...], dot_nt) * slope(pre)
        dpool = small_dot(dsq, sq[...], dot_nt) / half_count

        def step_two(p):
            v = conv[p].astype(f32)
            g = (dg[p].astype(f32) * gate + dpool) * mask_row(0, 0, p)
            g = g * slope(v * norm[0] + norm[1])
            out[p] = g
            return g, g * (v * norm[2] + norm[3])

        return over_rows(step_two, 2), dpre, dsq

    def excite_grads(name, kept, dpre, dsq):
        pooled, pre, inner, gate = kept
        put("sq" + name, small_outer(dsq, pooled))
        put("ex" + name, small_outer(inner, dpre))
        vec_grads["exb" + name] = dpre
        count = dsq.shape[1]
        eye = (
            lax.broadcasted_iota(jnp.int32, (count, width), 0)
            == lax.broadcasted_iota(jnp.int32, (count, width), 1)
        ).astype(f32).astype(bf16)
        vec_grads["sqb" + name] = small_dot(dsq, eye, dot)

    def turn(gradient_ref, start):
        out = []
        for h in range(width // wide):
            piece = flat(gradient_ref[start : start + side, :, h * wide : (h + 1) * wide])
            out.append(piece.astype(f32).T.astype(bf16))
        return out

    d1, dg, GR = ref["d1"], ref["dg"], ref["GR"]
    tot = fetch(6)
    rule = back_rule((tot[0:1], tot[1:2]), inv_half, vector("eg2"), ne2)

    def step(p):
        d1[p] = (rule[0] * D[p] - mask_row(0, 0, p) * (rule[1] + rule[2] * E2[p])).astype(bf16)

    over_rows(step)
    full_dot(dg, lines(d1), ref["e2"], dot_nt)
    parts, dpre, dsq = back_excite(dg, kept2, H2, c2, nc2, ref["sq2"], ref["ex2"], GR)
    vec_grads["gb2"], vec_grads["gg2"] = parts
    post(7, parts)
    put("e2", dot_tn(lines(ga2), lines(d1)))
    excite_grads("2", kept2, dpre, dsq)
    tot = fetch(7)
    rule = back_rule((tot[0:1], tot[1:2]), inv_half, vector("gg2"), nc2)
    vd = ref["vd"]
    vd[:, 0:1] = jnp.zeros((3, 1, side, width), bf16)
    vd[:, side + 1 :] = jnp.zeros((3, 1, side, width), bf16)

    def step(p):
        v = rule[0] * GR[p] - mask_row(0, 0, p) * (rule[1] + rule[2] * c2[p].astype(f32))
        three(vd, p, v)

    over_rows(step)

    def convolve_back(taps, weights, out):
        for h in range(width // wide):
            cut = slice(h * wide, (h + 1) * wide)
            acc = None
            for t, var, start in taps:
                term = dot_nt(flat(var[start : start + side, :, cut]), weights[t, h])
                acc = term if acc is None else acc + term
            out[:, :, cut] = acc.reshape(side, side, wide)

    DA = ref["DA"]
    convolve_back(
        [(t, vd.at[2 - t % 3], 2 - t // 3) for t in range(9)],
        ref["bd2"],
        DA.at[0],
    )

    def step(p):
        v = R2[p]
        g = DA[0, p] * mask_row(0, 0, p) * slope(v * n2[0] + n2[1])
        GR[p] = g
        return g, g * (v * n2[2] + n2[3])

    parts = over_rows(step, 2)
    vec_grads["b2"], vec_grads["g2"] = parts
    post(8, parts)
    groups_grad("k2", taps2, turn(vd.at[1], 1))
    tot = fetch(8)
    rule = back_rule((tot[0:1], tot[1:2]), inv_half, vector("g2"), n2)

    def step(p):
        d1[p] = (rule[0] * GR[p] - mask_row(0, 0, p) * (rule[1] + rule[2] * R2[p])).astype(bf16)

    over_rows(step)
    full_dot(GR, lines(d1), ref["w2"], dot_nt)

    def step(p):
        e, sc = E1[p], SC[p]
        g = (D[p] + GR[p]).astype(bf16).astype(f32)
        g = g * mask_row(0, 0, p) * slope(e * ne[0] + sc * ns[0] + (ne[1] + ns[1]))
        D[p] = g
        return g, g * (e * ne[2] + ne[3]), g * (sc * ns[2] + ns[3])

    parts = over_rows(step, 3)
    vec_grads["eb1"], vec_grads["eg1"], vec_grads["sg1"] = parts
    vec_grads["sb1"] = parts[0]
    post(9, parts)
    put("w2", dot_tn(lines(ent), lines(d1)))
    tot = fetch(9)
    rule_e = back_rule((tot[0:1], tot[1:2]), inv_half, vector("eg1"), ne)
    rule_s = back_rule((tot[0:1], tot[2:3]), inv_half, vector("sg1"), ns)
    d2 = ref["d2"]

    def step(p):
        g, m = D[p], mask_row(0, 0, p)
        d1[p] = (rule_e[0] * g - m * (rule_e[1] + rule_e[2] * E1[p])).astype(bf16)
        d2[p] = (rule_s[0] * g - m * (rule_s[1] + rule_s[2] * SC[p])).astype(bf16)

    over_rows(step)
    full_dot(dg, lines(d1), ref["e1"], dot_nt)
    parts, dpre, dsq = back_excite(dg, kept1, H1, c1, nc1, ref["sq1"], ref["ex1"], GR)
    vec_grads["gb1"], vec_grads["gg1"] = parts
    post(10, parts)
    put("e1", dot_tn(lines(ga1), lines(d1)))
    put("s1", dot_tn(flat(xp[0]), lines(d2)))
    excite_grads("1", kept1, dpre, dsq)
    tot = fetch(10)
    rule = back_rule((tot[0:1], tot[1:2]), inv_half, vector("gg1"), nc1)

    def step(p):
        v = rule[0] * GR[p] - mask_row(0, 0, p) * (rule[1] + rule[2] * c1[p].astype(f32))
        three(vd, p, v)

    over_rows(step)
    sums = []
    for ab, (a, b) in enumerate(PHASES):
        chosen = []
        for t in range(9):
            u, v = t // 3, t % 3
            if (u != 1) == bool(a) and (v != 1) == bool(b):
                chosen.append((t, vd.at[2 if v == 0 else 1], 2 if u == 0 else 1))
        convolve_back(chosen, ref["bd1"], DA.at[ab])

        def step(p, ab=ab, a=a, b=b):
            v = R1[ab, p]
            g = DA[ab, p] * mask_row(a, b, p) * slope(v * n1[0] + n1[1])
            DA[ab, p] = g
            return g, g * (v * n1[2] + n1[3])

        sums.append(over_rows(step, 2))
    parts = (sum(x[0] for x in sums), sum(x[1] for x in sums))
    vec_grads["b1"], vec_grads["g1"] = parts
    post(11, parts)
    groups_grad("k1", taps1, turn(vd.at[1], 1))
    ids = lax.broadcasted_iota(jnp.int32, (VEC_ROWS, width), 0)
    value = jnp.zeros((VEC_ROWS, width), f32)
    for name, at in VEC.items():
        value = jnp.where(ids == at, jnp.broadcast_to(vec_grads[name], value.shape), value)
    put("vec", value)
    tot = fetch(11)
    rule = back_rule((tot[0:1], tot[1:2]), inv_full, vector("g1"), n1)
    dr = ref["dr"]
    for ab, (a, b) in enumerate(PHASES):

        def step(p, ab=ab, a=a, b=b):
            v = rule[0] * DA[ab, p] - mask_row(a, b, p) * (rule[1] + rule[2] * R1[ab, p])
            dr[ab, p] = v.astype(bf16)

        over_rows(step)
    cut = cin // 2
    for part in range(2):
        dxp, dxo = ref["dxp"], ref[f"dxo{part}"]
        rows = slice(part * cut, (part + 1) * cut)
        for ab in range(4):
            v = dot_nt(flat(dr[ab]), ref["w1"][rows, :])
            if ab == 0:
                v = v + dot_nt(lines(d2), ref["s1"][rows, :])
            dxp[ab] = v.astype(bf16).reshape(side, side, cut)
        for k in range(2 * side // band):
            block = jnp.concatenate(
                [
                    dxp[ab, k * bhalf : (k + 1) * bhalf].reshape(bhalf * side, cut)
                    for ab in range(4)
                ],
                axis=0,
            )
            block = dot(ref["unsort"][...], block).astype(bf16)
            dxo[k * band : (k + 1) * band] = block.reshape(band, plan.cols, cut)
        send_out(dxo, "dx", plan.rows, part, 0)
    total = None
    for ab in range(4):
        term = dot_tn(flat(xp[ab]), flat(dr[ab]))
        total = term if total is None else total + term
    put("w1", total)

    for wait in waits:
        wait()
    for m in range(plan.M):
        t = (m % plan.each) * plan.copies + lax.rem(r, plan.copies)
        for out in ("act", "dx"):
            there = ref[out].at[0, m, 0] if out == "act" else ref[out].at[m, 0]
            pltpu.make_async_copy(there, there, ref[out + "_recv"].at[m]).wait()


WEIGHTS = ("w1", "k1", "sq1", "ex1", "e1", "s1", "w2", "k2", "sq2", "ex2", "e2")


def run_main(plan, arrays):
    side, width, cin = plan.side, plan.width, plan.cin
    wide = 4 * plan.gw
    field = (side, side, width)
    scratch = {
        "x_in": pltpu.VMEM((2 * side, plan.cols, cin), bf16),
        "og_in": pltpu.VMEM(field, bf16),
        "st": pltpu.VMEM((EXCHANGES, plan.I, 8, width), f32),
        "cm": pltpu.VMEM((2, side, width), f32),
        "bd1": pltpu.VMEM((plan.taps, width // wide, wide, wide), bf16),
        "bd2": pltpu.VMEM((plan.taps, width // wide, wide, wide), bf16),
        "sort": pltpu.VMEM((plan.pix, plan.pix), bf16),
        "unsort": pltpu.VMEM((plan.pix, plan.pix), bf16),
        "xp": pltpu.VMEM((4, side, side, cin), bf16),
        "R1": pltpu.VMEM((4,) + field, f32),
        "va": pltpu.VMEM((6, side + 1, side, width), bf16),
        "vb": pltpu.VMEM((3, side + 2, side, width), bf16),
        "vd": pltpu.VMEM((3, side + 2, side, width), bf16),
        "DA": pltpu.VMEM((4,) + field, f32),
        "dr": pltpu.VMEM((4,) + field, bf16),
        "dxp": pltpu.VMEM((4, side, side, cin // 2), bf16),
        "dxo0": pltpu.VMEM((2 * side, plan.cols, cin // 2), bf16),
        "dxo1": pltpu.VMEM((2 * side, plan.cols, cin // 2), bf16),
    }
    for name in ("SC", "H1", "E1", "R2", "H2", "E2", "D", "GR"):
        scratch[name] = pltpu.VMEM(field, f32)
    for name in ("c1", "ga1", "ent", "c2", "ga2", "leave", "d1", "d2", "dg"):
        scratch[name] = pltpu.VMEM(field, bf16)
    for name in ("x", "og"):
        scratch[name + "_send"] = pltpu.SemaphoreType.DMA((max(plan.R - 1, 1),))
        scratch[name + "_recv"] = pltpu.SemaphoreType.DMA((plan.R,))
    scratch["st_send"] = pltpu.SemaphoreType.DMA((EXCHANGES, max(plan.I - 1, 1)))
    scratch["st_recv"] = pltpu.SemaphoreType.DMA((EXCHANGES, plan.I))
    for name in ("act", "dx"):
        scratch[name + "_send"] = pltpu.SemaphoreType.DMA((2, plan.R // plan.copies))
        scratch[name + "_recv"] = pltpu.SemaphoreType.DMA((plan.M,))
    inputs = ("x", "og", "vr", "vc", "vec") + WEIGHTS
    outputs = ("act", "dx", "grads")
    names = inputs + outputs + tuple(scratch)
    any_space = pl.BlockSpec(memory_space=pl.ANY)
    smem = pl.BlockSpec(memory_space=pltpu.SMEM)
    vmem = pl.BlockSpec(memory_space=pltpu.VMEM)
    return pl.pallas_call(
        functools.partial(main_kernel, plan, names),
        out_shape=(
            jax.ShapeDtypeStruct((1, plan.M, 1, plan.hrows, side, width), bf16),
            jax.ShapeDtypeStruct((plan.M, 1, plan.rows, plan.cols, cin // 2), bf16),
            jax.ShapeDtypeStruct((plan.total_rows, width), bf16),
        ),
        in_specs=[any_space, any_space, smem, smem, vmem] + [vmem] * len(WEIGHTS),
        out_specs=(any_space, any_space, vmem),
        scratch_shapes=list(scratch.values()),
        compiler_params=pltpu.CompilerParams(
            collective_id=0, has_side_effects=True, vmem_limit_bytes=56 * 1024 * 1024
        ),
        name="blocks",
    )(*[arrays[name] for name in inputs])


def unpack(plan, flat):
    starts = plan.starts

    def rows(name, count):
        return flat[starts[name] : starts[name] + count]

    def group(name):
        piece = rows(name, plan.taps * plan.gw).reshape(plan.taps, plan.gw, plan.groups, plan.gw)
        return piece.transpose(0, 2, 3, 1)

    vec = rows("vec", VEC_ROWS)

    def v(name, count=None):
        return vec[VEC[name], :count]

    return (
        rows("w1", plan.cin), v("g1"), v("b1"), group("k1"), v("gg1"), v("gb1"),
        rows("sq1", plan.q1).T, v("sqb1", plan.q1), rows("ex1", plan.q1), v("exb1"),
        rows("e1", plan.width), v("eg1"), v("eb1"),
        rows("s1", plan.cin), v("sg1"), v("sb1"),
        rows("w2", plan.width), v("g2"), v("b2"), group("k2"), v("gg2"), v("gb2"),
        rows("sq2", plan.q2).T, v("sqb2", plan.q2), rows("ex2", plan.q2), v("exb2"),
        rows("e2", plan.width), v("eg2"), v("eb2"),
    )


def body(sizes, input_maps, valid_rows, valid_cols, *rest):
    weights, output_grad = rest[:-1], rest[-1]
    (w1, g1, b1, k1, gg1, gb1, sq1, sqb1, ex1, exb1, e1, eg1, eb1, s1, sg1, sb1) = weights[:16]
    (w2, g2, b2, k2, gg2, gb2, sq2, sqb2, ex2, exb2, e2, eg2, eb2) = weights[16:]
    plan = Plan(sizes, [v.shape for v in (input_maps, output_grad, w1, k1, sq1, sq2)])
    vectors = (
        g1, b1, gg1, gb1, exb1, eg1, eb1, sg1, sb1, sqb1, g2, b2, gg2, gb2, exb2, eg2, eb2, sqb2,
    )
    vec = jnp.stack([jnp.pad(v, (0, plan.width - v.shape[0])) for v in vectors])
    vec = jnp.pad(vec, ((0, VEC_ROWS - len(vectors)), (0, 0))).astype(f32)
    act, dx, grads = run_main(
        plan,
        dict(
            x=input_maps, og=output_grad, vr=valid_rows, vc=valid_cols, vec=vec, w1=w1, k1=k1,
            sq1=sq1, ex1=ex1, e1=e1, s1=s1, w2=w2, k2=k2, sq2=sq2, ex2=ex2, e2=e2,
        ),
    )
    grads = lax.psum(grads.astype(f32), ("section", "img", "row"))
    return (act, dx, *unpack(plan, grads))


def solution(mesh):
    tiled = P(None, "img", "row", None, None)
    image = P(None, "img")
    sizes = tuple(mesh.shape[name] for name in ("section", "img", "row"))
    return jax.shard_map(
        functools.partial(body, sizes),
        mesh=mesh,
        in_specs=(tiled, image, image) + (P(),) * 29 + (tiled,),
        out_specs=(
            P("section", None, "img", "row", None, None),
            P(None, "img", "row", None, "section"),
        )
        + (P(),) * 29,
        check_vma=False,
    )
```

```python
import functools

import jax
import jax.numpy as jnp
from jax import lax
from jax.experimental import pallas as pl
from jax.experimental.pallas import tpu as pltpu
from jax.sharding import PartitionSpec as P

epsilon = 1e-05
f32 = jnp.float32
bf16 = jnp.bfloat16
MESH = pl.DeviceIdType.MESH
PHASES = ((0, 0), (0, 1), (1, 0), (1, 1))
EXCHANGES = 12
NAMES = (
    "g1", "b1", "gg1", "gb1", "exb1", "eg1", "eb1", "sg1", "sb1", "sqb1",
    "g2", "b2", "gg2", "gb2", "exb2", "eg2", "eb2", "sqb2",
)
VEC = {name: k for k, name in enumerate(NAMES)}
VEC_ROWS = 32


def segments_of(cin, width, taps, group, sq1, sq2, devices):
    layout = (
        (("e2", width), ("sq2", sq2), ("ex2", sq2)),
        (("k2", taps * group), ("w2", width)),
        (("e1", width), ("s1", cin), ("sq1", sq1), ("ex1", sq1)),
        (("k1", taps * group), ("vec", VEC_ROWS)),
        (("w1", cin),),
    )
    starts, segments, at = {}, [], 0
    for parts in layout:
        base = at
        for name, rows in parts:
            starts[name] = (at, rows // 16)
            at += rows // 16 * (width // 128)
        used = at
        at = base + -(-(at - base) // devices) * devices
        segments.append((base, at - base, used))
    return starts, tuple(segments), at


def sigmoid(v):
    return 0.5 * jnp.tanh(0.5 * v) + 0.5


def silu(v):
    return v * sigmoid(v)


def slope(v):
    s = sigmoid(v)
    return s * (1.0 + v * (1.0 - s))


def dot(left, right):
    return jnp.dot(left, right, preferred_element_type=f32)


def dot_nt(left, right):
    return lax.dot_general(left, right, (((1,), (1,)), ((), ())), preferred_element_type=f32)


def dot_tn(left, right):
    return lax.dot_general(left, right, (((0,), (0,)), ((), ())), preferred_element_type=f32)


def parts_of(v):
    high = v.astype(bf16).astype(f32)
    return high, v - high


def stacked(rows, width):
    ids = lax.broadcasted_iota(jnp.int32, (16, width), 0)
    total = jnp.zeros((16, width), f32)
    for k, row in enumerate(rows):
        total = jnp.where(ids == k, jnp.broadcast_to(row, (16, width)), total)
    return total.astype(bf16)


def small_dot(row, weight, form):
    out = form(stacked(parts_of(row), row.shape[1]), weight)
    return out[0:1] + out[1:2]


def small_outer(left, right):
    lh, ll = parts_of(left)
    rh, rl = parts_of(right)
    return dot_tn(
        stacked((lh, ll, lh, ll), left.shape[1]), stacked((rh, rh, rl, rl), right.shape[1])
    )


def fold(v):
    return v[0:8] + v[8:16]


def column(acc):
    return jnp.sum(acc, axis=0, keepdims=True)


class Plan:
    def __init__(self, mesh_sizes, args):
        self.S, self.I, self.R = mesh_sizes
        x, og, w1, k1, sq1, sq2 = args
        self.M, _, self.rows, self.cols, self.cin = x
        _, _, self.hrows, self.side, self.width = og
        self.taps, self.groups, self.gw, _ = k1
        self.q1, self.q2 = sq1[0], sq2[1]
        self.each = self.M // self.S
        self.copies = self.R // self.each
        self.pix = self.side * self.side
        self.starts, self.segments, self.blocks = segments_of(
            self.cin, self.width, self.taps, self.gw, self.q1, self.q2, self.S * self.I * self.R
        )


def main_kernel(plan, names, *refs):
    ref = dict(zip(names, refs))
    S, I, R = plan.S, plan.I, plan.R
    side, width, pix, cin = plan.side, plan.width, plan.pix, plan.cin
    half_width = width // 2
    s, i, r = lax.axis_index("section"), lax.axis_index("img"), lax.axis_index("row")
    mine = s * plan.each + r // plan.copies
    waits = []

    barrier = pltpu.get_barrier_semaphore()
    peers = []
    for ds in range(S):
        for dr in range(R):
            if ds or dr:
                peers.append((lax.rem(s + ds, S), i, lax.rem(r + dr, R)))
    for di in range(1, I):
        peers.append((s, lax.rem(i + di, I), r))
    for peer in peers:
        pl.semaphore_signal(barrier, inc=1, device_id=peer, device_id_type=MESH)

    own = []
    for name, rows in (("x", plan.rows), ("og", plan.hrows)):
        copy = pltpu.make_async_copy(
            ref[name].at[mine, 0],
            ref[name + "_in"].at[pl.ds(r * rows, rows)],
            ref[name + "_recv"].at[r],
        )
        copy.start()
        own.append(copy)
    pl.semaphore_wait(barrier, len(peers))
    for name, rows in (("x", plan.rows), ("og", plan.hrows)):
        for d in range(1, R):
            t = lax.rem(r + d, R)
            copy = pltpu.make_async_remote_copy(
                src_ref=ref[name].at[s * plan.each + t // plan.copies, 0],
                dst_ref=ref[name + "_in"].at[pl.ds(r * rows, rows)],
                send_sem=ref[name + "_send"].at[d - 1],
                recv_sem=ref[name + "_recv"].at[r],
                device_id=(s, i, t),
                device_id_type=MESH,
            )
            copy.start()
            waits.append(copy.wait_send)

    def arrived(name, rows, position):
        own[position].wait()
        for d in range(1, R):
            t = lax.rem(r + d, R)
            there = ref[name + "_in"].at[pl.ds(t * rows, rows)]
            pltpu.make_async_remote_copy(
                src_ref=there,
                dst_ref=there,
                send_sem=ref[name + "_send"].at[d - 1],
                recv_sem=ref[name + "_recv"].at[t],
                device_id=(s, i, t),
                device_id_type=MESH,
            ).wait_recv()

    st = ref["st"]

    def stats_copy(k, d, slot):
        return pltpu.make_async_remote_copy(
            src_ref=st.at[k, slot],
            dst_ref=st.at[k, slot],
            send_sem=ref["st_send"].at[k, d - 1],
            recv_sem=ref["st_recv"].at[k, slot],
            device_id=(s, lax.rem(i + d, I), r),
            device_id_type=MESH,
        )

    def post(k, rows):
        ids = lax.broadcasted_iota(jnp.int32, (8, width), 0)
        value = jnp.zeros((8, width), f32)
        for j, row in enumerate(rows):
            value = jnp.where(ids == j, jnp.broadcast_to(row, (8, width)), value)
        st[k, i] = value
        for d in range(1, I):
            stats_copy(k, d, i).start()

    def fetch(k):
        for d in range(1, I):
            stats_copy(k, d, i).wait_send()
            stats_copy(k, d, lax.rem(i + d, I)).wait_recv()
        value = st[k, 0]
        for j in range(1, I):
            value = value + st[k, j]
        return value

    vec = ref["vec"]
    for name, at in VEC.items():
        row = ref[name][...].astype(f32)
        vec[at : at + 1, : row.shape[0]] = row.reshape(1, row.shape[0])

    def vector(name):
        return vec[VEC[name] : VEC[name] + 1]

    vr, vc = ref["vr"][0, mine], ref["vc"][0, mine]
    q_ids = lax.broadcasted_iota(jnp.int32, (side, width), 0)
    first_col, last_col = q_ids == 0, q_ids == side - 1
    cm = ref["cm"]
    for b in range(2):
        cm[b] = (2 * q_ids + b < vc).astype(f32)

    def mask_row(a, b, p):
        return cm[b] * (2 * p + a < vr).astype(f32)

    row_count = jnp.full((1, width), vr * vc, jnp.int32).astype(f32)
    half_count = jnp.full((1, width), ((vr + 1) // 2) * ((vc + 1) // 2), jnp.int32).astype(f32)

    def over_rows(step, *accs):
        init = tuple(jnp.zeros((8, width), f32) for _ in range(accs[0] if accs else 0))

        def run(p, carry):
            out = step(p)
            if not carry:
                return carry
            return tuple(c + fold(o) for c, o in zip(carry, out))

        return tuple(column(c) for c in lax.fori_loop(0, side, run, init, unroll=2))

    def full_dot(out, left, weight, form=dot):
        wide = out.shape[-1]
        step = min(256, wide)
        for h in range(wide // step):
            cut = slice(h * step, h * step + step)
            w = weight[:, cut] if form is dot else weight[cut, :]
            out[:, :, cut] = form(left, w).reshape(side, side, step).astype(out.dtype)

    def flat(value):
        return value.reshape(pix, value.shape[-1])

    def lines(ref_, start=0):
        return flat(ref_[start : start + side])

    G, F = ref["local"], ref["grads"]
    lead = None if plan.copies == 1 else (lax.rem(r, plan.copies) == 0).astype(f32)

    def put(name, value, row=0, lane=0):
        if lead is not None:
            value = value * lead
        start, per_tile = plan.starts[name]
        count = value.shape[0] // 16
        for k in range(value.shape[1] // 128):
            piece = value[:, 128 * k : 128 * k + 128].astype(bf16).reshape(count, 16, 128)
            at = start + (lane // 128 + k) * per_tile + row // 16
            G[at : at + count] = piece

    levels = (
        (S, s, lambda t: (t, i, r), G, ref["got0"], ref["sum0"]),
        (R, r, lambda t: (s, i, t), ref["sum0"], ref["got1"], ref["sum1"]),
        (I, i, lambda t: (s, t, r), ref["sum1"], ref["got2"], None),
    )
    shares = (1, S, S * R, S * R * I)

    def scatter_copies(g, level, outgoing):
        count, me, device, source, got, _ = levels[level]
        base = plan.segments[g][0] // shares[level]
        piece = plan.segments[g][1] // shares[level + 1]
        for d in range(1, count):
            t = lax.rem(me + d, count)
            slot = me if outgoing else t
            copy = pltpu.make_async_remote_copy(
                src_ref=source.at[pl.ds(base + t * piece, piece)],
                dst_ref=got.at[pl.ds(base + slot * piece, piece)],
                send_sem=ref["rs_send"].at[g, level, d - 1],
                recv_sem=ref["rs_recv"].at[g, level, slot],
                device_id=device(t),
                device_id_type=MESH,
            )
            if outgoing:
                copy.start()
                waits.append(copy.wait_send)
            else:
                copy.wait_recv()

    def add_up(g, level):
        count, me, _, source, got, out = levels[level]
        base = plan.segments[g][0] // shares[level]
        piece = plan.segments[g][1] // shares[level + 1]
        at = plan.segments[g][0] // shares[level + 1]
        if out is None:
            out = F
            at = plan.segments[g][0] + ((s * R + r) * I + i) * piece
        step = next(k for k in (18, 16, 14, 12, 10, 9, 8, 7, 6, 5, 4, 3, 2, 1) if piece % k == 0)

        def run(k, carry):
            total = source[pl.ds(base + me * piece + k * step, step)].astype(f32)
            for d in range(1, count):
                t = lax.rem(me + d, count)
                total = total + got[pl.ds(base + t * piece + k * step, step)].astype(f32)
            out[pl.ds(at + k * step, step)] = total.astype(bf16)
            return carry

        lax.fori_loop(0, piece // step, run, 0)

    def gather_copies(g, level, outgoing):
        count, me, device, _, _, _ = levels[level]
        base, size, _ = plan.segments[g]
        for above in range(level):
            base = base + levels[above][1] * (size // shares[above + 1])
        piece = size // shares[level + 1]
        for d in range(1, count):
            t = lax.rem(me + d, count)
            slot = me if outgoing else t
            there = F.at[pl.ds(base + slot * piece, piece)]
            copy = pltpu.make_async_remote_copy(
                src_ref=there,
                dst_ref=there,
                send_sem=ref["ag_send"].at[g, level, d - 1],
                recv_sem=ref["ag_recv"].at[g, level, slot],
                device_id=device(t),
                device_id_type=MESH,
            )
            if outgoing:
                copy.start()
                waits.append(copy.wait_send)
            else:
                copy.wait_recv()

    done = [0] * len(plan.segments)

    def advance(*which):
        for g in which:
            k = done[g]
            done[g] += 1
            if k == 0:
                base, size, used = plan.segments[g]
                if used < base + size:
                    G[used : base + size] = jnp.zeros((base + size - used, 16, 128), bf16)
            elif k <= 3:
                scatter_copies(g, k - 1, False)
                add_up(g, k - 1)
            else:
                gather_copies(g, 6 - k, False)
            if k < 3:
                scatter_copies(g, k, True)
            elif k < 6:
                gather_copies(g, 5 - k, True)

    vec_grads = {}

    gw = plan.gw
    wide = 4 * gw
    spread = (
        lax.rem(lax.broadcasted_iota(jnp.int32, (gw, wide), 1), gw)
        == lax.broadcasted_iota(jnp.int32, (gw, wide), 0)
    ).astype(f32).astype(bf16)
    on_diagonal = (
        lax.rem(lax.broadcasted_iota(jnp.int32, (width, wide), 0) // gw, 4)
        == lax.broadcasted_iota(jnp.int32, (width, wide), 1) // gw
    )

    def blocks(kernel_ref, out):
        def run(t, carry):
            rep = dot(kernel_ref[t].reshape(width, gw), spread)
            rep = jnp.where(on_diagonal, rep, 0.0).astype(bf16)
            for h in range(width // wide):
                out[t, h] = rep[h * wide : (h + 1) * wide]
            return carry

        lax.fori_loop(0, plan.taps, run, 0)

    def groups_grad(name, taps, turned):
        lane = lax.broadcasted_iota(jnp.int32, (gw, wide), 1) // gw
        for t, (var, start) in enumerate(taps):
            for h in range(width // wide):
                cut = slice(h * wide, (h + 1) * wide)
                res = dot(turned[h], flat(var[start : start + side, :, cut]))
                out = res[0:gw]
                for j in range(1, 4):
                    out = jnp.where(lane == j, res[j * gw : (j + 1) * gw], out)
                put(name, out, t * gw, h * wide)

    blocks(ref["k1"], ref["bd1"])
    band = pix // plan.cols
    bhalf = band // 2
    out_id = lax.broadcasted_iota(jnp.int32, (pix, pix), 0)
    in_id = lax.broadcasted_iota(jnp.int32, (pix, pix), 1)

    def source(o):
        quarter = o // (bhalf * side)
        down = lax.rem(o, bhalf * side) // side
        return (2 * down + quarter // 2) * plan.cols + 2 * lax.rem(o, side) + lax.rem(quarter, 2)

    ref["sort"][...] = (source(out_id) == in_id).astype(f32).astype(bf16)
    ref["unsort"][...] = (source(in_id) == out_id).astype(f32).astype(bf16)

    xp, R1 = ref["xp"], ref["R1"]
    arrived("x", plan.rows, 0)
    for k in range(2 * side // band):
        block = ref["x_in"][k * band : (k + 1) * band].reshape(pix, cin)
        block = dot(ref["sort"][...], block).astype(bf16)
        for ab in range(4):
            piece = block[ab * bhalf * side : (ab + 1) * bhalf * side]
            xp[ab, k * bhalf : (k + 1) * bhalf] = piece.reshape(bhalf, side, cin)
    sums = []
    for ab, (a, b) in enumerate(PHASES):
        full_dot(R1.at[ab], flat(xp[ab]), ref["w1"])

        def step(p, ab=ab, a=a, b=b):
            v = R1[ab, p]
            mv = v * mask_row(a, b, p)
            return mv, mv * v

        sums.append(over_rows(step, 2))
    post(0, [sum(x[0] for x in sums), sum(x[1] for x in sums), row_count, half_count])
    SC = ref["SC"]
    full_dot(SC, flat(xp[0]), ref["s1"])

    def moments(field):
        def step(p):
            v = field[p].astype(f32)
            mv = v * mask_row(0, 0, p)
            return mv, mv * v

        return over_rows(step, 2)

    short_sums = moments(SC)

    def coefficients(first, second, inverse, gain, shift):
        mean = first * inverse
        scale = lax.rsqrt(second * inverse - mean * mean + epsilon)
        a = scale * gain
        return a, shift - mean * a, scale, -mean * scale

    tot = fetch(0)
    inv_full, inv_half = 1.0 / tot[2:3], 1.0 / tot[3:4]
    n1 = coefficients(tot[0:1], tot[1:2], inv_full, vector("g1"), vector("b1"))

    va = ref["va"]
    va[3:6, 0:1] = jnp.zeros((3, 1, side, width), bf16)

    def shifted(v, edge, amount):
        return jnp.where(edge, 0.0, pltpu.roll(v, amount, 0))

    for ab, (a, b) in enumerate(PHASES):

        def step(p, ab=ab, a=a, b=b):
            v = mask_row(a, b, p) * silu(R1[ab, p] * n1[0] + n1[1])
            slot = (0, 1, 3, 4)[ab]
            va[slot, p + a] = v.astype(bf16)
            if b:
                va[slot + 1, p + a] = shifted(v, first_col, 1).astype(bf16)

        over_rows(step)
    taps1 = []
    for t in range(9):
        u, v = t // 3, t % 3
        slot = (0, 1, 3, 4)[2 * (u != 1) + (v != 1)] + (v == 0)
        taps1.append((va.at[slot], 1 if u == 2 else 0))

    def convolve(taps, weights, out):
        for h in range(width // wide):
            cut = slice(h * wide, (h + 1) * wide)
            acc = None
            for t, (var, start) in enumerate(taps):
                term = dot(flat(var[start : start + side, :, cut]), weights[t, h])
                acc = term if acc is None else acc + term
            out[:, :, cut] = acc.astype(bf16).reshape(side, side, wide)

    c1 = ref["c1"]
    convolve(taps1, ref["bd1"], c1)
    post(1, [*moments(c1), *short_sums])
    blocks(ref["k2"], ref["bd2"])
    tot = fetch(1)
    nc1 = coefficients(tot[0:1], tot[1:2], inv_half, vector("gg1"), vector("gb1"))
    ns = coefficients(tot[2:3], tot[3:4], inv_half, vector("sg1"), vector("sb1"))

    def excite(conv, norm, hidden, gated, sq, sq_form, sqb, ex, exb):
        def step(p):
            v = mask_row(0, 0, p) * silu(conv[p].astype(f32) * norm[0] + norm[1])
            hidden[p] = v
            return (v,)

        (total,) = over_rows(step, 1)
        pooled = total / half_count
        pre = small_dot(pooled, sq[...], sq_form) + sqb
        inner = silu(pre)
        gate = sigmoid(small_dot(inner, ex[...], dot) + exb)

        def step_two(p):
            gated[p] = (hidden[p] * gate).astype(bf16)

        over_rows(step_two)
        return pooled, pre, inner, gate

    H1, ga1 = ref["H1"], ref["ga1"]
    kept1 = excite(
        c1, nc1, H1, ga1, ref["sq1"], dot_nt, vector("sqb1")[:, : plan.q1], ref["ex1"], vector("exb1")
    )
    E1 = ref["E1"]
    full_dot(E1, lines(ga1), ref["e1"])
    post(2, moments(E1))
    tot = fetch(2)
    ne = coefficients(tot[0:1], tot[1:2], inv_half, vector("eg1"), vector("eb1"))
    ent = ref["ent"]

    def step(p):
        v = E1[p] * ne[0] + SC[p] * ns[0] + (ne[1] + ns[1])
        ent[p] = (mask_row(0, 0, p) * silu(v)).astype(bf16)

    over_rows(step)

    def send_out(source, out, rows, target, base):
        for k in range(R // plan.copies):
            t = lax.rem(r + plan.copies * k, R)
            there = ref[out].at[0, mine, 0] if out == "act" else ref[out].at[mine, 0]
            here = source.at[pl.ds(t * rows, rows)]
            copy = pltpu.make_async_remote_copy(
                src_ref=here,
                dst_ref=there,
                send_sem=ref[out + "_send"].at[target, k],
                recv_sem=ref[out + "_recv"].at[mine],
                device_id=(target, i, t),
                device_id_type=MESH,
            )
            if k:
                copy.start()
                waits.append(copy.wait_send)
            else:
                local = pltpu.make_async_copy(here, there, ref[out + "_recv"].at[mine])

                @pl.when(s == target)
                def _():
                    local.start()

                @pl.when(s != target)
                def _():
                    copy.start()

                def finish(copy=copy):
                    @pl.when(s != target)
                    def _():
                        copy.wait_send()

                waits.append(finish)

    send_out(ent, "act", plan.hrows, 0, 0)

    R2 = ref["R2"]
    full_dot(R2, lines(ent), ref["w2"])
    post(3, moments(R2))
    tot = fetch(3)
    n2 = coefficients(tot[0:1], tot[1:2], inv_half, vector("g2"), vector("b2"))
    vb = ref["vb"]
    vb[:, 0:1] = jnp.zeros((3, 1, side, width), bf16)
    vb[:, side + 1 :] = jnp.zeros((3, 1, side, width), bf16)

    def three(out, p, v):
        out[0, p + 1] = shifted(v, first_col, 1).astype(bf16)
        out[1, p + 1] = v.astype(bf16)
        out[2, p + 1] = shifted(v, last_col, side - 1).astype(bf16)

    def step(p):
        three(vb, p, mask_row(0, 0, p) * silu(R2[p] * n2[0] + n2[1]))

    over_rows(step)
    taps2 = [(vb.at[t % 3], t // 3) for t in range(9)]
    c2 = ref["c2"]
    convolve(taps2, ref["bd2"], c2)
    post(4, moments(c2))
    tot = fetch(4)
    nc2 = coefficients(tot[0:1], tot[1:2], inv_half, vector("gg2"), vector("gb2"))
    H2, ga2 = ref["H2"], ref["ga2"]
    kept2 = excite(
        c2, nc2, H2, ga2, ref["sq2"], dot, vector("sqb2")[:, : plan.q2], ref["ex2"], vector("exb2")
    )
    E2 = ref["E2"]
    full_dot(E2, lines(ga2), ref["e2"])
    post(5, moments(E2))
    arrived("og", plan.hrows, 1)
    tot = fetch(5)
    ne2 = coefficients(tot[0:1], tot[1:2], inv_half, vector("eg2"), vector("eb2"))
    leave, D, og = ref["leave"], ref["D"], ref["og_in"]

    def step(p):
        e = E2[p]
        v = e * ne2[0] + ne2[1] + ent[p].astype(f32)
        sg = sigmoid(v)
        m = mask_row(0, 0, p)
        leave[p] = (m * v * sg).astype(bf16)
        g = og[p].astype(f32) * m * (sg * (1.0 + v * (1.0 - sg)))
        D[p] = g
        return g, g * (e * ne2[2] + ne2[3])

    parts = over_rows(step, 2)
    vec_grads["eb2"], vec_grads["eg2"] = parts
    post(6, parts)
    send_out(leave, "act", plan.hrows, 1, 0)

    def back_rule(sums, inverse, gain, norm):
        a = gain * norm[2]
        k0 = a * (sums[0] + norm[3] * sums[1]) * inverse
        return a, k0, a * norm[2] * sums[1] * inverse

    def back_excite(dg, kept, hidden, conv, norm, sq, sq_form, ex, out):
        pooled, pre, inner, gate = kept

        def step(p):
            return (dg[p].astype(f32) * hidden[p],)

        (dgate,) = over_rows(step, 1)
        dpre = dgate * gate * (1.0 - gate)
        dsq = small_dot(dpre, ex[...], dot_nt) * slope(pre)
        dpool = small_dot(dsq, sq[...], sq_form) / half_count

        def step_two(p):
            v = conv[p].astype(f32)
            g = (dg[p].astype(f32) * gate + dpool) * mask_row(0, 0, p)
            g = g * slope(v * norm[0] + norm[1])
            out[p] = g
            return g, g * (v * norm[2] + norm[3])

        return over_rows(step_two, 2), dpre, dsq

    def excite_grads(name, kept, dpre, dsq):
        pooled, pre, inner, gate = kept
        put("sq" + name, small_outer(dsq, pooled))
        put("ex" + name, small_outer(inner, dpre))
        vec_grads["exb" + name] = dpre
        count = dsq.shape[1]
        eye = (
            lax.broadcasted_iota(jnp.int32, (count, width), 0)
            == lax.broadcasted_iota(jnp.int32, (count, width), 1)
        ).astype(f32).astype(bf16)
        vec_grads["sqb" + name] = small_dot(dsq, eye, dot)

    def turn(gradient_ref, start):
        out = []
        for h in range(width // wide):
            piece = flat(gradient_ref[start : start + side, :, h * wide : (h + 1) * wide])
            out.append(piece.astype(f32).T.astype(bf16))
        return out

    d1, dg, GR = ref["d1"], ref["dg"], ref["GR"]
    tot = fetch(6)
    rule = back_rule((tot[0:1], tot[1:2]), inv_half, vector("eg2"), ne2)

    def step(p):
        d1[p] = (rule[0] * D[p] - mask_row(0, 0, p) * (rule[1] + rule[2] * E2[p])).astype(bf16)

    over_rows(step)
    full_dot(dg, lines(d1), ref["e2"], dot_nt)
    parts, dpre, dsq = back_excite(dg, kept2, H2, c2, nc2, ref["sq2"], dot_nt, ref["ex2"], GR)
    vec_grads["gb2"], vec_grads["gg2"] = parts
    post(7, parts)
    put("e2", dot_tn(lines(ga2), lines(d1)))
    excite_grads("2", kept2, dpre, dsq)
    advance(0)
    tot = fetch(7)
    rule = back_rule((tot[0:1], tot[1:2]), inv_half, vector("gg2"), nc2)
    vd = ref["vd"]
    vd[:, 0:1] = jnp.zeros((3, 1, side, width), bf16)
    vd[:, side + 1 :] = jnp.zeros((3, 1, side, width), bf16)

    def step(p):
        v = rule[0] * GR[p] - mask_row(0, 0, p) * (rule[1] + rule[2] * c2[p].astype(f32))
        three(vd, p, v)

    over_rows(step)

    def convolve_back(taps, weights, out):
        for h in range(width // wide):
            cut = slice(h * wide, (h + 1) * wide)
            acc = None
            for t, var, start in taps:
                term = dot_nt(flat(var[start : start + side, :, cut]), weights[t, h])
                acc = term if acc is None else acc + term
            out[:, :, cut] = acc.reshape(side, side, wide)

    DA = ref["DA"]
    convolve_back(
        [(t, vd.at[2 - t % 3], 2 - t // 3) for t in range(9)],
        ref["bd2"],
        DA.at[0],
    )

    def step(p):
        v = R2[p]
        g = DA[0, p] * mask_row(0, 0, p) * slope(v * n2[0] + n2[1])
        GR[p] = g
        return g, g * (v * n2[2] + n2[3])

    parts = over_rows(step, 2)
    vec_grads["b2"], vec_grads["g2"] = parts
    post(8, parts)
    groups_grad("k2", taps2, turn(vd.at[1], 1))
    advance(0)
    tot = fetch(8)
    rule = back_rule((tot[0:1], tot[1:2]), inv_half, vector("g2"), n2)

    def step(p):
        d1[p] = (rule[0] * GR[p] - mask_row(0, 0, p) * (rule[1] + rule[2] * R2[p])).astype(bf16)

    over_rows(step)
    full_dot(GR, lines(d1), ref["w2"], dot_nt)

    def step(p):
        e, sc = E1[p], SC[p]
        g = (D[p] + GR[p]).astype(bf16).astype(f32)
        g = g * mask_row(0, 0, p) * slope(e * ne[0] + sc * ns[0] + (ne[1] + ns[1]))
        D[p] = g
        return g, g * (e * ne[2] + ne[3]), g * (sc * ns[2] + ns[3])

    parts = over_rows(step, 3)
    vec_grads["eb1"], vec_grads["eg1"], vec_grads["sg1"] = parts
    vec_grads["sb1"] = parts[0]
    post(9, parts)
    put("w2", dot_tn(lines(ent), lines(d1)))
    advance(1, 0)
    tot = fetch(9)
    rule_e = back_rule((tot[0:1], tot[1:2]), inv_half, vector("eg1"), ne)
    rule_s = back_rule((tot[0:1], tot[2:3]), inv_half, vector("sg1"), ns)
    d2 = ref["d2"]

    def step(p):
        g, m = D[p], mask_row(0, 0, p)
        d1[p] = (rule_e[0] * g - m * (rule_e[1] + rule_e[2] * E1[p])).astype(bf16)
        d2[p] = (rule_s[0] * g - m * (rule_s[1] + rule_s[2] * SC[p])).astype(bf16)

    over_rows(step)
    full_dot(dg, lines(d1), ref["e1"], dot_nt)
    parts, dpre, dsq = back_excite(dg, kept1, H1, c1, nc1, ref["sq1"], dot, ref["ex1"], GR)
    vec_grads["gb1"], vec_grads["gg1"] = parts
    post(10, parts)
    put("e1", dot_tn(lines(ga1), lines(d1)))
    put("s1", dot_tn(flat(xp[0]), lines(d2)))
    excite_grads("1", kept1, dpre, dsq)
    advance(2, 1, 0)
    tot = fetch(10)
    rule = back_rule((tot[0:1], tot[1:2]), inv_half, vector("gg1"), nc1)

    def step(p):
        v = rule[0] * GR[p] - mask_row(0, 0, p) * (rule[1] + rule[2] * c1[p].astype(f32))
        three(vd, p, v)

    over_rows(step)
    sums = []
    for ab, (a, b) in enumerate(PHASES):
        chosen = []
        for t in range(9):
            u, v = t // 3, t % 3
            if (u != 1) == bool(a) and (v != 1) == bool(b):
                chosen.append((t, vd.at[2 if v == 0 else 1], 2 if u == 0 else 1))
        convolve_back(chosen, ref["bd1"], DA.at[ab])

        def step(p, ab=ab, a=a, b=b):
            v = R1[ab, p]
            g = DA[ab, p] * mask_row(a, b, p) * slope(v * n1[0] + n1[1])
            DA[ab, p] = g
            return g, g * (v * n1[2] + n1[3])

        sums.append(over_rows(step, 2))
    parts = (sum(x[0] for x in sums), sum(x[1] for x in sums))
    vec_grads["b1"], vec_grads["g1"] = parts
    post(11, parts)
    groups_grad("k1", taps1, turn(vd.at[1], 1))
    ids = lax.broadcasted_iota(jnp.int32, (VEC_ROWS, width), 0)
    value = jnp.zeros((VEC_ROWS, width), f32)
    for name, at in VEC.items():
        value = jnp.where(ids == at, jnp.broadcast_to(vec_grads[name], value.shape), value)
    put("vec", value)
    advance(3, 2, 1, 0)
    tot = fetch(11)
    rule = back_rule((tot[0:1], tot[1:2]), inv_full, vector("g1"), n1)
    dr = ref["dr"]
    for ab, (a, b) in enumerate(PHASES):

        def step(p, ab=ab, a=a, b=b):
            v = rule[0] * DA[ab, p] - mask_row(a, b, p) * (rule[1] + rule[2] * R1[ab, p])
            dr[ab, p] = v.astype(bf16)

        over_rows(step)
    total = None
    for ab in range(4):
        term = dot_tn(flat(xp[ab]), flat(dr[ab]))
        total = term if total is None else total + term
    put("w1", total)

    advance(4, 3, 2, 1, 0)
    cut = cin // 2
    for part in range(2):
        dxp, dxo = ref["dxp"], ref[f"dxo{part}"]
        rows = slice(part * cut, (part + 1) * cut)
        for ab in range(4):
            v = dot_nt(flat(dr[ab]), ref["w1"][rows, :])
            if ab == 0:
                v = v + dot_nt(lines(d2), ref["s1"][rows, :])
            dxp[ab] = v.astype(bf16).reshape(side, side, cut)
        for k in range(2 * side // band):
            block = jnp.concatenate(
                [
                    dxp[ab, k * bhalf : (k + 1) * bhalf].reshape(bhalf * side, cut)
                    for ab in range(4)
                ],
                axis=0,
            )
            block = dot(ref["unsort"][...], block).astype(bf16)
            dxo[k * band : (k + 1) * band] = block.reshape(band, plan.cols, cut)
        send_out(dxo, "dx", plan.rows, part, 0)
        advance(4, 3, 2, 1)
    while min(done) < 7:
        advance(*[g for g in range(len(done)) if done[g] < 7])
    for wait in waits:
        wait()
    for m in range(plan.M):
        t = (m % plan.each) * plan.copies + lax.rem(r, plan.copies)
        for out in ("act", "dx"):
            there = ref[out].at[0, m, 0] if out == "act" else ref[out].at[m, 0]
            pltpu.make_async_copy(there, there, ref[out + "_recv"].at[m]).wait()


WEIGHTS = ("w1", "k1", "sq1", "ex1", "e1", "s1", "w2", "k2", "sq2", "ex2", "e2")


def run_main(plan, arrays):
    side, width, cin = plan.side, plan.width, plan.cin
    wide = 4 * plan.gw
    field = (side, side, width)
    scratch = {
        "x_in": pltpu.VMEM((2 * side, plan.cols, cin), bf16),
        "og_in": pltpu.VMEM(field, bf16),
        "st": pltpu.VMEM((EXCHANGES, plan.I, 8, width), f32),
        "cm": pltpu.VMEM((2, side, width), f32),
        "bd1": pltpu.VMEM((plan.taps, width // wide, wide, wide), bf16),
        "bd2": pltpu.VMEM((plan.taps, width // wide, wide, wide), bf16),
        "sort": pltpu.VMEM((plan.pix, plan.pix), bf16),
        "unsort": pltpu.VMEM((plan.pix, plan.pix), bf16),
        "xp": pltpu.VMEM((4, side, side, cin), bf16),
        "R1": pltpu.VMEM((4,) + field, f32),
        "va": pltpu.VMEM((6, side + 1, side, width), bf16),
        "vb": pltpu.VMEM((3, side + 2, side, width), bf16),
        "vd": pltpu.VMEM((3, side + 2, side, width), bf16),
        "DA": pltpu.VMEM((4,) + field, f32),
        "dr": pltpu.VMEM((4,) + field, bf16),
        "dxp": pltpu.VMEM((4, side, side, cin // 2), bf16),
        "dxo0": pltpu.VMEM((2 * side, plan.cols, cin // 2), bf16),
        "dxo1": pltpu.VMEM((2 * side, plan.cols, cin // 2), bf16),
    }
    for name in ("SC", "H1", "E1", "R2", "H2", "E2", "D", "GR"):
        scratch[name] = pltpu.VMEM(field, f32)
    for name in ("c1", "ga1", "ent", "c2", "ga2", "leave", "d1", "d2", "dg"):
        scratch[name] = pltpu.VMEM(field, bf16)
    for name in ("x", "og"):
        scratch[name + "_send"] = pltpu.SemaphoreType.DMA((max(plan.R - 1, 1),))
        scratch[name + "_recv"] = pltpu.SemaphoreType.DMA((plan.R,))
    scratch["st_send"] = pltpu.SemaphoreType.DMA((EXCHANGES, max(plan.I - 1, 1)))
    scratch["st_recv"] = pltpu.SemaphoreType.DMA((EXCHANGES, plan.I))
    for name in ("act", "dx"):
        scratch[name + "_send"] = pltpu.SemaphoreType.DMA((2, plan.R // plan.copies))
        scratch[name + "_recv"] = pltpu.SemaphoreType.DMA((plan.M,))
    scratch["vec"] = pltpu.VMEM((VEC_ROWS, width), f32)
    scratch["local"] = pltpu.VMEM((plan.blocks, 16, 128), bf16)
    shares = (1, plan.S, plan.S * plan.R)
    for level, share in enumerate(shares):
        scratch[f"got{level}"] = pltpu.VMEM((plan.blocks // share, 16, 128), bf16)
        if level:
            scratch[f"sum{level - 1}"] = pltpu.VMEM((plan.blocks // share, 16, 128), bf16)
    most = max(plan.S, plan.R, plan.I)
    for name in ("rs", "ag"):
        scratch[name + "_send"] = pltpu.SemaphoreType.DMA((len(plan.segments), 3, most - 1))
        scratch[name + "_recv"] = pltpu.SemaphoreType.DMA((len(plan.segments), 3, most))
    inputs = ("x", "og", "vr", "vc") + NAMES + WEIGHTS
    outputs = ("act", "dx", "grads")
    names = inputs + outputs + tuple(scratch)
    any_space = pl.BlockSpec(memory_space=pl.ANY)
    smem = pl.BlockSpec(memory_space=pltpu.SMEM)
    vmem = pl.BlockSpec(memory_space=pltpu.VMEM)
    return pl.pallas_call(
        functools.partial(main_kernel, plan, names),
        out_shape=(
            jax.ShapeDtypeStruct((1, plan.M, 1, plan.hrows, side, width), bf16),
            jax.ShapeDtypeStruct((plan.M, 1, plan.rows, plan.cols, cin // 2), bf16),
            jax.ShapeDtypeStruct((plan.blocks, 16, 128), bf16),
        ),
        in_specs=[any_space, any_space, smem, smem] + [vmem] * (len(NAMES) + len(WEIGHTS)),
        out_specs=(any_space, any_space, vmem),
        scratch_shapes=list(scratch.values()),
        compiler_params=pltpu.CompilerParams(
            collective_id=0, has_side_effects=True, vmem_limit_bytes=56 * 1024 * 1024
        ),
        name="blocks",
    )(*[arrays[name] for name in inputs])


OUTS = (
    "w1", "g1", "b1", "k1", "gg1", "gb1", "sq1", "sqb1", "ex1", "exb1", "e1", "eg1", "eb1",
    "s1", "sg1", "sb1", "w2", "g2", "b2", "k2", "gg2", "gb2", "sq2", "sqb2", "ex2", "exb2",
    "e2", "eg2", "eb2",
)


def unpack_kernel(plan, blocks, act_in, dx_in, *rest):
    count = len(OUTS) + 2
    outs, bufs, sems = rest[:count], rest[count:-1], rest[-1]
    copies = []
    for k, source in enumerate((act_in, dx_in)):
        copies.append(pltpu.make_async_copy(source, outs[k], sems.at[k]))
        copies[-1].start()

    def tile(name, k, first=0, rows=None):
        start, per_tile = plan.starts[name]
        rows = 16 * per_tile if rows is None else rows
        at = start + k * per_tile + first // 16
        return blocks[at : at + rows // 16].reshape(rows, 128).astype(f32)

    tiles = plan.width // 128
    vec = jnp.concatenate([tile("vec", k) for k in range(tiles)], axis=1)
    for k, name in enumerate(OUTS):
        out = bufs[k]
        if name in VEC:
            size = out.shape[0]
            out[...] = vec[VEC[name] : VEC[name] + 1, :size].reshape(size)
        elif name[0] == "k":

            def run(t, carry, name=name, out=out):
                for lane in range(tiles):
                    start, per_tile = plan.starts[name]
                    at = start + lane * per_tile + t * (plan.gw // 16)
                    piece = blocks[pl.ds(at, plan.gw // 16)].reshape(plan.gw, 128)
                    piece = piece.astype(f32).T
                    for j in range(128 // plan.gw):
                        out[t, lane * (128 // plan.gw) + j] = piece[j * plan.gw : (j + 1) * plan.gw]
                return carry

            lax.fori_loop(0, plan.taps, run, 0)
        elif name == "sq2":
            for lane in range(tiles):
                out[128 * lane : 128 * lane + 128] = tile(name, lane).T
        else:
            for lane in range(tiles):
                out[:, 128 * lane : 128 * lane + 128] = tile(name, lane)
        copies.append(pltpu.make_async_copy(out, outs[k + 2], sems.at[k + 2]))
        copies[-1].start()
    for copy in copies:
        copy.wait()


def unpack(plan, act, dx, grads, weights):
    shapes = [jax.ShapeDtypeStruct(w.shape, f32) for w in weights]
    any_space = pl.BlockSpec(memory_space=pl.ANY)
    return pl.pallas_call(
        functools.partial(unpack_kernel, plan),
        out_shape=[jax.ShapeDtypeStruct(v.shape, v.dtype) for v in (act, dx)] + shapes,
        in_specs=[pl.BlockSpec(memory_space=pltpu.VMEM), any_space, any_space],
        out_specs=[any_space] * (len(shapes) + 2),
        scratch_shapes=[pltpu.VMEM(v.shape, v.dtype) for v in shapes]
        + [pltpu.SemaphoreType.DMA((len(shapes) + 2,))],
        compiler_params=pltpu.CompilerParams(vmem_limit_bytes=60 * 1024 * 1024),
        name="unpack",
    )(grads, act, dx)


def body(sizes, input_maps, valid_rows, valid_cols, *rest):
    weights, output_grad = rest[:-1], rest[-1]
    (w1, g1, b1, k1, gg1, gb1, sq1, sqb1, ex1, exb1, e1, eg1, eb1, s1, sg1, sb1) = weights[:16]
    (w2, g2, b2, k2, gg2, gb2, sq2, sqb2, ex2, exb2, e2, eg2, eb2) = weights[16:]
    turned = sq1.T
    plan = Plan(sizes, [v.shape for v in (input_maps, output_grad, w1, k1, turned, sq2)])
    vectors = (
        g1, b1, gg1, gb1, exb1, eg1, eb1, sg1, sb1, sqb1, g2, b2, gg2, gb2, exb2, eg2, eb2, sqb2,
    )
    arrays = dict(
        x=input_maps, og=output_grad, vr=valid_rows.T, vc=valid_cols.T, w1=w1, k1=k1,
        sq1=turned, ex1=ex1, e1=e1, s1=s1, w2=w2, k2=k2, sq2=sq2, ex2=ex2, e2=e2,
        **dict(zip(NAMES, vectors)),
    )
    act, dx, grads = run_main(plan, arrays)
    act, dx, *out = unpack(plan, act, dx, grads, weights[:6] + (turned,) + weights[7:])
    out[6] = out[6].T
    return (act, dx, *out)


def solution(mesh):
    tiled = P(None, "img", "row", None, None)
    image = P(None, "img")
    sizes = tuple(mesh.shape[name] for name in ("section", "img", "row"))
    return jax.shard_map(
        functools.partial(body, sizes),
        mesh=mesh,
        in_specs=(tiled, image, image) + (P(),) * 29 + (tiled,),
        out_specs=(
            P("section", None, "img", "row", None, None),
            P(None, "img", "row", None, "section"),
        )
        + (P(),) * 29,
        check_vma=False,
    )
```

```python
import functools

import jax
import jax.numpy as jnp
from jax import lax
from jax.experimental import pallas as pl
from jax.experimental.pallas import tpu as pltpu
from jax.sharding import PartitionSpec as P

epsilon = 1e-05
f32 = jnp.float32
bf16 = jnp.bfloat16
MESH = pl.DeviceIdType.MESH
PHASES = ((0, 0), (0, 1), (1, 0), (1, 1))
EXCHANGES = 12
NAMES = (
    "g1", "b1", "gg1", "gb1", "exb1", "eg1", "eb1", "sg1", "sb1", "sqb1",
    "g2", "b2", "gg2", "gb2", "exb2", "eg2", "eb2", "sqb2",
)
VEC = {name: k for k, name in enumerate(NAMES)}
VEC_ROWS = 32


def segments_of(cin, width, taps, group, sq1, sq2, devices):
    layout = (
        (("e2", width), ("sq2", sq2), ("ex2", sq2)),
        (("k2", taps * group), ("w2", width)),
        (("e1", width), ("s1", cin), ("sq1", sq1), ("ex1", sq1)),
        (("k1", taps * group), ("vec", VEC_ROWS)),
        (("w1", cin),),
    )
    starts, segments, at = {}, [], 0
    for parts in layout:
        base = at
        for name, rows in parts:
            starts[name] = (at, rows // 16)
            at += rows // 16 * (width // 128)
        used = at
        at = base + -(-(at - base) // devices) * devices
        segments.append((base, at - base, used))
    return starts, tuple(segments), at


def sigmoid(v):
    return 0.5 * jnp.tanh(0.5 * v) + 0.5


def silu(v):
    return v * sigmoid(v)


def slope(v):
    s = sigmoid(v)
    return s * (1.0 + v * (1.0 - s))


def dot(left, right):
    return jnp.dot(left, right, preferred_element_type=f32)


def dot_nt(left, right):
    return lax.dot_general(left, right, (((1,), (1,)), ((), ())), preferred_element_type=f32)


def dot_tn(left, right):
    return lax.dot_general(left, right, (((0,), (0,)), ((), ())), preferred_element_type=f32)


def parts_of(v):
    high = v.astype(bf16).astype(f32)
    return high, v - high


def stacked(rows, width):
    ids = lax.broadcasted_iota(jnp.int32, (16, width), 0)
    total = jnp.zeros((16, width), f32)
    for k, row in enumerate(rows):
        total = jnp.where(ids == k, jnp.broadcast_to(row, (16, width)), total)
    return total.astype(bf16)


def small_dot(row, weight, form):
    out = form(stacked(parts_of(row), row.shape[1]), weight)
    return out[0:1] + out[1:2]


def small_outer(left, right):
    lh, ll = parts_of(left)
    rh, rl = parts_of(right)
    return dot_tn(
        stacked((lh, ll, lh, ll), left.shape[1]), stacked((rh, rh, rl, rl), right.shape[1])
    )


def fold(v):
    return v[0:8] + v[8:16]


def column(acc):
    return jnp.sum(acc, axis=0, keepdims=True)


class Plan:
    def __init__(self, mesh_sizes, args):
        self.S, self.I, self.R = mesh_sizes
        x, og, w1, k1, sq1, sq2 = args
        self.M, _, self.rows, self.cols, self.cin = x
        _, _, self.hrows, self.side, self.width = og
        self.taps, self.groups, self.gw, _ = k1
        self.q1, self.q2 = sq1[0], sq2[1]
        self.each = self.M // self.S
        self.copies = self.R // self.each
        self.pix = self.side * self.side
        self.band = self.pix // self.cols
        self.bands = 2 * self.side // self.band
        self.starts, self.segments, self.blocks = segments_of(
            self.cin, self.width, self.taps, self.gw, self.q1, self.q2, self.S * self.I * self.R
        )


def main_kernel(plan, names, *refs):
    ref = dict(zip(names, refs))
    S, I, R = plan.S, plan.I, plan.R
    side, width, pix, cin = plan.side, plan.width, plan.pix, plan.cin
    half_width = width // 2
    s, i, r = lax.axis_index("section"), lax.axis_index("img"), lax.axis_index("row")
    mine = s * plan.each + r // plan.copies
    waits = []

    barrier = pltpu.get_barrier_semaphore()
    peers = []
    for ds in range(S):
        for dr in range(R):
            if ds or dr:
                peers.append((lax.rem(s + ds, S), i, lax.rem(r + dr, R)))
    for di in range(1, I):
        peers.append((s, lax.rem(i + di, I), r))
    for peer in peers:
        pl.semaphore_signal(barrier, inc=1, device_id=peer, device_id_type=MESH)

    own = []
    loads = {}

    def load(*which):
        for name in which:
            at = (NAMES + WEIGHTS).index(name)
            loads[name] = pltpu.make_async_copy(ref[name], ref[name + "_v"], ref["loads"].at[at])
            loads[name].start()

    def need(name):
        if name in loads:
            loads.pop(name).wait()
        return ref[name + "_v"]

    load("w1", "g1", "b1")
    for name, rows in (("x", plan.rows), ("og", plan.hrows)):
        copy = pltpu.make_async_copy(
            ref[name].at[mine, 0],
            ref[name + "_in"].at[pl.ds(r * rows, rows)],
            ref[name + "_recv"].at[r],
        )
        copy.start()
        own.append(copy)
    pl.semaphore_wait(barrier, len(peers))
    for name, rows in (("x", plan.rows), ("og", plan.hrows)):
        for d in range(1, R):
            t = lax.rem(r + d, R)
            copy = pltpu.make_async_remote_copy(
                src_ref=ref[name].at[s * plan.each + t // plan.copies, 0],
                dst_ref=ref[name + "_in"].at[pl.ds(r * rows, rows)],
                send_sem=ref[name + "_send"].at[d - 1],
                recv_sem=ref[name + "_recv"].at[r],
                device_id=(s, i, t),
                device_id_type=MESH,
            )
            copy.start()
            waits.append(copy.wait_send)

    load("s1", "kk", *NAMES[2:], "sq1", "ex1", "e1", "w2", "sq2", "ex2", "e2")

    def arrived(name, rows, position, d):
        if d == 0:
            own[position].wait()
        else:
            t = lax.rem(r + d, R)
            there = ref[name + "_in"].at[pl.ds(t * rows, rows)]
            pltpu.make_async_remote_copy(
                src_ref=there,
                dst_ref=there,
                send_sem=ref[name + "_send"].at[d - 1],
                recv_sem=ref[name + "_recv"].at[t],
                device_id=(s, i, t),
                device_id_type=MESH,
            ).wait_recv()

    st = ref["st"]

    def pairs_of(k):
        return 2 if k in (0, 1, 9) else 1

    def stats_copy(k, d, slot):
        return pltpu.make_async_remote_copy(
            src_ref=st.at[k, slot, pl.ds(0, pairs_of(k))],
            dst_ref=st.at[k, slot, pl.ds(0, pairs_of(k))],
            send_sem=ref["st_send"].at[k, d - 1],
            recv_sem=ref["st_recv"].at[k, slot],
            device_id=(s, lax.rem(i + d, I), r),
            device_id_type=MESH,
        )

    def post(k, rows):
        ids = lax.broadcasted_iota(jnp.int32, (8, 128), 0)
        rows = [*rows, *([None] * (len(rows) % 2))]
        for pair in range(len(rows) // 2):
            value = jnp.zeros((8, 128), f32)
            for j in range(8):
                row = rows[2 * pair + j // 4]
                if row is not None:
                    piece = row[:, 128 * (j % 4) : 128 * (j % 4) + 128]
                    value = jnp.where(ids == j, jnp.broadcast_to(piece, (8, 128)), value)
            st[k, i, pair] = value
        for d in range(1, I):
            stats_copy(k, d, i).start()

    def fetch(k, count=2):
        for d in range(1, I):
            stats_copy(k, d, i).wait_send()
            stats_copy(k, d, lax.rem(i + d, I)).wait_recv()
        out = []
        for pair in range((count + 1) // 2):
            value = st[k, 0, pair]
            for j in range(1, I):
                value = value + st[k, j, pair]
            for half in range(2):
                out.append(
                    jnp.concatenate([value[4 * half + j : 4 * half + j + 1] for j in range(4)], 1)
                )
        return out

    def vector(name):
        row = need(name)[...].astype(f32)
        return row.reshape(1, row.shape[0])

    vr, vc = ref["vr"][0, mine], ref["vc"][0, mine]
    q_ids = lax.broadcasted_iota(jnp.int32, (side, width), 0)
    first_col, last_col = q_ids == 0, q_ids == side - 1
    cm = ref["cm"]
    for b in range(2):
        cm[b] = (2 * q_ids + b < vc).astype(f32)

    def mask_row(a, b, p):
        return cm[b] * (2 * p + a < vr).astype(f32)

    row_count = jnp.full((1, width), vr * vc, jnp.int32).astype(f32)
    half_count = jnp.full((1, width), ((vr + 1) // 2) * ((vc + 1) // 2), jnp.int32).astype(f32)

    def over_rows(step, *accs):
        init = tuple(jnp.zeros((8, width), f32) for _ in range(accs[0] if accs else 0))

        def run(p, carry):
            out = step(p)
            if not carry:
                return carry
            return tuple(c + fold(o) for c, o in zip(carry, out))

        return tuple(column(c) for c in lax.fori_loop(0, side, run, init, unroll=4))

    def full_dot(out, left, weight, form=dot):
        wide = out.shape[-1]
        step = min(256, wide)
        for h in range(wide // step):
            cut = slice(h * step, h * step + step)
            w = weight[:, cut] if form is dot else weight[cut, :]
            out[:, :, cut] = form(left, w).reshape(side, side, step).astype(out.dtype)

    def flat(value):
        return value.reshape(pix, value.shape[-1])

    def lines(ref_, start=0):
        return flat(ref_[start : start + side])

    G, F = ref["local"], ref["grads"]
    lead = None if plan.copies == 1 else (lax.rem(r, plan.copies) == 0).astype(f32)

    def put(name, value, row=0, lane=0):
        if lead is not None:
            value = value * lead
        start, per_tile = plan.starts[name]
        count = value.shape[0] // 16
        for k in range(value.shape[1] // 128):
            piece = value[:, 128 * k : 128 * k + 128].astype(bf16).reshape(count, 16, 128)
            at = start + (lane // 128 + k) * per_tile + row // 16
            G[at : at + count] = piece

    levels = (
        (S, s, lambda t: (t, i, r), G, ref["got0"], ref["sum0"]),
        (R, r, lambda t: (s, i, t), ref["sum0"], ref["got1"], ref["sum1"]),
        (I, i, lambda t: (s, t, r), ref["sum1"], ref["got2"], None),
    )
    shares = (1, S, S * R, S * R * I)

    def scatter_copies(g, level, outgoing):
        count, me, device, source, got, _ = levels[level]
        base = plan.segments[g][0] // shares[level]
        piece = plan.segments[g][1] // shares[level + 1]
        for d in range(1, count):
            t = lax.rem(me + d, count)
            slot = me if outgoing else t
            copy = pltpu.make_async_remote_copy(
                src_ref=source.at[pl.ds(base + t * piece, piece)],
                dst_ref=got.at[pl.ds(base + slot * piece, piece)],
                send_sem=ref["rs_send"].at[g, level, d - 1],
                recv_sem=ref["rs_recv"].at[g, level, slot],
                device_id=device(t),
                device_id_type=MESH,
            )
            if outgoing:
                copy.start()
                waits.append(copy.wait_send)
            else:
                copy.wait_recv()

    def add_up(g, level):
        count, me, _, source, got, out = levels[level]
        base = plan.segments[g][0] // shares[level]
        piece = plan.segments[g][1] // shares[level + 1]
        at = plan.segments[g][0] // shares[level + 1]
        if out is None:
            out = F
            at = plan.segments[g][0] + ((s * R + r) * I + i) * piece
        step = next(k for k in (18, 16, 14, 12, 10, 9, 8, 7, 6, 5, 4, 3, 2, 1) if piece % k == 0)

        def run(k, carry):
            total = source[pl.ds(base + me * piece + k * step, step)].astype(f32)
            for d in range(1, count):
                t = lax.rem(me + d, count)
                total = total + got[pl.ds(base + t * piece + k * step, step)].astype(f32)
            out[pl.ds(at + k * step, step)] = total.astype(bf16)
            return carry

        lax.fori_loop(0, piece // step, run, 0)

    def gather_copies(g, level, outgoing):
        count, me, device, _, _, _ = levels[level]
        base, size, _ = plan.segments[g]
        for above in range(level):
            base = base + levels[above][1] * (size // shares[above + 1])
        piece = size // shares[level + 1]
        for d in range(1, count):
            t = lax.rem(me + d, count)
            slot = me if outgoing else t
            there = F.at[pl.ds(base + slot * piece, piece)]
            copy = pltpu.make_async_remote_copy(
                src_ref=there,
                dst_ref=there,
                send_sem=ref["ag_send"].at[g, level, d - 1],
                recv_sem=ref["ag_recv"].at[g, level, slot],
                device_id=device(t),
                device_id_type=MESH,
            )
            if outgoing:
                copy.start()
                waits.append(copy.wait_send)
            else:
                copy.wait_recv()

    done = [0] * len(plan.segments)

    def advance(*which):
        for g in which:
            k = done[g]
            if k == 7:
                continue
            done[g] += 1
            if k == 0:
                base, size, used = plan.segments[g]
                if used < base + size:
                    G[used : base + size] = jnp.zeros((base + size - used, 16, 128), bf16)
            elif k <= 3:
                scatter_copies(g, k - 1, False)
                add_up(g, k - 1)
            else:
                gather_copies(g, 6 - k, False)
            if k < 3:
                scatter_copies(g, k, True)
            elif k < 6:
                gather_copies(g, 5 - k, True)

    vec_grads = {}

    gw = plan.gw
    wide = 4 * gw
    on_diagonal = (
        lax.rem(lax.broadcasted_iota(jnp.int32, (width, wide), 0) // gw, 4)
        == lax.broadcasted_iota(jnp.int32, (width, wide), 1) // gw
    )

    def blocks(block, out):
        kernels = need("kk")
        spread = (
            lax.rem(lax.broadcasted_iota(jnp.int32, (2 * gw, wide), 1), gw) + block * gw
            == lax.broadcasted_iota(jnp.int32, (2 * gw, wide), 0)
        ).astype(f32).astype(bf16)

        def run(t, carry):
            rep = dot(kernels[t].reshape(width, 2 * gw), spread)
            rep = jnp.where(on_diagonal, rep, 0.0).astype(bf16)
            for h in range(width // wide):
                out[t, h] = rep[h * wide : (h + 1) * wide]
            return carry

        lax.fori_loop(0, plan.taps, run, 0)

    def groups_grad(name, taps, turned):
        lane = lax.broadcasted_iota(jnp.int32, (gw, wide), 1) // gw
        for t, (var, start) in enumerate(taps):
            for h in range(width // wide):
                cut = slice(h * wide, (h + 1) * wide)
                res = dot(turned[h], flat(var[start : start + side, :, cut]))
                out = res[0:gw]
                for j in range(1, 4):
                    out = jnp.where(lane == j, res[j * gw : (j + 1) * gw], out)
                put(name, out, t * gw, h * wide)

    band, bands = plan.band, plan.bands
    bhalf = band // 2
    out_id = lax.broadcasted_iota(jnp.int32, (pix, pix), 0)
    in_id = lax.broadcasted_iota(jnp.int32, (pix, pix), 1)

    def source(o):
        quarter = o // (bhalf * side)
        down = lax.rem(o, bhalf * side) // side
        return (2 * down + quarter // 2) * plan.cols + 2 * lax.rem(o, side) + lax.rem(quarter, 2)

    ref["sort"][...] = (source(out_id) == in_id).astype(f32).astype(bf16)
    ref["unsort"][...] = (source(in_id) == out_id).astype(f32).astype(bf16)

    xp, R1 = ref["xp"], ref["R1"]
    totals = [jnp.zeros((8, width), f32)] * 2
    by_band = plan.rows % band == 0
    if not by_band:
        for d in range(R):
            arrived("x", plan.rows, 0, d)
    for d in range(bands):
        if by_band:
            if d % (plan.rows // band) == 0:
                arrived("x", plan.rows, 0, d // (plan.rows // band))
            k = lax.rem(r * (plan.rows // band) + d, bands)
        else:
            k = d
        block = ref["x_in"][pl.ds(k * band, band)].reshape(pix, cin)
        block = dot(ref["sort"][...], block).astype(bf16)
        xp[k] = block.reshape(4 * bhalf, side, cin)
        full_dot(R1.at[k], block, need("w1"))
        for j in range(4 * bhalf):
            a, b = PHASES[j // bhalf]
            v = R1[k, j]
            mv = v * mask_row(a, b, k * bhalf + j % bhalf)
            totals = [totals[0] + fold(mv), totals[1] + fold(mv * v)]
    even = xp.at[:, 0:bhalf]

    def at_phase(ab, p):
        return p // bhalf, ab * bhalf + lax.rem(p, bhalf)

    post(0, [column(totals[0]), column(totals[1]), row_count, half_count])
    SC = ref["SC"]
    full_dot(SC, even[...].reshape(pix, cin), need("s1"))
    blocks(0, ref["bd1"])

    def moments(field):
        def step(p):
            v = field[p].astype(f32)
            mv = v * mask_row(0, 0, p)
            return mv, mv * v

        return over_rows(step, 2)

    short_sums = moments(SC)

    def coefficients(first, second, inverse, gain, shift):
        mean = first * inverse
        scale = lax.rsqrt(second * inverse - mean * mean + epsilon)
        a = scale * gain
        return a, shift - mean * a, scale, -mean * scale

    tot = fetch(0, 4)
    inv_full, inv_half = 1.0 / tot[2], 1.0 / tot[3]
    n1 = coefficients(tot[0], tot[1], inv_full, vector("g1"), vector("b1"))

    va = ref["va"]
    va[3:6, 0:1] = jnp.zeros((3, 1, side, width), bf16)

    def shifted(v, edge, amount):
        return jnp.where(edge, 0.0, pltpu.roll(v, amount, 0))

    for ab, (a, b) in enumerate(PHASES):

        def step(p, ab=ab, a=a, b=b):
            v = mask_row(a, b, p) * silu(R1[at_phase(ab, p)] * n1[0] + n1[1])
            slot = (0, 1, 3, 4)[ab]
            va[slot, p + a] = v.astype(bf16)
            if b:
                va[slot + 1, p + a] = shifted(v, first_col, 1).astype(bf16)

        over_rows(step)
    taps1 = []
    for t in range(9):
        u, v = t // 3, t % 3
        slot = (0, 1, 3, 4)[2 * (u != 1) + (v != 1)] + (v == 0)
        taps1.append((va.at[slot], 1 if u == 2 else 0))

    def convolve(taps, weights, out):
        for h in range(width // wide):
            cut = slice(h * wide, (h + 1) * wide)
            acc = None
            for t, (var, start) in enumerate(taps):
                term = dot(flat(var[start : start + side, :, cut]), weights[t, h])
                acc = term if acc is None else acc + term
            out[:, :, cut] = acc.astype(bf16).reshape(side, side, wide)

    c1 = ref["c1"]
    convolve(taps1, ref["bd1"], c1)
    post(1, [*moments(c1), *short_sums])
    blocks(1, ref["bd2"])
    tot = fetch(1, 4)
    nc1 = coefficients(tot[0], tot[1], inv_half, vector("gg1"), vector("gb1"))
    ns = coefficients(tot[2], tot[3], inv_half, vector("sg1"), vector("sb1"))

    def excite(conv, norm, hidden, gated, sq, sq_form, sqb, ex, exb):
        def step(p):
            v = mask_row(0, 0, p) * silu(conv[p].astype(f32) * norm[0] + norm[1])
            hidden[p] = v
            return (v,)

        (total,) = over_rows(step, 1)
        pooled = total / half_count
        pre = small_dot(pooled, sq[...], sq_form) + sqb
        inner = silu(pre)
        gate = sigmoid(small_dot(inner, ex[...], dot) + exb)

        def step_two(p):
            gated[p] = (hidden[p] * gate).astype(bf16)

        over_rows(step_two)
        return pooled, pre, inner, gate

    H1, ga1 = ref["H1"], ref["ga1"]
    kept1 = excite(
        c1, nc1, H1, ga1, need("sq1"), dot_nt, vector("sqb1"), need("ex1"), vector("exb1")
    )
    E1 = ref["E1"]
    full_dot(E1, lines(ga1), need("e1"))
    post(2, moments(E1))
    tot = fetch(2)
    ne = coefficients(tot[0], tot[1], inv_half, vector("eg1"), vector("eb1"))
    ent = ref["ent"]

    def step(p):
        v = E1[p] * ne[0] + SC[p] * ns[0] + (ne[1] + ns[1])
        ent[p] = (mask_row(0, 0, p) * silu(v)).astype(bf16)

    over_rows(step)

    def send_out(source, out, rows, target, steps=None):
        for k in range(R // plan.copies) if steps is None else steps:
            t = lax.rem(r + plan.copies * k, R)
            there = ref[out].at[0, mine, 0] if out == "act" else ref[out].at[mine, 0]
            here = source.at[pl.ds(t * rows, rows)]
            copy = pltpu.make_async_remote_copy(
                src_ref=here,
                dst_ref=there,
                send_sem=ref[out + "_send"].at[target, k],
                recv_sem=ref[out + "_recv"].at[mine],
                device_id=(target, i, t),
                device_id_type=MESH,
            )
            if k:
                copy.start()
                waits.append(copy.wait_send)
            else:
                local = pltpu.make_async_copy(here, there, ref[out + "_recv"].at[mine])

                @pl.when(s == target)
                def _():
                    local.start()

                @pl.when(s != target)
                def _():
                    copy.start()

                def finish(copy=copy):
                    @pl.when(s != target)
                    def _():
                        copy.wait_send()

                waits.append(finish)

    send_out(ent, "act", plan.hrows, 0)

    R2 = ref["R2"]
    full_dot(R2, lines(ent), need("w2"))
    post(3, moments(R2))
    tot = fetch(3)
    n2 = coefficients(tot[0], tot[1], inv_half, vector("g2"), vector("b2"))
    vb = ref["vb"]
    vb[:, 0:1] = jnp.zeros((3, 1, side, width), bf16)
    vb[:, side + 1 :] = jnp.zeros((3, 1, side, width), bf16)

    def three(out, p, v):
        out[0, p + 1] = shifted(v, first_col, 1).astype(bf16)
        out[1, p + 1] = v.astype(bf16)
        out[2, p + 1] = shifted(v, last_col, side - 1).astype(bf16)

    def step(p):
        three(vb, p, mask_row(0, 0, p) * silu(R2[p] * n2[0] + n2[1]))

    over_rows(step)
    taps2 = [(vb.at[t % 3], t // 3) for t in range(9)]
    c2 = ref["c2"]
    convolve(taps2, ref["bd2"], c2)
    post(4, moments(c2))
    tot = fetch(4)
    nc2 = coefficients(tot[0], tot[1], inv_half, vector("gg2"), vector("gb2"))
    H2, ga2 = ref["H2"], ref["ga2"]
    kept2 = excite(
        c2, nc2, H2, ga2, need("sq2"), dot, vector("sqb2"), need("ex2"), vector("exb2")
    )
    E2 = ref["E2"]
    full_dot(E2, lines(ga2), need("e2"))
    post(5, moments(E2))
    for d in range(R):
        arrived("og", plan.hrows, 1, d)
    tot = fetch(5)
    ne2 = coefficients(tot[0], tot[1], inv_half, vector("eg2"), vector("eb2"))
    leave, D, og = ref["leave"], ref["D"], ref["og_in"]

    def step(p):
        e = E2[p]
        v = e * ne2[0] + ne2[1] + ent[p].astype(f32)
        sg = sigmoid(v)
        m = mask_row(0, 0, p)
        leave[p] = (m * v * sg).astype(bf16)
        g = og[p].astype(f32) * m * (sg * (1.0 + v * (1.0 - sg)))
        D[p] = g
        return g, g * (e * ne2[2] + ne2[3])

    parts = over_rows(step, 2)
    vec_grads["eb2"], vec_grads["eg2"] = parts
    post(6, parts)
    send_out(leave, "act", plan.hrows, 1)

    def back_rule(sums, inverse, gain, norm):
        a = gain * norm[2]
        k0 = a * (sums[0] + norm[3] * sums[1]) * inverse
        return a, k0, a * norm[2] * sums[1] * inverse

    def back_excite(dg, kept, hidden, conv, norm, sq, sq_form, ex, out):
        pooled, pre, inner, gate = kept

        def step(p):
            return (dg[p].astype(f32) * hidden[p],)

        (dgate,) = over_rows(step, 1)
        dpre = dgate * gate * (1.0 - gate)
        dsq = small_dot(dpre, ex[...], dot_nt) * slope(pre)
        dpool = small_dot(dsq, sq[...], sq_form) / half_count

        def step_two(p):
            v = conv[p].astype(f32)
            g = (dg[p].astype(f32) * gate + dpool) * mask_row(0, 0, p)
            g = g * slope(v * norm[0] + norm[1])
            out[p] = g
            return g, g * (v * norm[2] + norm[3])

        return over_rows(step_two, 2), dpre, dsq

    def excite_grads(name, kept, dpre, dsq):
        pooled, pre, inner, gate = kept
        put("sq" + name, small_outer(dsq, pooled))
        put("ex" + name, small_outer(inner, dpre))
        vec_grads["exb" + name] = dpre
        count = dsq.shape[1]
        eye = (
            lax.broadcasted_iota(jnp.int32, (count, width), 0)
            == lax.broadcasted_iota(jnp.int32, (count, width), 1)
        ).astype(f32).astype(bf16)
        vec_grads["sqb" + name] = small_dot(dsq, eye, dot)

    def turn(gradient_ref, start):
        out = []
        for h in range(width // wide):
            piece = flat(gradient_ref[start : start + side, :, h * wide : (h + 1) * wide])
            out.append(piece.astype(f32).T.astype(bf16))
        return out

    d1, dg, GR = ref["d1"], ref["dg"], ref["GR"]
    tot = fetch(6)
    rule = back_rule((tot[0], tot[1]), inv_half, vector("eg2"), ne2)

    def step(p):
        d1[p] = (rule[0] * D[p] - mask_row(0, 0, p) * (rule[1] + rule[2] * E2[p])).astype(bf16)

    over_rows(step)
    full_dot(dg, lines(d1), need("e2"), dot_nt)
    parts, dpre, dsq = back_excite(dg, kept2, H2, c2, nc2, need("sq2"), dot_nt, need("ex2"), GR)
    vec_grads["gb2"], vec_grads["gg2"] = parts
    post(7, parts)
    put("e2", dot_tn(lines(ga2), lines(d1)))
    excite_grads("2", kept2, dpre, dsq)
    advance(0)
    tot = fetch(7)
    advance(0)
    rule = back_rule((tot[0], tot[1]), inv_half, vector("gg2"), nc2)
    vd = ref["vd"]
    vd[:, 0:1] = jnp.zeros((3, 1, side, width), bf16)
    vd[:, side + 1 :] = jnp.zeros((3, 1, side, width), bf16)

    def step(p):
        v = rule[0] * GR[p] - mask_row(0, 0, p) * (rule[1] + rule[2] * c2[p].astype(f32))
        three(vd, p, v)

    over_rows(step)

    def convolve_back(taps, weights, out):
        for h in range(width // wide):
            cut = slice(h * wide, (h + 1) * wide)
            acc = None
            for t, var, start in taps:
                term = dot_nt(flat(var[start : start + side, :, cut]), weights[t, h])
                acc = term if acc is None else acc + term
            out[:, :, cut] = acc.reshape(side, side, wide)

    DA = ref["DA"]
    convolve_back(
        [(t, vd.at[2 - t % 3], 2 - t // 3) for t in range(9)],
        ref["bd2"],
        DA.at[0],
    )

    def step(p):
        v = R2[p]
        g = DA[0, p] * mask_row(0, 0, p) * slope(v * n2[0] + n2[1])
        GR[p] = g
        return g, g * (v * n2[2] + n2[3])

    parts = over_rows(step, 2)
    vec_grads["b2"], vec_grads["g2"] = parts
    post(8, parts)
    groups_grad("k2", taps2, turn(vd.at[1], 1))
    advance(0)
    tot = fetch(8)
    rule = back_rule((tot[0], tot[1]), inv_half, vector("g2"), n2)

    def step(p):
        d1[p] = (rule[0] * GR[p] - mask_row(0, 0, p) * (rule[1] + rule[2] * R2[p])).astype(bf16)

    over_rows(step)
    full_dot(GR, lines(d1), need("w2"), dot_nt)
    advance(0)

    def step(p):
        e, sc = E1[p], SC[p]
        g = (D[p] + GR[p]).astype(bf16).astype(f32)
        g = g * mask_row(0, 0, p) * slope(e * ne[0] + sc * ns[0] + (ne[1] + ns[1]))
        D[p] = g
        return g, g * (e * ne[2] + ne[3]), g * (sc * ns[2] + ns[3])

    parts = over_rows(step, 3)
    vec_grads["eb1"], vec_grads["eg1"], vec_grads["sg1"] = parts
    vec_grads["sb1"] = parts[0]
    post(9, parts)
    put("w2", dot_tn(lines(ent), lines(d1)))
    advance(1, 0)
    tot = fetch(9, 3)
    rule_e = back_rule((tot[0], tot[1]), inv_half, vector("eg1"), ne)
    rule_s = back_rule((tot[0], tot[2]), inv_half, vector("sg1"), ns)
    d2 = ref["d2"]

    def step(p):
        g, m = D[p], mask_row(0, 0, p)
        d1[p] = (rule_e[0] * g - m * (rule_e[1] + rule_e[2] * E1[p])).astype(bf16)
        d2[p] = (rule_s[0] * g - m * (rule_s[1] + rule_s[2] * SC[p])).astype(bf16)

    over_rows(step)
    full_dot(dg, lines(d1), need("e1"), dot_nt)
    advance(1, 0)
    parts, dpre, dsq = back_excite(dg, kept1, H1, c1, nc1, need("sq1"), dot, need("ex1"), GR)
    vec_grads["gb1"], vec_grads["gg1"] = parts
    post(10, parts)
    put("e1", dot_tn(lines(ga1), lines(d1)))
    put("s1", dot_tn(even[...].reshape(pix, cin), lines(d2)))
    excite_grads("1", kept1, dpre, dsq)
    advance(2, 1, 0)
    tot = fetch(10)
    rule = back_rule((tot[0], tot[1]), inv_half, vector("gg1"), nc1)

    def step(p):
        v = rule[0] * GR[p] - mask_row(0, 0, p) * (rule[1] + rule[2] * c1[p].astype(f32))
        three(vd, p, v)

    over_rows(step)
    sums = []
    for ab, (a, b) in enumerate(PHASES):
        chosen = []
        for t in range(9):
            u, v = t // 3, t % 3
            if (u != 1) == bool(a) and (v != 1) == bool(b):
                chosen.append((t, vd.at[2 if v == 0 else 1], 2 if u == 0 else 1))
        convolve_back(chosen, ref["bd1"], DA.at[ab])
        if ab == 1:
            advance(2, 1, 0)

        def step(p, ab=ab, a=a, b=b):
            v = R1[at_phase(ab, p)]
            g = DA[ab, p] * mask_row(a, b, p) * slope(v * n1[0] + n1[1])
            DA[ab, p] = g
            return g, g * (v * n1[2] + n1[3])

        sums.append(over_rows(step, 2))
    parts = (sum(x[0] for x in sums), sum(x[1] for x in sums))
    vec_grads["b1"], vec_grads["g1"] = parts
    post(11, parts)
    groups_grad("k1", taps1, turn(vd.at[1], 1))
    ids = lax.broadcasted_iota(jnp.int32, (VEC_ROWS, width), 0)
    value = jnp.zeros((VEC_ROWS, width), f32)
    for name, at in VEC.items():
        value = jnp.where(ids == at, jnp.broadcast_to(vec_grads[name], value.shape), value)
    put("vec", value)
    advance(3, 2, 1, 0)
    tot = fetch(11)
    rule = back_rule((tot[0], tot[1]), inv_full, vector("g1"), n1)
    dr = ref["dr"]
    for ab, (a, b) in enumerate(PHASES):

        def step(p, ab=ab, a=a, b=b):
            v = rule[0] * DA[ab, p]
            v = v - mask_row(a, b, p) * (rule[1] + rule[2] * R1[at_phase(ab, p)])
            dr[at_phase(ab, p)] = v.astype(bf16)

        over_rows(step)
    total = None
    for k in range(bands):
        term = dot_tn(xp[k].reshape(pix, cin), dr[k].reshape(pix, width))
        total = term if total is None else total + term
    put("w1", total)
    advance(4, 3, 2, 1, 0)
    cut = cin // 2
    ref["dxo0"][...] = jnp.zeros((2 * side, plan.cols, 128), bf16)
    ref["dxo1"][...] = jnp.zeros((2 * side, plan.cols, 128), bf16)
    stepwise = plan.each == bands
    for d in [*range(1, bands), 0]:
        k = lax.rem(r + plan.copies * d, R) * plan.rows // band if stepwise else d
        for part in range(2):
            dxo = ref[f"dxo{part}"]
            rows = slice(part * cut, (part + 1) * cut)
            v = dot_nt(dr[k].reshape(pix, width), need("w1")[rows, :])
            w = dot_nt(
                d2[pl.ds(k * bhalf, bhalf)].reshape(bhalf * side, width), need("s1")[rows, :]
            )
            v = jnp.concatenate([v[: bhalf * side] + w, v[bhalf * side :]], axis=0)
            v = dot(ref["unsort"][...], v.astype(bf16)).astype(bf16)
            dxo[pl.ds(k * band, band), :, :cut] = v.reshape(band, plan.cols, cut)
            if stepwise:
                send_out(dxo, "dx", plan.rows, part, (d,))
        if d % 2 == 0:
            advance(0, 1, 2, 3, 4)
    if not stepwise:
        send_out(ref["dxo0"], "dx", plan.rows, 0)
        send_out(ref["dxo1"], "dx", plan.rows, 1)
    while min(done) < 7:
        advance(0, 1, 2, 3, 4)
    for wait in waits:
        wait()
    for m in range(plan.M):
        t = (m % plan.each) * plan.copies + lax.rem(r, plan.copies)
        for out in ("act", "dx"):
            there = ref[out].at[0, m, 0] if out == "act" else ref[out].at[m, 0]
            pltpu.make_async_copy(there, there, ref[out + "_recv"].at[m]).wait()


WEIGHTS = ("w1", "kk", "sq1", "ex1", "e1", "s1", "w2", "sq2", "ex2", "e2")


def run_main(plan, arrays):
    side, width, cin = plan.side, plan.width, plan.cin
    wide = 4 * plan.gw
    field = (side, side, width)
    scratch = {
        "x_in": pltpu.VMEM((2 * side, plan.cols, cin), bf16),
        "og_in": pltpu.VMEM(field, bf16),
        "st": pltpu.VMEM((EXCHANGES, plan.I, 2, 8, 128), f32),
        "cm": pltpu.VMEM((2, side, width), f32),
        "bd1": pltpu.VMEM((plan.taps, width // wide, wide, wide), bf16),
        "bd2": pltpu.VMEM((plan.taps, width // wide, wide, wide), bf16),
        "sort": pltpu.VMEM((plan.pix, plan.pix), bf16),
        "unsort": pltpu.VMEM((plan.pix, plan.pix), bf16),
        "xp": pltpu.VMEM((plan.bands, 2 * plan.band, side, cin), bf16),
        "R1": pltpu.VMEM((plan.bands, 2 * plan.band, side, width), f32),
        "va": pltpu.VMEM((6, side + 1, side, width), bf16),
        "vb": pltpu.VMEM((3, side + 2, side, width), bf16),
        "vd": pltpu.VMEM((3, side + 2, side, width), bf16),
        "DA": pltpu.VMEM((4,) + field, f32),
        "dr": pltpu.VMEM((plan.bands, 2 * plan.band, side, width), bf16),
        "dxo0": pltpu.VMEM((2 * side, plan.cols, 128), bf16),
        "dxo1": pltpu.VMEM((2 * side, plan.cols, 128), bf16),
    }
    for name in ("SC", "H1", "E1", "R2", "H2", "E2", "D", "GR"):
        scratch[name] = pltpu.VMEM(field, f32)
    for name in ("c1", "ga1", "ent", "c2", "ga2", "leave", "d1", "d2", "dg"):
        scratch[name] = pltpu.VMEM(field, bf16)
    for name in ("x", "og"):
        scratch[name + "_send"] = pltpu.SemaphoreType.DMA((max(plan.R - 1, 1),))
        scratch[name + "_recv"] = pltpu.SemaphoreType.DMA((plan.R,))
    scratch["st_send"] = pltpu.SemaphoreType.DMA((EXCHANGES, max(plan.I - 1, 1)))
    scratch["st_recv"] = pltpu.SemaphoreType.DMA((EXCHANGES, plan.I))
    for name in ("act", "dx"):
        scratch[name + "_send"] = pltpu.SemaphoreType.DMA((2, plan.R // plan.copies))
        scratch[name + "_recv"] = pltpu.SemaphoreType.DMA((plan.M,))
    for name in NAMES + WEIGHTS:
        scratch[name + "_v"] = pltpu.VMEM(arrays[name].shape, bf16)
    scratch["loads"] = pltpu.SemaphoreType.DMA((len(NAMES + WEIGHTS),))
    scratch["local"] = pltpu.VMEM((plan.blocks, 16, 128), bf16)
    shares = (1, plan.S, plan.S * plan.R)
    for level, share in enumerate(shares):
        scratch[f"got{level}"] = pltpu.VMEM((plan.blocks // share, 16, 128), bf16)
        if level:
            scratch[f"sum{level - 1}"] = pltpu.VMEM((plan.blocks // share, 16, 128), bf16)
    most = max(plan.S, plan.R, plan.I)
    for name in ("rs", "ag"):
        scratch[name + "_send"] = pltpu.SemaphoreType.DMA((len(plan.segments), 3, most - 1))
        scratch[name + "_recv"] = pltpu.SemaphoreType.DMA((len(plan.segments), 3, most))
    inputs = ("x", "og", "vr", "vc") + NAMES + WEIGHTS
    outputs = ("act", "dx", "grads")
    names = inputs + outputs + tuple(scratch)
    any_space = pl.BlockSpec(memory_space=pl.ANY)
    smem = pl.BlockSpec(memory_space=pltpu.SMEM)
    vmem = pl.BlockSpec(memory_space=pltpu.VMEM)
    return pl.pallas_call(
        functools.partial(main_kernel, plan, names),
        out_shape=(
            jax.ShapeDtypeStruct((1, plan.M, 1, plan.hrows, side, width), bf16),
            jax.ShapeDtypeStruct((plan.M, 1, plan.rows, plan.cols, 128), bf16),
            jax.ShapeDtypeStruct((plan.blocks, 16, 128), bf16),
        ),
        in_specs=[any_space, any_space, smem, smem] + [any_space] * (len(NAMES) + len(WEIGHTS)),
        out_specs=(any_space, any_space, vmem),
        scratch_shapes=list(scratch.values()),
        compiler_params=pltpu.CompilerParams(
            collective_id=0, has_side_effects=True, vmem_limit_bytes=56 * 1024 * 1024
        ),
        name="blocks",
    )(*[arrays[name] for name in inputs])


OUTS = (
    "w1", "g1", "b1", "k1", "gg1", "gb1", "sq1", "sqb1", "ex1", "exb1", "e1", "eg1", "eb1",
    "s1", "sg1", "sb1", "w2", "g2", "b2", "k2", "gg2", "gb2", "sq2", "sqb2", "ex2", "exb2",
    "e2", "eg2", "eb2",
)


def unpack_kernel(plan, blocks, *rest):
    count = len(OUTS)
    outs, bufs, sems = rest[:count], rest[count:-1], rest[-1]
    copies = []

    def tile(name, k, first=0, rows=None):
        start, per_tile = plan.starts[name]
        rows = 16 * per_tile if rows is None else rows
        at = start + k * per_tile + first // 16
        return blocks[at : at + rows // 16].reshape(rows, 128).astype(f32)

    tiles = plan.width // 128
    vec = jnp.concatenate([tile("vec", k) for k in range(tiles)], axis=1)
    for k, name in enumerate(OUTS):
        out = bufs[k]
        if name in VEC:
            size = out.shape[0]
            out[...] = vec[VEC[name] : VEC[name] + 1, :size].reshape(size)
        elif name[0] == "k":

            def run(t, carry, name=name, out=out):
                for lane in range(tiles):
                    start, per_tile = plan.starts[name]
                    at = start + lane * per_tile + t * (plan.gw // 16)
                    piece = blocks[pl.ds(at, plan.gw // 16)].reshape(plan.gw, 128)
                    piece = piece.astype(f32).T
                    for j in range(128 // plan.gw):
                        group = lane * (128 // plan.gw) + j
                        out[t, group, :, : plan.gw] = piece[j * plan.gw : (j + 1) * plan.gw]
                return carry

            lax.fori_loop(0, plan.taps, run, 0)
        elif name == "sq2":
            for lane in range(tiles):
                out[128 * lane : 128 * lane + 128] = tile(name, lane).T
        else:
            for lane in range(tiles):
                out[:, 128 * lane : 128 * lane + 128] = tile(name, lane)
        copies.append(pltpu.make_async_copy(out, outs[k], sems.at[k]))
        copies[-1].start()
    for copy in copies:
        copy.wait()


def unpack(plan, grads, weights):
    shapes = []
    for name, w in zip(OUTS, weights):
        shape = w.shape[:3] + (128,) if name[0] == "k" else w.shape
        shapes.append(jax.ShapeDtypeStruct(shape, f32))
    any_space = pl.BlockSpec(memory_space=pl.ANY)
    return pl.pallas_call(
        functools.partial(unpack_kernel, plan),
        out_shape=shapes,
        in_specs=[pl.BlockSpec(memory_space=pltpu.VMEM)],
        out_specs=[any_space] * len(shapes),
        scratch_shapes=[pltpu.VMEM(v.shape, v.dtype) for v in shapes]
        + [pltpu.SemaphoreType.DMA((len(shapes),))],
        compiler_params=pltpu.CompilerParams(vmem_limit_bytes=60 * 1024 * 1024),
        name="unpack",
    )(grads)


def body(sizes, input_maps, valid_rows, valid_cols, *rest):
    weights, output_grad = rest[:-1], rest[-1]
    (w1, g1, b1, k1, gg1, gb1, sq1, sqb1, ex1, exb1, e1, eg1, eb1, s1, sg1, sb1) = weights[:16]
    (w2, g2, b2, k2, gg2, gb2, sq2, sqb2, ex2, exb2, e2, eg2, eb2) = weights[16:]
    turned = sq1.T
    plan = Plan(sizes, [v.shape for v in (input_maps, output_grad, w1, k1, turned, sq2)])
    vectors = (
        g1, b1, gg1, gb1, exb1, eg1, eb1, sg1, sb1, sqb1, g2, b2, gg2, gb2, exb2, eg2, eb2, sqb2,
    )
    arrays = dict(
        x=input_maps, og=output_grad, vr=valid_rows.T, vc=valid_cols.T, w1=w1,
        kk=jnp.concatenate([k1, k2], axis=3),
        sq1=turned, ex1=ex1, e1=e1, s1=s1, w2=w2, sq2=sq2, ex2=ex2, e2=e2,
        **dict(zip(NAMES, vectors)),
    )
    act, dx, grads = run_main(plan, arrays)
    out = list(unpack(plan, grads, weights[:6] + (turned,) + weights[7:]))
    out[6] = out[6].T
    for at in (3, 19):
        out[at] = out[at][..., : plan.gw]
    dx = dx[..., : plan.cin // 2]
    return (act, dx, *out)


def solution(mesh):
    tiled = P(None, "img", "row", None, None)
    image = P(None, "img")
    sizes = tuple(mesh.shape[name] for name in ("section", "img", "row"))
    return jax.shard_map(
        functools.partial(body, sizes),
        mesh=mesh,
        in_specs=(tiled, image, image) + (P(),) * 29 + (tiled,),
        out_specs=(
            P("section", None, "img", "row", None, None),
            P(None, "img", "row", None, "section"),
        )
        + (P(),) * 29,
        check_vma=False,
    )
```

```python
import functools

import jax
import jax.numpy as jnp
from jax import lax
from jax.experimental import pallas as pl
from jax.experimental.pallas import tpu as pltpu
from jax.sharding import PartitionSpec as P

epsilon = 1e-05
f32 = jnp.float32
bf16 = jnp.bfloat16
MESH = pl.DeviceIdType.MESH
PHASES = ((0, 0), (0, 1), (1, 0), (1, 1))
ORDER = (4, 3, 5, 1, 7, 0, 2, 6, 8)
EXCHANGES = 12
NAMES = (
    "g1", "b1", "gg1", "gb1", "exb1", "eg1", "eb1", "sg1", "sb1", "sqb1",
    "g2", "b2", "gg2", "gb2", "exb2", "eg2", "eb2", "sqb2",
)
VEC = {name: k for k, name in enumerate(NAMES)}
VEC_ROWS = 32


def segments_of(cin, width, taps, group, sq1, sq2, devices):
    layout = (
        (("e2", width), ("sq2", sq2), ("ex2", sq2)),
        (("k2", taps * group), ("w2", width)),
        (("e1", width), ("s1", cin), ("sq1", sq1), ("ex1", sq1)),
        (("k1", taps * group), ("vec", VEC_ROWS)),
        (("w1", cin),),
    )
    starts, segments, at = {}, [], 0
    for parts in layout:
        base = at
        for name, rows in parts:
            starts[name] = (at, rows // 16)
            at += rows // 16 * (width // 128)
        units = -(-(at - base) // devices)
        first = units // 2 * devices if len(segments) < len(layout) - 2 else 0
        second = units * devices - first
        segments.append(((base, first), (base + first, second), at))
        at = base + units * devices
    return starts, tuple(segments), at


def sigmoid(v):
    return 0.5 * jnp.tanh(0.5 * v) + 0.5


def silu(v):
    return v * sigmoid(v)


def slope(v):
    s = sigmoid(v)
    return s * (1.0 + v * (1.0 - s))


def dot(left, right):
    return jnp.dot(left, right, preferred_element_type=f32)


def dot_nt(left, right):
    return lax.dot_general(left, right, (((1,), (1,)), ((), ())), preferred_element_type=f32)


def dot_tn(left, right):
    return lax.dot_general(left, right, (((0,), (0,)), ((), ())), preferred_element_type=f32)


def parts_of(v):
    high = v.astype(bf16).astype(f32)
    return high, v - high


def stacked(rows, width):
    ids = lax.broadcasted_iota(jnp.int32, (16, width), 0)
    total = jnp.zeros((16, width), f32)
    for k, row in enumerate(rows):
        total = jnp.where(ids == k, jnp.broadcast_to(row, (16, width)), total)
    return total.astype(bf16)


def small_dot(row, weight, form):
    out = form(stacked(parts_of(row), row.shape[1]), weight)
    return out[0:1] + out[1:2]


def small_outer(left, right):
    lh, ll = parts_of(left)
    rh, rl = parts_of(right)
    return dot_tn(
        stacked((lh, ll, lh, ll), left.shape[1]), stacked((rh, rh, rl, rl), right.shape[1])
    )


def fold(v):
    return v[0] + v[1]


def column(acc):
    return jnp.sum(acc, axis=0, keepdims=True)


class Plan:
    def __init__(self, mesh_sizes, args):
        self.S, self.I, self.R = mesh_sizes
        x, og, w1, k1, sq1, sq2 = args
        self.M, _, self.rows, self.cols, self.cin = x
        _, _, self.hrows, self.side, self.width = og
        self.taps, self.groups, self.gw, _ = k1
        self.q1, self.q2 = sq1[0], sq2[1]
        self.each = self.M // self.S
        self.copies = self.R // self.each
        self.pix = self.side * self.side
        self.band = self.pix // self.cols
        self.bands = 2 * self.side // self.band
        self.starts, self.segments, self.blocks = segments_of(
            self.cin, self.width, self.taps, self.gw, self.q1, self.q2, self.S * self.I * self.R
        )
        self.X = 1
        while self.X * self.X < self.R:
            self.X *= 2
        self.Y = self.R // self.X
        self.sizes = {"s": self.S, "x": self.X, "y": self.Y, "r": self.R, "i": self.I}
        self.streams = []
        self.members = []
        self.rooms = [0] * 4
        for first, second, _ in self.segments:
            members = []
            orders = ("sxyi", "syxi") if first[1] else (None, "sri")
            for (base, size), order in zip((first, second), orders):
                if not size:
                    continue
                members.append(len(self.streams))
                self.streams.append((base, size, order, tuple(self.rooms)))
                for level, axis in enumerate(order):
                    self.rooms[level] += size
                    size //= self.sizes[axis]
            self.members.append(tuple(members))

    def piece(self, stream, level):
        _, size, order, _ = self.streams[stream]
        for axis in order[: level + 1]:
            size //= self.sizes[axis]
        return size


def main_kernel(plan, names, *refs):
    ref = dict(zip(names, refs))
    S, I, R = plan.S, plan.I, plan.R
    side, width, pix, cin = plan.side, plan.width, plan.pix, plan.cin
    half_width = width // 2
    s, i, r = lax.axis_index("section"), lax.axis_index("img"), lax.axis_index("row")
    mine = s * plan.each + r // plan.copies
    waits = []

    barrier = pltpu.get_barrier_semaphore()
    peers = []
    for ds in range(S):
        for dr in range(R):
            if ds or dr:
                peers.append((lax.rem(s + ds, S), i, lax.rem(r + dr, R)))
    for di in range(1, I):
        peers.append((s, lax.rem(i + di, I), r))
    for peer in peers:
        pl.semaphore_signal(barrier, inc=1, device_id=peer, device_id_type=MESH)

    own = []
    loads = {}

    def load(*which):
        for name in which:
            at = (NAMES + WEIGHTS).index(name)
            loads[name] = pltpu.make_async_copy(ref[name], ref[name + "_v"], ref["loads"].at[at])
            loads[name].start()

    def need(name):
        if name in loads:
            loads.pop(name).wait()
        return ref[name + "_v"]

    load("w1", "g1", "b1")
    for name, rows in (("x", plan.rows), ("og", plan.hrows)):
        copy = pltpu.make_async_copy(
            ref[name].at[mine, 0],
            ref[name + "_in"].at[pl.ds(r * rows, rows)],
            ref[name + "_r"].at[r],
        )
        copy.start()
        own.append(copy)
    pl.semaphore_wait(barrier, len(peers))
    for name, rows in (("x", plan.rows), ("og", plan.hrows)):
        for d in range(1, R):
            t = lax.rem(r + d, R)
            copy = pltpu.make_async_remote_copy(
                src_ref=ref[name].at[s * plan.each + t // plan.copies, 0],
                dst_ref=ref[name + "_in"].at[pl.ds(r * rows, rows)],
                send_sem=ref[name + "_s"].at[d - 1],
                recv_sem=ref[name + "_r"].at[r],
                device_id=(s, i, t),
                device_id_type=MESH,
            )
            copy.start()
            waits.append(copy.wait_send)

    load("k1", "s1", "k2", *NAMES[2:], "sq1", "ex1", "e1", "w2", "sq2", "ex2", "e2")

    def arrived(name, rows, position, d):
        if d == 0:
            own[position].wait()
        else:
            t = lax.rem(r + d, R)
            there = ref[name + "_in"].at[pl.ds(t * rows, rows)]
            pltpu.make_async_remote_copy(
                src_ref=there,
                dst_ref=there,
                send_sem=ref[name + "_s"].at[d - 1],
                recv_sem=ref[name + "_r"].at[t],
                device_id=(s, i, t),
                device_id_type=MESH,
            ).wait_recv()

    st = ref["st"]

    def pairs_of(k):
        return 2 if k in (0, 1, 9) else 1

    def stats_copy(k, d, slot):
        return pltpu.make_async_remote_copy(
            src_ref=st.at[k, slot, pl.ds(0, pairs_of(k))],
            dst_ref=st.at[k, slot, pl.ds(0, pairs_of(k))],
            send_sem=ref["st_s"].at[k, d - 1],
            recv_sem=ref["st_r"].at[k, slot],
            device_id=(s, lax.rem(i + d, I), r),
            device_id_type=MESH,
        )

    def post(k, rows):
        ids = lax.broadcasted_iota(jnp.int32, (8, 128), 0)
        rows = [*rows, *([None] * (len(rows) % 2))]
        for pair in range(len(rows) // 2):
            value = jnp.zeros((8, 128), f32)
            for j in range(8):
                row = rows[2 * pair + j // 4]
                if row is not None:
                    piece = row[:, 128 * (j % 4) : 128 * (j % 4) + 128]
                    value = jnp.where(ids == j, jnp.broadcast_to(piece, (8, 128)), value)
            st[k, i, pair] = value
        for d in range(1, I):
            stats_copy(k, d, i).start()

    def fetch(k, count=2):
        for d in range(1, I):
            stats_copy(k, d, i).wait_send()
            stats_copy(k, d, lax.rem(i + d, I)).wait_recv()
        out = []
        for pair in range((count + 1) // 2):
            value = st[k, 0, pair]
            for j in range(1, I):
                value = value + st[k, j, pair]
            for half in range(2):
                out.append(
                    jnp.concatenate(
                        [
                            jnp.broadcast_to(value[4 * half + j : 4 * half + j + 1], (8, 128))
                            for j in range(4)
                        ],
                        axis=1,
                    )
                )
        return out

    vec = ref["vec"]

    def keep_vectors():
        for name in NAMES:
            row = need(name)[...].astype(f32)
            size = row.shape[0]
            vec[VEC[name], :, :size] = jnp.broadcast_to(row.reshape(1, size), (8, size))

    def vector(name):
        return vec[VEC[name]]

    vr, vc = ref["vr"][0, mine], ref["vc"][0, mine]
    q_ids = lax.broadcasted_iota(jnp.int32, (side, width), 0)
    first_col, last_col = q_ids == 0, q_ids == side - 1
    cm = ref["cm"]
    for b in range(2):
        cm[b] = (2 * q_ids + b < vc).astype(f32)

    def line(value):
        return value.astype(f32).reshape(2, 8, width)

    def pixels(value):
        return value.reshape(side, width)

    def mask_row(a, b, p):
        return line(cm[b]) * (2 * p + a < vr).astype(f32)

    def wide(row):
        return jnp.broadcast_to(row, (8, width))

    row_count = jnp.full((1, width), vr * vc, jnp.int32).astype(f32)
    half_count = jnp.full((1, width), ((vr + 1) // 2) * ((vc + 1) // 2), jnp.int32).astype(f32)

    def over_rows(step, *accs):
        init = tuple(jnp.zeros((8, width), f32) for _ in range(accs[0] if accs else 0))

        def run(p, carry):
            out = step(p)
            if not carry:
                return carry
            return tuple(c + fold(o) for c, o in zip(carry, out))

        return tuple(column(c) for c in lax.fori_loop(0, side, run, init, unroll=4))

    def full_dot(out, left, weight, form=dot):
        wide = out.shape[-1]
        step = min(256, wide)
        for h in range(wide // step):
            cut = slice(h * step, h * step + step)
            w = weight[:, cut] if form is dot else weight[cut, :]
            out[:, :, cut] = form(left, w).reshape(side, side, step).astype(out.dtype)

    def flat(value):
        return value.reshape(pix, value.shape[-1])

    def lines(ref_, start=0):
        return flat(ref_[start : start + side])

    G, F = ref["local"], ref["grads"]
    lead = None if plan.copies == 1 else (lax.rem(r, plan.copies) == 0).astype(f32)

    def put(name, value, row=0, lane=0):
        if lead is not None:
            value = value * lead
        start, per_tile = plan.starts[name]
        count = value.shape[0] // 16
        for k in range(value.shape[1] // 128):
            piece = value[:, 128 * k : 128 * k + 128].astype(bf16).reshape(count, 16, 128)
            at = start + (lane // 128 + k) * per_tile + row // 16
            G[at : at + count] = piece

    X, Y = plan.X, plan.Y
    x, y = lax.rem(r, X), r // X
    axes = {
        "s": (S, s, lambda t: (t, i, r)),
        "r": (R, r, lambda t: (s, i, t)),
        "x": (X, x, lambda t: (s, i, y * X + t)),
        "y": (Y, y, lambda t: (s, i, t * X + x)),
        "i": (I, i, lambda t: (s, t, r)),
    }

    def scatter_source(stream, level):
        base, _, order, offsets = plan.streams[stream]
        if level == 0:
            return G, base
        return ref[f"sum{level - 1}"], offsets[level]

    def scatter_copies(stream, level, outgoing):
        base, size, order, offsets = plan.streams[stream]
        count, me, device = axes[order[level]]
        piece = plan.piece(stream, level)
        source, first = scatter_source(stream, level)
        for d in range(1, count):
            t = lax.rem(me + d, count)
            slot = me if outgoing else t
            copy = pltpu.make_async_remote_copy(
                src_ref=source.at[pl.ds(first + t * piece, piece)],
                dst_ref=ref[f"got{level}"].at[pl.ds(offsets[level] + slot * piece, piece)],
                send_sem=ref["rs_s"].at[stream, level, d - 1],
                recv_sem=ref["rs_r"].at[stream, level, slot],
                device_id=device(t),
                device_id_type=MESH,
            )
            if outgoing:
                copy.start()
                waits.append(copy.wait_send)
            else:
                copy.wait_recv()

    def add_up(stream, level):
        base, size, order, offsets = plan.streams[stream]
        count, me, _ = axes[order[level]]
        piece = plan.piece(stream, level)
        source, first = scatter_source(stream, level)
        got = ref[f"got{level}"]
        if level < len(order) - 1:
            out, at = ref[f"sum{level}"], offsets[level + 1]
        else:
            out, at = F, own_part(stream, len(order))
        step = next(k for k in (16, 12, 10, 9, 8, 7, 6, 5, 4, 3, 2, 1) if piece % k == 0)

        def run(k, carry):
            total = source[pl.ds(first + me * piece + k * step, step)].astype(f32)
            for d in range(1, count):
                t = lax.rem(me + d, count)
                total = total + got[pl.ds(offsets[level] + t * piece + k * step, step)].astype(f32)
            out[pl.ds(at + k * step, step)] = total.astype(bf16)
            return carry

        lax.fori_loop(0, piece // step, run, 0)

    def own_part(stream, depth):
        at, _, order, _ = plan.streams[stream]
        for level in range(depth):
            at = at + axes[order[level]][1] * plan.piece(stream, level)
        return at

    def gather_copies(stream, level, outgoing):
        count, me, device = axes[plan.streams[stream][2][level]]
        base = own_part(stream, level)
        piece = plan.piece(stream, level)
        for d in range(1, count):
            t = lax.rem(me + d, count)
            slot = me if outgoing else t
            there = F.at[pl.ds(base + slot * piece, piece)]
            copy = pltpu.make_async_remote_copy(
                src_ref=there,
                dst_ref=there,
                send_sem=ref["ag_s"].at[stream, level, d - 1],
                recv_sem=ref["ag_r"].at[stream, level, slot],
                device_id=device(t),
                device_id_type=MESH,
            )
            if outgoing:
                copy.start()
                waits.append(copy.wait_send)
            else:
                copy.wait_recv()

    done = [0] * len(plan.segments)
    started = []

    def pump(*fresh):
        started.extend(fresh)
        for g in started:
            k = done[g]
            depth = len(plan.streams[plan.members[g][0]][2])
            if k > 2 * depth:
                continue
            done[g] += 1
            if k == 0:
                (_, _), (base, size), used = plan.segments[g]
                if used < base + size:
                    G[used : base + size] = jnp.zeros((base + size - used, 16, 128), bf16)
            for stream in plan.members[g]:
                if 1 <= k <= depth:
                    scatter_copies(stream, k - 1, False)
                    add_up(stream, k - 1)
                elif k > depth:
                    gather_copies(stream, 2 * depth - k, False)
                if k < depth:
                    scatter_copies(stream, k, True)
                elif k < 2 * depth:
                    gather_copies(stream, 2 * depth - 1 - k, True)

    vec_grads = {}

    gw = plan.gw
    span = 4 * gw
    def blocks(name, out, turned=False):
        kernels = need(name)
        shape = (span, 128) if turned else (128, span)
        long = lax.broadcasted_iota(jnp.int32, shape, 0 if turned else 1)
        short = lax.broadcasted_iota(jnp.int32, shape, 1 if turned else 0)
        spread = (lax.rem(long, gw) == short).astype(f32).astype(bf16)
        row = lax.broadcasted_iota(jnp.int32, (span, span), 0) // gw
        col = lax.broadcasted_iota(jnp.int32, (span, span), 1) // gw
        for k, t in enumerate(ORDER):
            for h in range(width // span):
                piece = kernels[t, 4 * h : 4 * h + 4].reshape(span, 128)
                full = dot_nt(spread, piece) if turned else dot(piece, spread)
                out[h, k * span : (k + 1) * span] = jnp.where(row == col, full, 0.0).astype(bf16)

    def groups_grad(name, taps, turned):
        lane = lax.broadcasted_iota(jnp.int32, (gw, span), 1) // gw
        for t, (var, start) in enumerate(taps):
            for h in range(width // span):
                cut = slice(h * span, (h + 1) * span)
                res = dot(turned[h], flat(var[start : start + side, :, cut]))
                out = res[0:gw]
                for j in range(1, 4):
                    out = jnp.where(lane == j, res[j * gw : (j + 1) * gw], out)
                put(name, out, t * gw, h * span)

    band, bands = plan.band, plan.bands
    bhalf = band // 2
    out_id = lax.broadcasted_iota(jnp.int32, (pix, pix), 0)
    in_id = lax.broadcasted_iota(jnp.int32, (pix, pix), 1)

    def source(o):
        quarter = o // (bhalf * side)
        down = lax.rem(o, bhalf * side) // side
        return (2 * down + quarter // 2) * plan.cols + 2 * lax.rem(o, side) + lax.rem(quarter, 2)

    ref["sort"][...] = (source(out_id) == in_id).astype(f32).astype(bf16)
    ref["unsort"][...] = (source(in_id) == out_id).astype(f32).astype(bf16)

    xp, R1 = ref["xp"], ref["R1"]
    blocks("k1", ref["bd1"])
    keep_vectors()

    def transpose(source, out):
        out[...] = source.astype(f32).T.astype(bf16)

    totals = [jnp.zeros((8, width), f32)] * 2
    by_band = plan.rows % band == 0
    if not by_band:
        for d in range(R):
            arrived("x", plan.rows, 0, d)
    for d in range(bands):
        if by_band:
            if d % (plan.rows // band) == 0:
                arrived("x", plan.rows, 0, d // (plan.rows // band))
            k = lax.rem(r * (plan.rows // band) + d, bands)
        else:
            k = d
        block = ref["x_in"][pl.ds(k * band, band)].reshape(pix, cin)
        block = dot(ref["sort"][...], block).astype(bf16)
        xp[k] = block.reshape(4 * bhalf, side, cin)
        full_dot(R1.at[k], block, need("w1"))
        for j in range(4 * bhalf):
            a, b = PHASES[j // bhalf]
            v = line(R1[k, j])
            mv = v * mask_row(a, b, k * bhalf + j % bhalf)
            totals = [totals[0] + fold(mv), totals[1] + fold(mv * v)]
    even = xp.at[:, 0:bhalf]

    def at_phase(ab, p):
        return p // bhalf, ab * bhalf + lax.rem(p, bhalf)

    post(0, [column(totals[0]), column(totals[1]), row_count, half_count])
    SC = ref["SC"]
    full_dot(SC, even[...].reshape(pix, cin), need("s1"))

    def moments(field):
        def step(p):
            v = line(field[p])
            mv = v * mask_row(0, 0, p)
            return mv, mv * v

        return over_rows(step, 2)

    short_sums = moments(SC)
    for k in range(bands):
        transpose(xp[k].reshape(pix, cin), ref["xpt"].at[k])

    def coefficients(first, second, inverse, gain, shift):
        mean = first * inverse
        scale = lax.rsqrt(second * inverse - mean * mean + epsilon)
        a = scale * gain
        return a, shift - mean * a, scale, -mean * scale

    tot = fetch(0, 4)
    inv_full, inv_half = 1.0 / tot[2], 1.0 / tot[3]
    n1 = coefficients(tot[0], tot[1], inv_full, vector("g1"), vector("b1"))

    va = ref["va"]
    va[3:6, 0:1] = jnp.zeros((3, 1, side, width), bf16)

    def shifted(v, edge, amount):
        return jnp.where(edge, 0.0, pltpu.roll(v, amount, 0))

    for ab, (a, b) in enumerate(PHASES):

        def step(p, ab=ab, a=a, b=b):
            v = mask_row(a, b, p) * silu(line(R1[at_phase(ab, p)]) * n1[0] + n1[1])
            v = pixels(v)
            slot = (0, 1, 3, 4)[ab]
            va[slot, p + a] = v.astype(bf16)
            if b:
                va[slot + 1, p + a] = shifted(v, first_col, 1).astype(bf16)

        over_rows(step)
    taps1 = []
    for t in range(9):
        u, v = t // 3, t % 3
        slot = (0, 1, 3, 4)[2 * (u != 1) + (v != 1)] + (v == 0)
        taps1.append((va.at[slot], 1 if u == 2 else 0))

    def convolve(taps, weights, out):
        for h in range(width // span):
            cut = slice(h * span, (h + 1) * span)
            left = [flat(taps[t][0][taps[t][1] : taps[t][1] + side, :, cut]) for t in ORDER]
            acc = dot(jnp.concatenate(left, axis=1), weights[h])
            out[:, :, cut] = acc.astype(bf16).reshape(side, side, span)

    c1 = ref["c1"]
    convolve(taps1, ref["bd1"], c1)
    post(1, [*moments(c1), *short_sums])
    blocks("k2", ref["bd2"])
    tot = fetch(1, 4)
    nc1 = coefficients(tot[0], tot[1], inv_half, vector("gg1"), vector("gb1"))
    ns = coefficients(tot[2], tot[3], inv_half, vector("sg1"), vector("sb1"))

    def excite(conv, norm, hidden, gated, sq, sq_form, sqb, ex, exb):
        def step(p):
            v = mask_row(0, 0, p) * silu(line(conv[p]) * norm[0] + norm[1])
            hidden[p] = pixels(v)
            return (v,)

        (total,) = over_rows(step, 1)
        pooled = total / half_count
        pre = small_dot(pooled, sq[...], sq_form) + sqb
        inner = silu(pre)
        gate = sigmoid(small_dot(inner, ex[...], dot) + exb)
        gate_wide = wide(gate)

        def step_two(p):
            gated[p] = pixels(line(hidden[p]) * gate_wide).astype(bf16)

        over_rows(step_two)
        return pooled, pre, inner, gate

    H1, ga1 = ref["H1"], ref["ga1"]
    kept1 = excite(
        c1, nc1, H1, ga1, need("sq1"), dot_nt, vec[VEC["sqb1"], 0:1, : plan.q1], need("ex1"), vec[VEC["exb1"], 0:1]
    )
    E1 = ref["E1"]
    full_dot(E1, lines(ga1), need("e1"))
    post(2, moments(E1))
    transpose(lines(ga1), ref["ga1t"])
    blocks("k1", ref["bd1t"], True)
    tot = fetch(2)
    ne = coefficients(tot[0], tot[1], inv_half, vector("eg1"), vector("eb1"))
    ent = ref["ent"]
    both_shifts = ne[1] + ns[1]

    def step(p):
        v = line(E1[p]) * ne[0] + line(SC[p]) * ns[0] + both_shifts
        ent[p] = pixels(mask_row(0, 0, p) * silu(v)).astype(bf16)

    over_rows(step)

    def send_out(source, out, rows, target, steps=None):
        for k in range(R // plan.copies) if steps is None else steps:
            t = lax.rem(r + plan.copies * k, R)
            there = ref[out].at[0, mine, 0] if out == "act" else ref[out].at[mine, 0]
            here = source.at[pl.ds(t * rows, rows)]
            copy = pltpu.make_async_remote_copy(
                src_ref=here,
                dst_ref=there,
                send_sem=ref[out + "_s"].at[target, k],
                recv_sem=ref[out + "_r"].at[mine],
                device_id=(target, i, t),
                device_id_type=MESH,
            )
            if k:
                copy.start()
                waits.append(copy.wait_send)
            else:
                local = pltpu.make_async_copy(here, there, ref[out + "_r"].at[mine])

                @pl.when(s == target)
                def _():
                    local.start()

                @pl.when(s != target)
                def _():
                    copy.start()

                def finish(copy=copy):
                    @pl.when(s != target)
                    def _():
                        copy.wait_send()

                waits.append(finish)

    send_out(ent, "act", plan.hrows, 0)

    R2 = ref["R2"]
    full_dot(R2, lines(ent), need("w2"))
    post(3, moments(R2))
    transpose(lines(ent), ref["entt"])
    tot = fetch(3)
    n2 = coefficients(tot[0], tot[1], inv_half, vector("g2"), vector("b2"))
    vb = ref["vb"]
    vb[:, 0:1] = jnp.zeros((3, 1, side, width), bf16)
    vb[:, side + 1 :] = jnp.zeros((3, 1, side, width), bf16)

    def three(out, p, v):
        out[0, p + 1] = shifted(v, first_col, 1).astype(bf16)
        out[1, p + 1] = v.astype(bf16)
        out[2, p + 1] = shifted(v, last_col, side - 1).astype(bf16)

    def step(p):
        three(vb, p, pixels(mask_row(0, 0, p) * silu(line(R2[p]) * n2[0] + n2[1])))

    over_rows(step)
    taps2 = [(vb.at[t % 3], t // 3) for t in range(9)]
    c2 = ref["c2"]
    convolve(taps2, ref["bd2"], c2)
    post(4, moments(c2))
    blocks("k2", ref["bd2t"], True)
    tot = fetch(4)
    nc2 = coefficients(tot[0], tot[1], inv_half, vector("gg2"), vector("gb2"))
    H2, ga2 = ref["H2"], ref["ga2"]
    kept2 = excite(
        c2, nc2, H2, ga2, need("sq2"), dot, vec[VEC["sqb2"], 0:1, : plan.q2], need("ex2"), vec[VEC["exb2"], 0:1]
    )
    E2 = ref["E2"]
    full_dot(E2, lines(ga2), need("e2"))
    post(5, moments(E2))
    transpose(lines(ga2), ref["ga2t"])
    for d in range(R):
        arrived("og", plan.hrows, 1, d)
    tot = fetch(5)
    ne2 = coefficients(tot[0], tot[1], inv_half, vector("eg2"), vector("eb2"))
    leave, D, og = ref["leave"], ref["D"], ref["og_in"]

    def step(p):
        e = line(E2[p])
        v = e * ne2[0] + ne2[1] + line(ent[p])
        sg = sigmoid(v)
        m = mask_row(0, 0, p)
        leave[p] = pixels(m * v * sg).astype(bf16)
        g = line(og[p]) * m * (sg * (1.0 + v * (1.0 - sg)))
        D[p] = pixels(g)
        return g, g * (e * ne2[2] + ne2[3])

    parts = over_rows(step, 2)
    vec_grads["eb2"], vec_grads["eg2"] = parts
    post(6, parts)
    send_out(leave, "act", plan.hrows, 1)

    def back_rule(sums, inverse, gain, norm):
        a = gain * norm[2]
        k0 = a * (sums[0] + norm[3] * sums[1]) * inverse
        return a, k0, a * norm[2] * sums[1] * inverse

    def back_excite(dg, kept, hidden, conv, norm, sq, sq_form, ex, out):
        pooled, pre, inner, gate = kept

        def step(p):
            return (line(dg[p]) * line(hidden[p]),)

        (dgate,) = over_rows(step, 1)
        dpre = dgate * gate * (1.0 - gate)
        dsq = small_dot(dpre, ex[...], dot_nt) * slope(pre)
        dpool = wide(small_dot(dsq, sq[...], sq_form) / half_count)
        gate_wide = wide(gate)

        def step_two(p):
            v = line(conv[p])
            g = (line(dg[p]) * gate_wide + dpool) * mask_row(0, 0, p)
            g = g * slope(v * norm[0] + norm[1])
            out[p] = pixels(g)
            return g, g * (v * norm[2] + norm[3])

        return over_rows(step_two, 2), dpre, dsq

    def excite_grads(name, kept, dpre, dsq):
        pooled, pre, inner, gate = kept
        put("sq" + name, small_outer(dsq, pooled))
        put("ex" + name, small_outer(inner, dpre))
        vec_grads["exb" + name] = dpre
        count = dsq.shape[1]
        eye = (
            lax.broadcasted_iota(jnp.int32, (count, width), 0)
            == lax.broadcasted_iota(jnp.int32, (count, width), 1)
        ).astype(f32).astype(bf16)
        vec_grads["sqb" + name] = small_dot(dsq, eye, dot)

    def turn(gradient_ref, start):
        out = []
        for h in range(width // span):
            piece = flat(gradient_ref[start : start + side, :, h * span : (h + 1) * span])
            out.append(piece.astype(f32).T.astype(bf16))
        return out

    d1, dg, GR = ref["d1"], ref["dg"], ref["GR"]
    tot = fetch(6)
    rule = back_rule((tot[0], tot[1]), inv_half, vector("eg2"), ne2)

    def step(p):
        v = rule[0] * line(D[p]) - mask_row(0, 0, p) * (rule[1] + rule[2] * line(E2[p]))
        d1[p] = pixels(v).astype(bf16)

    over_rows(step)
    full_dot(dg, lines(d1), need("e2"), dot_nt)
    parts, dpre, dsq = back_excite(dg, kept2, H2, c2, nc2, need("sq2"), dot_nt, need("ex2"), GR)
    vec_grads["gb2"], vec_grads["gg2"] = parts
    post(7, parts)
    put("e2", dot(ref["ga2t"][...], lines(d1)))
    excite_grads("2", kept2, dpre, dsq)
    pump(0)
    tot = fetch(7)
    rule = back_rule((tot[0], tot[1]), inv_half, vector("gg2"), nc2)
    vd = ref["vd"]
    vd[:, 0:1] = jnp.zeros((3, 1, side, width), bf16)
    vd[:, side + 1 :] = jnp.zeros((3, 1, side, width), bf16)

    def step(p):
        v = rule[0] * line(GR[p]) - mask_row(0, 0, p) * (rule[1] + rule[2] * line(c2[p]))
        three(vd, p, pixels(v))

    over_rows(step)
    pump()

    def convolve_back(taps, first, weights, out):
        for h in range(width // span):
            cut = slice(h * span, (h + 1) * span)
            left = [flat(var[start : start + side, :, cut]) for var, start in taps]
            rows = slice(first * span, (first + len(taps)) * span)
            acc = dot(jnp.concatenate(left, axis=1), weights[h, rows])
            out[:, :, cut] = acc.reshape(side, side, span)

    DA = ref["DA"]
    convolve_back(
        [(vd.at[2 - t % 3], 2 - t // 3) for t in ORDER],
        0,
        ref["bd2t"],
        DA.at[0],
    )
    pump()

    def step(p):
        v = line(R2[p])
        g = line(DA[0, p]) * mask_row(0, 0, p) * slope(v * n2[0] + n2[1])
        GR[p] = pixels(g)
        return g, g * (v * n2[2] + n2[3])

    parts = over_rows(step, 2)
    vec_grads["b2"], vec_grads["g2"] = parts
    post(8, parts)
    groups_grad("k2", taps2, turn(vd.at[1], 1))
    pump()
    tot = fetch(8)
    rule = back_rule((tot[0], tot[1]), inv_half, vector("g2"), n2)

    def step(p):
        v = rule[0] * line(GR[p]) - mask_row(0, 0, p) * (rule[1] + rule[2] * line(R2[p]))
        d1[p] = pixels(v).astype(bf16)

    over_rows(step)
    full_dot(GR, lines(d1), need("w2"), dot_nt)
    pump()

    def step(p):
        e, sc = line(E1[p]), line(SC[p])
        g = line((D[p] + GR[p]).astype(bf16))
        g = g * mask_row(0, 0, p) * slope(e * ne[0] + sc * ns[0] + both_shifts)
        D[p] = pixels(g)
        return g, g * (e * ne[2] + ne[3]), g * (sc * ns[2] + ns[3])

    parts = over_rows(step, 3)
    vec_grads["eb1"], vec_grads["eg1"], vec_grads["sg1"] = parts
    vec_grads["sb1"] = parts[0]
    post(9, parts)
    put("w2", dot(ref["entt"][...], lines(d1)))
    pump(1)
    tot = fetch(9, 3)
    rule_e = back_rule((tot[0], tot[1]), inv_half, vector("eg1"), ne)
    rule_s = back_rule((tot[0], tot[2]), inv_half, vector("sg1"), ns)
    d2 = ref["d2"]

    def step(p):
        g, m = line(D[p]), mask_row(0, 0, p)
        v = rule_e[0] * g - m * (rule_e[1] + rule_e[2] * line(E1[p]))
        d1[p] = pixels(v).astype(bf16)
        v = rule_s[0] * g - m * (rule_s[1] + rule_s[2] * line(SC[p]))
        d2[p] = pixels(v).astype(bf16)

    over_rows(step)
    pump()
    full_dot(dg, lines(d1), need("e1"), dot_nt)
    pump()
    parts, dpre, dsq = back_excite(dg, kept1, H1, c1, nc1, need("sq1"), dot, need("ex1"), GR)
    vec_grads["gb1"], vec_grads["gg1"] = parts
    post(10, parts)
    put("e1", dot(ref["ga1t"][...], lines(d1)))
    put("s1", dot_tn(even[...].reshape(pix, cin), lines(d2)))
    excite_grads("1", kept1, dpre, dsq)
    pump(2)
    tot = fetch(10)
    rule = back_rule((tot[0], tot[1]), inv_half, vector("gg1"), nc1)

    def step(p):
        v = rule[0] * line(GR[p]) - mask_row(0, 0, p) * (rule[1] + rule[2] * line(c1[p]))
        three(vd, p, pixels(v))

    over_rows(step)
    pump()
    sums = []
    for ab, (a, b) in enumerate(PHASES):
        chosen = []
        first = (0, 1, 3, 5)[ab]
        for t in ORDER[first : first + (1, 2, 2, 4)[ab]]:
            chosen.append((vd.at[2 if t % 3 == 0 else 1], 2 if t // 3 == 0 else 1))
        convolve_back(chosen, first, ref["bd1t"], DA.at[ab])
        if ab % 2:
            pump()

        def step(p, ab=ab, a=a, b=b):
            v = line(R1[at_phase(ab, p)])
            g = line(DA[ab, p]) * mask_row(a, b, p) * slope(v * n1[0] + n1[1])
            DA[ab, p] = pixels(g)
            return g, g * (v * n1[2] + n1[3])

        sums.append(over_rows(step, 2))
    parts = (sum(x[0] for x in sums), sum(x[1] for x in sums))
    vec_grads["b1"], vec_grads["g1"] = parts
    post(11, parts)
    groups_grad("k1", taps1, turn(vd.at[1], 1))
    ids = lax.broadcasted_iota(jnp.int32, (VEC_ROWS, width), 0)
    value = jnp.zeros((VEC_ROWS, width), f32)
    for name, at in VEC.items():
        value = jnp.where(ids == at, jnp.broadcast_to(vec_grads[name], value.shape), value)
    put("vec", value)
    pump(3)
    tot = fetch(11)
    rule = back_rule((tot[0], tot[1]), inv_full, vector("g1"), n1)
    dr = ref["dr"]
    for ab, (a, b) in enumerate(PHASES):

        def step(p, ab=ab, a=a, b=b):
            v = rule[0] * line(DA[ab, p])
            v = v - mask_row(a, b, p) * (rule[1] + rule[2] * line(R1[at_phase(ab, p)]))
            dr[at_phase(ab, p)] = pixels(v).astype(bf16)

        over_rows(step)
    total = None
    for k in range(bands):
        term = dot(ref["xpt"][k], dr[k].reshape(pix, width))
        total = term if total is None else total + term
    put("w1", total)
    pump(4)
    cut = cin // 2
    ref["dxo0"][...] = jnp.zeros((2 * side, plan.cols, 128), bf16)
    ref["dxo1"][...] = jnp.zeros((2 * side, plan.cols, 128), bf16)
    stepwise = plan.each == bands
    for d in [*range(1, bands), 0]:
        k = lax.rem(r + plan.copies * d, R) * plan.rows // band if stepwise else d
        for part in range(2):
            dxo = ref[f"dxo{part}"]
            rows = slice(part * cut, (part + 1) * cut)
            v = dot_nt(dr[k].reshape(pix, width), need("w1")[rows, :])
            w = dot_nt(
                d2[pl.ds(k * bhalf, bhalf)].reshape(bhalf * side, width), need("s1")[rows, :]
            )
            v = jnp.concatenate([v[: bhalf * side] + w, v[bhalf * side :]], axis=0)
            v = dot(ref["unsort"][...], v.astype(bf16)).astype(bf16)
            dxo[pl.ds(k * band, band), :, :cut] = v.reshape(band, plan.cols, cut)
            if stepwise:
                send_out(dxo, "dx", plan.rows, part, (d,))
        pump()
    if not stepwise:
        send_out(ref["dxo0"], "dx", plan.rows, 0)
        send_out(ref["dxo1"], "dx", plan.rows, 1)
    for _ in range(9):
        pump()
    for wait in waits:
        wait()
    for m in range(plan.M):
        t = (m % plan.each) * plan.copies + lax.rem(r, plan.copies)
        for out in ("act", "dx"):
            there = ref[out].at[0, m, 0] if out == "act" else ref[out].at[m, 0]
            pltpu.make_async_copy(there, there, ref[out + "_r"].at[m]).wait()


WEIGHTS = ("w1", "k1", "k2", "sq1", "ex1", "e1", "s1", "w2", "sq2", "ex2", "e2")


def run_main(plan, arrays):
    side, width, cin = plan.side, plan.width, plan.cin
    wide = 4 * plan.gw
    field = (side, side, width)
    scratch = {
        "x_in": pltpu.VMEM((2 * side, plan.cols, cin), bf16),
        "og_in": pltpu.VMEM(field, bf16),
        "st": pltpu.VMEM((EXCHANGES, plan.I, 2, 8, 128), f32),
        "cm": pltpu.VMEM((2, side, width), f32),
        **{
            name: pltpu.VMEM((width // wide, plan.taps * wide, wide), bf16)
            for name in ("bd1", "bd2", "bd1t", "bd2t")
        },
        "xpt": pltpu.VMEM((plan.bands, cin, plan.pix), bf16),
        **{name: pltpu.VMEM((width, plan.pix), bf16) for name in ("ga1t", "ga2t", "entt")},
        "sort": pltpu.VMEM((plan.pix, plan.pix), bf16),
        "unsort": pltpu.VMEM((plan.pix, plan.pix), bf16),
        "xp": pltpu.VMEM((plan.bands, 2 * plan.band, side, cin), bf16),
        "R1": pltpu.VMEM((plan.bands, 2 * plan.band, side, width), f32),
        "va": pltpu.VMEM((6, side + 1, side, width), bf16),
        "vb": pltpu.VMEM((3, side + 2, side, width), bf16),
        "vd": pltpu.VMEM((3, side + 2, side, width), bf16),
        "DA": pltpu.VMEM((4,) + field, f32),
        "dr": pltpu.VMEM((plan.bands, 2 * plan.band, side, width), bf16),
        "dxo0": pltpu.VMEM((2 * side, plan.cols, 128), bf16),
        "dxo1": pltpu.VMEM((2 * side, plan.cols, 128), bf16),
    }
    for name in ("SC", "H1", "E1", "R2", "H2", "E2", "D", "GR"):
        scratch[name] = pltpu.VMEM(field, f32)
    for name in ("c1", "ga1", "ent", "c2", "ga2", "leave", "d1", "d2", "dg"):
        scratch[name] = pltpu.VMEM(field, bf16)
    for name in ("x", "og"):
        scratch[name + "_s"] = pltpu.SemaphoreType.DMA((max(plan.R - 1, 1),))
        scratch[name + "_r"] = pltpu.SemaphoreType.DMA((plan.R,))
    scratch["st_s"] = pltpu.SemaphoreType.DMA((EXCHANGES, max(plan.I - 1, 1)))
    scratch["st_r"] = pltpu.SemaphoreType.DMA((EXCHANGES, plan.I))
    for name in ("act", "dx"):
        scratch[name + "_s"] = pltpu.SemaphoreType.DMA((2, plan.R // plan.copies))
        scratch[name + "_r"] = pltpu.SemaphoreType.DMA((plan.M,))
    for name in NAMES + WEIGHTS:
        scratch[name + "_v"] = pltpu.VMEM(arrays[name].shape, bf16)
    scratch["vec"] = pltpu.VMEM((len(NAMES), 8, width), f32)
    scratch["loads"] = pltpu.SemaphoreType.DMA((len(NAMES + WEIGHTS),))
    scratch["local"] = pltpu.VMEM((plan.blocks, 16, 128), bf16)
    for level, room in enumerate(plan.rooms):
        scratch[f"got{level}"] = pltpu.VMEM((room, 16, 128), bf16)
        if level:
            scratch[f"sum{level - 1}"] = pltpu.VMEM((room, 16, 128), bf16)
    most = max(plan.sizes.values())
    for name in ("rs", "ag"):
        scratch[name + "_s"] = pltpu.SemaphoreType.DMA((len(plan.streams), 4, most - 1))
        scratch[name + "_r"] = pltpu.SemaphoreType.DMA((len(plan.streams), 4, most))
    inputs = ("x", "og", "vr", "vc") + NAMES + WEIGHTS
    outputs = ("act", "dx", "grads")
    names = inputs + outputs + tuple(scratch)
    any_space = pl.BlockSpec(memory_space=pl.ANY)
    smem = pl.BlockSpec(memory_space=pltpu.SMEM)
    vmem = pl.BlockSpec(memory_space=pltpu.VMEM)
    return pl.pallas_call(
        functools.partial(main_kernel, plan, names),
        out_shape=(
            jax.ShapeDtypeStruct((1, plan.M, 1, plan.hrows, side, width), bf16),
            jax.ShapeDtypeStruct((plan.M, 1, plan.rows, plan.cols, 128), bf16),
            jax.ShapeDtypeStruct((plan.blocks, 16, 128), bf16),
        ),
        in_specs=[any_space, any_space, smem, smem] + [any_space] * (len(NAMES) + len(WEIGHTS)),
        out_specs=(any_space, any_space, vmem),
        scratch_shapes=list(scratch.values()),
        compiler_params=pltpu.CompilerParams(
            collective_id=0, has_side_effects=True, vmem_limit_bytes=60 * 1024 * 1024
        ),
        name="blocks",
    )(*[arrays[name] for name in inputs])


OUTS = (
    "w1", "g1", "b1", "k1", "gg1", "gb1", "sq1", "sqb1", "ex1", "exb1", "e1", "eg1", "eb1",
    "s1", "sg1", "sb1", "w2", "g2", "b2", "k2", "gg2", "gb2", "sq2", "sqb2", "ex2", "exb2",
    "e2", "eg2", "eb2",
)


def unpack_kernel(plan, blocks, *rest):
    count = len(OUTS)
    outs, bufs, sems = rest[:count], rest[count:-1], rest[-1]
    copies = []

    def tile(name, k, first=0, rows=None):
        start, per_tile = plan.starts[name]
        rows = 16 * per_tile if rows is None else rows
        at = start + k * per_tile + first // 16
        return blocks[at : at + rows // 16].reshape(rows, 128).astype(f32)

    tiles = plan.width // 128
    vec = jnp.concatenate([tile("vec", k) for k in range(tiles)], axis=1)
    for k, name in enumerate(OUTS):
        out = bufs[k]
        if name in VEC:
            size = out.shape[0]
            out[...] = vec[VEC[name] : VEC[name] + 1, :size].reshape(size)
        elif name[0] == "k":

            def run(t, carry, name=name, out=out):
                for lane in range(tiles):
                    start, per_tile = plan.starts[name]
                    at = start + lane * per_tile + t * (plan.gw // 16)
                    piece = blocks[pl.ds(at, plan.gw // 16)].reshape(plan.gw, 128)
                    piece = piece.astype(f32).T
                    for j in range(128 // plan.gw):
                        group = lane * (128 // plan.gw) + j
                        out[t, group, :, : plan.gw] = piece[j * plan.gw : (j + 1) * plan.gw]
                return carry

            lax.fori_loop(0, plan.taps, run, 0)
        elif name == "sq2":
            for lane in range(tiles):
                out[128 * lane : 128 * lane + 128] = tile(name, lane).T
        else:
            for lane in range(tiles):
                out[:, 128 * lane : 128 * lane + 128] = tile(name, lane)
        copies.append(pltpu.make_async_copy(out, outs[k], sems.at[k]))
        copies[-1].start()
    for copy in copies:
        copy.wait()


def unpack(plan, grads, weights):
    shapes = []
    for name, w in zip(OUTS, weights):
        shape = w.shape[:3] + (128,) if name[0] == "k" else w.shape
        shapes.append(jax.ShapeDtypeStruct(shape, f32))
    any_space = pl.BlockSpec(memory_space=pl.ANY)
    return pl.pallas_call(
        functools.partial(unpack_kernel, plan),
        out_shape=shapes,
        in_specs=[pl.BlockSpec(memory_space=pltpu.VMEM)],
        out_specs=[any_space] * len(shapes),
        scratch_shapes=[pltpu.VMEM(v.shape, v.dtype) for v in shapes]
        + [pltpu.SemaphoreType.DMA((len(shapes),))],
        compiler_params=pltpu.CompilerParams(vmem_limit_bytes=60 * 1024 * 1024),
        name="unpack",
    )(grads)


def body(sizes, input_maps, valid_rows, valid_cols, *rest):
    weights, output_grad = rest[:-1], rest[-1]
    (w1, g1, b1, k1, gg1, gb1, sq1, sqb1, ex1, exb1, e1, eg1, eb1, s1, sg1, sb1) = weights[:16]
    (w2, g2, b2, k2, gg2, gb2, sq2, sqb2, ex2, exb2, e2, eg2, eb2) = weights[16:]
    turned = sq1.T
    plan = Plan(sizes, [v.shape for v in (input_maps, output_grad, w1, k1, turned, sq2)])
    vectors = (
        g1, b1, gg1, gb1, exb1, eg1, eb1, sg1, sb1, sqb1, g2, b2, gg2, gb2, exb2, eg2, eb2, sqb2,
    )
    arrays = dict(
        x=input_maps, og=output_grad, vr=valid_rows.T, vc=valid_cols.T, w1=w1,
        k1=jnp.pad(k1, ((0, 0), (0, 0), (0, 0), (0, 128 - plan.gw))),
        k2=jnp.pad(k2, ((0, 0), (0, 0), (0, 0), (0, 128 - plan.gw))),
        sq1=turned, ex1=ex1, e1=e1, s1=s1, w2=w2, sq2=sq2, ex2=ex2, e2=e2,
        **dict(zip(NAMES, vectors)),
    )
    act, dx, grads = run_main(plan, arrays)
    out = list(unpack(plan, grads, weights[:6] + (turned,) + weights[7:]))
    out[6] = out[6].T
    for at in (3, 19):
        out[at] = out[at][..., : plan.gw]
    dx = dx[..., : plan.cin // 2]
    return (act, dx, *out)


def solution(mesh):
    tiled = P(None, "img", "row", None, None)
    image = P(None, "img")
    sizes = tuple(mesh.shape[name] for name in ("section", "img", "row"))
    return jax.shard_map(
        functools.partial(body, sizes),
        mesh=mesh,
        in_specs=(tiled, image, image) + (P(),) * 29 + (tiled,),
        out_specs=(
            P("section", None, "img", "row", None, None),
            P(None, "img", "row", None, "section"),
        )
        + (P(),) * 29,
        check_vma=False,
    )
```

```python
import functools

import jax
import jax.numpy as jnp
from jax import lax
from jax.experimental import pallas as pl
from jax.experimental.pallas import tpu as pltpu
from jax.sharding import PartitionSpec as P

epsilon = 1e-05
f32 = jnp.float32
bf16 = jnp.bfloat16
MESH = pl.DeviceIdType.MESH
PHASES = ((0, 0), (0, 1), (1, 0), (1, 1))
ORDER = (4, 3, 5, 1, 7, 0, 2, 6, 8)
EXCHANGES = 12
NAMES = (
    "g1", "b1", "gg1", "gb1", "exb1", "eg1", "eb1", "sg1", "sb1", "sqb1",
    "g2", "b2", "gg2", "gb2", "exb2", "eg2", "eb2", "sqb2",
)
VEC = {name: k for k, name in enumerate(NAMES)}
VEC_ROWS = 32
VECTORS = "vec"


def segments_of(cin, width, taps, group, sq1, sq2, devices):
    layout = (
        (("e2", width), ("sq2", sq2), ("ex2", sq2)),
        (("k2", taps * group), ("w2", width)),
        (("e1", width), ("s1", cin), ("sq1", sq1), ("ex1", sq1)),
        (("k1", taps * group), (VECTORS, VEC_ROWS)),
        (("w1", cin),),
    )
    starts, segments, at = {}, [], 0
    for parts in layout:
        base = at
        for name, rows in parts:
            starts[name] = (at, rows // 16)
            at += rows // 16 * (width // 128)
        units = -(-(at - base) // devices)
        first = units // 2 * devices if len(segments) < len(layout) - 2 else 0
        second = units * devices - first
        segments.append(((base, first), (base + first, second), at))
        at = base + units * devices
    return starts, tuple(segments), at


def sigmoid(v):
    return 0.5 * jnp.tanh(0.5 * v) + 0.5


def silu(v):
    return v * sigmoid(v)


def slope(v):
    s = sigmoid(v)
    return s * (1.0 + v * (1.0 - s))


def dot(left, right):
    return jnp.dot(left, right, preferred_element_type=f32)


def dot_nt(left, right):
    return lax.dot_general(left, right, (((1,), (1,)), ((), ())), preferred_element_type=f32)


def dot_tn(left, right):
    return lax.dot_general(left, right, (((0,), (0,)), ((), ())), preferred_element_type=f32)


def parts_of(v):
    high = v.astype(bf16).astype(f32)
    return high, v - high


def stacked(rows, width):
    ids = lax.broadcasted_iota(jnp.int32, (16, width), 0)
    total = jnp.zeros((16, width), f32)
    for k, row in enumerate(rows):
        total = jnp.where(ids == k, jnp.broadcast_to(row, (16, width)), total)
    return total.astype(bf16)


def small_dot(row, weight, form):
    out = form(stacked(parts_of(row), row.shape[1]), weight)
    return out[0:1] + out[1:2]


def small_outer(left, right):
    lh, ll = parts_of(left)
    rh, rl = parts_of(right)
    return dot_tn(
        stacked((lh, ll, lh, ll), left.shape[1]), stacked((rh, rh, rl, rl), right.shape[1])
    )


def fold(v):
    return v[0] + v[1]


def column(acc):
    return jnp.sum(acc, axis=0, keepdims=True)


class Plan:
    def __init__(self, mesh_sizes, args):
        self.S, self.I, self.R = mesh_sizes
        x, og, w1, k1, sq1, sq2 = args
        self.M, _, self.rows, self.cols, self.cin = x
        _, _, self.hrows, self.side, self.width = og
        self.taps, self.groups, self.gw, _ = k1
        self.q1, self.q2 = sq1[0], sq2[1]
        self.each = self.M // self.S
        self.copies = self.R // self.each
        self.pix = self.side * self.side
        self.band = self.pix // self.cols
        self.bands = 2 * self.side // self.band
        self.starts, self.segments, self.blocks = segments_of(
            self.cin, self.width, self.taps, self.gw, self.q1, self.q2, self.S * self.I * self.R
        )
        self.X = 1
        while self.X * self.X < self.R:
            self.X *= 2
        self.Y = self.R // self.X
        self.sizes = {"s": self.S, "x": self.X, "y": self.Y, "r": self.R, "i": self.I}
        self.streams = []
        self.members = []
        self.rooms = [0] * 4
        for first, second, _ in self.segments:
            members = []
            orders = ("sxyi", "syxi") if first[1] else (None, "sri")
            for (base, size), order in zip((first, second), orders):
                if not size:
                    continue
                members.append(len(self.streams))
                self.streams.append((base, size, order, tuple(self.rooms)))
                for level, axis in enumerate(order):
                    self.rooms[level] += size
                    size //= self.sizes[axis]
            self.members.append(tuple(members))

    def piece(self, stream, level):
        _, size, order, _ = self.streams[stream]
        for axis in order[: level + 1]:
            size //= self.sizes[axis]
        return size


def main_kernel(plan, names, *refs):
    ref = dict(zip(names, refs))
    S, I, R = plan.S, plan.I, plan.R
    side, width, pix, cin = plan.side, plan.width, plan.pix, plan.cin
    half_width = width // 2
    s, i, r = lax.axis_index("section"), lax.axis_index("img"), lax.axis_index("row")
    mine = s * plan.each + r // plan.copies
    waits = []

    barrier = pltpu.get_barrier_semaphore()
    peers = []
    for ds in range(S):
        for dr in range(R):
            if ds or dr:
                peers.append((lax.rem(s + ds, S), i, lax.rem(r + dr, R)))
    for di in range(1, I):
        peers.append((s, lax.rem(i + di, I), r))
    for peer in peers:
        pl.semaphore_signal(barrier, inc=1, device_id=peer, device_id_type=MESH)

    own = []
    loads = {}

    def load(*which):
        for name in which:
            at = (NAMES + WEIGHTS).index(name)
            loads[name] = pltpu.make_async_copy(ref[name], ref[name + "_v"], ref["loads"].at[at])
            loads[name].start()

    def need(name):
        if name in loads:
            loads.pop(name).wait()
        return ref[name + "_v"]

    load("w1", "g1", "b1")
    for name, rows in (("x", plan.rows), ("og", plan.hrows)):
        copy = pltpu.make_async_copy(
            ref[name].at[mine, 0],
            ref[name + "_in"].at[pl.ds(r * rows, rows)],
            ref[name + "_r"].at[r],
        )
        copy.start()
        own.append(copy)
    pl.semaphore_wait(barrier, len(peers))
    for name, rows in (("x", plan.rows), ("og", plan.hrows)):
        for d in range(1, R):
            t = lax.rem(r + d, R)
            copy = pltpu.make_async_remote_copy(
                src_ref=ref[name].at[s * plan.each + t // plan.copies, 0],
                dst_ref=ref[name + "_in"].at[pl.ds(r * rows, rows)],
                send_sem=ref[name + "_s"].at[d - 1],
                recv_sem=ref[name + "_r"].at[r],
                device_id=(s, i, t),
                device_id_type=MESH,
            )
            copy.start()
            waits.append(copy.wait_send)

    load("k1", "s1", "k2", *NAMES[2:], "sq1", "ex1", "e1", "w2", "sq2", "ex2", "e2")

    def arrived(name, rows, position, d):
        if d == 0:
            own[position].wait()
        else:
            t = lax.rem(r + d, R)
            there = ref[name + "_in"].at[pl.ds(t * rows, rows)]
            pltpu.make_async_remote_copy(
                src_ref=there,
                dst_ref=there,
                send_sem=ref[name + "_s"].at[d - 1],
                recv_sem=ref[name + "_r"].at[t],
                device_id=(s, i, t),
                device_id_type=MESH,
            ).wait_recv()

    st = ref["st"]

    def pairs_of(k):
        return 2 if k in (0, 1, 9) else 1

    def stats_copy(k, d, slot):
        return pltpu.make_async_remote_copy(
            src_ref=st.at[k, slot, pl.ds(0, pairs_of(k))],
            dst_ref=st.at[k, slot, pl.ds(0, pairs_of(k))],
            send_sem=ref["st_s"].at[k, d - 1],
            recv_sem=ref["st_r"].at[k, slot],
            device_id=(s, lax.rem(i + d, I), r),
            device_id_type=MESH,
        )

    def post(k, rows):
        ids = lax.broadcasted_iota(jnp.int32, (8, 128), 0)
        rows = [*rows, *([None] * (len(rows) % 2))]
        for pair in range(len(rows) // 2):
            value = jnp.zeros((8, 128), f32)
            for j in range(8):
                row = rows[2 * pair + j // 4]
                if row is not None:
                    piece = row[:, 128 * (j % 4) : 128 * (j % 4) + 128]
                    value = jnp.where(ids == j, jnp.broadcast_to(piece, (8, 128)), value)
            st[k, i, pair] = value
        for d in range(1, I):
            stats_copy(k, d, i).start()

    def fetch(k, count=2):
        for d in range(1, I):
            stats_copy(k, d, i).wait_send()
            stats_copy(k, d, lax.rem(i + d, I)).wait_recv()
        out = []
        for pair in range((count + 1) // 2):
            value = st[k, 0, pair]
            for j in range(1, I):
                value = value + st[k, j, pair]
            for half in range(2):
                out.append(
                    jnp.concatenate(
                        [
                            jnp.broadcast_to(value[4 * half + j : 4 * half + j + 1], (8, 128))
                            for j in range(4)
                        ],
                        axis=1,
                    )
                )
        return out

    vec = ref["vec"]

    def keep_vectors():
        for name in NAMES:
            row = need(name)[...].astype(f32)
            size = row.shape[0]
            vec[VEC[name], :, :size] = jnp.broadcast_to(row.reshape(1, size), (8, size))

    def vector(name):
        return vec[VEC[name]]

    vr, vc = ref["vr"][0, mine], ref["vc"][0, mine]
    q_ids = lax.broadcasted_iota(jnp.int32, (side, width), 0)
    first_col, last_col = q_ids == 0, q_ids == side - 1
    cm = ref["cm"]
    for b in range(2):
        cm[b] = (2 * q_ids + b < vc).astype(f32)

    def line(value):
        return value.astype(f32).reshape(2, 8, width)

    def pixels(value):
        return value.reshape(side, width)

    def mask_row(a, b, p):
        return line(cm[b]) * (2 * p + a < vr).astype(f32)

    def wide(row):
        return jnp.broadcast_to(row, (8, width))

    row_count = jnp.full((1, width), vr * vc, jnp.int32).astype(f32)
    half_count = jnp.full((1, width), ((vr + 1) // 2) * ((vc + 1) // 2), jnp.int32).astype(f32)

    def over_rows(step, *accs):
        init = tuple(jnp.zeros((8, width), f32) for _ in range(accs[0] if accs else 0))

        def run(p, carry):
            out = step(p)
            if not carry:
                return carry
            return tuple(c + fold(o) for c, o in zip(carry, out))

        return tuple(column(c) for c in lax.fori_loop(0, side, run, init, unroll=4))

    def full_dot(out, left, weight, form=dot):
        wide = out.shape[-1]
        step = min(256, wide)
        for h in range(wide // step):
            cut = slice(h * step, h * step + step)
            w = weight[:, cut] if form is dot else weight[cut, :]
            out[:, :, cut] = form(left, w).reshape(side, side, step).astype(out.dtype)

    def flat(value):
        return value.reshape(pix, value.shape[-1])

    def lines(ref_, start=0):
        return flat(ref_[start : start + side])

    G, F = ref["local"], ref["grads"]
    lead = None if plan.copies == 1 else (lax.rem(r, plan.copies) == 0).astype(f32)

    def put(name, value, row=0, lane=0):
        if lead is not None:
            value = value * lead
        start, per_tile = plan.starts[name]
        count = value.shape[0] // 16
        for k in range(value.shape[1] // 128):
            piece = value[:, 128 * k : 128 * k + 128].astype(bf16).reshape(count, 16, 128)
            at = start + (lane // 128 + k) * per_tile + row // 16
            G[at : at + count] = piece

    X, Y = plan.X, plan.Y
    x, y = lax.rem(r, X), r // X
    axes = {
        "s": (S, s, lambda t: (t, i, r)),
        "r": (R, r, lambda t: (s, i, t)),
        "x": (X, x, lambda t: (s, i, y * X + t)),
        "y": (Y, y, lambda t: (s, i, t * X + x)),
        "i": (I, i, lambda t: (s, t, r)),
    }

    def scatter_source(stream, level):
        base, _, order, offsets = plan.streams[stream]
        if level == 0:
            return G, base
        return ref[f"sum{level - 1}"], offsets[level]

    def scatter_copies(stream, level, outgoing):
        base, size, order, offsets = plan.streams[stream]
        count, me, device = axes[order[level]]
        piece = plan.piece(stream, level)
        source, first = scatter_source(stream, level)
        for d in range(1, count):
            t = lax.rem(me + d, count)
            slot = me if outgoing else t
            copy = pltpu.make_async_remote_copy(
                src_ref=source.at[pl.ds(first + t * piece, piece)],
                dst_ref=ref[f"got{level}"].at[pl.ds(offsets[level] + slot * piece, piece)],
                send_sem=ref["rs_s"].at[stream, level, d - 1],
                recv_sem=ref["rs_r"].at[stream, level, slot],
                device_id=device(t),
                device_id_type=MESH,
            )
            if outgoing:
                copy.start()
                waits.append(copy.wait_send)
            else:
                copy.wait_recv()

    def add_up(stream, level):
        base, size, order, offsets = plan.streams[stream]
        count, me, _ = axes[order[level]]
        piece = plan.piece(stream, level)
        source, first = scatter_source(stream, level)
        got = ref[f"got{level}"]
        if level < len(order) - 1:
            out, at = ref[f"sum{level}"], offsets[level + 1]
        else:
            out, at = F, own_part(stream, len(order))
        step = next(k for k in (16, 12, 10, 9, 8, 7, 6, 5, 4, 3, 2, 1) if piece % k == 0)

        def run(k, carry):
            total = source[pl.ds(first + me * piece + k * step, step)].astype(f32)
            for d in range(1, count):
                t = lax.rem(me + d, count)
                total = total + got[pl.ds(offsets[level] + t * piece + k * step, step)].astype(f32)
            out[pl.ds(at + k * step, step)] = total.astype(bf16)
            return carry

        lax.fori_loop(0, piece // step, run, 0)

    def own_part(stream, depth):
        at, _, order, _ = plan.streams[stream]
        for level in range(depth):
            at = at + axes[order[level]][1] * plan.piece(stream, level)
        return at

    def gather_copies(stream, level, outgoing):
        count, me, device = axes[plan.streams[stream][2][level]]
        base = own_part(stream, level)
        piece = plan.piece(stream, level)
        for d in range(1, count):
            t = lax.rem(me + d, count)
            slot = me if outgoing else t
            there = F.at[pl.ds(base + slot * piece, piece)]
            copy = pltpu.make_async_remote_copy(
                src_ref=there,
                dst_ref=there,
                send_sem=ref["ag_s"].at[stream, level, d - 1],
                recv_sem=ref["ag_r"].at[stream, level, slot],
                device_id=device(t),
                device_id_type=MESH,
            )
            if outgoing:
                copy.start()
                waits.append(copy.wait_send)
            else:
                copy.wait_recv()

    done = [0] * len(plan.segments)
    started = []

    def pump(*which):
        for g in which or tuple(started):
            if g not in started:
                started.insert(0, g)
            k = done[g]
            depth = len(plan.streams[plan.members[g][0]][2])
            if k > 2 * depth:
                continue
            done[g] += 1
            if k == 0:
                (_, _), (base, size), used = plan.segments[g]
                if used < base + size:
                    G[used : base + size] = jnp.zeros((base + size - used, 16, 128), bf16)
            for stream in plan.members[g]:
                if 1 <= k <= depth:
                    scatter_copies(stream, k - 1, False)
                    add_up(stream, k - 1)
                elif k > depth:
                    gather_copies(stream, 2 * depth - k, False)
                if k < depth:
                    scatter_copies(stream, k, True)
                elif k < 2 * depth:
                    gather_copies(stream, 2 * depth - 1 - k, True)

    vec_grads = {}

    gw = plan.gw
    span = 4 * gw
    def blocks(name, out, turned=False):
        kernels = need(name)
        shape = (span, 128) if turned else (128, span)
        long = lax.broadcasted_iota(jnp.int32, shape, 0 if turned else 1)
        short = lax.broadcasted_iota(jnp.int32, shape, 1 if turned else 0)
        spread = (lax.rem(long, gw) == short).astype(f32).astype(bf16)
        row = lax.broadcasted_iota(jnp.int32, (span, span), 0) // gw
        col = lax.broadcasted_iota(jnp.int32, (span, span), 1) // gw
        for k, t in enumerate(ORDER):
            for h in range(width // span):
                piece = kernels[t, 4 * h : 4 * h + 4].reshape(span, 128)
                full = dot_nt(spread, piece) if turned else dot(piece, spread)
                out[h, k * span : (k + 1) * span] = jnp.where(row == col, full, 0.0).astype(bf16)

    def groups_grad(name, taps, turned):
        lane = lax.broadcasted_iota(jnp.int32, (gw, span), 1) // gw
        for t, (var, start) in enumerate(taps):
            for h in range(width // span):
                cut = slice(h * span, (h + 1) * span)
                res = dot(turned[h], flat(var[start : start + side, :, cut]))
                out = res[0:gw]
                for j in range(1, 4):
                    out = jnp.where(lane == j, res[j * gw : (j + 1) * gw], out)
                put(name, out, t * gw, h * span)

    band, bands = plan.band, plan.bands
    bhalf = band // 2
    out_id = lax.broadcasted_iota(jnp.int32, (pix, pix), 0)
    in_id = lax.broadcasted_iota(jnp.int32, (pix, pix), 1)

    def source(o):
        quarter = o // (bhalf * side)
        down = lax.rem(o, bhalf * side) // side
        return (2 * down + quarter // 2) * plan.cols + 2 * lax.rem(o, side) + lax.rem(quarter, 2)

    ref["sort"][...] = (source(out_id) == in_id).astype(f32).astype(bf16)
    ref["unsort"][...] = (source(in_id) == out_id).astype(f32).astype(bf16)

    xp, R1 = ref["xp"], ref["R1"]
    blocks("k1", ref["bd1"])
    keep_vectors()

    def transpose(source, out):
        out[...] = source.astype(f32).T.astype(bf16)

    totals = [jnp.zeros((8, width), f32)] * 2
    by_band = plan.rows % band == 0
    if not by_band:
        for d in range(R):
            arrived("x", plan.rows, 0, d)
    for d in range(bands):
        if by_band:
            if d % (plan.rows // band) == 0:
                arrived("x", plan.rows, 0, d // (plan.rows // band))
            k = lax.rem(r * (plan.rows // band) + d, bands)
        else:
            k = d
        block = ref["x_in"][pl.ds(k * band, band)].reshape(pix, cin)
        block = dot(ref["sort"][...], block).astype(bf16)
        xp[k] = block.reshape(4 * bhalf, side, cin)
        full_dot(R1.at[k], block, need("w1"))
        for j in range(4 * bhalf):
            a, b = PHASES[j // bhalf]
            v = line(R1[k, j])
            mv = v * mask_row(a, b, k * bhalf + j % bhalf)
            totals = [totals[0] + fold(mv), totals[1] + fold(mv * v)]
    even = xp.at[:, 0:bhalf]

    def at_phase(ab, p):
        return p // bhalf, ab * bhalf + lax.rem(p, bhalf)

    post(0, [column(totals[0]), column(totals[1]), row_count, half_count])
    SC = ref["SC"]
    full_dot(SC, even[...].reshape(pix, cin), need("s1"))

    def moments(field):
        def step(p):
            v = line(field[p])
            mv = v * mask_row(0, 0, p)
            return mv, mv * v

        return over_rows(step, 2)

    short_sums = moments(SC)
    for k in range(bands):
        transpose(xp[k].reshape(pix, cin), ref["xpt"].at[k])

    def coefficients(first, second, inverse, gain, shift):
        mean = first * inverse
        scale = lax.rsqrt(second * inverse - mean * mean + epsilon)
        a = scale * gain
        return a, shift - mean * a, scale, -mean * scale

    tot = fetch(0, 4)
    inv_full, inv_half = 1.0 / tot[2], 1.0 / tot[3]
    n1 = coefficients(tot[0], tot[1], inv_full, vector("g1"), vector("b1"))

    va = ref["va"]
    va[3:6, 0:1] = jnp.zeros((3, 1, side, width), bf16)

    def shifted(v, edge, amount):
        return jnp.where(edge, 0.0, pltpu.roll(v, amount, 0))

    for ab, (a, b) in enumerate(PHASES):

        def step(p, ab=ab, a=a, b=b):
            v = mask_row(a, b, p) * silu(line(R1[at_phase(ab, p)]) * n1[0] + n1[1])
            v = pixels(v)
            slot = (0, 1, 3, 4)[ab]
            va[slot, p + a] = v.astype(bf16)
            if b:
                va[slot + 1, p + a] = shifted(v, first_col, 1).astype(bf16)

        over_rows(step)
    taps1 = []
    for t in range(9):
        u, v = t // 3, t % 3
        slot = (0, 1, 3, 4)[2 * (u != 1) + (v != 1)] + (v == 0)
        taps1.append((va.at[slot], 1 if u == 2 else 0))

    def convolve(taps, weights, out):
        for h in range(width // span):
            cut = slice(h * span, (h + 1) * span)
            left = [flat(taps[t][0][taps[t][1] : taps[t][1] + side, :, cut]) for t in ORDER]
            acc = dot(jnp.concatenate(left, axis=1), weights[h])
            out[:, :, cut] = acc.astype(bf16).reshape(side, side, span)

    c1 = ref["c1"]
    convolve(taps1, ref["bd1"], c1)
    post(1, [*moments(c1), *short_sums])
    blocks("k2", ref["bd2"])
    tot = fetch(1, 4)
    nc1 = coefficients(tot[0], tot[1], inv_half, vector("gg1"), vector("gb1"))
    ns = coefficients(tot[2], tot[3], inv_half, vector("sg1"), vector("sb1"))

    def excite(conv, norm, hidden, gated, sq, sq_form, sqb, ex, exb):
        def step(p):
            v = mask_row(0, 0, p) * silu(line(conv[p]) * norm[0] + norm[1])
            hidden[p] = pixels(v)
            return (v,)

        (total,) = over_rows(step, 1)
        pooled = total / half_count
        pre = small_dot(pooled, sq[...], sq_form) + sqb
        inner = silu(pre)
        gate = sigmoid(small_dot(inner, ex[...], dot) + exb)
        gate_wide = wide(gate)

        def step_two(p):
            gated[p] = pixels(line(hidden[p]) * gate_wide).astype(bf16)

        over_rows(step_two)
        return pooled, pre, inner, gate

    H1, ga1 = ref["H1"], ref["ga1"]
    kept1 = excite(
        c1, nc1, H1, ga1, need("sq1"), dot_nt, vec[VEC["sqb1"], 0:1, : plan.q1], need("ex1"), vec[VEC["exb1"], 0:1]
    )
    E1 = ref["E1"]
    full_dot(E1, lines(ga1), need("e1"))
    post(2, moments(E1))
    transpose(lines(ga1), ref["ga1t"])
    blocks("k1", ref["bd1t"], True)
    tot = fetch(2)
    ne = coefficients(tot[0], tot[1], inv_half, vector("eg1"), vector("eb1"))
    ent = ref["ent"]
    both_shifts = ne[1] + ns[1]

    def step(p):
        v = line(E1[p]) * ne[0] + line(SC[p]) * ns[0] + both_shifts
        ent[p] = pixels(mask_row(0, 0, p) * silu(v)).astype(bf16)

    over_rows(step)

    def send_out(source, out, rows, target, steps=None):
        for k in range(R // plan.copies) if steps is None else steps:
            t = lax.rem(r + plan.copies * k, R)
            there = ref[out].at[0, mine, 0] if out == "act" else ref[out].at[mine, 0]
            here = source.at[pl.ds(t * rows, rows)]
            copy = pltpu.make_async_remote_copy(
                src_ref=here,
                dst_ref=there,
                send_sem=ref[out + "_s"].at[target, k],
                recv_sem=ref[out + "_r"].at[mine],
                device_id=(target, i, t),
                device_id_type=MESH,
            )
            if k:
                copy.start()
                waits.append(copy.wait_send)
            else:
                local = pltpu.make_async_copy(here, there, ref[out + "_r"].at[mine])

                @pl.when(s == target)
                def _():
                    local.start()

                @pl.when(s != target)
                def _():
                    copy.start()

                def finish(copy=copy):
                    @pl.when(s != target)
                    def _():
                        copy.wait_send()

                waits.append(finish)

    send_out(ent, "act", plan.hrows, 0)

    R2 = ref["R2"]
    full_dot(R2, lines(ent), need("w2"))
    post(3, moments(R2))
    transpose(lines(ent), ref["entt"])
    tot = fetch(3)
    n2 = coefficients(tot[0], tot[1], inv_half, vector("g2"), vector("b2"))
    vb = ref["vb"]
    vb[:, 0:1] = jnp.zeros((3, 1, side, width), bf16)
    vb[:, side + 1 :] = jnp.zeros((3, 1, side, width), bf16)

    def three(out, p, v):
        out[0, p + 1] = shifted(v, first_col, 1).astype(bf16)
        out[1, p + 1] = v.astype(bf16)
        out[2, p + 1] = shifted(v, last_col, side - 1).astype(bf16)

    def step(p):
        three(vb, p, pixels(mask_row(0, 0, p) * silu(line(R2[p]) * n2[0] + n2[1])))

    over_rows(step)
    taps2 = [(vb.at[t % 3], t // 3) for t in range(9)]
    c2 = ref["c2"]
    convolve(taps2, ref["bd2"], c2)
    post(4, moments(c2))
    blocks("k2", ref["bd2t"], True)
    tot = fetch(4)
    nc2 = coefficients(tot[0], tot[1], inv_half, vector("gg2"), vector("gb2"))
    H2, ga2 = ref["H2"], ref["ga2"]
    kept2 = excite(
        c2, nc2, H2, ga2, need("sq2"), dot, vec[VEC["sqb2"], 0:1, : plan.q2], need("ex2"), vec[VEC["exb2"], 0:1]
    )
    E2 = ref["E2"]
    full_dot(E2, lines(ga2), need("e2"))
    post(5, moments(E2))
    transpose(lines(ga2), ref["ga2t"])
    for d in range(R):
        arrived("og", plan.hrows, 1, d)
    tot = fetch(5)
    ne2 = coefficients(tot[0], tot[1], inv_half, vector("eg2"), vector("eb2"))
    leave, D, og = ref["leave"], ref["D"], ref["og_in"]

    def step(p):
        e = line(E2[p])
        v = e * ne2[0] + ne2[1] + line(ent[p])
        sg = sigmoid(v)
        m = mask_row(0, 0, p)
        leave[p] = pixels(m * v * sg).astype(bf16)
        g = line(og[p]) * m * (sg * (1.0 + v * (1.0 - sg)))
        D[p] = pixels(g)
        return g, g * (e * ne2[2] + ne2[3])

    parts = over_rows(step, 2)
    vec_grads["eb2"], vec_grads["eg2"] = parts
    post(6, parts)
    send_out(leave, "act", plan.hrows, 1)

    def back_rule(sums, inverse, gain, norm):
        a = gain * norm[2]
        k0 = a * (sums[0] + norm[3] * sums[1]) * inverse
        return a, k0, a * norm[2] * sums[1] * inverse

    def back_excite(dg, kept, hidden, conv, norm, sq, sq_form, ex, out):
        pooled, pre, inner, gate = kept

        def step(p):
            return (line(dg[p]) * line(hidden[p]),)

        (dgate,) = over_rows(step, 1)
        dpre = dgate * gate * (1.0 - gate)
        dsq = small_dot(dpre, ex[...], dot_nt) * slope(pre)
        dpool = wide(small_dot(dsq, sq[...], sq_form) / half_count)
        gate_wide = wide(gate)

        def step_two(p):
            v = line(conv[p])
            g = (line(dg[p]) * gate_wide + dpool) * mask_row(0, 0, p)
            g = g * slope(v * norm[0] + norm[1])
            out[p] = pixels(g)
            return g, g * (v * norm[2] + norm[3])

        return over_rows(step_two, 2), dpre, dsq

    def excite_grads(name, kept, dpre, dsq):
        pooled, pre, inner, gate = kept
        put("sq" + name, small_outer(dsq, pooled))
        put("ex" + name, small_outer(inner, dpre))
        vec_grads["exb" + name] = dpre
        count = dsq.shape[1]
        eye = (
            lax.broadcasted_iota(jnp.int32, (count, width), 0)
            == lax.broadcasted_iota(jnp.int32, (count, width), 1)
        ).astype(f32).astype(bf16)
        vec_grads["sqb" + name] = small_dot(dsq, eye, dot)

    def turn(gradient_ref, start):
        out = []
        for h in range(width // span):
            piece = flat(gradient_ref[start : start + side, :, h * span : (h + 1) * span])
            out.append(piece.astype(f32).T.astype(bf16))
        return out

    d1, dg, GR = ref["d1"], ref["dg"], ref["GR"]
    tot = fetch(6)
    rule = back_rule((tot[0], tot[1]), inv_half, vector("eg2"), ne2)

    def step(p):
        v = rule[0] * line(D[p]) - mask_row(0, 0, p) * (rule[1] + rule[2] * line(E2[p]))
        d1[p] = pixels(v).astype(bf16)

    over_rows(step)
    full_dot(dg, lines(d1), need("e2"), dot_nt)
    parts, dpre, dsq = back_excite(dg, kept2, H2, c2, nc2, need("sq2"), dot_nt, need("ex2"), GR)
    vec_grads["gb2"], vec_grads["gg2"] = parts
    post(7, parts)
    put("e2", dot(ref["ga2t"][...], lines(d1)))
    excite_grads("2", kept2, dpre, dsq)
    pump(0)
    tot = fetch(7)
    rule = back_rule((tot[0], tot[1]), inv_half, vector("gg2"), nc2)
    vd = ref["vd"]
    vd[:, 0:1] = jnp.zeros((3, 1, side, width), bf16)
    vd[:, side + 1 :] = jnp.zeros((3, 1, side, width), bf16)

    def step(p):
        v = rule[0] * line(GR[p]) - mask_row(0, 0, p) * (rule[1] + rule[2] * line(c2[p]))
        three(vd, p, pixels(v))

    over_rows(step)

    def convolve_back(taps, first, weights, out):
        for h in range(width // span):
            cut = slice(h * span, (h + 1) * span)
            left = [flat(var[start : start + side, :, cut]) for var, start in taps]
            rows = slice(first * span, (first + len(taps)) * span)
            acc = dot(jnp.concatenate(left, axis=1), weights[h, rows])
            out[:, :, cut] = acc.reshape(side, side, span)

    DA = ref["DA"]
    convolve_back(
        [(vd.at[2 - t % 3], 2 - t // 3) for t in ORDER],
        0,
        ref["bd2t"],
        DA.at[0],
    )

    def step(p):
        v = line(R2[p])
        g = line(DA[0, p]) * mask_row(0, 0, p) * slope(v * n2[0] + n2[1])
        GR[p] = pixels(g)
        return g, g * (v * n2[2] + n2[3])

    parts = over_rows(step, 2)
    vec_grads["b2"], vec_grads["g2"] = parts
    post(8, parts)
    pump()
    groups_grad("k2", taps2, turn(vd.at[1], 1))
    pump()
    tot = fetch(8)
    rule = back_rule((tot[0], tot[1]), inv_half, vector("g2"), n2)

    def step(p):
        v = rule[0] * line(GR[p]) - mask_row(0, 0, p) * (rule[1] + rule[2] * line(R2[p]))
        d1[p] = pixels(v).astype(bf16)

    over_rows(step)
    full_dot(GR, lines(d1), need("w2"), dot_nt)

    def step(p):
        e, sc = line(E1[p]), line(SC[p])
        g = line((D[p] + GR[p]).astype(bf16))
        g = g * mask_row(0, 0, p) * slope(e * ne[0] + sc * ns[0] + both_shifts)
        D[p] = pixels(g)
        return g, g * (e * ne[2] + ne[3]), g * (sc * ns[2] + ns[3])

    parts = over_rows(step, 3)
    vec_grads["eb1"], vec_grads["eg1"], vec_grads["sg1"] = parts
    vec_grads["sb1"] = parts[0]
    post(9, parts)
    pump()
    put("w2", dot(ref["entt"][...], lines(d1)))
    pump(1)
    tot = fetch(9, 3)
    rule_e = back_rule((tot[0], tot[1]), inv_half, vector("eg1"), ne)
    rule_s = back_rule((tot[0], tot[2]), inv_half, vector("sg1"), ns)
    d2 = ref["d2"]

    def step(p):
        g, m = line(D[p]), mask_row(0, 0, p)
        v = rule_e[0] * g - m * (rule_e[1] + rule_e[2] * line(E1[p]))
        d1[p] = pixels(v).astype(bf16)
        v = rule_s[0] * g - m * (rule_s[1] + rule_s[2] * line(SC[p]))
        d2[p] = pixels(v).astype(bf16)

    over_rows(step)
    full_dot(dg, lines(d1), need("e1"), dot_nt)
    parts, dpre, dsq = back_excite(dg, kept1, H1, c1, nc1, need("sq1"), dot, need("ex1"), GR)
    vec_grads["gb1"], vec_grads["gg1"] = parts
    post(10, parts)
    pump()
    put("e1", dot(ref["ga1t"][...], lines(d1)))
    put("s1", dot_tn(even[...].reshape(pix, cin), lines(d2)))
    excite_grads("1", kept1, dpre, dsq)
    pump(2)
    tot = fetch(10)
    rule = back_rule((tot[0], tot[1]), inv_half, vector("gg1"), nc1)

    def step(p):
        v = rule[0] * line(GR[p]) - mask_row(0, 0, p) * (rule[1] + rule[2] * line(c1[p]))
        three(vd, p, pixels(v))

    over_rows(step)
    sums = []
    for ab, (a, b) in enumerate(PHASES):
        chosen = []
        first = (0, 1, 3, 5)[ab]
        for t in ORDER[first : first + (1, 2, 2, 4)[ab]]:
            chosen.append((vd.at[2 if t % 3 == 0 else 1], 2 if t // 3 == 0 else 1))
        convolve_back(chosen, first, ref["bd1t"], DA.at[ab])

        def step(p, ab=ab, a=a, b=b):
            v = line(R1[at_phase(ab, p)])
            g = line(DA[ab, p]) * mask_row(a, b, p) * slope(v * n1[0] + n1[1])
            DA[ab, p] = pixels(g)
            return g, g * (v * n1[2] + n1[3])

        sums.append(over_rows(step, 2))
    parts = (sum(x[0] for x in sums), sum(x[1] for x in sums))
    vec_grads["b1"], vec_grads["g1"] = parts
    post(11, parts)
    pump()
    groups_grad("k1", taps1, turn(vd.at[1], 1))
    ids = lax.broadcasted_iota(jnp.int32, (VEC_ROWS, width), 0)
    value = jnp.zeros((VEC_ROWS, width), f32)
    for name, at in VEC.items():
        value = jnp.where(ids == at, jnp.broadcast_to(vec_grads[name], value.shape), value)
    put(VECTORS, value)
    pump(3)
    pump(1, 0)
    tot = fetch(11)
    rule = back_rule((tot[0], tot[1]), inv_full, vector("g1"), n1)
    dr = ref["dr"]
    for ab, (a, b) in enumerate(PHASES):

        def step(p, ab=ab, a=a, b=b):
            v = rule[0] * line(DA[ab, p])
            v = v - mask_row(a, b, p) * (rule[1] + rule[2] * line(R1[at_phase(ab, p)]))
            dr[at_phase(ab, p)] = pixels(v).astype(bf16)

        over_rows(step)
    total = None
    for k in range(bands):
        term = dot(ref["xpt"][k], dr[k].reshape(pix, width))
        total = term if total is None else total + term
    put("w1", total)
    pump(4)
    pump(3, 2, 1, 0)
    cut = cin // 2
    ref["dxo0"][...] = jnp.zeros((2 * side, plan.cols, 128), bf16)
    ref["dxo1"][...] = jnp.zeros((2 * side, plan.cols, 128), bf16)
    stepwise = plan.each == bands
    for d in [*range(1, bands), 0]:
        k = lax.rem(r + plan.copies * d, R) * plan.rows // band if stepwise else d
        for part in range(2):
            dxo = ref[f"dxo{part}"]
            rows = slice(part * cut, (part + 1) * cut)
            v = dot_nt(dr[k].reshape(pix, width), need("w1")[rows, :])
            w = dot_nt(
                d2[pl.ds(k * bhalf, bhalf)].reshape(bhalf * side, width), need("s1")[rows, :]
            )
            v = jnp.concatenate([v[: bhalf * side] + w, v[bhalf * side :]], axis=0)
            v = dot(ref["unsort"][...], v.astype(bf16)).astype(bf16)
            dxo[pl.ds(k * band, band), :, :cut] = v.reshape(band, plan.cols, cut)
            if stepwise:
                send_out(dxo, "dx", plan.rows, part, (d,))
        pump()
    if not stepwise:
        send_out(ref["dxo0"], "dx", plan.rows, 0)
        send_out(ref["dxo1"], "dx", plan.rows, 1)
    for _ in range(9):
        pump()
    for wait in waits:
        wait()
    for m in range(plan.M):
        t = (m % plan.each) * plan.copies + lax.rem(r, plan.copies)
        for out in ("act", "dx"):
            there = ref[out].at[0, m, 0] if out == "act" else ref[out].at[m, 0]
            pltpu.make_async_copy(there, there, ref[out + "_r"].at[m]).wait()


WEIGHTS = ("w1", "k1", "k2", "sq1", "ex1", "e1", "s1", "w2", "sq2", "ex2", "e2")


def run_main(plan, arrays):
    side, width, cin = plan.side, plan.width, plan.cin
    wide = 4 * plan.gw
    field = (side, side, width)
    scratch = {
        "x_in": pltpu.VMEM((2 * side, plan.cols, cin), bf16),
        "og_in": pltpu.VMEM(field, bf16),
        "st": pltpu.VMEM((EXCHANGES, plan.I, 2, 8, 128), f32),
        "cm": pltpu.VMEM((2, side, width), f32),
        **{
            name: pltpu.VMEM((width // wide, plan.taps * wide, wide), bf16)
            for name in ("bd1", "bd2", "bd1t", "bd2t")
        },
        "xpt": pltpu.VMEM((plan.bands, cin, plan.pix), bf16),
        **{name: pltpu.VMEM((width, plan.pix), bf16) for name in ("ga1t", "ga2t", "entt")},
        "sort": pltpu.VMEM((plan.pix, plan.pix), bf16),
        "unsort": pltpu.VMEM((plan.pix, plan.pix), bf16),
        "xp": pltpu.VMEM((plan.bands, 2 * plan.band, side, cin), bf16),
        "R1": pltpu.VMEM((plan.bands, 2 * plan.band, side, width), f32),
        "va": pltpu.VMEM((6, side + 1, side, width), bf16),
        "vb": pltpu.VMEM((3, side + 2, side, width), bf16),
        "vd": pltpu.VMEM((3, side + 2, side, width), bf16),
        "DA": pltpu.VMEM((4,) + field, f32),
        "dr": pltpu.VMEM((plan.bands, 2 * plan.band, side, width), bf16),
        "dxo0": pltpu.VMEM((2 * side, plan.cols, 128), bf16),
        "dxo1": pltpu.VMEM((2 * side, plan.cols, 128), bf16),
    }
    for name in ("SC", "H1", "E1", "R2", "H2", "E2", "D", "GR"):
        scratch[name] = pltpu.VMEM(field, f32)
    for name in ("c1", "ga1", "ent", "c2", "ga2", "leave", "d1", "d2", "dg"):
        scratch[name] = pltpu.VMEM(field, bf16)
    for name in ("x", "og"):
        scratch[name + "_s"] = pltpu.SemaphoreType.DMA((max(plan.R - 1, 1),))
        scratch[name + "_r"] = pltpu.SemaphoreType.DMA((plan.R,))
    scratch["st_s"] = pltpu.SemaphoreType.DMA((EXCHANGES, max(plan.I - 1, 1)))
    scratch["st_r"] = pltpu.SemaphoreType.DMA((EXCHANGES, plan.I))
    for name in ("act", "dx"):
        scratch[name + "_s"] = pltpu.SemaphoreType.DMA((2, plan.R // plan.copies))
        scratch[name + "_r"] = pltpu.SemaphoreType.DMA((plan.M,))
    for name in NAMES + WEIGHTS:
        scratch[name + "_v"] = pltpu.VMEM(arrays[name].shape, bf16)
    scratch["vec"] = pltpu.VMEM((len(NAMES), 8, width), f32)
    scratch["loads"] = pltpu.SemaphoreType.DMA((len(NAMES + WEIGHTS),))
    scratch["local"] = pltpu.VMEM((plan.blocks, 16, 128), bf16)
    for level, room in enumerate(plan.rooms):
        scratch[f"got{level}"] = pltpu.VMEM((room, 16, 128), bf16)
        if level:
            scratch[f"sum{level - 1}"] = pltpu.VMEM((room, 16, 128), bf16)
    most = max(plan.sizes.values())
    for name in ("rs", "ag"):
        scratch[name + "_s"] = pltpu.SemaphoreType.DMA((len(plan.streams), 4, most - 1))
        scratch[name + "_r"] = pltpu.SemaphoreType.DMA((len(plan.streams), 4, most))
    inputs = ("x", "og", "vr", "vc") + NAMES + WEIGHTS
    outputs = ("act", "dx", "grads")
    names = inputs + outputs + tuple(scratch)
    any_space = pl.BlockSpec(memory_space=pl.ANY)
    smem = pl.BlockSpec(memory_space=pltpu.SMEM)
    vmem = pl.BlockSpec(memory_space=pltpu.VMEM)
    return pl.pallas_call(
        functools.partial(main_kernel, plan, names),
        out_shape=(
            jax.ShapeDtypeStruct((1, plan.M, 1, plan.hrows, side, width), bf16),
            jax.ShapeDtypeStruct((plan.M, 1, plan.rows, plan.cols, 128), bf16),
            jax.ShapeDtypeStruct((plan.blocks, 16, 128), bf16),
        ),
        in_specs=[any_space, any_space, smem, smem] + [any_space] * (len(NAMES) + len(WEIGHTS)),
        out_specs=(any_space, any_space, vmem),
        scratch_shapes=list(scratch.values()),
        compiler_params=pltpu.CompilerParams(
            collective_id=0, has_side_effects=True, vmem_limit_bytes=60 * 1024 * 1024
        ),
        name="blocks",
    )(*[arrays[name] for name in inputs])


OUTS = (
    "w1", "g1", "b1", "k1", "gg1", "gb1", "sq1", "sqb1", "ex1", "exb1", "e1", "eg1", "eb1",
    "s1", "sg1", "sb1", "w2", "g2", "b2", "k2", "gg2", "gb2", "sq2", "sqb2", "ex2", "exb2",
    "e2", "eg2", "eb2",
)


def unpack_kernel(plan, source, *rest):
    count = len(OUTS)
    outs, bufs, loads_at, sems = rest[:count], rest[count:-3], rest[-3:-1], rest[-1]
    copies = []
    loads = []
    order = sorted(plan.starts, key=lambda name: plan.starts[name])
    order = [name for name in order if name != VECTORS] + [VECTORS]
    blocks = loads_at[0]
    for k, name in enumerate(order):
        start, per_tile = plan.starts[name]
        part = pl.ds(start, per_tile * (plan.width // 128))
        loads.append(pltpu.make_async_copy(source.at[part], blocks.at[part], loads_at[1].at[k]))
        loads[-1].start()

    def tile(name, k):
        start, per_tile = plan.starts[name]
        at = start + k * per_tile
        return blocks[at : at + per_tile].reshape(16 * per_tile, 128).astype(f32)

    tiles = plan.width // 128
    vec = None
    turn = [OUTS.index(name) for name in order if name != VECTORS]
    turn += [k for k, name in enumerate(OUTS) if name in VEC]
    for position, k in enumerate(turn):
        name, out = OUTS[k], bufs[k]
        if position < len(loads):
            loads[position].wait()
        if name in VEC and vec is None:
            vec = jnp.concatenate([tile(VECTORS, k) for k in range(tiles)], axis=1)
        if name in VEC:
            size = out.shape[0]
            out[...] = vec[VEC[name] : VEC[name] + 1, :size].reshape(size)
        elif name[0] == "k":

            def run(t, carry, name=name, out=out):
                for lane in range(tiles):
                    start, per_tile = plan.starts[name]
                    at = start + lane * per_tile + t * (plan.gw // 16)
                    piece = blocks[pl.ds(at, plan.gw // 16)].reshape(plan.gw, 128)
                    piece = piece.astype(f32).T
                    for j in range(128 // plan.gw):
                        group = lane * (128 // plan.gw) + j
                        out[t, group, :, : plan.gw] = piece[j * plan.gw : (j + 1) * plan.gw]
                return carry

            lax.fori_loop(0, plan.taps, run, 0)
        elif name == "sq2":
            for lane in range(tiles):
                out[128 * lane : 128 * lane + 128] = tile(name, lane).T
        else:
            for lane in range(tiles):
                out[:, 128 * lane : 128 * lane + 128] = tile(name, lane)
        copies.append(pltpu.make_async_copy(out, outs[k], sems.at[k]))
        copies[-1].start()
    for copy in copies:
        copy.wait()


def unpack(plan, grads, weights):
    shapes = []
    for name, w in zip(OUTS, weights):
        shape = w.shape[:3] + (128,) if name[0] == "k" else w.shape
        shapes.append(jax.ShapeDtypeStruct(shape, f32))
    any_space = pl.BlockSpec(memory_space=pl.ANY)
    return pl.pallas_call(
        functools.partial(unpack_kernel, plan),
        out_shape=shapes,
        in_specs=[any_space],
        out_specs=[any_space] * len(shapes),
        scratch_shapes=[pltpu.VMEM(v.shape, v.dtype) for v in shapes]
        + [pltpu.VMEM(grads.shape, bf16), pltpu.SemaphoreType.DMA((len(plan.starts),))]
        + [pltpu.SemaphoreType.DMA((len(shapes),))],
        compiler_params=pltpu.CompilerParams(vmem_limit_bytes=60 * 1024 * 1024),
        name="unpack",
    )(grads)


def body(sizes, input_maps, valid_rows, valid_cols, *rest):
    weights, output_grad = rest[:-1], rest[-1]
    (w1, g1, b1, k1, gg1, gb1, sq1, sqb1, ex1, exb1, e1, eg1, eb1, s1, sg1, sb1) = weights[:16]
    (w2, g2, b2, k2, gg2, gb2, sq2, sqb2, ex2, exb2, e2, eg2, eb2) = weights[16:]
    turned = sq1.T
    plan = Plan(sizes, [v.shape for v in (input_maps, output_grad, w1, k1, turned, sq2)])
    vectors = (
        g1, b1, gg1, gb1, exb1, eg1, eb1, sg1, sb1, sqb1, g2, b2, gg2, gb2, exb2, eg2, eb2, sqb2,
    )
    arrays = dict(
        x=input_maps, og=output_grad, vr=valid_rows.T, vc=valid_cols.T, w1=w1,
        k1=jnp.pad(k1, ((0, 0), (0, 0), (0, 0), (0, 128 - plan.gw))),
        k2=jnp.pad(k2, ((0, 0), (0, 0), (0, 0), (0, 128 - plan.gw))),
        sq1=turned, ex1=ex1, e1=e1, s1=s1, w2=w2, sq2=sq2, ex2=ex2, e2=e2,
        **dict(zip(NAMES, vectors)),
    )
    act, dx, grads = run_main(plan, arrays)
    out = list(unpack(plan, grads, weights[:6] + (turned,) + weights[7:]))
    out[6] = out[6].T
    for at in (3, 19):
        out[at] = out[at][..., : plan.gw]
    dx = dx[..., : plan.cin // 2]
    return (act, dx, *out)


def solution(mesh):
    tiled = P(None, "img", "row", None, None)
    image = P(None, "img")
    sizes = tuple(mesh.shape[name] for name in ("section", "img", "row"))
    return jax.shard_map(
        functools.partial(body, sizes),
        mesh=mesh,
        in_specs=(tiled, image, image) + (P(),) * 29 + (tiled,),
        out_specs=(
            P("section", None, "img", "row", None, None),
            P(None, "img", "row", None, "section"),
        )
        + (P(),) * 29,
        check_vma=False,
    )
```

```python
import functools

import jax
import jax.numpy as jnp
from jax import lax
from jax.experimental import pallas as pl
from jax.experimental.pallas import tpu as pltpu
from jax.sharding import PartitionSpec as P

epsilon = 1e-05
f32 = jnp.float32
bf16 = jnp.bfloat16
MESH = pl.DeviceIdType.MESH
PHASES = ((0, 0), (0, 1), (1, 0), (1, 1))
ORDER = (4, 3, 5, 1, 7, 0, 2, 6, 8)
EXCHANGES = 12
NAMES = (
    "g1", "b1", "gg1", "gb1", "exb1", "eg1", "eb1", "sg1", "sb1", "sqb1",
    "g2", "b2", "gg2", "gb2", "exb2", "eg2", "eb2", "sqb2",
)
VEC = {name: k for k, name in enumerate(NAMES)}
VEC_ROWS = 32
VECTORS = "vec"


def segments_of(cin, width, taps, group, sq1, sq2, devices):
    layout = (
        (("e2", width), ("sq2", sq2), ("ex2", sq2)),
        (("k2", taps * group), ("w2", width)),
        (("e1", width), ("s1", cin), ("sq1", sq1), ("ex1", sq1)),
        (("k1", taps * group), (VECTORS, VEC_ROWS)),
        (("w1", cin),),
    )
    starts, segments, at = {}, [], 0
    for parts in layout:
        base = at
        for name, rows in parts:
            starts[name] = (at, rows // 16)
            at += rows // 16 * (width // 128)
        units = -(-(at - base) // devices)
        segments.append((base, units * devices, at))
        at = base + units * devices
    return starts, tuple(segments), at


def sigmoid(v):
    return 0.5 * jnp.tanh(0.5 * v) + 0.5


def silu(v):
    return v * sigmoid(v)


def slope(v):
    s = sigmoid(v)
    return s * (1.0 + v * (1.0 - s))


def dot(left, right):
    return jnp.dot(left, right, preferred_element_type=f32)


def dot_nt(left, right):
    return lax.dot_general(left, right, (((1,), (1,)), ((), ())), preferred_element_type=f32)


def dot_tn(left, right):
    return lax.dot_general(left, right, (((0,), (0,)), ((), ())), preferred_element_type=f32)


def parts_of(v):
    high = v.astype(bf16).astype(f32)
    return high, v - high


def stacked(rows, width):
    ids = lax.broadcasted_iota(jnp.int32, (16, width), 0)
    total = jnp.zeros((16, width), f32)
    for k, row in enumerate(rows):
        total = jnp.where(ids == k, jnp.broadcast_to(row, (16, width)), total)
    return total.astype(bf16)


def small_dot(row, weight, form):
    out = form(stacked(parts_of(row), row.shape[1]), weight)
    return out[0:1] + out[1:2]


def small_outer(left, right):
    lh, ll = parts_of(left)
    rh, rl = parts_of(right)
    return dot_tn(
        stacked((lh, ll, lh, ll), left.shape[1]), stacked((rh, rh, rl, rl), right.shape[1])
    )


def fold(v):
    return v[0] + v[1]


def column(acc):
    return jnp.sum(acc, axis=0, keepdims=True)


class Plan:
    def __init__(self, mesh_sizes, args):
        self.S, self.I, self.R = mesh_sizes
        x, og, w1, k1, sq1, sq2 = args
        self.M, _, self.rows, self.cols, self.cin = x
        _, _, self.hrows, self.side, self.width = og
        self.taps, self.groups, self.gw, _ = k1
        self.q1, self.q2 = sq1[0], sq2[1]
        self.each = self.M // self.S
        self.copies = self.R // self.each
        self.pix = self.side * self.side
        self.band = self.pix // self.cols
        self.bands = 2 * self.side // self.band
        self.starts, self.segments, self.blocks = segments_of(
            self.cin, self.width, self.taps, self.gw, self.q1, self.q2, self.S * self.I * self.R
        )
        self.X = 1
        while self.X * self.X < self.R:
            self.X *= 2
        self.Y = self.R // self.X
        self.sizes = {"s": self.S, "x": self.X, "y": self.Y, "r": self.R, "i": self.I}
        self.streams = []
        self.rooms = [0] * 4
        for (base, size, _), order in zip(self.segments, ("sxyi", "syxi", "sxyi", "sri", "sri")):
            self.streams.append((base, size, order, tuple(self.rooms)))
            for level, axis in enumerate(order):
                self.rooms[level] += size
                size //= self.sizes[axis]

    def piece(self, stream, level):
        _, size, order, _ = self.streams[stream]
        for axis in order[: level + 1]:
            size //= self.sizes[axis]
        return size


def main_kernel(plan, names, *refs):
    ref = dict(zip(names, refs))
    S, I, R = plan.S, plan.I, plan.R
    side, width, pix, cin = plan.side, plan.width, plan.pix, plan.cin
    half_width = width // 2
    s, i, r = lax.axis_index("section"), lax.axis_index("img"), lax.axis_index("row")
    mine = s * plan.each + r // plan.copies
    waits = []

    barrier = pltpu.get_barrier_semaphore()
    peers = []
    for ds in range(S):
        for dr in range(R):
            if ds or dr:
                peers.append((lax.rem(s + ds, S), i, lax.rem(r + dr, R)))
    for di in range(1, I):
        peers.append((s, lax.rem(i + di, I), r))
    for peer in peers:
        pl.semaphore_signal(barrier, inc=1, device_id=peer, device_id_type=MESH)

    own = []
    loads = {}

    def load(*which):
        for name in which:
            at = (NAMES + WEIGHTS).index(name)
            loads[name] = pltpu.make_async_copy(ref[name], ref[name + "_v"], ref["loads"].at[at])
            loads[name].start(priority=int(name[0] == "k"))

    def need(name):
        if name in loads:
            loads.pop(name).wait()
        return ref[name + "_v"]

    load("w1", "g1", "b1", "k1", "k2")
    for name, rows in (("x", plan.rows), ("og", plan.hrows)):
        copy = pltpu.make_async_copy(
            ref[name].at[mine, 0],
            ref[name + "_in"].at[pl.ds(r * rows, rows)],
            ref[name + "_r"].at[r],
        )
        copy.start()
        own.append(copy)
    pl.semaphore_wait(barrier, len(peers))
    for name, rows in (("x", plan.rows), ("og", plan.hrows)):
        for d in range(1, R):
            t = lax.rem(r + d, R)
            copy = pltpu.make_async_remote_copy(
                src_ref=ref[name].at[s * plan.each + t // plan.copies, 0],
                dst_ref=ref[name + "_in"].at[pl.ds(r * rows, rows)],
                send_sem=ref[name + "_s"].at[d - 1],
                recv_sem=ref[name + "_r"].at[r],
                device_id=(s, i, t),
                device_id_type=MESH,
            )
            copy.start()
            waits.append(copy.wait_send)

    load("s1", *NAMES[2:], "sq1", "ex1", "e1", "w2", "sq2", "ex2", "e2")

    def arrived(name, rows, position, d):
        if d == 0:
            own[position].wait()
        else:
            t = lax.rem(r + d, R)
            there = ref[name + "_in"].at[pl.ds(t * rows, rows)]
            pltpu.make_async_remote_copy(
                src_ref=there,
                dst_ref=there,
                send_sem=ref[name + "_s"].at[d - 1],
                recv_sem=ref[name + "_r"].at[t],
                device_id=(s, i, t),
                device_id_type=MESH,
            ).wait_recv()

    st = ref["st"]

    def pairs_of(k):
        return 2 if k in (0, 1, 9) else 1

    def stats_copy(k, d, slot):
        return pltpu.make_async_remote_copy(
            src_ref=st.at[k, slot, pl.ds(0, pairs_of(k))],
            dst_ref=st.at[k, slot, pl.ds(0, pairs_of(k))],
            send_sem=ref["st_s"].at[k, d - 1],
            recv_sem=ref["st_r"].at[k, slot],
            device_id=(s, lax.rem(i + d, I), r),
            device_id_type=MESH,
        )

    def post(k, rows):
        ids = lax.broadcasted_iota(jnp.int32, (8, 128), 0)
        rows = [*rows, *([None] * (len(rows) % 2))]
        for pair in range(len(rows) // 2):
            value = jnp.zeros((8, 128), f32)
            for j in range(8):
                row = rows[2 * pair + j // 4]
                if row is not None:
                    piece = row[:, 128 * (j % 4) : 128 * (j % 4) + 128]
                    value = jnp.where(ids == j, jnp.broadcast_to(piece, (8, 128)), value)
            st[k, i, pair] = value
        for d in range(1, I):
            stats_copy(k, d, i).start()

    def fetch(k, count=2):
        for d in range(1, I):
            stats_copy(k, d, i).wait_send()
            stats_copy(k, d, lax.rem(i + d, I)).wait_recv()
        out = []
        for pair in range((count + 1) // 2):
            value = st[k, 0, pair]
            for j in range(1, I):
                value = value + st[k, j, pair]
            for half in range(2):
                out.append(
                    jnp.concatenate(
                        [
                            jnp.broadcast_to(value[4 * half + j : 4 * half + j + 1], (8, 128))
                            for j in range(4)
                        ],
                        axis=1,
                    )
                )
        return out

    vec = ref["vec"]

    def keep_vectors():
        for name in NAMES:
            row = need(name)[...].astype(f32)
            size = row.shape[0]
            vec[VEC[name], :, :size] = jnp.broadcast_to(row.reshape(1, size), (8, size))

    def vector(name):
        return vec[VEC[name]]

    vr, vc = ref["vr"][0, mine], ref["vc"][0, mine]
    q_ids = lax.broadcasted_iota(jnp.int32, (side, width), 0)
    first_col, last_col = q_ids == 0, q_ids == side - 1
    cm = ref["cm"]
    for b in range(2):
        cm[b] = (2 * q_ids + b < vc).astype(f32)

    def line(value):
        return value.astype(f32).reshape(2, 8, width)

    def pixels(value):
        return value.reshape(side, width)

    def mask_row(a, b, p):
        return line(cm[b]) * (2 * p + a < vr).astype(f32)

    def wide(row):
        return jnp.broadcast_to(row, (8, width))

    row_count = jnp.full((1, width), vr * vc, jnp.int32).astype(f32)
    half_count = jnp.full((1, width), ((vr + 1) // 2) * ((vc + 1) // 2), jnp.int32).astype(f32)

    def over_rows(step, *accs):
        init = tuple(jnp.zeros((8, width), f32) for _ in range(accs[0] if accs else 0))

        def run(p, carry):
            out = step(p)
            if not carry:
                return carry
            return tuple(c + fold(o) for c, o in zip(carry, out))

        return tuple(column(c) for c in lax.fori_loop(0, side, run, init, unroll=16))

    def full_dot(out, left, weight, form=dot):
        wide = out.shape[-1]
        step = min(256, wide)
        for h in range(wide // step):
            cut = slice(h * step, h * step + step)
            w = weight[:, cut] if form is dot else weight[cut, :]
            out[:, :, cut] = form(left, w).reshape(side, side, step).astype(out.dtype)

    hm = ref["hm"]
    for p in range(side):
        hm[p * side : (p + 1) * side] = cm[0][:, :128] * (2 * p < vr).astype(f32)

    def with_moments(out, products):
        sums = []
        for h, product in enumerate(products):
            span = product.shape[1]
            value = product.astype(out.dtype)
            out[:, :, h * span : (h + 1) * span] = value.reshape(side, side, span)
            value = value.astype(f32)
            valid = value * jnp.concatenate([hm[...]] * (span // 128), axis=1)
            sums.append(
                [
                    jnp.sum(x.reshape(pix // 8, 8, span), axis=0)
                    for x in (valid, valid * value)
                ]
            )
        return [column(jnp.concatenate(x, axis=1)) for x in zip(*sums)]

    def dot_moments(out, left, weight):
        return with_moments(
            out, (dot(left, weight[:, cut : cut + 256]) for cut in range(0, width, 256))
        )

    def flat(value):
        return value.reshape(pix, value.shape[-1])

    def lines(ref_, start=0):
        return flat(ref_[start : start + side])

    G, F = ref["local"], ref["grads"]
    lead = None if plan.copies == 1 else (lax.rem(r, plan.copies) == 0).astype(f32)

    def put(name, value, row=0, lane=0):
        if lead is not None:
            value = value * lead
        start, per_tile = plan.starts[name]
        count = value.shape[0] // 16
        for k in range(value.shape[1] // 128):
            piece = value[:, 128 * k : 128 * k + 128].astype(bf16).reshape(count, 16, 128)
            at = start + (lane // 128 + k) * per_tile + row // 16
            G[at : at + count] = piece

    X, Y = plan.X, plan.Y
    x, y = lax.rem(r, X), r // X
    axes = {
        "s": (S, s, lambda t: (t, i, r)),
        "r": (R, r, lambda t: (s, i, t)),
        "x": (X, x, lambda t: (s, i, y * X + t)),
        "y": (Y, y, lambda t: (s, i, t * X + x)),
        "i": (I, i, lambda t: (s, t, r)),
    }

    def scatter_source(stream, level):
        base, _, order, offsets = plan.streams[stream]
        if level == 0:
            return G, base
        return ref[f"sum{level - 1}"], offsets[level]

    def scatter_copies(stream, level, outgoing):
        base, size, order, offsets = plan.streams[stream]
        count, me, device = axes[order[level]]
        piece = plan.piece(stream, level)
        source, first = scatter_source(stream, level)
        for d in range(1, count):
            t = lax.rem(me + d, count)
            slot = me if outgoing else t
            copy = pltpu.make_async_remote_copy(
                src_ref=source.at[pl.ds(first + t * piece, piece)],
                dst_ref=ref[f"got{level}"].at[pl.ds(offsets[level] + slot * piece, piece)],
                send_sem=ref["rs_s"].at[stream, level, d - 1],
                recv_sem=ref["rs_r"].at[stream, level, slot],
                device_id=device(t),
                device_id_type=MESH,
            )
            if outgoing:
                copy.start()
                sent[stream].append(copy)
            else:
                copy.wait_recv()

    def add_up(stream, level):
        base, size, order, offsets = plan.streams[stream]
        count, me, _ = axes[order[level]]
        piece = plan.piece(stream, level)
        source, first = scatter_source(stream, level)
        got = ref[f"got{level}"]
        if level < len(order) - 1:
            out, at = ref[f"sum{level}"], offsets[level + 1]
        else:
            out, at = F, own_part(stream, len(order))
        step = next(k for k in (16, 12, 10, 9, 8, 7, 6, 5, 4, 3, 2, 1) if piece % k == 0)

        def run(k, carry):
            total = source[pl.ds(first + me * piece + k * step, step)].astype(f32)
            for d in range(1, count):
                t = lax.rem(me + d, count)
                total = total + got[pl.ds(offsets[level] + t * piece + k * step, step)].astype(f32)
            out[pl.ds(at + k * step, step)] = total.astype(bf16)
            return carry

        lax.fori_loop(0, piece // step, run, 0)

    def own_part(stream, depth):
        at, _, order, _ = plan.streams[stream]
        for level in range(depth):
            at = at + axes[order[level]][1] * plan.piece(stream, level)
        return at

    def gather_copies(stream, level, outgoing):
        count, me, device = axes[plan.streams[stream][2][level]]
        base = own_part(stream, level)
        piece = plan.piece(stream, level)
        for d in range(1, count):
            t = lax.rem(me + d, count)
            slot = me if outgoing else t
            there = F.at[pl.ds(base + slot * piece, piece)]
            copy = pltpu.make_async_remote_copy(
                src_ref=there,
                dst_ref=there,
                send_sem=ref["ag_s"].at[stream, level, d - 1],
                recv_sem=ref["ag_r"].at[stream, level, slot],
                device_id=device(t),
                device_id_type=MESH,
            )
            if outgoing:
                copy.start()
                sent[stream].append(copy)
            else:
                copy.wait_recv()

    done = [0] * len(plan.segments)
    started = []
    sent = [[] for _ in plan.segments]

    def pump(*which):
        for g in which or tuple(started):
            if g not in started:
                started.insert(0, g)
            k = done[g]
            depth = len(plan.streams[g][2])
            if k > 2 * depth:
                continue
            done[g] += 1
            if k == 0:
                base, size, used = plan.segments[g]
                if used < base + size:
                    G[used : base + size] = jnp.zeros((base + size - used, 16, 128), bf16)
            if 1 <= k <= depth:
                scatter_copies(g, k - 1, False)
                add_up(g, k - 1)
            elif k > depth:
                gather_copies(g, 2 * depth - k, False)
            for copy in sent[g]:
                copy.wait_send()
            sent[g] = []
            if k < depth:
                scatter_copies(g, k, True)
            elif k < 2 * depth:
                gather_copies(g, 2 * depth - 1 - k, True)

    vec_grads = {}

    gw = plan.gw
    span = 4 * gw
    def blocks(name, out, turned=False):
        kernels = need(name)
        shape = (span, gw) if turned else (gw, span)
        long = lax.broadcasted_iota(jnp.int32, shape, 0 if turned else 1)
        short = lax.broadcasted_iota(jnp.int32, shape, 1 if turned else 0)
        spread = (lax.rem(long, gw) == short).astype(f32).astype(bf16)
        row = lax.broadcasted_iota(jnp.int32, (span, span), 0) // gw
        col = lax.broadcasted_iota(jnp.int32, (span, span), 1) // gw
        for k, t in enumerate(ORDER):
            for h in range(width // span):
                piece = kernels[t, 4 * h : 4 * h + 4].reshape(span, gw)
                full = dot_nt(spread, piece) if turned else dot(piece, spread)
                out[h, k * span : (k + 1) * span] = jnp.where(row == col, full, 0.0).astype(bf16)

    def groups_grad(name, taps, turned):
        lane = lax.broadcasted_iota(jnp.int32, (gw, span), 1) // gw
        for t, (var, start) in enumerate(taps):
            for h in range(width // span):
                cut = slice(h * span, (h + 1) * span)
                res = dot(turned[h], flat(var[start : start + side, :, cut]))
                out = res[0:gw]
                for j in range(1, 4):
                    out = jnp.where(lane == j, res[j * gw : (j + 1) * gw], out)
                put(name, out, t * gw, h * span)

    band, bands = plan.band, plan.bands
    bhalf = band // 2
    out_id = lax.broadcasted_iota(jnp.int32, (pix, pix), 0)
    in_id = lax.broadcasted_iota(jnp.int32, (pix, pix), 1)

    def source(o):
        quarter = o // (bhalf * side)
        down = lax.rem(o, bhalf * side) // side
        return (2 * down + quarter // 2) * plan.cols + 2 * lax.rem(o, side) + lax.rem(quarter, 2)

    ref["sort"][...] = (source(out_id) == in_id).astype(f32).astype(bf16)
    ref["unsort"][...] = (source(in_id) == out_id).astype(f32).astype(bf16)

    xp, R1 = ref["xp"], ref["R1"]
    keep_vectors()

    def transpose(source, out):
        out[...] = source.astype(f32).T.astype(bf16)

    totals = [jnp.zeros((8, width), f32)] * 2
    by_band = plan.rows % band == 0
    if not by_band:
        for d in range(R):
            arrived("x", plan.rows, 0, d)
    for d in range(bands):
        if by_band:
            if d % (plan.rows // band) == 0:
                arrived("x", plan.rows, 0, d // (plan.rows // band))
            k = lax.rem(r * (plan.rows // band) + d, bands)
        else:
            k = d
        block = ref["x_in"][pl.ds(k * band, band)].reshape(pix, cin)
        block = dot(ref["sort"][...], block).astype(bf16)
        xp[k] = block.reshape(4 * bhalf, side, cin)
        full_dot(R1.at[k], block, need("w1"))
        for j in range(4 * bhalf):
            a, b = PHASES[j // bhalf]
            v = line(R1[k, j])
            mv = v * mask_row(a, b, k * bhalf + j % bhalf)
            totals = [totals[0] + fold(mv), totals[1] + fold(mv * v)]
    even = xp.at[:, 0:bhalf]

    def at_phase(ab, p):
        return p // bhalf, ab * bhalf + lax.rem(p, bhalf)

    post(0, [column(totals[0]), column(totals[1]), row_count, half_count])
    SC = ref["SC"]
    short_sums = dot_moments(SC, even[...].reshape(pix, cin), need("s1"))

    for k in range(bands):
        transpose(xp[k].reshape(pix, cin), ref["xpt"].at[k])
    blocks("k1", ref["bd1"])

    def coefficients(first, second, inverse, gain, shift):
        mean = first * inverse
        scale = lax.rsqrt(second * inverse - mean * mean + epsilon)
        a = scale * gain
        return a, shift - mean * a, scale, -mean * scale

    tot = fetch(0, 4)
    inv_full, inv_half = 1.0 / tot[2], 1.0 / tot[3]
    n1 = coefficients(tot[0], tot[1], inv_full, vector("g1"), vector("b1"))

    va = ref["va"]
    va[3:6, 0:1] = jnp.zeros((3, 1, side, width), bf16)

    def shifted(v, edge, amount):
        return jnp.where(edge, 0.0, pltpu.roll(v, amount, 0))

    for ab, (a, b) in enumerate(PHASES):

        def step(p, ab=ab, a=a, b=b):
            v = mask_row(a, b, p) * silu(line(R1[at_phase(ab, p)]) * n1[0] + n1[1])
            v = pixels(v)
            slot = (0, 1, 3, 4)[ab]
            va[slot, p + a] = v.astype(bf16)
            if b:
                va[slot + 1, p + a] = shifted(v, first_col, 1).astype(bf16)

        over_rows(step)
    taps1 = []
    for t in range(9):
        u, v = t // 3, t % 3
        slot = (0, 1, 3, 4)[2 * (u != 1) + (v != 1)] + (v == 0)
        taps1.append((va.at[slot], 1 if u == 2 else 0))

    def convolve(taps, weights, out):
        def half(h):
            cut = slice(h * span, (h + 1) * span)
            left = [flat(taps[t][0][taps[t][1] : taps[t][1] + side, :, cut]) for t in ORDER]
            return dot(jnp.concatenate(left, axis=1), weights[h])

        return with_moments(out, (half(h) for h in range(width // span)))

    c1 = ref["c1"]
    post(1, [*convolve(taps1, ref["bd1"], c1), *short_sums])
    blocks("k2", ref["bd2"])
    tot = fetch(1, 4)
    nc1 = coefficients(tot[0], tot[1], inv_half, vector("gg1"), vector("gb1"))
    ns = coefficients(tot[2], tot[3], inv_half, vector("sg1"), vector("sb1"))

    def excite(conv, norm, hidden, gated, sq, sq_form, sqb, ex, exb):
        def step(p):
            v = mask_row(0, 0, p) * silu(line(conv[p]) * norm[0] + norm[1])
            hidden[p] = pixels(v)
            return (v,)

        (total,) = over_rows(step, 1)
        pooled = total / half_count
        pre = small_dot(pooled, sq[...], sq_form) + sqb
        inner = silu(pre)
        gate = sigmoid(small_dot(inner, ex[...], dot) + exb)
        gate_wide = wide(gate)

        def step_two(p):
            gated[p] = pixels(line(hidden[p]) * gate_wide).astype(bf16)

        over_rows(step_two)
        return pooled, pre, inner, gate

    H1, ga1 = ref["H1"], ref["ga1"]
    kept1 = excite(
        c1, nc1, H1, ga1, need("sq1"), dot_nt, vec[VEC["sqb1"], 0:1, : plan.q1], need("ex1"), vec[VEC["exb1"], 0:1]
    )
    E1 = ref["E1"]
    post(2, dot_moments(E1, lines(ga1), need("e1")))
    transpose(lines(ga1), ref["ga1t"])
    blocks("k1", ref["bd1t"], True)
    tot = fetch(2)
    ne = coefficients(tot[0], tot[1], inv_half, vector("eg1"), vector("eb1"))
    ent = ref["ent"]
    both_shifts = ne[1] + ns[1]

    def step(p):
        v = line(E1[p]) * ne[0] + line(SC[p]) * ns[0] + both_shifts
        ent[p] = pixels(mask_row(0, 0, p) * silu(v)).astype(bf16)

    over_rows(step)

    def send_out(source, out, rows, target, steps=None):
        for k in range(R // plan.copies) if steps is None else steps:
            t = lax.rem(r + plan.copies * k, R)
            there = ref[out].at[0, mine, 0] if out == "act" else ref[out].at[mine, 0]
            here = source.at[pl.ds(t * rows, rows)]
            copy = pltpu.make_async_remote_copy(
                src_ref=here,
                dst_ref=there,
                send_sem=ref[out + "_s"].at[target, k],
                recv_sem=ref[out + "_r"].at[mine],
                device_id=(target, i, t),
                device_id_type=MESH,
            )
            if k:
                copy.start()
                waits.append(copy.wait_send)
            else:
                local = pltpu.make_async_copy(here, there, ref[out + "_r"].at[mine])

                @pl.when(s == target)
                def _():
                    local.start()

                @pl.when(s != target)
                def _():
                    copy.start()

                def finish(copy=copy):
                    @pl.when(s != target)
                    def _():
                        copy.wait_send()

                waits.append(finish)

    send_out(ent, "act", plan.hrows, 0)

    R2 = ref["R2"]
    post(3, dot_moments(R2, lines(ent), need("w2")))
    transpose(lines(ent), ref["entt"])
    tot = fetch(3)
    n2 = coefficients(tot[0], tot[1], inv_half, vector("g2"), vector("b2"))
    vb = ref["vb"]
    vb[:, 0:1] = jnp.zeros((3, 1, side, width), bf16)
    vb[:, side + 1 :] = jnp.zeros((3, 1, side, width), bf16)

    def three(out, p, v):
        out[0, p + 1] = shifted(v, first_col, 1).astype(bf16)
        out[1, p + 1] = v.astype(bf16)
        out[2, p + 1] = shifted(v, last_col, side - 1).astype(bf16)

    def step(p):
        three(vb, p, pixels(mask_row(0, 0, p) * silu(line(R2[p]) * n2[0] + n2[1])))

    over_rows(step)
    taps2 = [(vb.at[t % 3], t // 3) for t in range(9)]
    c2 = ref["c2"]
    post(4, convolve(taps2, ref["bd2"], c2))
    blocks("k2", ref["bd2t"], True)
    tot = fetch(4)
    nc2 = coefficients(tot[0], tot[1], inv_half, vector("gg2"), vector("gb2"))
    H2, ga2 = ref["H2"], ref["ga2"]
    kept2 = excite(
        c2, nc2, H2, ga2, need("sq2"), dot, vec[VEC["sqb2"], 0:1, : plan.q2], need("ex2"), vec[VEC["exb2"], 0:1]
    )
    E2 = ref["E2"]
    post(5, dot_moments(E2, lines(ga2), need("e2")))
    transpose(lines(ga2), ref["ga2t"])
    for d in range(R):
        arrived("og", plan.hrows, 1, d)
    tot = fetch(5)
    ne2 = coefficients(tot[0], tot[1], inv_half, vector("eg2"), vector("eb2"))
    leave, D, og = ref["leave"], ref["D"], ref["og_in"]

    def step(p):
        e = line(E2[p])
        v = e * ne2[0] + ne2[1] + line(ent[p])
        sg = sigmoid(v)
        m = mask_row(0, 0, p)
        leave[p] = pixels(m * v * sg).astype(bf16)
        g = line(og[p]) * m * (sg * (1.0 + v * (1.0 - sg)))
        D[p] = pixels(g)
        return g, g * (e * ne2[2] + ne2[3])

    parts = over_rows(step, 2)
    vec_grads["eb2"], vec_grads["eg2"] = parts
    post(6, parts)
    send_out(leave, "act", plan.hrows, 1)

    def back_rule(sums, inverse, gain, norm):
        a = gain * norm[2]
        k0 = a * (sums[0] + norm[3] * sums[1]) * inverse
        return a, k0, a * norm[2] * sums[1] * inverse

    def back_excite(dg, kept, hidden, conv, norm, sq, sq_form, ex, out):
        pooled, pre, inner, gate = kept

        def step(p):
            return (line(dg[p]) * line(hidden[p]),)

        (dgate,) = over_rows(step, 1)
        dpre = dgate * gate * (1.0 - gate)
        dsq = small_dot(dpre, ex[...], dot_nt) * slope(pre)
        dpool = wide(small_dot(dsq, sq[...], sq_form) / half_count)
        gate_wide = wide(gate)

        def step_two(p):
            v = line(conv[p])
            g = (line(dg[p]) * gate_wide + dpool) * mask_row(0, 0, p)
            g = g * slope(v * norm[0] + norm[1])
            out[p] = pixels(g)
            return g, g * (v * norm[2] + norm[3])

        return over_rows(step_two, 2), dpre, dsq

    def excite_grads(name, kept, dpre, dsq):
        pooled, pre, inner, gate = kept
        put("sq" + name, small_outer(dsq, pooled))
        put("ex" + name, small_outer(inner, dpre))
        vec_grads["exb" + name] = dpre
        count = dsq.shape[1]
        eye = (
            lax.broadcasted_iota(jnp.int32, (count, width), 0)
            == lax.broadcasted_iota(jnp.int32, (count, width), 1)
        ).astype(f32).astype(bf16)
        vec_grads["sqb" + name] = small_dot(dsq, eye, dot)

    def turn(gradient_ref, start):
        out = []
        for h in range(width // span):
            piece = flat(gradient_ref[start : start + side, :, h * span : (h + 1) * span])
            out.append(piece.astype(f32).T.astype(bf16))
        return out

    d1, dg, GR = ref["d1"], ref["dg"], ref["GR"]
    tot = fetch(6)
    rule = back_rule((tot[0], tot[1]), inv_half, vector("eg2"), ne2)

    def step(p):
        v = rule[0] * line(D[p]) - mask_row(0, 0, p) * (rule[1] + rule[2] * line(E2[p]))
        d1[p] = pixels(v).astype(bf16)

    over_rows(step)
    full_dot(dg, lines(d1), need("e2"), dot_nt)
    parts, dpre, dsq = back_excite(dg, kept2, H2, c2, nc2, need("sq2"), dot_nt, need("ex2"), GR)
    vec_grads["gb2"], vec_grads["gg2"] = parts
    post(7, parts)
    put("e2", dot(ref["ga2t"][...], lines(d1)))
    excite_grads("2", kept2, dpre, dsq)
    pump(0)
    tot = fetch(7)
    rule = back_rule((tot[0], tot[1]), inv_half, vector("gg2"), nc2)
    vd = ref["vd"]
    vd[:, 0:1] = jnp.zeros((3, 1, side, width), bf16)
    vd[:, side + 1 :] = jnp.zeros((3, 1, side, width), bf16)

    def step(p):
        v = rule[0] * line(GR[p]) - mask_row(0, 0, p) * (rule[1] + rule[2] * line(c2[p]))
        three(vd, p, pixels(v))

    over_rows(step)

    def convolve_back(taps, first, weights, out):
        for h in range(width // span):
            cut = slice(h * span, (h + 1) * span)
            left = [flat(var[start : start + side, :, cut]) for var, start in taps]
            rows = slice(first * span, (first + len(taps)) * span)
            acc = dot(jnp.concatenate(left, axis=1), weights[h, rows])
            out[:, :, cut] = acc.reshape(side, side, span)

    DA = ref["DA"]
    convolve_back(
        [(vd.at[2 - t % 3], 2 - t // 3) for t in ORDER],
        0,
        ref["bd2t"],
        DA.at[0],
    )

    def step(p):
        v = line(R2[p])
        g = line(DA[0, p]) * mask_row(0, 0, p) * slope(v * n2[0] + n2[1])
        GR[p] = pixels(g)
        return g, g * (v * n2[2] + n2[3])

    parts = over_rows(step, 2)
    vec_grads["b2"], vec_grads["g2"] = parts
    post(8, parts)
    pump()
    groups_grad("k2", taps2, turn(vd.at[1], 1))
    pump()
    tot = fetch(8)
    rule = back_rule((tot[0], tot[1]), inv_half, vector("g2"), n2)

    def step(p):
        v = rule[0] * line(GR[p]) - mask_row(0, 0, p) * (rule[1] + rule[2] * line(R2[p]))
        d1[p] = pixels(v).astype(bf16)

    over_rows(step)
    full_dot(GR, lines(d1), need("w2"), dot_nt)

    def step(p):
        e, sc = line(E1[p]), line(SC[p])
        g = line((D[p] + GR[p]).astype(bf16))
        g = g * mask_row(0, 0, p) * slope(e * ne[0] + sc * ns[0] + both_shifts)
        D[p] = pixels(g)
        return g, g * (e * ne[2] + ne[3]), g * (sc * ns[2] + ns[3])

    parts = over_rows(step, 3)
    vec_grads["eb1"], vec_grads["eg1"], vec_grads["sg1"] = parts
    vec_grads["sb1"] = parts[0]
    post(9, parts)
    pump()
    put("w2", dot(ref["entt"][...], lines(d1)))
    pump(1)
    tot = fetch(9, 3)
    rule_e = back_rule((tot[0], tot[1]), inv_half, vector("eg1"), ne)
    rule_s = back_rule((tot[0], tot[2]), inv_half, vector("sg1"), ns)
    d2 = ref["d2"]

    def step(p):
        g, m = line(D[p]), mask_row(0, 0, p)
        v = rule_e[0] * g - m * (rule_e[1] + rule_e[2] * line(E1[p]))
        d1[p] = pixels(v).astype(bf16)
        v = rule_s[0] * g - m * (rule_s[1] + rule_s[2] * line(SC[p]))
        d2[p] = pixels(v).astype(bf16)

    over_rows(step)
    full_dot(dg, lines(d1), need("e1"), dot_nt)
    parts, dpre, dsq = back_excite(dg, kept1, H1, c1, nc1, need("sq1"), dot, need("ex1"), GR)
    vec_grads["gb1"], vec_grads["gg1"] = parts
    post(10, parts)
    pump()
    put("e1", dot(ref["ga1t"][...], lines(d1)))
    put("s1", dot_tn(even[...].reshape(pix, cin), lines(d2)))
    excite_grads("1", kept1, dpre, dsq)
    pump(2)
    tot = fetch(10)
    rule = back_rule((tot[0], tot[1]), inv_half, vector("gg1"), nc1)

    def step(p):
        v = rule[0] * line(GR[p]) - mask_row(0, 0, p) * (rule[1] + rule[2] * line(c1[p]))
        three(vd, p, pixels(v))

    over_rows(step)
    sums = []
    for ab, (a, b) in enumerate(PHASES):
        chosen = []
        first = (0, 1, 3, 5)[ab]
        for t in ORDER[first : first + (1, 2, 2, 4)[ab]]:
            chosen.append((vd.at[2 if t % 3 == 0 else 1], 2 if t // 3 == 0 else 1))
        convolve_back(chosen, first, ref["bd1t"], DA.at[ab])

        def step(p, ab=ab, a=a, b=b):
            v = line(R1[at_phase(ab, p)])
            g = line(DA[ab, p]) * mask_row(a, b, p) * slope(v * n1[0] + n1[1])
            DA[ab, p] = pixels(g)
            return g, g * (v * n1[2] + n1[3])

        sums.append(over_rows(step, 2))
    parts = (sum(x[0] for x in sums), sum(x[1] for x in sums))
    vec_grads["b1"], vec_grads["g1"] = parts
    post(11, parts)
    pump()
    groups_grad("k1", taps1, turn(vd.at[1], 1))
    ids = lax.broadcasted_iota(jnp.int32, (VEC_ROWS, width), 0)
    value = jnp.zeros((VEC_ROWS, width), f32)
    for name, at in VEC.items():
        value = jnp.where(ids == at, jnp.broadcast_to(vec_grads[name], value.shape), value)
    put(VECTORS, value)
    pump(3)
    pump(1, 0)
    tot = fetch(11)
    rule = back_rule((tot[0], tot[1]), inv_full, vector("g1"), n1)
    dr = ref["dr"]
    for ab, (a, b) in enumerate(PHASES):

        def step(p, ab=ab, a=a, b=b):
            v = rule[0] * line(DA[ab, p])
            v = v - mask_row(a, b, p) * (rule[1] + rule[2] * line(R1[at_phase(ab, p)]))
            dr[at_phase(ab, p)] = pixels(v).astype(bf16)

        over_rows(step)
    total = None
    for k in range(bands):
        term = dot(ref["xpt"][k], dr[k].reshape(pix, width))
        total = term if total is None else total + term
    put("w1", total)
    pump(4)
    pump(3, 2, 1, 0)
    cut = cin // 2
    ref["dxo0"][...] = jnp.zeros((2 * side, plan.cols, 128), bf16)
    ref["dxo1"][...] = jnp.zeros((2 * side, plan.cols, 128), bf16)
    stepwise = plan.each == bands
    for d in [*range(1, bands), 0]:
        k = lax.rem(r + plan.copies * d, R) * plan.rows // band if stepwise else d
        for part in range(2):
            dxo = ref[f"dxo{part}"]
            rows = slice(part * cut, (part + 1) * cut)
            v = dot_nt(dr[k].reshape(pix, width), need("w1")[rows, :])
            w = dot_nt(
                d2[pl.ds(k * bhalf, bhalf)].reshape(bhalf * side, width), need("s1")[rows, :]
            )
            v = jnp.concatenate([v[: bhalf * side] + w, v[bhalf * side :]], axis=0)
            v = dot(ref["unsort"][...], v.astype(bf16)).astype(bf16)
            dxo[pl.ds(k * band, band), :, :cut] = v.reshape(band, plan.cols, cut)
            if stepwise:
                send_out(dxo, "dx", plan.rows, part, (d,))
        pump()
    if not stepwise:
        send_out(ref["dxo0"], "dx", plan.rows, 0)
        send_out(ref["dxo1"], "dx", plan.rows, 1)
    for _ in range(9):
        pump()
    for wait in waits:
        wait()
    for m in range(plan.M):
        t = (m % plan.each) * plan.copies + lax.rem(r, plan.copies)
        for out in ("act", "dx"):
            there = ref[out].at[0, m, 0] if out == "act" else ref[out].at[m, 0]
            pltpu.make_async_copy(there, there, ref[out + "_r"].at[m]).wait()


WEIGHTS = ("w1", "k1", "k2", "sq1", "ex1", "e1", "s1", "w2", "sq2", "ex2", "e2")


def run_main(plan, arrays):
    side, width, cin = plan.side, plan.width, plan.cin
    wide = 4 * plan.gw
    field = (side, side, width)
    scratch = {
        "x_in": pltpu.VMEM((2 * side, plan.cols, cin), bf16),
        "og_in": pltpu.VMEM(field, bf16),
        "st": pltpu.VMEM((EXCHANGES, plan.I, 2, 8, 128), f32),
        "hm": pltpu.VMEM((plan.pix, 128), f32),
        "cm": pltpu.VMEM((2, side, width), f32),
        **{
            name: pltpu.VMEM((width // wide, plan.taps * wide, wide), bf16)
            for name in ("bd1", "bd2", "bd1t", "bd2t")
        },
        "xpt": pltpu.VMEM((plan.bands, cin, plan.pix), bf16),
        **{name: pltpu.VMEM((width, plan.pix), bf16) for name in ("ga1t", "ga2t", "entt")},
        "sort": pltpu.VMEM((plan.pix, plan.pix), bf16),
        "unsort": pltpu.VMEM((plan.pix, plan.pix), bf16),
        "xp": pltpu.VMEM((plan.bands, 2 * plan.band, side, cin), bf16),
        "R1": pltpu.VMEM((plan.bands, 2 * plan.band, side, width), f32),
        "va": pltpu.VMEM((6, side + 1, side, width), bf16),
        "vb": pltpu.VMEM((3, side + 2, side, width), bf16),
        "vd": pltpu.VMEM((3, side + 2, side, width), bf16),
        "DA": pltpu.VMEM((4,) + field, f32),
        "dr": pltpu.VMEM((plan.bands, 2 * plan.band, side, width), bf16),
        "dxo0": pltpu.VMEM((2 * side, plan.cols, 128), bf16),
        "dxo1": pltpu.VMEM((2 * side, plan.cols, 128), bf16),
    }
    for name in ("SC", "H1", "E1", "R2", "H2", "E2", "D", "GR"):
        scratch[name] = pltpu.VMEM(field, f32)
    for name in ("c1", "ga1", "ent", "c2", "ga2", "leave", "d1", "d2", "dg"):
        scratch[name] = pltpu.VMEM(field, bf16)
    for name in ("x", "og"):
        scratch[name + "_s"] = pltpu.SemaphoreType.DMA((max(plan.R - 1, 1),))
        scratch[name + "_r"] = pltpu.SemaphoreType.DMA((plan.R,))
    scratch["st_s"] = pltpu.SemaphoreType.DMA((EXCHANGES, max(plan.I - 1, 1)))
    scratch["st_r"] = pltpu.SemaphoreType.DMA((EXCHANGES, plan.I))
    for name in ("act", "dx"):
        scratch[name + "_s"] = pltpu.SemaphoreType.DMA((2, plan.R // plan.copies))
        scratch[name + "_r"] = pltpu.SemaphoreType.DMA((plan.M,))
    for name in NAMES + WEIGHTS:
        scratch[name + "_v"] = pltpu.VMEM(arrays[name].shape, bf16)
    scratch["vec"] = pltpu.VMEM((len(NAMES), 8, width), f32)
    scratch["loads"] = pltpu.SemaphoreType.DMA((len(NAMES + WEIGHTS),))
    scratch["local"] = pltpu.VMEM((plan.blocks, 16, 128), bf16)
    for level, room in enumerate(plan.rooms):
        scratch[f"got{level}"] = pltpu.VMEM((room, 16, 128), bf16)
        if level:
            scratch[f"sum{level - 1}"] = pltpu.VMEM((room, 16, 128), bf16)
    most = max(plan.sizes.values())
    for name in ("rs", "ag"):
        scratch[name + "_s"] = pltpu.SemaphoreType.DMA((len(plan.streams), 4, most - 1))
        scratch[name + "_r"] = pltpu.SemaphoreType.DMA((len(plan.streams), 4, most))
    inputs = ("x", "og", "vr", "vc") + NAMES + WEIGHTS
    outputs = ("act", "dx", "grads")
    names = inputs + outputs + tuple(scratch)
    any_space = pl.BlockSpec(memory_space=pl.ANY)
    smem = pl.BlockSpec(memory_space=pltpu.SMEM)
    vmem = pl.BlockSpec(memory_space=pltpu.VMEM)
    return pl.pallas_call(
        functools.partial(main_kernel, plan, names),
        out_shape=(
            jax.ShapeDtypeStruct((1, plan.M, 1, plan.hrows, side, width), bf16),
            jax.ShapeDtypeStruct((plan.M, 1, plan.rows, plan.cols, 128), bf16),
            jax.ShapeDtypeStruct((plan.blocks, 16, 128), bf16),
        ),
        in_specs=[any_space, any_space, smem, smem] + [any_space] * (len(NAMES) + len(WEIGHTS)),
        out_specs=(any_space, any_space, vmem),
        scratch_shapes=list(scratch.values()),
        compiler_params=pltpu.CompilerParams(
            collective_id=0, has_side_effects=True, vmem_limit_bytes=60 * 1024 * 1024
        ),
        name="blocks",
    )(*[arrays[name] for name in inputs])


OUTS = (
    "w1", "g1", "b1", "k1", "gg1", "gb1", "sq1", "sqb1", "ex1", "exb1", "e1", "eg1", "eb1",
    "s1", "sg1", "sb1", "w2", "g2", "b2", "k2", "gg2", "gb2", "sq2", "sqb2", "ex2", "exb2",
    "e2", "eg2", "eb2",
)


def unpack_kernel(plan, source, *rest):
    count = len(OUTS)
    outs, bufs, loads_at, sems = rest[:count], rest[count:-3], rest[-3:-1], rest[-1]
    copies = []
    loads = []
    order = sorted(plan.starts, key=lambda name: plan.starts[name])
    order = [name for name in order if name != VECTORS] + [VECTORS]
    blocks = loads_at[0]
    for k, name in enumerate(order):
        start, per_tile = plan.starts[name]
        part = pl.ds(start, per_tile * (plan.width // 128))
        loads.append(pltpu.make_async_copy(source.at[part], blocks.at[part], loads_at[1].at[k]))
        loads[-1].start()

    def tile(name, k):
        start, per_tile = plan.starts[name]
        at = start + k * per_tile
        return blocks[at : at + per_tile].reshape(16 * per_tile, 128).astype(f32)

    tiles = plan.width // 128
    vec = None
    turn = [OUTS.index(name) for name in order if name != VECTORS]
    turn += [k for k, name in enumerate(OUTS) if name in VEC]
    for position, k in enumerate(turn):
        name, out = OUTS[k], bufs[k]
        if position < len(loads):
            loads[position].wait()
        if name in VEC and vec is None:
            vec = jnp.concatenate([tile(VECTORS, k) for k in range(tiles)], axis=1)
        if name in VEC:
            size = out.shape[0]
            out[...] = vec[VEC[name] : VEC[name] + 1, :size].reshape(size)
        elif name[0] == "k":

            def run(t, carry, name=name, out=out):
                for lane in range(tiles):
                    start, per_tile = plan.starts[name]
                    at = start + lane * per_tile + t * (plan.gw // 16)
                    piece = blocks[pl.ds(at, plan.gw // 16)].reshape(plan.gw, 128)
                    piece = piece.astype(f32).T
                    for j in range(128 // plan.gw):
                        group = lane * (128 // plan.gw) + j
                        out[t, group, :, : plan.gw] = piece[j * plan.gw : (j + 1) * plan.gw]
                return carry

            lax.fori_loop(0, plan.taps, run, 0)
        elif name == "sq2":
            for lane in range(tiles):
                out[128 * lane : 128 * lane + 128] = tile(name, lane).T
        else:
            for lane in range(tiles):
                out[:, 128 * lane : 128 * lane + 128] = tile(name, lane)
        copies.append(pltpu.make_async_copy(out, outs[k], sems.at[k]))
        copies[-1].start()
    for copy in copies:
        copy.wait()


def unpack(plan, grads, weights):
    shapes = []
    for name, w in zip(OUTS, weights):
        shape = w.shape[:3] + (128,) if name[0] == "k" else w.shape
        shapes.append(jax.ShapeDtypeStruct(shape, f32))
    any_space = pl.BlockSpec(memory_space=pl.ANY)
    return pl.pallas_call(
        functools.partial(unpack_kernel, plan),
        out_shape=shapes,
        in_specs=[any_space],
        out_specs=[any_space] * len(shapes),
        scratch_shapes=[pltpu.VMEM(v.shape, v.dtype) for v in shapes]
        + [pltpu.VMEM(grads.shape, bf16), pltpu.SemaphoreType.DMA((len(plan.starts),))]
        + [pltpu.SemaphoreType.DMA((len(shapes),))],
        compiler_params=pltpu.CompilerParams(vmem_limit_bytes=60 * 1024 * 1024),
        name="unpack",
    )(grads)


def body(sizes, input_maps, valid_rows, valid_cols, *rest):
    weights, output_grad = rest[:-1], rest[-1]
    (w1, g1, b1, k1, gg1, gb1, sq1, sqb1, ex1, exb1, e1, eg1, eb1, s1, sg1, sb1) = weights[:16]
    (w2, g2, b2, k2, gg2, gb2, sq2, sqb2, ex2, exb2, e2, eg2, eb2) = weights[16:]
    turned = sq1.T
    plan = Plan(sizes, [v.shape for v in (input_maps, output_grad, w1, k1, turned, sq2)])
    vectors = (
        g1, b1, gg1, gb1, exb1, eg1, eb1, sg1, sb1, sqb1, g2, b2, gg2, gb2, exb2, eg2, eb2, sqb2,
    )
    arrays = dict(
        x=input_maps, og=output_grad, vr=valid_rows.T, vc=valid_cols.T, w1=w1,
        k1=k1, k2=k2,
        sq1=turned, ex1=ex1, e1=e1, s1=s1, w2=w2, sq2=sq2, ex2=ex2, e2=e2,
        **dict(zip(NAMES, vectors)),
    )
    act, dx, grads = run_main(plan, arrays)
    out = list(unpack(plan, grads, weights[:6] + (turned,) + weights[7:]))
    out[6] = out[6].T
    for at in (3, 19):
        out[at] = out[at][..., : plan.gw]
    dx = dx[..., : plan.cin // 2]
    return (act, dx, *out)


def solution(mesh):
    tiled = P(None, "img", "row", None, None)
    image = P(None, "img")
    sizes = tuple(mesh.shape[name] for name in ("section", "img", "row"))
    return jax.shard_map(
        functools.partial(body, sizes),
        mesh=mesh,
        in_specs=(tiled, image, image) + (P(),) * 29 + (tiled,),
        out_specs=(
            P("section", None, "img", "row", None, None),
            P(None, "img", "row", None, "section"),
        )
        + (P(),) * 29,
        check_vma=False,
    )
```

```python
import functools

import jax
import jax.numpy as jnp
from jax import lax
from jax.experimental import pallas as pl
from jax.experimental.pallas import tpu as pltpu
from jax.sharding import PartitionSpec as P

epsilon = 1e-05
f32 = jnp.float32
bf16 = jnp.bfloat16
MESH = pl.DeviceIdType.MESH
PHASES = ((0, 0), (0, 1), (1, 0), (1, 1))
ORDER = (4, 3, 5, 1, 7, 0, 2, 6, 8)
EXCHANGES = 12
NAMES = (
    "g1", "b1", "gg1", "gb1", "exb1", "eg1", "eb1", "sg1", "sb1", "sqb1",
    "g2", "b2", "gg2", "gb2", "exb2", "eg2", "eb2", "sqb2",
)
VEC = {name: k for k, name in enumerate(NAMES)}
VEC_ROWS = 32
VECTORS = "vec"
LAST_TAP = "k9"


def segments_of(cin, width, taps, group, sq1, sq2, devices):
    layout = (
        (("e2", width), ("sq2", sq2), ("ex2", sq2)),
        (("k2", (taps - 1) * group), ("w2", width)),
        (("e1", width), ("s1", cin), ("sq1", sq1), ("ex1", sq1), (LAST_TAP, group)),
        (("k1", taps * group), (VECTORS, VEC_ROWS)),
        (("w1", cin),),
    )
    starts, segments, at = {}, [], 0
    for parts in layout:
        base = at
        for name, rows in parts:
            starts[name] = (at, rows // 16)
            at += rows // 16 * (width // 128)
        units = -(-(at - base) // devices)
        first = units // 2 * devices if len(segments) < len(layout) - 1 else 0
        segments.append((base, units * devices, at, first))
        at = base + units * devices
    return starts, tuple(segments), at


def sigmoid(v):
    return 0.5 * jnp.tanh(0.5 * v) + 0.5


def silu(v):
    return v * sigmoid(v)


def slope(v):
    s = sigmoid(v)
    return s * (1.0 + v * (1.0 - s))


def dot(left, right):
    return jnp.dot(left, right, preferred_element_type=f32)


def dot_nt(left, right):
    return lax.dot_general(left, right, (((1,), (1,)), ((), ())), preferred_element_type=f32)


def dot_tn(left, right):
    return lax.dot_general(left, right, (((0,), (0,)), ((), ())), preferred_element_type=f32)


def parts_of(v):
    high = v.astype(bf16).astype(f32)
    return high, v - high


def stacked(rows, width):
    ids = lax.broadcasted_iota(jnp.int32, (16, width), 0)
    total = jnp.zeros((16, width), f32)
    for k, row in enumerate(rows):
        total = jnp.where(ids == k, jnp.broadcast_to(row, (16, width)), total)
    return total.astype(bf16)


def small_dot(row, weight, form):
    out = form(stacked(parts_of(row), row.shape[1]), weight)
    return out[0:1] + out[1:2]


def small_outer(left, right):
    lh, ll = parts_of(left)
    rh, rl = parts_of(right)
    return dot_tn(
        stacked((lh, ll, lh, ll), left.shape[1]), stacked((rh, rh, rl, rl), right.shape[1])
    )


def fold(v):
    return v[0] + v[1]


def column(acc):
    return jnp.sum(acc, axis=0, keepdims=True)


class Plan:
    def __init__(self, mesh_sizes, args):
        self.S, self.I, self.R = mesh_sizes
        x, og, w1, k1, sq1, sq2 = args
        self.M, _, self.rows, self.cols, self.cin = x
        _, _, self.hrows, self.side, self.width = og
        self.taps, self.groups, self.gw, _ = k1
        self.q1, self.q2 = sq1[0], sq2[1]
        self.each = self.M // self.S
        self.copies = self.R // self.each
        self.pix = self.side * self.side
        self.band = self.pix // self.cols
        self.bands = 2 * self.side // self.band
        self.starts, self.segments, self.blocks = segments_of(
            self.cin, self.width, self.taps, self.gw, self.q1, self.q2, self.S * self.I * self.R
        )
        self.X = 1
        while self.X * self.X < self.R:
            self.X *= 2
        self.Y = self.R // self.X
        self.sizes = {"s": self.S, "x": self.X, "y": self.Y, "r": self.R, "i": self.I}
        self.streams = []
        self.members = []
        self.rooms = [0] * 4
        for base, size, _, first in self.segments:
            halves = [(base, first, "sxyi"), (base + first, size - first, "syxi")]
            if not first:
                halves = [(base, size, "sri")]
            self.members.append(range(len(self.streams), len(self.streams) + len(halves)))
            for start, count, order in halves:
                self.streams.append((start, count, order, tuple(self.rooms)))
                for level, axis in enumerate(order):
                    self.rooms[level] += count
                    count //= self.sizes[axis]

    def piece(self, stream, level):
        _, size, order, _ = self.streams[stream]
        for axis in order[: level + 1]:
            size //= self.sizes[axis]
        return size


def main_kernel(plan, names, *refs):
    ref = dict(zip(names, refs))
    S, I, R = plan.S, plan.I, plan.R
    side, width, pix, cin = plan.side, plan.width, plan.pix, plan.cin
    half_width = width // 2
    s, i, r = lax.axis_index("section"), lax.axis_index("img"), lax.axis_index("row")
    mine = s * plan.each + r // plan.copies
    waits = []

    barrier = pltpu.get_barrier_semaphore()
    peers = []
    for ds in range(S):
        for dr in range(R):
            if ds or dr:
                peers.append((lax.rem(s + ds, S), i, lax.rem(r + dr, R)))
    for di in range(1, I):
        peers.append((s, lax.rem(i + di, I), r))
    for peer in peers:
        pl.semaphore_signal(barrier, inc=1, device_id=peer, device_id_type=MESH)

    own = []
    loads = {}

    def load(*which):
        for name in which:
            at = (NAMES + WEIGHTS).index(name)
            loads[name] = pltpu.make_async_copy(ref[name], ref[name + "_v"], ref["loads"].at[at])
            loads[name].start(priority=int(name[0] == "k"))

    def need(name):
        if name in loads:
            loads.pop(name).wait()
        return ref[name + "_v"]

    load("w1", "g1", "b1", "k1", "k2")
    for name, rows in (("x", plan.rows), ("og", plan.hrows)):
        copy = pltpu.make_async_copy(
            ref[name].at[mine, 0],
            ref[name + "_in"].at[pl.ds(r * rows, rows)],
            ref[name + "_r"].at[r],
        )
        copy.start()
        own.append(copy)
    pl.semaphore_wait(barrier, len(peers))
    for name, rows in (("x", plan.rows), ("og", plan.hrows)):
        for d in range(1, R):
            t = lax.rem(r + d, R)
            copy = pltpu.make_async_remote_copy(
                src_ref=ref[name].at[s * plan.each + t // plan.copies, 0],
                dst_ref=ref[name + "_in"].at[pl.ds(r * rows, rows)],
                send_sem=ref[name + "_s"].at[d - 1],
                recv_sem=ref[name + "_r"].at[r],
                device_id=(s, i, t),
                device_id_type=MESH,
            )
            copy.start()
            waits.append(copy.wait_send)

    load("s1", *NAMES[2:], "sq1", "ex1", "e1", "w2", "sq2", "ex2", "e2")

    def arrived(name, rows, position, d):
        if d == 0:
            own[position].wait()
        else:
            t = lax.rem(r + d, R)
            there = ref[name + "_in"].at[pl.ds(t * rows, rows)]
            pltpu.make_async_remote_copy(
                src_ref=there,
                dst_ref=there,
                send_sem=ref[name + "_s"].at[d - 1],
                recv_sem=ref[name + "_r"].at[t],
                device_id=(s, i, t),
                device_id_type=MESH,
            ).wait_recv()

    st = ref["st"]

    def pairs_of(k):
        return 2 if k in (0, 1, 9) else 1

    def stats_copy(k, d, slot):
        return pltpu.make_async_remote_copy(
            src_ref=st.at[k, slot, pl.ds(0, pairs_of(k))],
            dst_ref=st.at[k, slot, pl.ds(0, pairs_of(k))],
            send_sem=ref["st_s"].at[k, d - 1],
            recv_sem=ref["st_r"].at[k, slot],
            device_id=(s, lax.rem(i + d, I), r),
            device_id_type=MESH,
        )

    def post(k, rows):
        ids = lax.broadcasted_iota(jnp.int32, (8, 128), 0)
        rows = [*rows, *([None] * (len(rows) % 2))]
        for pair in range(len(rows) // 2):
            value = jnp.zeros((8, 128), f32)
            for j in range(8):
                row = rows[2 * pair + j // 4]
                if row is not None:
                    piece = row[:, 128 * (j % 4) : 128 * (j % 4) + 128]
                    value = jnp.where(ids == j, jnp.broadcast_to(piece, (8, 128)), value)
            st[k, i, pair] = value
        for d in range(1, I):
            stats_copy(k, d, i).start()

    def fetch(k, count=2):
        for d in range(1, I):
            stats_copy(k, d, i).wait_send()
            stats_copy(k, d, lax.rem(i + d, I)).wait_recv()
        out = []
        for pair in range((count + 1) // 2):
            value = st[k, 0, pair]
            for j in range(1, I):
                value = value + st[k, j, pair]
            for half in range(2):
                out.append(
                    jnp.concatenate(
                        [
                            jnp.broadcast_to(value[4 * half + j : 4 * half + j + 1], (8, 128))
                            for j in range(4)
                        ],
                        axis=1,
                    )
                )
        return out

    vec = ref["vec"]

    def keep_vectors():
        for name in NAMES:
            row = need(name)[...].astype(f32)
            size = row.shape[0]
            vec[VEC[name], :, :size] = jnp.broadcast_to(row.reshape(1, size), (8, size))

    def vector(name):
        return vec[VEC[name]]

    vr, vc = ref["vr"][0, mine], ref["vc"][0, mine]
    q_ids = lax.broadcasted_iota(jnp.int32, (side, width), 0)
    first_col, last_col = q_ids == 0, q_ids == side - 1
    cm = ref["cm"]
    for b in range(2):
        cm[b] = (2 * q_ids + b < vc).astype(f32)

    def line(value):
        return value.astype(f32).reshape(2, 8, width)

    def pixels(value):
        return value.reshape(side, width)

    def mask_row(a, b, p):
        return line(cm[b]) * (2 * p + a < vr).astype(f32)

    def wide(row):
        return jnp.broadcast_to(row, (8, width))

    row_count = jnp.full((1, width), vr * vc, jnp.int32).astype(f32)
    half_count = jnp.full((1, width), ((vr + 1) // 2) * ((vc + 1) // 2), jnp.int32).astype(f32)

    def over_rows(step, *accs):
        init = tuple(jnp.zeros((8, width), f32) for _ in range(accs[0] if accs else 0))

        def run(p, carry):
            out = step(p)
            if not carry:
                return carry
            return tuple(c + fold(o) for c, o in zip(carry, out))

        return tuple(column(c) for c in lax.fori_loop(0, side, run, init, unroll=16))

    def full_dot(out, left, weight, form=dot):
        wide = out.shape[-1]
        step = min(256, wide)
        for h in range(wide // step):
            cut = slice(h * step, h * step + step)
            w = weight[:, cut] if form is dot else weight[cut, :]
            out[:, :, cut] = form(left, w).reshape(side, side, step).astype(out.dtype)

    hm = ref["hm"]
    for p in range(side):
        hm[p * side : (p + 1) * side] = cm[0][:, :128] * (2 * p < vr).astype(f32)

    def with_moments(out, products):
        sums = []
        for h, product in enumerate(products):
            span = product.shape[1]
            value = product.astype(out.dtype)
            out[:, :, h * span : (h + 1) * span] = value.reshape(side, side, span)
            value = value.astype(f32)
            valid = value * jnp.concatenate([hm[...]] * (span // 128), axis=1)
            sums.append(
                [
                    jnp.sum(x.reshape(pix // 8, 8, span), axis=0)
                    for x in (valid, valid * value)
                ]
            )
        return [column(jnp.concatenate(x, axis=1)) for x in zip(*sums)]

    def dot_moments(out, left, weight):
        return with_moments(
            out, (dot(left, weight[:, cut : cut + 256]) for cut in range(0, width, 256))
        )

    def flat(value):
        return value.reshape(pix, value.shape[-1])

    def lines(ref_, start=0):
        return flat(ref_[start : start + side])

    G, F = ref["local"], ref["grads"]
    lead = None if plan.copies == 1 else (lax.rem(r, plan.copies) == 0).astype(f32)

    def put(name, value, row=0, lane=0):
        if lead is not None:
            value = value * lead
        start, per_tile = plan.starts[name]
        count = value.shape[0] // 16
        for k in range(value.shape[1] // 128):
            piece = value[:, 128 * k : 128 * k + 128].astype(bf16).reshape(count, 16, 128)
            at = start + (lane // 128 + k) * per_tile + row // 16
            G[at : at + count] = piece

    X, Y = plan.X, plan.Y
    x, y = lax.rem(r, X), r // X
    axes = {
        "s": (S, s, lambda t: (t, i, r)),
        "r": (R, r, lambda t: (s, i, t)),
        "x": (X, x, lambda t: (s, i, y * X + t)),
        "y": (Y, y, lambda t: (s, i, t * X + x)),
        "i": (I, i, lambda t: (s, t, r)),
    }

    def scatter_source(stream, level):
        base, _, order, offsets = plan.streams[stream]
        if level == 0:
            return G, base
        return ref[f"sum{level - 1}"], offsets[level]

    def scatter_copies(stream, level, outgoing):
        base, size, order, offsets = plan.streams[stream]
        count, me, device = axes[order[level]]
        piece = plan.piece(stream, level)
        source, first = scatter_source(stream, level)
        for d in range(1, count):
            t = lax.rem(me + d, count)
            slot = me if outgoing else t
            copy = pltpu.make_async_remote_copy(
                src_ref=source.at[pl.ds(first + t * piece, piece)],
                dst_ref=ref[f"got{level}"].at[pl.ds(offsets[level] + slot * piece, piece)],
                send_sem=ref["rs_s"].at[stream, level, d - 1],
                recv_sem=ref["rs_r"].at[stream, level, slot],
                device_id=device(t),
                device_id_type=MESH,
            )
            if outgoing:
                copy.start()
                sent[stream].append(copy)
            else:
                copy.wait_recv()

    def add_up(stream, level):
        base, size, order, offsets = plan.streams[stream]
        count, me, _ = axes[order[level]]
        piece = plan.piece(stream, level)
        source, first = scatter_source(stream, level)
        got = ref[f"got{level}"]
        if level < len(order) - 1:
            out, at = ref[f"sum{level}"], offsets[level + 1]
        else:
            out, at = F, own_part(stream, len(order))
        step = next(k for k in (16, 12, 10, 9, 8, 7, 6, 5, 4, 3, 2, 1) if piece % k == 0)

        def run(k, carry):
            total = source[pl.ds(first + me * piece + k * step, step)].astype(f32)
            for d in range(1, count):
                t = lax.rem(me + d, count)
                total = total + got[pl.ds(offsets[level] + t * piece + k * step, step)].astype(f32)
            out[pl.ds(at + k * step, step)] = total.astype(bf16)
            return carry

        lax.fori_loop(0, piece // step, run, 0)

    def own_part(stream, depth):
        at, _, order, _ = plan.streams[stream]
        for level in range(depth):
            at = at + axes[order[level]][1] * plan.piece(stream, level)
        return at

    def gather_copies(stream, level, outgoing):
        count, me, device = axes[plan.streams[stream][2][level]]
        base = own_part(stream, level)
        piece = plan.piece(stream, level)
        for d in range(1, count):
            t = lax.rem(me + d, count)
            slot = me if outgoing else t
            there = F.at[pl.ds(base + slot * piece, piece)]
            copy = pltpu.make_async_remote_copy(
                src_ref=there,
                dst_ref=there,
                send_sem=ref["ag_s"].at[stream, level, d - 1],
                recv_sem=ref["ag_r"].at[stream, level, slot],
                device_id=device(t),
                device_id_type=MESH,
            )
            if outgoing:
                copy.start()
                sent[stream].append(copy)
            else:
                copy.wait_recv()

    done = [0] * len(plan.segments)
    started = []
    sent = [[] for _ in plan.streams]

    def pump(*which):
        for g in which or tuple(started):
            if g not in started:
                started.insert(0, g)
            k = done[g]
            depth = len(plan.streams[plan.members[g][0]][2])
            if k > 2 * depth:
                continue
            done[g] += 1
            if k == 0:
                base, size, used, _ = plan.segments[g]
                if used < base + size:
                    G[used : base + size] = jnp.zeros((base + size - used, 16, 128), bf16)
            for stream in plan.members[g]:
                if 1 <= k <= depth:
                    scatter_copies(stream, k - 1, False)
                    add_up(stream, k - 1)
                elif k > depth:
                    gather_copies(stream, 2 * depth - k, False)
                for copy in sent[stream]:
                    copy.wait_send()
                sent[stream] = []
                if k < depth:
                    scatter_copies(stream, k, True)
                elif k < 2 * depth:
                    gather_copies(stream, 2 * depth - 1 - k, True)

    vec_grads = {}

    gw = plan.gw
    span = 4 * gw
    def blocks(name, out, turned=False):
        kernels = need(name)
        shape = (span, gw) if turned else (gw, span)
        long = lax.broadcasted_iota(jnp.int32, shape, 0 if turned else 1)
        short = lax.broadcasted_iota(jnp.int32, shape, 1 if turned else 0)
        spread = (lax.rem(long, gw) == short).astype(f32).astype(bf16)
        row = lax.broadcasted_iota(jnp.int32, (span, span), 0) // gw
        col = lax.broadcasted_iota(jnp.int32, (span, span), 1) // gw
        for k, t in enumerate(ORDER):
            for h in range(width // span):
                piece = kernels[t, 4 * h : 4 * h + 4].reshape(span, gw)
                full = dot_nt(spread, piece) if turned else dot(piece, spread)
                out[h, k * span : (k + 1) * span] = jnp.where(row == col, full, 0.0).astype(bf16)

    def groups_grad(name, taps, turned):
        lane = lax.broadcasted_iota(jnp.int32, (gw, span), 1) // gw
        for t, (var, start) in enumerate(taps):
            for h in range(width // span):
                cut = slice(h * span, (h + 1) * span)
                res = dot(turned[h], flat(var[start : start + side, :, cut]))
                out = res[0:gw]
                for j in range(1, 4):
                    out = jnp.where(lane == j, res[j * gw : (j + 1) * gw], out)
                if name == "k2" and t == plan.taps - 1:
                    put(LAST_TAP, out, 0, h * span)
                else:
                    put(name, out, t * gw, h * span)

    band, bands = plan.band, plan.bands
    bhalf = band // 2
    out_id = lax.broadcasted_iota(jnp.int32, (pix, pix), 0)
    in_id = lax.broadcasted_iota(jnp.int32, (pix, pix), 1)

    def source(o):
        quarter = o // (bhalf * side)
        down = lax.rem(o, bhalf * side) // side
        return (2 * down + quarter // 2) * plan.cols + 2 * lax.rem(o, side) + lax.rem(quarter, 2)

    ref["sort"][...] = (source(out_id) == in_id).astype(f32).astype(bf16)
    ref["unsort"][...] = (source(in_id) == out_id).astype(f32).astype(bf16)

    xp, R1 = ref["xp"], ref["R1"]
    keep_vectors()

    def transpose(source, out):
        out[...] = source.astype(f32).T.astype(bf16)

    totals = [jnp.zeros((8, width), f32)] * 2
    by_band = plan.rows % band == 0
    if not by_band:
        for d in range(R):
            arrived("x", plan.rows, 0, d)
    for d in range(bands):
        if by_band:
            if d % (plan.rows // band) == 0:
                arrived("x", plan.rows, 0, d // (plan.rows // band))
            k = lax.rem(r * (plan.rows // band) + d, bands)
        else:
            k = d
        block = ref["x_in"][pl.ds(k * band, band)].reshape(pix, cin)
        block = dot(ref["sort"][...], block).astype(bf16)
        xp[k] = block.reshape(4 * bhalf, side, cin)
        full_dot(R1.at[k], block, need("w1"))
        for j in range(4 * bhalf):
            a, b = PHASES[j // bhalf]
            v = line(R1[k, j])
            mv = v * mask_row(a, b, k * bhalf + j % bhalf)
            totals = [totals[0] + fold(mv), totals[1] + fold(mv * v)]
    even = xp.at[:, 0:bhalf]

    def at_phase(ab, p):
        return p // bhalf, ab * bhalf + lax.rem(p, bhalf)

    post(0, [column(totals[0]), column(totals[1]), row_count, half_count])
    SC = ref["SC"]
    short_sums = dot_moments(SC, even[...].reshape(pix, cin), need("s1"))

    for k in range(bands):
        transpose(xp[k].reshape(pix, cin), ref["xpt"].at[k])
    blocks("k1", ref["bd1"])

    def coefficients(first, second, inverse, gain, shift):
        mean = first * inverse
        scale = lax.rsqrt(second * inverse - mean * mean + epsilon)
        a = scale * gain
        return a, shift - mean * a, scale, -mean * scale

    tot = fetch(0, 4)
    inv_full, inv_half = 1.0 / tot[2], 1.0 / tot[3]
    n1 = coefficients(tot[0], tot[1], inv_full, vector("g1"), vector("b1"))

    va = ref["va"]
    va[3:6, 0:1] = jnp.zeros((3, 1, side, width), bf16)

    def shifted(v, edge, amount):
        return jnp.where(edge, 0.0, pltpu.roll(v, amount, 0))

    for ab, (a, b) in enumerate(PHASES):

        def step(p, ab=ab, a=a, b=b):
            v = mask_row(a, b, p) * silu(line(R1[at_phase(ab, p)]) * n1[0] + n1[1])
            v = pixels(v)
            slot = (0, 1, 3, 4)[ab]
            va[slot, p + a] = v.astype(bf16)
            if b:
                va[slot + 1, p + a] = shifted(v, first_col, 1).astype(bf16)

        over_rows(step)
    taps1 = []
    for t in range(9):
        u, v = t // 3, t % 3
        slot = (0, 1, 3, 4)[2 * (u != 1) + (v != 1)] + (v == 0)
        taps1.append((va.at[slot], 1 if u == 2 else 0))

    def convolve(taps, weights, out):
        def half(h):
            cut = slice(h * span, (h + 1) * span)
            left = [flat(taps[t][0][taps[t][1] : taps[t][1] + side, :, cut]) for t in ORDER]
            return dot(jnp.concatenate(left, axis=1), weights[h])

        return with_moments(out, (half(h) for h in range(width // span)))

    c1 = ref["c1"]
    post(1, [*convolve(taps1, ref["bd1"], c1), *short_sums])
    blocks("k2", ref["bd2"])
    tot = fetch(1, 4)
    nc1 = coefficients(tot[0], tot[1], inv_half, vector("gg1"), vector("gb1"))
    ns = coefficients(tot[2], tot[3], inv_half, vector("sg1"), vector("sb1"))

    def excite(conv, norm, hidden, gated, sq, sq_form, sqb, ex, exb):
        def step(p):
            v = mask_row(0, 0, p) * silu(line(conv[p]) * norm[0] + norm[1])
            hidden[p] = pixels(v)
            return (v,)

        (total,) = over_rows(step, 1)
        pooled = total / half_count
        pre = small_dot(pooled, sq[...], sq_form) + sqb
        inner = silu(pre)
        gate = sigmoid(small_dot(inner, ex[...], dot) + exb)
        gate_wide = wide(gate)

        def step_two(p):
            gated[p] = pixels(line(hidden[p]) * gate_wide).astype(bf16)

        over_rows(step_two)
        return pooled, pre, inner, gate

    H1, ga1 = ref["H1"], ref["ga1"]
    kept1 = excite(
        c1, nc1, H1, ga1, need("sq1"), dot_nt, vec[VEC["sqb1"], 0:1, : plan.q1], need("ex1"), vec[VEC["exb1"], 0:1]
    )
    E1 = ref["E1"]
    post(2, dot_moments(E1, lines(ga1), need("e1")))
    transpose(lines(ga1), ref["ga1t"])
    blocks("k1", ref["bd1t"], True)
    tot = fetch(2)
    ne = coefficients(tot[0], tot[1], inv_half, vector("eg1"), vector("eb1"))
    ent = ref["ent"]
    both_shifts = ne[1] + ns[1]

    def step(p):
        v = line(E1[p]) * ne[0] + line(SC[p]) * ns[0] + both_shifts
        ent[p] = pixels(mask_row(0, 0, p) * silu(v)).astype(bf16)

    over_rows(step)

    def send_out(source, out, rows, target, steps=None):
        for k in range(R // plan.copies) if steps is None else steps:
            t = lax.rem(r + plan.copies * k, R)
            there = ref[out].at[0, mine, 0] if out == "act" else ref[out].at[mine, 0]
            here = source.at[pl.ds(t * rows, rows)]
            copy = pltpu.make_async_remote_copy(
                src_ref=here,
                dst_ref=there,
                send_sem=ref[out + "_s"].at[target, k],
                recv_sem=ref[out + "_r"].at[mine],
                device_id=(target, i, t),
                device_id_type=MESH,
            )
            if k:
                copy.start()
                waits.append(copy.wait_send)
            else:
                local = pltpu.make_async_copy(here, there, ref[out + "_r"].at[mine])

                @pl.when(s == target)
                def _():
                    local.start()

                @pl.when(s != target)
                def _():
                    copy.start()

                def finish(copy=copy):
                    @pl.when(s != target)
                    def _():
                        copy.wait_send()

                waits.append(finish)

    send_out(ent, "act", plan.hrows, 0)

    R2 = ref["R2"]
    post(3, dot_moments(R2, lines(ent), need("w2")))
    transpose(lines(ent), ref["entt"])
    tot = fetch(3)
    n2 = coefficients(tot[0], tot[1], inv_half, vector("g2"), vector("b2"))
    vb = ref["vb"]
    vb[:, 0:1] = jnp.zeros((3, 1, side, width), bf16)
    vb[:, side + 1 :] = jnp.zeros((3, 1, side, width), bf16)

    def three(out, p, v):
        out[0, p + 1] = shifted(v, first_col, 1).astype(bf16)
        out[1, p + 1] = v.astype(bf16)
        out[2, p + 1] = shifted(v, last_col, side - 1).astype(bf16)

    def step(p):
        three(vb, p, pixels(mask_row(0, 0, p) * silu(line(R2[p]) * n2[0] + n2[1])))

    over_rows(step)
    taps2 = [(vb.at[t % 3], t // 3) for t in range(9)]
    c2 = ref["c2"]
    post(4, convolve(taps2, ref["bd2"], c2))
    blocks("k2", ref["bd2t"], True)
    tot = fetch(4)
    nc2 = coefficients(tot[0], tot[1], inv_half, vector("gg2"), vector("gb2"))
    H2, ga2 = ref["H2"], ref["ga2"]
    kept2 = excite(
        c2, nc2, H2, ga2, need("sq2"), dot, vec[VEC["sqb2"], 0:1, : plan.q2], need("ex2"), vec[VEC["exb2"], 0:1]
    )
    E2 = ref["E2"]
    post(5, dot_moments(E2, lines(ga2), need("e2")))
    transpose(lines(ga2), ref["ga2t"])
    for d in range(R):
        arrived("og", plan.hrows, 1, d)
    tot = fetch(5)
    ne2 = coefficients(tot[0], tot[1], inv_half, vector("eg2"), vector("eb2"))
    leave, D, og = ref["leave"], ref["D"], ref["og_in"]

    def step(p):
        e = line(E2[p])
        v = e * ne2[0] + ne2[1] + line(ent[p])
        sg = sigmoid(v)
        m = mask_row(0, 0, p)
        leave[p] = pixels(m * v * sg).astype(bf16)
        g = line(og[p]) * m * (sg * (1.0 + v * (1.0 - sg)))
        D[p] = pixels(g)
        return g, g * (e * ne2[2] + ne2[3])

    parts = over_rows(step, 2)
    vec_grads["eb2"], vec_grads["eg2"] = parts
    post(6, parts)
    send_out(leave, "act", plan.hrows, 1)

    def back_rule(sums, inverse, gain, norm):
        a = gain * norm[2]
        k0 = a * (sums[0] + norm[3] * sums[1]) * inverse
        return a, k0, a * norm[2] * sums[1] * inverse

    def back_excite(dg, kept, hidden, conv, norm, sq, sq_form, ex, out):
        pooled, pre, inner, gate = kept

        def step(p):
            return (line(dg[p]) * line(hidden[p]),)

        (dgate,) = over_rows(step, 1)
        dpre = dgate * gate * (1.0 - gate)
        dsq = small_dot(dpre, ex[...], dot_nt) * slope(pre)
        dpool = wide(small_dot(dsq, sq[...], sq_form) / half_count)
        gate_wide = wide(gate)

        def step_two(p):
            v = line(conv[p])
            g = (line(dg[p]) * gate_wide + dpool) * mask_row(0, 0, p)
            g = g * slope(v * norm[0] + norm[1])
            out[p] = pixels(g)
            return g, g * (v * norm[2] + norm[3])

        return over_rows(step_two, 2), dpre, dsq

    def excite_grads(name, kept, dpre, dsq):
        pooled, pre, inner, gate = kept
        put("sq" + name, small_outer(dsq, pooled))
        put("ex" + name, small_outer(inner, dpre))
        vec_grads["exb" + name] = dpre
        count = dsq.shape[1]
        eye = (
            lax.broadcasted_iota(jnp.int32, (count, width), 0)
            == lax.broadcasted_iota(jnp.int32, (count, width), 1)
        ).astype(f32).astype(bf16)
        vec_grads["sqb" + name] = small_dot(dsq, eye, dot)

    def turn(gradient_ref, start):
        out = []
        for h in range(width // span):
            piece = flat(gradient_ref[start : start + side, :, h * span : (h + 1) * span])
            out.append(piece.astype(f32).T.astype(bf16))
        return out

    d1, dg, GR = ref["d1"], ref["dg"], ref["GR"]
    tot = fetch(6)
    rule = back_rule((tot[0], tot[1]), inv_half, vector("eg2"), ne2)

    def step(p):
        v = rule[0] * line(D[p]) - mask_row(0, 0, p) * (rule[1] + rule[2] * line(E2[p]))
        d1[p] = pixels(v).astype(bf16)

    over_rows(step)
    full_dot(dg, lines(d1), need("e2"), dot_nt)
    parts, dpre, dsq = back_excite(dg, kept2, H2, c2, nc2, need("sq2"), dot_nt, need("ex2"), GR)
    vec_grads["gb2"], vec_grads["gg2"] = parts
    post(7, parts)
    put("e2", dot(ref["ga2t"][...], lines(d1)))
    excite_grads("2", kept2, dpre, dsq)
    pump(0)
    tot = fetch(7)
    rule = back_rule((tot[0], tot[1]), inv_half, vector("gg2"), nc2)
    vd = ref["vd"]
    vd[:, 0:1] = jnp.zeros((3, 1, side, width), bf16)
    vd[:, side + 1 :] = jnp.zeros((3, 1, side, width), bf16)

    def step(p):
        v = rule[0] * line(GR[p]) - mask_row(0, 0, p) * (rule[1] + rule[2] * line(c2[p]))
        three(vd, p, pixels(v))

    over_rows(step)

    def convolve_back(taps, first, weights, out):
        for h in range(width // span):
            cut = slice(h * span, (h + 1) * span)
            left = [flat(var[start : start + side, :, cut]) for var, start in taps]
            rows = slice(first * span, (first + len(taps)) * span)
            acc = dot(jnp.concatenate(left, axis=1), weights[h, rows])
            out[:, :, cut] = acc.reshape(side, side, span)

    DA = ref["DA"]
    convolve_back(
        [(vd.at[2 - t % 3], 2 - t // 3) for t in ORDER],
        0,
        ref["bd2t"],
        DA.at[0],
    )

    def step(p):
        v = line(R2[p])
        g = line(DA[0, p]) * mask_row(0, 0, p) * slope(v * n2[0] + n2[1])
        GR[p] = pixels(g)
        return g, g * (v * n2[2] + n2[3])

    parts = over_rows(step, 2)
    vec_grads["b2"], vec_grads["g2"] = parts
    post(8, parts)
    pump(0)
    groups_grad("k2", taps2, turn(vd.at[1], 1))
    tot = fetch(8)
    rule = back_rule((tot[0], tot[1]), inv_half, vector("g2"), n2)

    def step(p):
        v = rule[0] * line(GR[p]) - mask_row(0, 0, p) * (rule[1] + rule[2] * line(R2[p]))
        d1[p] = pixels(v).astype(bf16)

    over_rows(step)
    full_dot(GR, lines(d1), need("w2"), dot_nt)
    pump(0)

    def step(p):
        e, sc = line(E1[p]), line(SC[p])
        g = line((D[p] + GR[p]).astype(bf16))
        g = g * mask_row(0, 0, p) * slope(e * ne[0] + sc * ns[0] + both_shifts)
        D[p] = pixels(g)
        return g, g * (e * ne[2] + ne[3]), g * (sc * ns[2] + ns[3])

    parts = over_rows(step, 3)
    vec_grads["eb1"], vec_grads["eg1"], vec_grads["sg1"] = parts
    vec_grads["sb1"] = parts[0]
    post(9, parts)
    put("w2", dot(ref["entt"][...], lines(d1)))
    pump(1, 0)
    tot = fetch(9, 3)
    rule_e = back_rule((tot[0], tot[1]), inv_half, vector("eg1"), ne)
    rule_s = back_rule((tot[0], tot[2]), inv_half, vector("sg1"), ns)
    d2 = ref["d2"]

    def step(p):
        g, m = line(D[p]), mask_row(0, 0, p)
        v = rule_e[0] * g - m * (rule_e[1] + rule_e[2] * line(E1[p]))
        d1[p] = pixels(v).astype(bf16)
        v = rule_s[0] * g - m * (rule_s[1] + rule_s[2] * line(SC[p]))
        d2[p] = pixels(v).astype(bf16)

    over_rows(step)
    full_dot(dg, lines(d1), need("e1"), dot_nt)
    pump(1)
    parts, dpre, dsq = back_excite(dg, kept1, H1, c1, nc1, need("sq1"), dot, need("ex1"), GR)
    vec_grads["gb1"], vec_grads["gg1"] = parts
    post(10, parts)
    put("e1", dot(ref["ga1t"][...], lines(d1)))
    put("s1", dot_tn(even[...].reshape(pix, cin), lines(d2)))
    excite_grads("1", kept1, dpre, dsq)
    pump(2, 1)
    tot = fetch(10)
    rule = back_rule((tot[0], tot[1]), inv_half, vector("gg1"), nc1)

    def step(p):
        v = rule[0] * line(GR[p]) - mask_row(0, 0, p) * (rule[1] + rule[2] * line(c1[p]))
        three(vd, p, pixels(v))

    over_rows(step)
    pump(0)
    sums = []
    for ab, (a, b) in enumerate(PHASES):
        chosen = []
        first = (0, 1, 3, 5)[ab]
        for t in ORDER[first : first + (1, 2, 2, 4)[ab]]:
            chosen.append((vd.at[2 if t % 3 == 0 else 1], 2 if t // 3 == 0 else 1))
        convolve_back(chosen, first, ref["bd1t"], DA.at[ab])

        def step(p, ab=ab, a=a, b=b):
            v = line(R1[at_phase(ab, p)])
            g = line(DA[ab, p]) * mask_row(a, b, p) * slope(v * n1[0] + n1[1])
            DA[ab, p] = pixels(g)
            return g, g * (v * n1[2] + n1[3])

        sums.append(over_rows(step, 2))
        if ab == 1:
            pump(2, 1)
        elif ab == 3:
            pump(0)
    parts = (sum(x[0] for x in sums), sum(x[1] for x in sums))
    vec_grads["b1"], vec_grads["g1"] = parts
    post(11, parts)
    pump(2)
    groups_grad("k1", taps1, turn(vd.at[1], 1))
    ids = lax.broadcasted_iota(jnp.int32, (VEC_ROWS, width), 0)
    value = jnp.zeros((VEC_ROWS, width), f32)
    for name, at in VEC.items():
        value = jnp.where(ids == at, jnp.broadcast_to(vec_grads[name], value.shape), value)
    put(VECTORS, value)
    pump(3, 2, 0)
    tot = fetch(11)
    rule = back_rule((tot[0], tot[1]), inv_full, vector("g1"), n1)
    dr = ref["dr"]
    for ab, (a, b) in enumerate(PHASES):

        def step(p, ab=ab, a=a, b=b):
            v = rule[0] * line(DA[ab, p])
            v = v - mask_row(a, b, p) * (rule[1] + rule[2] * line(R1[at_phase(ab, p)]))
            dr[at_phase(ab, p)] = pixels(v).astype(bf16)

        over_rows(step)
    total = None
    for k in range(bands):
        term = dot(ref["xpt"][k], dr[k].reshape(pix, width))
        total = term if total is None else total + term
    put("w1", total)
    pump(4, 3, 1)
    cut = cin // 2
    ref["dxo0"][...] = jnp.zeros((2 * side, plan.cols, 128), bf16)
    ref["dxo1"][...] = jnp.zeros((2 * side, plan.cols, 128), bf16)
    stepwise = plan.each == bands
    for d in [*range(1, bands), 0]:
        k = lax.rem(r + plan.copies * d, R) * plan.rows // band if stepwise else d
        for part in range(2):
            dxo = ref[f"dxo{part}"]
            rows = slice(part * cut, (part + 1) * cut)
            v = dot_nt(dr[k].reshape(pix, width), need("w1")[rows, :])
            w = dot_nt(
                d2[pl.ds(k * bhalf, bhalf)].reshape(bhalf * side, width), need("s1")[rows, :]
            )
            v = jnp.concatenate([v[: bhalf * side] + w, v[bhalf * side :]], axis=0)
            v = dot(ref["unsort"][...], v.astype(bf16)).astype(bf16)
            dxo[pl.ds(k * band, band), :, :cut] = v.reshape(band, plan.cols, cut)
            if stepwise:
                send_out(dxo, "dx", plan.rows, part, (d,))
        pump(*((4, 3, 2, 1), (4, 3, 1), (4, 3, 2), (1, 0))[(d - 1) % 4])
    if not stepwise:
        send_out(ref["dxo0"], "dx", plan.rows, 0)
        send_out(ref["dxo1"], "dx", plan.rows, 1)
    for _ in range(9):
        pump()
    for wait in waits:
        wait()
    for m in range(plan.M):
        t = (m % plan.each) * plan.copies + lax.rem(r, plan.copies)
        for out in ("act", "dx"):
            there = ref[out].at[0, m, 0] if out == "act" else ref[out].at[m, 0]
            pltpu.make_async_copy(there, there, ref[out + "_r"].at[m]).wait()


WEIGHTS = ("w1", "k1", "k2", "sq1", "ex1", "e1", "s1", "w2", "sq2", "ex2", "e2")


def run_main(plan, arrays):
    side, width, cin = plan.side, plan.width, plan.cin
    wide = 4 * plan.gw
    field = (side, side, width)
    scratch = {
        "x_in": pltpu.VMEM((2 * side, plan.cols, cin), bf16),
        "og_in": pltpu.VMEM(field, bf16),
        "st": pltpu.VMEM((EXCHANGES, plan.I, 2, 8, 128), f32),
        "hm": pltpu.VMEM((plan.pix, 128), f32),
        "cm": pltpu.VMEM((2, side, width), f32),
        **{
            name: pltpu.VMEM((width // wide, plan.taps * wide, wide), bf16)
            for name in ("bd1", "bd2", "bd1t", "bd2t")
        },
        "xpt": pltpu.VMEM((plan.bands, cin, plan.pix), bf16),
        **{name: pltpu.VMEM((width, plan.pix), bf16) for name in ("ga1t", "ga2t", "entt")},
        "sort": pltpu.VMEM((plan.pix, plan.pix), bf16),
        "unsort": pltpu.VMEM((plan.pix, plan.pix), bf16),
        "xp": pltpu.VMEM((plan.bands, 2 * plan.band, side, cin), bf16),
        "R1": pltpu.VMEM((plan.bands, 2 * plan.band, side, width), f32),
        "va": pltpu.VMEM((6, side + 1, side, width), bf16),
        "vb": pltpu.VMEM((3, side + 2, side, width), bf16),
        "vd": pltpu.VMEM((3, side + 2, side, width), bf16),
        "DA": pltpu.VMEM((4,) + field, f32),
        "dr": pltpu.VMEM((plan.bands, 2 * plan.band, side, width), bf16),
        "dxo0": pltpu.VMEM((2 * side, plan.cols, 128), bf16),
        "dxo1": pltpu.VMEM((2 * side, plan.cols, 128), bf16),
    }
    for name in ("SC", "H1", "E1", "R2", "H2", "E2", "D", "GR"):
        scratch[name] = pltpu.VMEM(field, f32)
    for name in ("c1", "ga1", "ent", "c2", "ga2", "leave", "d1", "d2", "dg"):
        scratch[name] = pltpu.VMEM(field, bf16)
    for name in ("x", "og"):
        scratch[name + "_s"] = pltpu.SemaphoreType.DMA((max(plan.R - 1, 1),))
        scratch[name + "_r"] = pltpu.SemaphoreType.DMA((plan.R,))
    scratch["st_s"] = pltpu.SemaphoreType.DMA((EXCHANGES, max(plan.I - 1, 1)))
    scratch["st_r"] = pltpu.SemaphoreType.DMA((EXCHANGES, plan.I))
    for name in ("act", "dx"):
        scratch[name + "_s"] = pltpu.SemaphoreType.DMA((2, plan.R // plan.copies))
        scratch[name + "_r"] = pltpu.SemaphoreType.DMA((plan.M,))
    for name in NAMES + WEIGHTS:
        scratch[name + "_v"] = pltpu.VMEM(arrays[name].shape, bf16)
    scratch["vec"] = pltpu.VMEM((len(NAMES), 8, width), f32)
    scratch["loads"] = pltpu.SemaphoreType.DMA((len(NAMES + WEIGHTS),))
    scratch["local"] = pltpu.VMEM((plan.blocks, 16, 128), bf16)
    for level, room in enumerate(plan.rooms):
        scratch[f"got{level}"] = pltpu.VMEM((room, 16, 128), bf16)
        if level:
            scratch[f"sum{level - 1}"] = pltpu.VMEM((room, 16, 128), bf16)
    most = max(plan.sizes.values())
    for name in ("rs", "ag"):
        scratch[name + "_s"] = pltpu.SemaphoreType.DMA((len(plan.streams), 4, most - 1))
        scratch[name + "_r"] = pltpu.SemaphoreType.DMA((len(plan.streams), 4, most))
    inputs = ("x", "og", "vr", "vc") + NAMES + WEIGHTS
    outputs = ("act", "dx", "grads")
    names = inputs + outputs + tuple(scratch)
    any_space = pl.BlockSpec(memory_space=pl.ANY)
    smem = pl.BlockSpec(memory_space=pltpu.SMEM)
    vmem = pl.BlockSpec(memory_space=pltpu.VMEM)
    return pl.pallas_call(
        functools.partial(main_kernel, plan, names),
        out_shape=(
            jax.ShapeDtypeStruct((1, plan.M, 1, plan.hrows, side, width), bf16),
            jax.ShapeDtypeStruct((plan.M, 1, plan.rows, plan.cols, 128), bf16),
            jax.ShapeDtypeStruct((plan.blocks, 16, 128), bf16),
        ),
        in_specs=[any_space, any_space, smem, smem] + [any_space] * (len(NAMES) + len(WEIGHTS)),
        out_specs=(any_space, any_space, vmem),
        scratch_shapes=list(scratch.values()),
        compiler_params=pltpu.CompilerParams(
            collective_id=0, has_side_effects=True, vmem_limit_bytes=60 * 1024 * 1024
        ),
        name="blocks",
    )(*[arrays[name] for name in inputs])


OUTS = (
    "w1", "g1", "b1", "k1", "gg1", "gb1", "sq1", "sqb1", "ex1", "exb1", "e1", "eg1", "eb1",
    "s1", "sg1", "sb1", "w2", "g2", "b2", "k2", "gg2", "gb2", "sq2", "sqb2", "ex2", "exb2",
    "e2", "eg2", "eb2",
)


def unpack_kernel(plan, source, act_in, dx_in, *rest):
    count = len(OUTS) + 2
    outs, bufs, loads_at, sems = rest[:count], rest[count:-3], rest[-3:-1], rest[-1]
    copies = []
    for k, whole in enumerate((act_in, dx_in)):
        copies.append(pltpu.make_async_copy(whole, outs[k], sems.at[k]))
        copies[-1].start()
    loads = []
    order = sorted(plan.starts, key=lambda name: plan.starts[name])
    order = [name for name in order if name not in (VECTORS, LAST_TAP)] + [VECTORS, LAST_TAP]
    blocks = loads_at[0]
    for k, name in enumerate(order):
        start, per_tile = plan.starts[name]
        part = pl.ds(start, per_tile * (plan.width // 128))
        loads.append(pltpu.make_async_copy(source.at[part], blocks.at[part], loads_at[1].at[k]))
        loads[-1].start()

    def tile(name, k):
        start, per_tile = plan.starts[name]
        at = start + k * per_tile
        return blocks[at : at + per_tile].reshape(16 * per_tile, 128).astype(f32)

    tiles = plan.width // 128
    vec = None
    turn = [OUTS.index(name) for name in order[:-2]]
    turn += [k for k, name in enumerate(OUTS) if name in VEC]
    for position, k in enumerate(turn):
        name, out = OUTS[k], bufs[k]
        if position < len(loads) - 1:
            loads[position].wait()
        if name in VEC and vec is None:
            vec = jnp.concatenate([tile(VECTORS, k) for k in range(tiles)], axis=1)
        if name in VEC:
            size = out.shape[0]
            out[...] = vec[VEC[name] : VEC[name] + 1, :size].reshape(size)
        elif name[0] == "k":

            def run(t, carry, name=name, out=out, last_tap=False):
                for lane in range(tiles):
                    start, per_tile = plan.starts[name]
                    at = start + lane * per_tile + t * (plan.gw // 16)
                    if last_tap:
                        start, per_tile = plan.starts[LAST_TAP]
                        at = start + lane * per_tile
                    piece = blocks[pl.ds(at, plan.gw // 16)].reshape(plan.gw, 128)
                    piece = piece.astype(f32).T
                    for j in range(128 // plan.gw):
                        group = lane * (128 // plan.gw) + j
                        out[t, group, :, : plan.gw] = piece[j * plan.gw : (j + 1) * plan.gw]
                return carry

            if name == "k2":
                loads[order.index(LAST_TAP)].wait()
                lax.fori_loop(0, plan.taps - 1, run, 0)
                run(plan.taps - 1, 0, last_tap=True)
            else:
                lax.fori_loop(0, plan.taps, run, 0)
        elif name == "sq2":
            for lane in range(tiles):
                out[128 * lane : 128 * lane + 128] = tile(name, lane).T
        else:
            for lane in range(tiles):
                out[:, 128 * lane : 128 * lane + 128] = tile(name, lane)
        copies.append(pltpu.make_async_copy(out, outs[k + 2], sems.at[k + 2]))
        copies[-1].start()
    for copy in copies:
        copy.wait()


def unpack(plan, act, dx, grads, weights):
    shapes = []
    for name, w in zip(OUTS, weights):
        shape = w.shape[:3] + (128,) if name[0] == "k" else w.shape
        shapes.append(jax.ShapeDtypeStruct(shape, f32))
    any_space = pl.BlockSpec(memory_space=pl.ANY)
    return pl.pallas_call(
        functools.partial(unpack_kernel, plan),
        out_shape=[jax.ShapeDtypeStruct(v.shape, v.dtype) for v in (act, dx)] + shapes,
        in_specs=[any_space] * 3,
        out_specs=[any_space] * (len(shapes) + 2),
        scratch_shapes=[pltpu.VMEM(v.shape, v.dtype) for v in shapes]
        + [pltpu.VMEM(grads.shape, bf16), pltpu.SemaphoreType.DMA((len(plan.starts),))]
        + [pltpu.SemaphoreType.DMA((len(shapes) + 2,))],
        compiler_params=pltpu.CompilerParams(vmem_limit_bytes=60 * 1024 * 1024),
        name="unpack",
    )(grads, act, dx)


def body(sizes, input_maps, valid_rows, valid_cols, *rest):
    weights, output_grad = rest[:-1], rest[-1]
    (w1, g1, b1, k1, gg1, gb1, sq1, sqb1, ex1, exb1, e1, eg1, eb1, s1, sg1, sb1) = weights[:16]
    (w2, g2, b2, k2, gg2, gb2, sq2, sqb2, ex2, exb2, e2, eg2, eb2) = weights[16:]
    turned = sq1.T
    plan = Plan(sizes, [v.shape for v in (input_maps, output_grad, w1, k1, turned, sq2)])
    vectors = (
        g1, b1, gg1, gb1, exb1, eg1, eb1, sg1, sb1, sqb1, g2, b2, gg2, gb2, exb2, eg2, eb2, sqb2,
    )
    arrays = dict(
        x=input_maps, og=output_grad, vr=valid_rows.T, vc=valid_cols.T, w1=w1,
        k1=k1, k2=k2,
        sq1=turned, ex1=ex1, e1=e1, s1=s1, w2=w2, sq2=sq2, ex2=ex2, e2=e2,
        **dict(zip(NAMES, vectors)),
    )
    act, dx, grads = run_main(plan, arrays)
    act, dx, *out = unpack(plan, act, dx, grads, weights[:6] + (turned,) + weights[7:])
    out[6] = out[6].T
    for at in (3, 19):
        out[at] = out[at][..., : plan.gw]
    dx = dx[..., : plan.cin // 2]
    return (act, dx, *out)


def solution(mesh):
    tiled = P(None, "img", "row", None, None)
    image = P(None, "img")
    sizes = tuple(mesh.shape[name] for name in ("section", "img", "row"))
    return jax.shard_map(
        functools.partial(body, sizes),
        mesh=mesh,
        in_specs=(tiled, image, image) + (P(),) * 29 + (tiled,),
        out_specs=(
            P("section", None, "img", "row", None, None),
            P(None, "img", "row", None, "section"),
        )
        + (P(),) * 29,
        check_vma=False,
    )
```

```python
import functools

import jax
import jax.numpy as jnp
from jax import lax
from jax.experimental import pallas as pl
from jax.experimental.pallas import tpu as pltpu
from jax.sharding import PartitionSpec as P

epsilon = 1e-05
f32 = jnp.float32
bf16 = jnp.bfloat16
MESH = pl.DeviceIdType.MESH
PHASES = ((0, 0), (0, 1), (1, 0), (1, 1))
ORDER = (4, 3, 5, 1, 7, 0, 2, 6, 8)
EXCHANGES = 12
NAMES = (
    "g1", "b1", "gg1", "gb1", "exb1", "eg1", "eb1", "sg1", "sb1", "sqb1",
    "g2", "b2", "gg2", "gb2", "exb2", "eg2", "eb2", "sqb2",
)
VEC = {name: k for k, name in enumerate(NAMES)}
VEC_ROWS = 32
VECTORS = "vec"
LAST_TAP = "k9"


def segments_of(cin, width, taps, group, sq1, sq2, devices):
    layout = (
        (("e2", width), ("sq2", sq2), ("ex2", sq2)),
        (("k2", (taps - 1) * group), ("w2", width)),
        (("e1", width), ("s1", cin), ("sq1", sq1), ("ex1", sq1), (LAST_TAP, group)),
        (("k1", taps * group), (VECTORS, VEC_ROWS)),
        (("w1", cin),),
    )
    starts, segments, at = {}, [], 0
    for parts in layout:
        base = at
        for name, rows in parts:
            starts[name] = (at, rows // 16)
            at += rows // 16 * (width // 128)
        units = -(-(at - base) // devices)
        first = units // 2 * devices if len(segments) < len(layout) - 1 else 0
        segments.append((base, units * devices, at, first))
        at = base + units * devices
    return starts, tuple(segments), at


def sigmoid(v):
    return 0.5 * jnp.tanh(0.5 * v) + 0.5


def silu(v):
    return v * sigmoid(v)


def slope(v):
    s = sigmoid(v)
    return s * (1.0 + v * (1.0 - s))


def dot(left, right):
    return jnp.dot(left, right, preferred_element_type=f32)


def dot_nt(left, right):
    return lax.dot_general(left, right, (((1,), (1,)), ((), ())), preferred_element_type=f32)


def dot_tn(left, right):
    return lax.dot_general(left, right, (((0,), (0,)), ((), ())), preferred_element_type=f32)


def parts_of(v):
    high = v.astype(bf16).astype(f32)
    return high, v - high


def stacked(rows, width):
    ids = lax.broadcasted_iota(jnp.int32, (16, width), 0)
    total = jnp.zeros((16, width), f32)
    for k, row in enumerate(rows):
        total = jnp.where(ids == k, jnp.broadcast_to(row, (16, width)), total)
    return total.astype(bf16)


def small_dot(row, weight, form):
    out = form(stacked(parts_of(row), row.shape[1]), weight)
    return out[0:1] + out[1:2]


def small_outer(left, right):
    lh, ll = parts_of(left)
    rh, rl = parts_of(right)
    return dot_tn(
        stacked((lh, ll, lh, ll), left.shape[1]), stacked((rh, rh, rl, rl), right.shape[1])
    )


def fold(v):
    return v[0] + v[1]


def column(acc):
    return jnp.sum(acc, axis=0, keepdims=True)


class Plan:
    def __init__(self, mesh_sizes, args):
        self.S, self.I, self.R = mesh_sizes
        x, og, w1, k1, sq1, sq2 = args
        self.M, _, self.rows, self.cols, self.cin = x
        _, _, self.hrows, self.side, self.width = og
        self.taps, self.groups, self.gw, _ = k1
        self.q1, self.q2 = sq1[0], sq2[1]
        self.each = self.M // self.S
        self.copies = self.R // self.each
        self.pix = self.side * self.side
        self.band = self.pix // self.cols
        self.bands = 2 * self.side // self.band
        self.starts, self.segments, self.blocks = segments_of(
            self.cin, self.width, self.taps, self.gw, self.q1, self.q2, self.S * self.I * self.R
        )
        self.X = 1
        while self.X * self.X < self.R:
            self.X *= 2
        self.Y = self.R // self.X
        self.sizes = {"s": self.S, "x": self.X, "y": self.Y, "r": self.R, "i": self.I}
        self.streams = []
        self.members = []
        self.rooms = [0] * 4
        for base, size, _, first in self.segments:
            halves = [(base, first, "sxyi"), (base + first, size - first, "syxi")]
            if not first:
                halves = [(base, size, "sri")]
            self.members.append(range(len(self.streams), len(self.streams) + len(halves)))
            for start, count, order in halves:
                self.streams.append((start, count, order, tuple(self.rooms)))
                for level, axis in enumerate(order):
                    self.rooms[level] += count
                    count //= self.sizes[axis]

    def piece(self, stream, level):
        _, size, order, _ = self.streams[stream]
        for axis in order[: level + 1]:
            size //= self.sizes[axis]
        return size


def main_kernel(plan, names, *refs):
    ref = dict(zip(names, refs))
    S, I, R = plan.S, plan.I, plan.R
    side, width, pix, cin = plan.side, plan.width, plan.pix, plan.cin
    half_width = width // 2
    s, i, r = lax.axis_index("section"), lax.axis_index("img"), lax.axis_index("row")
    mine = s * plan.each + r // plan.copies
    waits = []

    barrier = pltpu.get_barrier_semaphore()
    peers = []
    for ds in range(S):
        for dr in range(R):
            if ds or dr:
                peers.append((lax.rem(s + ds, S), i, lax.rem(r + dr, R)))
    for di in range(1, I):
        peers.append((s, lax.rem(i + di, I), r))
    for peer in peers:
        pl.semaphore_signal(barrier, inc=1, device_id=peer, device_id_type=MESH)

    own = []
    loads = {}

    def load(*which):
        for name in which:
            at = (NAMES + WEIGHTS).index(name)
            loads[name] = pltpu.make_async_copy(ref[name], ref[name + "_v"], ref["loads"].at[at])
            loads[name].start(priority=int(name[0] == "k"))

    def need(name):
        if name in loads:
            loads.pop(name).wait()
        return ref[name + "_v"]

    load("w1", "g1", "b1", "k1", "k2")
    for name, rows in (("x", plan.rows), ("og", plan.hrows)):
        copy = pltpu.make_async_copy(
            ref[name].at[mine, 0],
            ref[name + "_in"].at[pl.ds(r * rows, rows)],
            ref[name + "_r"].at[r],
        )
        copy.start()
        own.append(copy)
    pl.semaphore_wait(barrier, len(peers))
    for name, rows in (("x", plan.rows), ("og", plan.hrows)):
        for d in range(1, R):
            t = lax.rem(r + d, R)
            copy = pltpu.make_async_remote_copy(
                src_ref=ref[name].at[s * plan.each + t // plan.copies, 0],
                dst_ref=ref[name + "_in"].at[pl.ds(r * rows, rows)],
                send_sem=ref[name + "_s"].at[d - 1],
                recv_sem=ref[name + "_r"].at[r],
                device_id=(s, i, t),
                device_id_type=MESH,
            )
            copy.start()
            waits.append(copy.wait_send)

    load("s1", *NAMES[2:], "sq1", "ex1", "e1", "w2", "sq2", "ex2", "e2")

    def arrived(name, rows, position, d):
        if d == 0:
            own[position].wait()
        else:
            t = lax.rem(r + d, R)
            there = ref[name + "_in"].at[pl.ds(t * rows, rows)]
            pltpu.make_async_remote_copy(
                src_ref=there,
                dst_ref=there,
                send_sem=ref[name + "_s"].at[d - 1],
                recv_sem=ref[name + "_r"].at[t],
                device_id=(s, i, t),
                device_id_type=MESH,
            ).wait_recv()

    st = ref["st"]

    def pairs_of(k):
        return 2 if k in (0, 1, 9) else 1

    def stats_copy(k, d, slot):
        return pltpu.make_async_remote_copy(
            src_ref=st.at[k, slot, pl.ds(0, pairs_of(k))],
            dst_ref=st.at[k, slot, pl.ds(0, pairs_of(k))],
            send_sem=ref["st_s"].at[k, d - 1],
            recv_sem=ref["st_r"].at[k, slot],
            device_id=(s, lax.rem(i + d, I), r),
            device_id_type=MESH,
        )

    def post(k, rows):
        ids = lax.broadcasted_iota(jnp.int32, (8, 128), 0)
        rows = [*rows, *([None] * (len(rows) % 2))]
        for pair in range(len(rows) // 2):
            value = jnp.zeros((8, 128), f32)
            for j in range(8):
                row = rows[2 * pair + j // 4]
                if row is not None:
                    piece = row[:, 128 * (j % 4) : 128 * (j % 4) + 128]
                    value = jnp.where(ids == j, jnp.broadcast_to(piece, (8, 128)), value)
            st[k, i, pair] = value
        for d in range(1, I):
            stats_copy(k, d, i).start()

    def fetch(k, count=2):
        for d in range(1, I):
            stats_copy(k, d, i).wait_send()
            stats_copy(k, d, lax.rem(i + d, I)).wait_recv()
        out = []
        for pair in range((count + 1) // 2):
            value = st[k, 0, pair]
            for j in range(1, I):
                value = value + st[k, j, pair]
            for half in range(2):
                out.append(
                    jnp.concatenate(
                        [
                            jnp.broadcast_to(value[4 * half + j : 4 * half + j + 1], (8, 128))
                            for j in range(4)
                        ],
                        axis=1,
                    )
                )
        return out

    vec = ref["vec"]

    def keep_vectors():
        for name in NAMES:
            row = need(name)[...].astype(f32)
            size = row.shape[0]
            vec[VEC[name], :, :size] = jnp.broadcast_to(row.reshape(1, size), (8, size))

    def vector(name):
        return vec[VEC[name]]

    vr, vc = ref["vr"][0, mine], ref["vc"][0, mine]
    q_ids = lax.broadcasted_iota(jnp.int32, (side, width), 0)
    first_col, last_col = q_ids == 0, q_ids == side - 1
    cm = ref["cm"]
    for b in range(2):
        cm[b] = (2 * q_ids + b < vc).astype(f32)

    def line(value):
        return value.astype(f32).reshape(2, 8, width)

    def pixels(value):
        return value.reshape(side, width)

    def mask_row(a, b, p):
        return line(cm[b]) * (2 * p + a < vr).astype(f32)

    def wide(row):
        return jnp.broadcast_to(row, (8, width))

    row_count = jnp.full((1, width), vr * vc, jnp.int32).astype(f32)
    half_count = jnp.full((1, width), ((vr + 1) // 2) * ((vc + 1) // 2), jnp.int32).astype(f32)

    def over_rows(step, *accs):
        init = tuple(jnp.zeros((8, width), f32) for _ in range(accs[0] if accs else 0))

        def run(p, carry):
            out = step(p)
            if not carry:
                return carry
            return tuple(c + fold(o) for c, o in zip(carry, out))

        return tuple(column(c) for c in lax.fori_loop(0, side, run, init, unroll=16))

    def full_dot(out, left, weight, form=dot):
        wide = out.shape[-1]
        step = min(256, wide)
        for h in range(wide // step):
            cut = slice(h * step, h * step + step)
            w = weight[:, cut] if form is dot else weight[cut, :]
            out[:, :, cut] = form(left, w).reshape(side, side, step).astype(out.dtype)

    hm = ref["hm"]
    for p in range(side):
        hm[p * side : (p + 1) * side] = cm[0][:, :128] * (2 * p < vr).astype(f32)

    def with_moments(out, products):
        sums = []
        for h, product in enumerate(products):
            span = product.shape[1]
            value = product.astype(out.dtype)
            out[:, :, h * span : (h + 1) * span] = value.reshape(side, side, span)
            value = value.astype(f32)
            valid = value * jnp.concatenate([hm[...]] * (span // 128), axis=1)
            sums.append(
                [
                    jnp.sum(x.reshape(pix // 8, 8, span), axis=0)
                    for x in (valid, valid * value)
                ]
            )
        return [column(jnp.concatenate(x, axis=1)) for x in zip(*sums)]

    def dot_moments(out, left, weight):
        return with_moments(
            out, (dot(left, weight[:, cut : cut + 256]) for cut in range(0, width, 256))
        )

    def flat(value):
        return value.reshape(pix, value.shape[-1])

    def lines(ref_, start=0):
        return flat(ref_[start : start + side])

    G, F = ref["local"], ref["grads"]
    lead = None if plan.copies == 1 else (lax.rem(r, plan.copies) == 0).astype(f32)

    def put(name, value, row=0, lane=0):
        if lead is not None:
            value = value * lead
        start, per_tile = plan.starts[name]
        count = value.shape[0] // 16
        for k in range(value.shape[1] // 128):
            piece = value[:, 128 * k : 128 * k + 128].astype(bf16).reshape(count, 16, 128)
            at = start + (lane // 128 + k) * per_tile + row // 16
            G[at : at + count] = piece

    X, Y = plan.X, plan.Y
    x, y = lax.rem(r, X), r // X
    axes = {
        "s": (S, s, lambda t: (t, i, r)),
        "r": (R, r, lambda t: (s, i, t)),
        "x": (X, x, lambda t: (s, i, y * X + t)),
        "y": (Y, y, lambda t: (s, i, t * X + x)),
        "i": (I, i, lambda t: (s, t, r)),
    }

    def scatter_source(stream, level):
        base, _, order, offsets = plan.streams[stream]
        if level == 0:
            return G, base
        return ref[f"sum{level - 1}"], offsets[level]

    def scatter_copies(stream, level, outgoing):
        base, size, order, offsets = plan.streams[stream]
        count, me, device = axes[order[level]]
        piece = plan.piece(stream, level)
        source, first = scatter_source(stream, level)
        for d in range(1, count):
            t = lax.rem(me + d, count)
            slot = me if outgoing else t
            copy = pltpu.make_async_remote_copy(
                src_ref=source.at[pl.ds(first + t * piece, piece)],
                dst_ref=ref[f"got{level}"].at[pl.ds(offsets[level] + slot * piece, piece)],
                send_sem=ref["rs_s"].at[stream, level, d - 1],
                recv_sem=ref["rs_r"].at[stream, level, slot],
                device_id=device(t),
                device_id_type=MESH,
            )
            if outgoing:
                copy.start()
                sent[stream].append(copy)
            else:
                copy.wait_recv()

    def add_up(stream, level):
        base, size, order, offsets = plan.streams[stream]
        count, me, _ = axes[order[level]]
        piece = plan.piece(stream, level)
        source, first = scatter_source(stream, level)
        got = ref[f"got{level}"]
        if level < len(order) - 1:
            out, at = ref[f"sum{level}"], offsets[level + 1]
        else:
            out, at = F, own_part(stream, len(order))
        step = next(k for k in (16, 12, 10, 9, 8, 7, 6, 5, 4, 3, 2, 1) if piece % k == 0)

        def run(k, carry):
            total = source[pl.ds(first + me * piece + k * step, step)].astype(f32)
            for d in range(1, count):
                t = lax.rem(me + d, count)
                total = total + got[pl.ds(offsets[level] + t * piece + k * step, step)].astype(f32)
            out[pl.ds(at + k * step, step)] = total.astype(bf16)
            return carry

        lax.fori_loop(0, piece // step, run, 0)

    def own_part(stream, depth):
        at, _, order, _ = plan.streams[stream]
        for level in range(depth):
            at = at + axes[order[level]][1] * plan.piece(stream, level)
        return at

    def gather_copies(stream, level, outgoing):
        count, me, device = axes[plan.streams[stream][2][level]]
        base = own_part(stream, level)
        piece = plan.piece(stream, level)
        for d in range(1, count):
            t = lax.rem(me + d, count)
            slot = me if outgoing else t
            there = F.at[pl.ds(base + slot * piece, piece)]
            copy = pltpu.make_async_remote_copy(
                src_ref=there,
                dst_ref=there,
                send_sem=ref["ag_s"].at[stream, level, d - 1],
                recv_sem=ref["ag_r"].at[stream, level, slot],
                device_id=device(t),
                device_id_type=MESH,
            )
            if outgoing:
                copy.start()
                sent[stream].append(copy)
            else:
                copy.wait_recv()

    done = [0] * len(plan.segments)
    started = []
    sent = [[] for _ in plan.streams]

    def pump(*which):
        for g in which or tuple(started):
            if g not in started:
                started.insert(0, g)
            k = done[g]
            depth = len(plan.streams[plan.members[g][0]][2])
            if k > 2 * depth:
                continue
            done[g] += 1
            if k == 0:
                base, size, used, _ = plan.segments[g]
                if used < base + size:
                    G[used : base + size] = jnp.zeros((base + size - used, 16, 128), bf16)
            for stream in plan.members[g]:
                if 1 <= k <= depth:
                    scatter_copies(stream, k - 1, False)
                    add_up(stream, k - 1)
                elif k > depth:
                    gather_copies(stream, 2 * depth - k, False)
                for copy in sent[stream]:
                    copy.wait_send()
                sent[stream] = []
                if k < depth:
                    scatter_copies(stream, k, True)
                elif k < 2 * depth:
                    gather_copies(stream, 2 * depth - 1 - k, True)

    vec_grads = {}

    gw = plan.gw
    span = 4 * gw
    def blocks(name, out, turned=False):
        kernels = need(name)
        shape = (span, gw) if turned else (gw, span)
        long = lax.broadcasted_iota(jnp.int32, shape, 0 if turned else 1)
        short = lax.broadcasted_iota(jnp.int32, shape, 1 if turned else 0)
        spread = (lax.rem(long, gw) == short).astype(f32).astype(bf16)
        row = lax.broadcasted_iota(jnp.int32, (span, span), 0) // gw
        col = lax.broadcasted_iota(jnp.int32, (span, span), 1) // gw
        for k, t in enumerate(ORDER):
            for h in range(width // span):
                piece = kernels[t, 4 * h : 4 * h + 4].reshape(span, gw)
                full = dot_nt(spread, piece) if turned else dot(piece, spread)
                out[h, k * span : (k + 1) * span] = jnp.where(row == col, full, 0.0).astype(bf16)

    def groups_grad(name, taps, turned):
        lane = lax.broadcasted_iota(jnp.int32, (gw, span), 1) // gw
        for t, (var, start) in enumerate(taps):
            for h in range(width // span):
                cut = slice(h * span, (h + 1) * span)
                res = dot(turned[h], flat(var[start : start + side, :, cut]))
                out = res[0:gw]
                for j in range(1, 4):
                    out = jnp.where(lane == j, res[j * gw : (j + 1) * gw], out)
                if name == "k2" and t == plan.taps - 1:
                    put(LAST_TAP, out, 0, h * span)
                else:
                    put(name, out, t * gw, h * span)

    band, bands = plan.band, plan.bands
    bhalf = band // 2
    out_id = lax.broadcasted_iota(jnp.int32, (pix, pix), 0)
    in_id = lax.broadcasted_iota(jnp.int32, (pix, pix), 1)

    def source(o):
        quarter = o // (bhalf * side)
        down = lax.rem(o, bhalf * side) // side
        return (2 * down + quarter // 2) * plan.cols + 2 * lax.rem(o, side) + lax.rem(quarter, 2)

    ref["sort"][...] = (source(out_id) == in_id).astype(f32).astype(bf16)
    ref["unsort"][...] = (source(in_id) == out_id).astype(f32).astype(bf16)

    xp, R1 = ref["xp"], ref["R1"]
    keep_vectors()

    def transpose(source, out):
        out[...] = source.astype(f32).T.astype(bf16)

    totals = [jnp.zeros((8, width), f32)] * 2
    by_band = plan.rows % band == 0
    if not by_band:
        for d in range(R):
            arrived("x", plan.rows, 0, d)
    for d in range(bands):
        if by_band:
            if d % (plan.rows // band) == 0:
                arrived("x", plan.rows, 0, d // (plan.rows // band))
            k = lax.rem(r * (plan.rows // band) + d, bands)
        else:
            k = d
        block = ref["x_in"][pl.ds(k * band, band)].reshape(pix, cin)
        block = dot(ref["sort"][...], block).astype(bf16)
        xp[k] = block.reshape(4 * bhalf, side, cin)
        full_dot(R1.at[k], block, need("w1"))
        for j in range(4 * bhalf):
            a, b = PHASES[j // bhalf]
            v = line(R1[k, j])
            mv = v * mask_row(a, b, k * bhalf + j % bhalf)
            totals = [totals[0] + fold(mv), totals[1] + fold(mv * v)]
    even = xp.at[:, 0:bhalf]

    def at_phase(ab, p):
        return p // bhalf, ab * bhalf + lax.rem(p, bhalf)

    post(0, [column(totals[0]), column(totals[1]), row_count, half_count])
    SC = ref["SC"]
    short_sums = dot_moments(SC, even[...].reshape(pix, cin), need("s1"))

    for k in range(bands):
        transpose(xp[k].reshape(pix, cin), ref["xpt"].at[k])
    blocks("k1", ref["bd1"])

    def coefficients(first, second, inverse, gain, shift):
        mean = first * inverse
        scale = lax.rsqrt(second * inverse - mean * mean + epsilon)
        a = scale * gain
        return a, shift - mean * a, scale, -mean * scale

    tot = fetch(0, 4)
    inv_full, inv_half = 1.0 / tot[2], 1.0 / tot[3]
    n1 = coefficients(tot[0], tot[1], inv_full, vector("g1"), vector("b1"))

    va = ref["va"]
    va[3:6, 0:1] = jnp.zeros((3, 1, side, width), bf16)

    def shifted(v, edge, amount):
        return jnp.where(edge, 0.0, pltpu.roll(v, amount, 0))

    for ab, (a, b) in enumerate(PHASES):

        def step(p, ab=ab, a=a, b=b):
            v = mask_row(a, b, p) * silu(line(R1[at_phase(ab, p)]) * n1[0] + n1[1])
            v = pixels(v)
            slot = (0, 1, 3, 4)[ab]
            va[slot, p + a] = v.astype(bf16)
            if b:
                va[slot + 1, p + a] = shifted(v, first_col, 1).astype(bf16)

        over_rows(step)
    taps1 = []
    for t in range(9):
        u, v = t // 3, t % 3
        slot = (0, 1, 3, 4)[2 * (u != 1) + (v != 1)] + (v == 0)
        taps1.append((va.at[slot], 1 if u == 2 else 0))

    def convolve(taps, weights, out):
        def half(h):
            cut = slice(h * span, (h + 1) * span)
            left = [flat(taps[t][0][taps[t][1] : taps[t][1] + side, :, cut]) for t in ORDER]
            return dot(jnp.concatenate(left, axis=1), weights[h])

        return with_moments(out, (half(h) for h in range(width // span)))

    c1 = ref["c1"]
    post(1, [*convolve(taps1, ref["bd1"], c1), *short_sums])
    blocks("k2", ref["bd2"])
    tot = fetch(1, 4)
    nc1 = coefficients(tot[0], tot[1], inv_half, vector("gg1"), vector("gb1"))
    ns = coefficients(tot[2], tot[3], inv_half, vector("sg1"), vector("sb1"))

    def excite(conv, norm, hidden, gated, sq, sq_form, sqb, ex, exb):
        def step(p):
            v = mask_row(0, 0, p) * silu(line(conv[p]) * norm[0] + norm[1])
            hidden[p] = pixels(v)
            return (v,)

        (total,) = over_rows(step, 1)
        pooled = total / half_count
        pre = small_dot(pooled, sq[...], sq_form) + sqb
        inner = silu(pre)
        gate = sigmoid(small_dot(inner, ex[...], dot) + exb)
        gate_wide = wide(gate)

        def step_two(p):
            gated[p] = pixels(line(hidden[p]) * gate_wide).astype(bf16)

        over_rows(step_two)
        return pooled, pre, inner, gate

    H1, ga1 = ref["H1"], ref["ga1"]
    kept1 = excite(
        c1, nc1, H1, ga1, need("sq1"), dot_nt, vec[VEC["sqb1"], 0:1, : plan.q1], need("ex1"), vec[VEC["exb1"], 0:1]
    )
    E1 = ref["E1"]
    post(2, dot_moments(E1, lines(ga1), need("e1")))
    transpose(lines(ga1), ref["ga1t"])
    blocks("k1", ref["bd1t"], True)
    tot = fetch(2)
    ne = coefficients(tot[0], tot[1], inv_half, vector("eg1"), vector("eb1"))
    ent = ref["ent"]
    both_shifts = ne[1] + ns[1]

    def step(p):
        v = line(E1[p]) * ne[0] + line(SC[p]) * ns[0] + both_shifts
        ent[p] = pixels(mask_row(0, 0, p) * silu(v)).astype(bf16)

    over_rows(step)

    def send_out(source, out, rows, target, steps=None):
        for k in range(R // plan.copies) if steps is None else steps:
            t = lax.rem(r + plan.copies * k, R)
            there = ref[out].at[0, mine, 0] if out == "act" else ref[out].at[mine, 0]
            here = source.at[pl.ds(t * rows, rows)]
            copy = pltpu.make_async_remote_copy(
                src_ref=here,
                dst_ref=there,
                send_sem=ref[out + "_s"].at[target, k],
                recv_sem=ref[out + "_r"].at[mine],
                device_id=(target, i, t),
                device_id_type=MESH,
            )
            if k:
                copy.start()
                waits.append(copy.wait_send)
            else:
                local = pltpu.make_async_copy(here, there, ref[out + "_r"].at[mine])

                @pl.when(s == target)
                def _():
                    local.start()

                @pl.when(s != target)
                def _():
                    copy.start()

                def finish(copy=copy):
                    @pl.when(s != target)
                    def _():
                        copy.wait_send()

                waits.append(finish)

    send_out(ent, "act", plan.hrows, 0)

    R2 = ref["R2"]
    post(3, dot_moments(R2, lines(ent), need("w2")))
    transpose(lines(ent), ref["entt"])
    tot = fetch(3)
    n2 = coefficients(tot[0], tot[1], inv_half, vector("g2"), vector("b2"))
    vb = ref["vb"]
    vb[:, 0:1] = jnp.zeros((3, 1, side, width), bf16)
    vb[:, side + 1 :] = jnp.zeros((3, 1, side, width), bf16)

    def three(out, p, v):
        out[0, p + 1] = shifted(v, first_col, 1).astype(bf16)
        out[1, p + 1] = v.astype(bf16)
        out[2, p + 1] = shifted(v, last_col, side - 1).astype(bf16)

    def step(p):
        three(vb, p, pixels(mask_row(0, 0, p) * silu(line(R2[p]) * n2[0] + n2[1])))

    over_rows(step)
    taps2 = [(vb.at[t % 3], t // 3) for t in range(9)]
    c2 = ref["c2"]
    post(4, convolve(taps2, ref["bd2"], c2))
    blocks("k2", ref["bd2t"], True)
    tot = fetch(4)
    nc2 = coefficients(tot[0], tot[1], inv_half, vector("gg2"), vector("gb2"))
    H2, ga2 = ref["H2"], ref["ga2"]
    kept2 = excite(
        c2, nc2, H2, ga2, need("sq2"), dot, vec[VEC["sqb2"], 0:1, : plan.q2], need("ex2"), vec[VEC["exb2"], 0:1]
    )
    E2 = ref["E2"]
    post(5, dot_moments(E2, lines(ga2), need("e2")))
    transpose(lines(ga2), ref["ga2t"])
    for d in range(R):
        arrived("og", plan.hrows, 1, d)
    tot = fetch(5)
    ne2 = coefficients(tot[0], tot[1], inv_half, vector("eg2"), vector("eb2"))
    leave, D, og = ref["leave"], ref["D"], ref["og_in"]

    def step(p):
        e = line(E2[p])
        v = e * ne2[0] + ne2[1] + line(ent[p])
        sg = sigmoid(v)
        m = mask_row(0, 0, p)
        leave[p] = pixels(m * v * sg).astype(bf16)
        g = line(og[p]) * m * (sg * (1.0 + v * (1.0 - sg)))
        D[p] = pixels(g)
        return g, g * (e * ne2[2] + ne2[3])

    parts = over_rows(step, 2)
    vec_grads["eb2"], vec_grads["eg2"] = parts
    post(6, parts)
    send_out(leave, "act", plan.hrows, 1)

    def back_rule(sums, inverse, gain, norm):
        a = gain * norm[2]
        k0 = a * (sums[0] + norm[3] * sums[1]) * inverse
        return a, k0, a * norm[2] * sums[1] * inverse

    def back_excite(dg, kept, hidden, conv, norm, sq, sq_form, ex, out):
        pooled, pre, inner, gate = kept

        def step(p):
            return (line(dg[p]) * line(hidden[p]),)

        (dgate,) = over_rows(step, 1)
        dpre = dgate * gate * (1.0 - gate)
        dsq = small_dot(dpre, ex[...], dot_nt) * slope(pre)
        dpool = wide(small_dot(dsq, sq[...], sq_form) / half_count)
        gate_wide = wide(gate)

        def step_two(p):
            v = line(conv[p])
            g = (line(dg[p]) * gate_wide + dpool) * mask_row(0, 0, p)
            g = g * slope(v * norm[0] + norm[1])
            out[p] = pixels(g)
            return g, g * (v * norm[2] + norm[3])

        return over_rows(step_two, 2), dpre, dsq

    def excite_grads(name, kept, dpre, dsq):
        pooled, pre, inner, gate = kept
        put("sq" + name, small_outer(dsq, pooled))
        put("ex" + name, small_outer(inner, dpre))
        vec_grads["exb" + name] = dpre
        count = dsq.shape[1]
        eye = (
            lax.broadcasted_iota(jnp.int32, (count, width), 0)
            == lax.broadcasted_iota(jnp.int32, (count, width), 1)
        ).astype(f32).astype(bf16)
        vec_grads["sqb" + name] = small_dot(dsq, eye, dot)

    def turn(gradient_ref, start):
        out = []
        for h in range(width // span):
            piece = flat(gradient_ref[start : start + side, :, h * span : (h + 1) * span])
            out.append(piece.astype(f32).T.astype(bf16))
        return out

    d1, dg, GR = ref["d1"], ref["dg"], ref["GR"]
    tot = fetch(6)
    rule = back_rule((tot[0], tot[1]), inv_half, vector("eg2"), ne2)

    def step(p):
        v = rule[0] * line(D[p]) - mask_row(0, 0, p) * (rule[1] + rule[2] * line(E2[p]))
        d1[p] = pixels(v).astype(bf16)

    over_rows(step)
    full_dot(dg, lines(d1), need("e2"), dot_nt)
    parts, dpre, dsq = back_excite(dg, kept2, H2, c2, nc2, need("sq2"), dot_nt, need("ex2"), GR)
    vec_grads["gb2"], vec_grads["gg2"] = parts
    post(7, parts)
    put("e2", dot(ref["ga2t"][...], lines(d1)))
    excite_grads("2", kept2, dpre, dsq)
    pump(0)
    tot = fetch(7)
    rule = back_rule((tot[0], tot[1]), inv_half, vector("gg2"), nc2)
    vd = ref["vd"]
    vd[:, 0:1] = jnp.zeros((3, 1, side, width), bf16)
    vd[:, side + 1 :] = jnp.zeros((3, 1, side, width), bf16)

    def step(p):
        v = rule[0] * line(GR[p]) - mask_row(0, 0, p) * (rule[1] + rule[2] * line(c2[p]))
        three(vd, p, pixels(v))

    over_rows(step)

    def convolve_back(taps, first, weights, out):
        for h in range(width // span):
            cut = slice(h * span, (h + 1) * span)
            left = [flat(var[start : start + side, :, cut]) for var, start in taps]
            rows = slice(first * span, (first + len(taps)) * span)
            acc = dot(jnp.concatenate(left, axis=1), weights[h, rows])
            out[:, :, cut] = acc.reshape(side, side, span)

    DA = ref["DA"]
    convolve_back(
        [(vd.at[2 - t % 3], 2 - t // 3) for t in ORDER],
        0,
        ref["bd2t"],
        DA.at[0],
    )

    def step(p):
        v = line(R2[p])
        g = line(DA[0, p]) * mask_row(0, 0, p) * slope(v * n2[0] + n2[1])
        GR[p] = pixels(g)
        return g, g * (v * n2[2] + n2[3])

    parts = over_rows(step, 2)
    vec_grads["b2"], vec_grads["g2"] = parts
    post(8, parts)
    pump(0)
    groups_grad("k2", taps2, turn(vd.at[1], 1))
    tot = fetch(8)
    rule = back_rule((tot[0], tot[1]), inv_half, vector("g2"), n2)

    def step(p):
        v = rule[0] * line(GR[p]) - mask_row(0, 0, p) * (rule[1] + rule[2] * line(R2[p]))
        d1[p] = pixels(v).astype(bf16)

    over_rows(step)
    full_dot(GR, lines(d1), need("w2"), dot_nt)
    pump(0)

    def step(p):
        e, sc = line(E1[p]), line(SC[p])
        g = line((D[p] + GR[p]).astype(bf16))
        g = g * mask_row(0, 0, p) * slope(e * ne[0] + sc * ns[0] + both_shifts)
        D[p] = pixels(g)
        return g, g * (e * ne[2] + ne[3]), g * (sc * ns[2] + ns[3])

    parts = over_rows(step, 3)
    vec_grads["eb1"], vec_grads["eg1"], vec_grads["sg1"] = parts
    vec_grads["sb1"] = parts[0]
    post(9, parts)
    put("w2", dot(ref["entt"][...], lines(d1)))
    pump(1, 0)
    tot = fetch(9, 3)
    rule_e = back_rule((tot[0], tot[1]), inv_half, vector("eg1"), ne)
    rule_s = back_rule((tot[0], tot[2]), inv_half, vector("sg1"), ns)
    d2 = ref["d2"]

    def step(p):
        g, m = line(D[p]), mask_row(0, 0, p)
        v = rule_e[0] * g - m * (rule_e[1] + rule_e[2] * line(E1[p]))
        d1[p] = pixels(v).astype(bf16)
        v = rule_s[0] * g - m * (rule_s[1] + rule_s[2] * line(SC[p]))
        d2[p] = pixels(v).astype(bf16)

    over_rows(step)
    full_dot(dg, lines(d1), need("e1"), dot_nt)
    pump(1)
    parts, dpre, dsq = back_excite(dg, kept1, H1, c1, nc1, need("sq1"), dot, need("ex1"), GR)
    vec_grads["gb1"], vec_grads["gg1"] = parts
    post(10, parts)
    put("e1", dot(ref["ga1t"][...], lines(d1)))
    put("s1", dot_tn(even[...].reshape(pix, cin), lines(d2)))
    excite_grads("1", kept1, dpre, dsq)
    pump(2, 1)
    tot = fetch(10)
    rule = back_rule((tot[0], tot[1]), inv_half, vector("gg1"), nc1)

    def step(p):
        v = rule[0] * line(GR[p]) - mask_row(0, 0, p) * (rule[1] + rule[2] * line(c1[p]))
        three(vd, p, pixels(v))

    over_rows(step)
    pump(0)
    sums = []
    for ab, (a, b) in enumerate(PHASES):
        chosen = []
        first = (0, 1, 3, 5)[ab]
        for t in ORDER[first : first + (1, 2, 2, 4)[ab]]:
            chosen.append((vd.at[2 if t % 3 == 0 else 1], 2 if t // 3 == 0 else 1))
        convolve_back(chosen, first, ref["bd1t"], DA.at[ab])

        def step(p, ab=ab, a=a, b=b):
            v = line(R1[at_phase(ab, p)])
            g = line(DA[ab, p]) * mask_row(a, b, p) * slope(v * n1[0] + n1[1])
            DA[ab, p] = pixels(g)
            return g, g * (v * n1[2] + n1[3])

        sums.append(over_rows(step, 2))
        if ab == 1:
            pump(2, 1)
        elif ab == 3:
            pump(0)
    parts = (sum(x[0] for x in sums), sum(x[1] for x in sums))
    vec_grads["b1"], vec_grads["g1"] = parts
    post(11, parts)
    pump(2)
    groups_grad("k1", taps1, turn(vd.at[1], 1))
    ids = lax.broadcasted_iota(jnp.int32, (VEC_ROWS, width), 0)
    value = jnp.zeros((VEC_ROWS, width), f32)
    for name, at in VEC.items():
        value = jnp.where(ids == at, jnp.broadcast_to(vec_grads[name], value.shape), value)
    put(VECTORS, value)
    pump(3, 2, 0)
    tot = fetch(11)
    rule = back_rule((tot[0], tot[1]), inv_full, vector("g1"), n1)
    dr = ref["dr"]
    for ab, (a, b) in enumerate(PHASES):

        def step(p, ab=ab, a=a, b=b):
            v = rule[0] * line(DA[ab, p])
            v = v - mask_row(a, b, p) * (rule[1] + rule[2] * line(R1[at_phase(ab, p)]))
            dr[at_phase(ab, p)] = pixels(v).astype(bf16)

        over_rows(step)
    total = None
    for k in range(bands):
        term = dot(ref["xpt"][k], dr[k].reshape(pix, width))
        total = term if total is None else total + term
    put("w1", total)
    pump(4, 3, 1)
    cut = cin // 2
    ref["dxo0"][...] = jnp.zeros((2 * side, plan.cols, 128), bf16)
    ref["dxo1"][...] = jnp.zeros((2 * side, plan.cols, 128), bf16)
    stepwise = plan.each == bands
    for d in [*range(1, bands), 0]:
        k = lax.rem(r + plan.copies * d, R) * plan.rows // band if stepwise else d
        for part in range(2):
            dxo = ref[f"dxo{part}"]
            rows = slice(part * cut, (part + 1) * cut)
            v = dot_nt(dr[k].reshape(pix, width), need("w1")[rows, :])
            w = dot_nt(
                d2[pl.ds(k * bhalf, bhalf)].reshape(bhalf * side, width), need("s1")[rows, :]
            )
            v = jnp.concatenate([v[: bhalf * side] + w, v[bhalf * side :]], axis=0)
            v = dot(ref["unsort"][...], v.astype(bf16)).astype(bf16)
            dxo[pl.ds(k * band, band), :, :cut] = v.reshape(band, plan.cols, cut)
            if stepwise:
                send_out(dxo, "dx", plan.rows, part, (d,))
        pump(*((4, 3, 2, 1), (4, 3, 1), (4, 3, 2), (1, 0))[(d - 1) % 4])
    if not stepwise:
        send_out(ref["dxo0"], "dx", plan.rows, 0)
        send_out(ref["dxo1"], "dx", plan.rows, 1)
    for _ in range(9):
        pump()
    for wait in waits:
        wait()
    for m in range(plan.M):
        t = (m % plan.each) * plan.copies + lax.rem(r, plan.copies)
        for out in ("act", "dx"):
            there = ref[out].at[0, m, 0] if out == "act" else ref[out].at[m, 0]
            pltpu.make_async_copy(there, there, ref[out + "_r"].at[m]).wait()


WEIGHTS = ("w1", "k1", "k2", "sq1", "ex1", "e1", "s1", "w2", "sq2", "ex2", "e2")


def run_main(plan, arrays):
    side, width, cin = plan.side, plan.width, plan.cin
    wide = 4 * plan.gw
    field = (side, side, width)
    scratch = {
        "x_in": pltpu.VMEM((2 * side, plan.cols, cin), bf16),
        "og_in": pltpu.VMEM(field, bf16),
        "st": pltpu.VMEM((EXCHANGES, plan.I, 2, 8, 128), f32),
        "hm": pltpu.VMEM((plan.pix, 128), f32),
        "cm": pltpu.VMEM((2, side, width), f32),
        **{
            name: pltpu.VMEM((width // wide, plan.taps * wide, wide), bf16)
            for name in ("bd1", "bd2", "bd1t", "bd2t")
        },
        "xpt": pltpu.VMEM((plan.bands, cin, plan.pix), bf16),
        **{name: pltpu.VMEM((width, plan.pix), bf16) for name in ("ga1t", "ga2t", "entt")},
        "sort": pltpu.VMEM((plan.pix, plan.pix), bf16),
        "unsort": pltpu.VMEM((plan.pix, plan.pix), bf16),
        "xp": pltpu.VMEM((plan.bands, 2 * plan.band, side, cin), bf16),
        "R1": pltpu.VMEM((plan.bands, 2 * plan.band, side, width), f32),
        "va": pltpu.VMEM((6, side + 1, side, width), bf16),
        "vb": pltpu.VMEM((3, side + 2, side, width), bf16),
        "vd": pltpu.VMEM((3, side + 2, side, width), bf16),
        "DA": pltpu.VMEM((4,) + field, f32),
        "dr": pltpu.VMEM((plan.bands, 2 * plan.band, side, width), bf16),
        "dxo0": pltpu.VMEM((2 * side, plan.cols, 128), bf16),
        "dxo1": pltpu.VMEM((2 * side, plan.cols, 128), bf16),
    }
    for name in ("SC", "H1", "E1", "R2", "H2", "E2", "D", "GR"):
        scratch[name] = pltpu.VMEM(field, f32)
    for name in ("c1", "ga1", "ent", "c2", "ga2", "leave", "d1", "d2", "dg"):
        scratch[name] = pltpu.VMEM(field, bf16)
    for name in ("x", "og"):
        scratch[name + "_s"] = pltpu.SemaphoreType.DMA((max(plan.R - 1, 1),))
        scratch[name + "_r"] = pltpu.SemaphoreType.DMA((plan.R,))
    scratch["st_s"] = pltpu.SemaphoreType.DMA((EXCHANGES, max(plan.I - 1, 1)))
    scratch["st_r"] = pltpu.SemaphoreType.DMA((EXCHANGES, plan.I))
    for name in ("act", "dx"):
        scratch[name + "_s"] = pltpu.SemaphoreType.DMA((2, plan.R // plan.copies))
        scratch[name + "_r"] = pltpu.SemaphoreType.DMA((plan.M,))
    for name in NAMES + WEIGHTS:
        scratch[name + "_v"] = pltpu.VMEM(arrays[name].shape, bf16)
    scratch["vec"] = pltpu.VMEM((len(NAMES), 8, width), f32)
    scratch["loads"] = pltpu.SemaphoreType.DMA((len(NAMES + WEIGHTS),))
    scratch["local"] = pltpu.VMEM((plan.blocks, 16, 128), bf16)
    for level, room in enumerate(plan.rooms):
        scratch[f"got{level}"] = pltpu.VMEM((room, 16, 128), bf16)
        if level:
            scratch[f"sum{level - 1}"] = pltpu.VMEM((room, 16, 128), bf16)
    most = max(plan.sizes.values())
    for name in ("rs", "ag"):
        scratch[name + "_s"] = pltpu.SemaphoreType.DMA((len(plan.streams), 4, most - 1))
        scratch[name + "_r"] = pltpu.SemaphoreType.DMA((len(plan.streams), 4, most))
    inputs = ("x", "og", "vr", "vc") + NAMES + WEIGHTS
    outputs = ("act", "dx", "grads")
    names = inputs + outputs + tuple(scratch)
    any_space = pl.BlockSpec(memory_space=pl.ANY)
    smem = pl.BlockSpec(memory_space=pltpu.SMEM)
    vmem = pl.BlockSpec(memory_space=pltpu.VMEM)
    return pl.pallas_call(
        functools.partial(main_kernel, plan, names),
        out_shape=(
            jax.ShapeDtypeStruct((1, plan.M, 1, plan.hrows, side, width), bf16),
            jax.ShapeDtypeStruct((plan.M, 1, plan.rows, plan.cols, 128), bf16),
            jax.ShapeDtypeStruct((plan.blocks, 16, 128), bf16),
        ),
        in_specs=[any_space, any_space, smem, smem] + [any_space] * (len(NAMES) + len(WEIGHTS)),
        out_specs=(any_space, any_space, vmem),
        scratch_shapes=list(scratch.values()),
        compiler_params=pltpu.CompilerParams(
            collective_id=0, has_side_effects=True, vmem_limit_bytes=60 * 1024 * 1024
        ),
        name="blocks",
    )(*[arrays[name] for name in inputs])


OUTS = (
    "w1", "g1", "b1", "k1", "gg1", "gb1", "sq1", "sqb1", "ex1", "exb1", "e1", "eg1", "eb1",
    "s1", "sg1", "sb1", "w2", "g2", "b2", "k2", "gg2", "gb2", "sq2", "sqb2", "ex2", "exb2",
    "e2", "eg2", "eb2",
)


def unpack_kernel(plan, source, act_in, dx_in, *rest):
    count = len(OUTS) + 2
    outs, bufs, loads_at, sems = rest[:count], rest[count:-4], rest[-4:-2], rest[-1]
    through = rest[-2]
    copies = []
    for k, whole in enumerate((act_in, dx_in)):
        copies.append(pltpu.make_async_copy(whole, bufs[k - 2], through.at[k]))
        copies[-1].start()
    loads = []
    order = sorted(plan.starts, key=lambda name: plan.starts[name])
    order = [name for name in order if name not in (VECTORS, LAST_TAP)] + [VECTORS, LAST_TAP]
    blocks = loads_at[0]
    for k, name in enumerate(order):
        start, per_tile = plan.starts[name]
        part = pl.ds(start, per_tile * (plan.width // 128))
        loads.append(pltpu.make_async_copy(source.at[part], blocks.at[part], loads_at[1].at[k]))
        loads[-1].start()

    def tile(name, k):
        start, per_tile = plan.starts[name]
        at = start + k * per_tile
        return blocks[at : at + per_tile].reshape(16 * per_tile, 128).astype(f32)

    tiles = plan.width // 128
    vec = None
    turn = [OUTS.index(name) for name in order[:-2]]
    turn += [k for k, name in enumerate(OUTS) if name in VEC]
    for position, k in enumerate(turn):
        name, out = OUTS[k], bufs[k]
        if position < len(loads) - 1:
            loads[position].wait()
        if position < 2:
            copies[position].wait()
            copies[position] = pltpu.make_async_copy(
                bufs[position - 2], outs[position], sems.at[position]
            )
            copies[position].start()
        if name in VEC and vec is None:
            vec = jnp.concatenate([tile(VECTORS, k) for k in range(tiles)], axis=1)
        if name in VEC:
            size = out.shape[0]
            out[...] = vec[VEC[name] : VEC[name] + 1, :size].reshape(size)
        elif name[0] == "k":

            def run(t, carry, name=name, out=out, last_tap=False):
                for lane in range(tiles):
                    start, per_tile = plan.starts[name]
                    at = start + lane * per_tile + t * (plan.gw // 16)
                    if last_tap:
                        start, per_tile = plan.starts[LAST_TAP]
                        at = start + lane * per_tile
                    piece = blocks[pl.ds(at, plan.gw // 16)].reshape(plan.gw, 128)
                    piece = piece.astype(f32).T
                    for j in range(128 // plan.gw):
                        group = lane * (128 // plan.gw) + j
                        out[t, group, :, : plan.gw] = piece[j * plan.gw : (j + 1) * plan.gw]
                return carry

            if name == "k2":
                loads[order.index(LAST_TAP)].wait()
                lax.fori_loop(0, plan.taps - 1, run, 0)
                run(plan.taps - 1, 0, last_tap=True)
            else:
                lax.fori_loop(0, plan.taps, run, 0)
        elif name == "sq2":
            for lane in range(tiles):
                out[128 * lane : 128 * lane + 128] = tile(name, lane).T
        else:
            for lane in range(tiles):
                out[:, 128 * lane : 128 * lane + 128] = tile(name, lane)
        copies.append(pltpu.make_async_copy(out, outs[k + 2], sems.at[k + 2]))
        copies[-1].start()
    for copy in copies:
        copy.wait()


def unpack(plan, act, dx, grads, weights):
    shapes = []
    for name, w in zip(OUTS, weights):
        shape = w.shape[:3] + (128,) if name[0] == "k" else w.shape
        shapes.append(jax.ShapeDtypeStruct(shape, f32))
    any_space = pl.BlockSpec(memory_space=pl.ANY)
    return pl.pallas_call(
        functools.partial(unpack_kernel, plan),
        out_shape=[jax.ShapeDtypeStruct(v.shape, v.dtype) for v in (act, dx)] + shapes,
        in_specs=[any_space] * 3,
        out_specs=[any_space] * (len(shapes) + 2),
        scratch_shapes=[pltpu.VMEM(v.shape, v.dtype) for v in (*shapes, act, dx)]
        + [pltpu.VMEM(grads.shape, bf16), pltpu.SemaphoreType.DMA((len(plan.starts),))]
        + [pltpu.SemaphoreType.DMA((2,))]
        + [pltpu.SemaphoreType.DMA((len(shapes) + 2,))],
        compiler_params=pltpu.CompilerParams(vmem_limit_bytes=60 * 1024 * 1024),
        name="unpack",
    )(grads, act, dx)


def body(sizes, input_maps, valid_rows, valid_cols, *rest):
    weights, output_grad = rest[:-1], rest[-1]
    (w1, g1, b1, k1, gg1, gb1, sq1, sqb1, ex1, exb1, e1, eg1, eb1, s1, sg1, sb1) = weights[:16]
    (w2, g2, b2, k2, gg2, gb2, sq2, sqb2, ex2, exb2, e2, eg2, eb2) = weights[16:]
    turned = sq1.T
    plan = Plan(sizes, [v.shape for v in (input_maps, output_grad, w1, k1, turned, sq2)])
    vectors = (
        g1, b1, gg1, gb1, exb1, eg1, eb1, sg1, sb1, sqb1, g2, b2, gg2, gb2, exb2, eg2, eb2, sqb2,
    )
    arrays = dict(
        x=input_maps, og=output_grad, vr=valid_rows.T, vc=valid_cols.T, w1=w1,
        k1=k1, k2=k2,
        sq1=turned, ex1=ex1, e1=e1, s1=s1, w2=w2, sq2=sq2, ex2=ex2, e2=e2,
        **dict(zip(NAMES, vectors)),
    )
    act, dx, grads = run_main(plan, arrays)
    act, dx, *out = unpack(plan, act, dx, grads, weights[:6] + (turned,) + weights[7:])
    out[6] = out[6].T
    for at in (3, 19):
        out[at] = out[at][..., : plan.gw]
    dx = dx[..., : plan.cin // 2]
    return (act, dx, *out)


def solution(mesh):
    tiled = P(None, "img", "row", None, None)
    image = P(None, "img")
    sizes = tuple(mesh.shape[name] for name in ("section", "img", "row"))
    return jax.shard_map(
        functools.partial(body, sizes),
        mesh=mesh,
        in_specs=(tiled, image, image) + (P(),) * 29 + (tiled,),
        out_specs=(
            P("section", None, "img", "row", None, None),
            P(None, "img", "row", None, "section"),
        )
        + (P(),) * 29,
        check_vma=False,
    )
```

```python
import functools

import jax
import jax.numpy as jnp
from jax import lax
from jax.experimental import pallas as pl
from jax.experimental.pallas import tpu as pltpu
from jax.sharding import PartitionSpec as P

epsilon = 1e-05
f32 = jnp.float32
bf16 = jnp.bfloat16
MESH = pl.DeviceIdType.MESH
PHASES = ((0, 0), (0, 1), (1, 0), (1, 1))
ORDER = (4, 3, 5, 1, 7, 0, 2, 6, 8)
EXCHANGES = 12
NAMES = (
    "g1", "b1", "gg1", "gb1", "exb1", "eg1", "eb1", "sg1", "sb1", "sqb1",
    "g2", "b2", "gg2", "gb2", "exb2", "eg2", "eb2", "sqb2",
)
VEC = {name: k for k, name in enumerate(NAMES)}
VEC_ROWS = 32
VECTORS = "vec"
LAST_TAP = "k9"


def segments_of(cin, width, taps, group, sq1, sq2, devices):
    layout = (
        (("e2", width), ("sq2", sq2), ("ex2", sq2)),
        (("k2", (taps - 1) * group), ("w2", width)),
        (("e1", width), ("s1", cin), ("sq1", sq1), ("ex1", sq1), (LAST_TAP, group)),
        (("k1", taps * group), (VECTORS, VEC_ROWS)),
        (("w1", cin),),
    )
    starts, segments, at = {}, [], 0
    for parts in layout:
        base = at
        for name, rows in parts:
            starts[name] = (at, rows // 16)
            at += rows // 16 * (width // 128)
        units = -(-(at - base) // devices)
        first = units // 2 * devices if len(segments) < len(layout) - 1 else 0
        segments.append((base, units * devices, at, first))
        at = base + units * devices
    return starts, tuple(segments), at


def sigmoid(v):
    return 0.5 * jnp.tanh(0.5 * v) + 0.5


def silu(v):
    return v * sigmoid(v)


def slope(v):
    s = sigmoid(v)
    return s * (1.0 + v * (1.0 - s))


def dot(left, right):
    return jnp.dot(left, right, preferred_element_type=f32)


def dot_nt(left, right):
    return lax.dot_general(left, right, (((1,), (1,)), ((), ())), preferred_element_type=f32)


def dot_tn(left, right):
    return lax.dot_general(left, right, (((0,), (0,)), ((), ())), preferred_element_type=f32)


def parts_of(v):
    high = v.astype(bf16).astype(f32)
    return high, v - high


def stacked(rows, width):
    ids = lax.broadcasted_iota(jnp.int32, (16, width), 0)
    total = jnp.zeros((16, width), f32)
    for k, row in enumerate(rows):
        total = jnp.where(ids == k, jnp.broadcast_to(row, (16, width)), total)
    return total.astype(bf16)


def small_dot(row, weight, form):
    out = form(stacked(parts_of(row), row.shape[1]), weight)
    return out[0:1] + out[1:2]


def small_outer(left, right):
    lh, ll = parts_of(left)
    rh, rl = parts_of(right)
    return dot_tn(
        stacked((lh, ll, lh, ll), left.shape[1]), stacked((rh, rh, rl, rl), right.shape[1])
    )


def fold(v):
    return v[0] + v[1]


def column(acc):
    return jnp.sum(acc, axis=0, keepdims=True)


class Plan:
    def __init__(self, mesh_sizes, args):
        self.S, self.I, self.R = mesh_sizes
        x, og, w1, k1, sq1, sq2 = args
        self.M, _, self.rows, self.cols, self.cin = x
        _, _, self.hrows, self.side, self.width = og
        self.taps, self.groups, self.gw, _ = k1
        self.q1, self.q2 = sq1[0], sq2[1]
        self.each = self.M // self.S
        self.copies = self.R // self.each
        self.pix = self.side * self.side
        self.band = self.pix // self.cols
        self.bands = 2 * self.side // self.band
        self.starts, self.segments, self.blocks = segments_of(
            self.cin, self.width, self.taps, self.gw, self.q1, self.q2, self.S * self.I * self.R
        )
        self.X = 1
        while self.X * self.X < self.R:
            self.X *= 2
        self.Y = self.R // self.X
        self.sizes = {"s": self.S, "x": self.X, "y": self.Y, "r": self.R, "i": self.I}
        self.streams = []
        self.members = []
        self.rooms = [0] * 4
        for base, size, _, first in self.segments:
            halves = [(base, first, "sxyi"), (base + first, size - first, "syxi")]
            if not first:
                halves = [(base, size, "sri")]
            self.members.append(range(len(self.streams), len(self.streams) + len(halves)))
            for start, count, order in halves:
                self.streams.append((start, count, order, tuple(self.rooms)))
                for level, axis in enumerate(order):
                    self.rooms[level] += count
                    count //= self.sizes[axis]

    def piece(self, stream, level):
        _, size, order, _ = self.streams[stream]
        for axis in order[: level + 1]:
            size //= self.sizes[axis]
        return size


def main_kernel(plan, names, *refs):
    ref = dict(zip(names, refs))
    S, I, R = plan.S, plan.I, plan.R
    side, width, pix, cin = plan.side, plan.width, plan.pix, plan.cin
    half_width = width // 2
    s, i, r = lax.axis_index("section"), lax.axis_index("img"), lax.axis_index("row")
    mine = s * plan.each + r // plan.copies
    waits = []

    barrier = pltpu.get_barrier_semaphore()
    peers = []
    for ds in range(S):
        for dr in range(R):
            if ds or dr:
                peers.append((lax.rem(s + ds, S), i, lax.rem(r + dr, R)))
    for di in range(1, I):
        peers.append((s, lax.rem(i + di, I), r))
    for peer in peers:
        pl.semaphore_signal(barrier, inc=1, device_id=peer, device_id_type=MESH)

    own = []
    loads = {}

    def load(*which):
        for name in which:
            at = (NAMES + WEIGHTS).index(name)
            loads[name] = pltpu.make_async_copy(ref[name], ref[name + "_v"], ref["loads"].at[at])
            loads[name].start(priority=int(name[0] == "k"))

    def need(name):
        if name in loads:
            loads.pop(name).wait()
        return ref[name + "_v"]

    load("w1", "g1", "b1", "k1", "k2")
    for name, rows in (("x", plan.rows), ("og", plan.hrows)):
        copy = pltpu.make_async_copy(
            ref[name].at[mine, 0],
            ref[name + "_in"].at[pl.ds(r * rows, rows)],
            ref[name + "_r"].at[r],
        )
        copy.start()
        own.append(copy)
    pl.semaphore_wait(barrier, len(peers))
    for name, rows in (("x", plan.rows), ("og", plan.hrows)):
        for d in range(1, R):
            t = lax.rem(r + d, R)
            copy = pltpu.make_async_remote_copy(
                src_ref=ref[name].at[s * plan.each + t // plan.copies, 0],
                dst_ref=ref[name + "_in"].at[pl.ds(r * rows, rows)],
                send_sem=ref[name + "_s"].at[d - 1],
                recv_sem=ref[name + "_r"].at[r],
                device_id=(s, i, t),
                device_id_type=MESH,
            )
            copy.start()
            waits.append(copy.wait_send)

    load("s1", *NAMES[2:], "sq1", "ex1", "e1", "w2", "sq2", "ex2", "e2")

    def arrived(name, rows, position, d):
        if d == 0:
            own[position].wait()
        else:
            t = lax.rem(r + d, R)
            there = ref[name + "_in"].at[pl.ds(t * rows, rows)]
            pltpu.make_async_remote_copy(
                src_ref=there,
                dst_ref=there,
                send_sem=ref[name + "_s"].at[d - 1],
                recv_sem=ref[name + "_r"].at[t],
                device_id=(s, i, t),
                device_id_type=MESH,
            ).wait_recv()

    st = ref["st"]

    def pairs_of(k):
        return 2 if k in (0, 1, 9) else 1

    def stats_copy(k, d, slot):
        return pltpu.make_async_remote_copy(
            src_ref=st.at[k, slot, pl.ds(0, pairs_of(k))],
            dst_ref=st.at[k, slot, pl.ds(0, pairs_of(k))],
            send_sem=ref["st_s"].at[k, d - 1],
            recv_sem=ref["st_r"].at[k, slot],
            device_id=(s, lax.rem(i + d, I), r),
            device_id_type=MESH,
        )

    def post(k, rows):
        ids = lax.broadcasted_iota(jnp.int32, (8, 128), 0)
        rows = [*rows, *([None] * (len(rows) % 2))]
        for pair in range(len(rows) // 2):
            value = jnp.zeros((8, 128), f32)
            for j in range(8):
                row = rows[2 * pair + j // 4]
                if row is not None:
                    piece = row[:, 128 * (j % 4) : 128 * (j % 4) + 128]
                    value = jnp.where(ids == j, jnp.broadcast_to(piece, (8, 128)), value)
            st[k, i, pair] = value
        for d in range(1, I):
            stats_copy(k, d, i).start()

    def fetch(k, count=2):
        for d in range(1, I):
            stats_copy(k, d, i).wait_send()
            stats_copy(k, d, lax.rem(i + d, I)).wait_recv()
        out = []
        for pair in range((count + 1) // 2):
            value = st[k, 0, pair]
            for j in range(1, I):
                value = value + st[k, j, pair]
            for half in range(2):
                out.append(
                    jnp.concatenate(
                        [
                            jnp.broadcast_to(value[4 * half + j : 4 * half + j + 1], (8, 128))
                            for j in range(4)
                        ],
                        axis=1,
                    )
                )
        return out

    vec = ref["vec"]

    def keep_vectors():
        for name in NAMES:
            row = need(name)[...].astype(f32)
            size = row.shape[0]
            vec[VEC[name], :, :size] = jnp.broadcast_to(row.reshape(1, size), (8, size))

    def vector(name):
        return vec[VEC[name]]

    vr, vc = ref["vr"][0, mine], ref["vc"][0, mine]
    q_ids = lax.broadcasted_iota(jnp.int32, (side, width), 0)
    first_col, last_col = q_ids == 0, q_ids == side - 1
    cm = ref["cm"]
    for b in range(2):
        cm[b] = (2 * q_ids + b < vc).astype(f32)

    def line(value):
        return value.astype(f32).reshape(2, 8, width)

    def pixels(value):
        return value.reshape(side, width)

    def mask_row(a, b, p):
        return line(cm[b]) * (2 * p + a < vr).astype(f32)

    def wide(row):
        return jnp.broadcast_to(row, (8, width))

    row_count = jnp.full((1, width), vr * vc, jnp.int32).astype(f32)
    half_count = jnp.full((1, width), ((vr + 1) // 2) * ((vc + 1) // 2), jnp.int32).astype(f32)

    def over_rows(step, *accs):
        init = tuple(jnp.zeros((8, width), f32) for _ in range(accs[0] if accs else 0))

        def run(p, carry):
            out = step(p)
            if not carry:
                return carry
            return tuple(c + fold(o) for c, o in zip(carry, out))

        return tuple(column(c) for c in lax.fori_loop(0, side, run, init, unroll=16))

    def full_dot(out, left, weight, form=dot):
        wide = out.shape[-1]
        step = min(256, wide)
        for h in range(wide // step):
            cut = slice(h * step, h * step + step)
            w = weight[:, cut] if form is dot else weight[cut, :]
            out[:, :, cut] = form(left, w).reshape(side, side, step).astype(out.dtype)

    hm = ref["hm"]
    for p in range(side):
        hm[p * side : (p + 1) * side] = cm[0][:, :128] * (2 * p < vr).astype(f32)

    def with_moments(out, products):
        sums = []
        for h, product in enumerate(products):
            span = product.shape[1]
            value = product.astype(out.dtype)
            out[:, :, h * span : (h + 1) * span] = value.reshape(side, side, span)
            value = value.astype(f32)
            valid = value * jnp.concatenate([hm[...]] * (span // 128), axis=1)
            sums.append(
                [
                    jnp.sum(x.reshape(pix // 8, 8, span), axis=0)
                    for x in (valid, valid * value)
                ]
            )
        return [column(jnp.concatenate(x, axis=1)) for x in zip(*sums)]

    def dot_moments(out, left, weight):
        return with_moments(
            out, (dot(left, weight[:, cut : cut + 256]) for cut in range(0, width, 256))
        )

    def flat(value):
        return value.reshape(pix, value.shape[-1])

    def lines(ref_, start=0):
        return flat(ref_[start : start + side])

    G, F = ref["local"], ref["grads"]
    lead = None if plan.copies == 1 else (lax.rem(r, plan.copies) == 0).astype(f32)

    def put(name, value, row=0, lane=0):
        if lead is not None:
            value = value * lead
        start, per_tile = plan.starts[name]
        count = value.shape[0] // 16
        for k in range(value.shape[1] // 128):
            piece = value[:, 128 * k : 128 * k + 128].astype(bf16).reshape(count, 16, 128)
            at = start + (lane // 128 + k) * per_tile + row // 16
            G[at : at + count] = piece

    X, Y = plan.X, plan.Y
    x, y = lax.rem(r, X), r // X
    axes = {
        "s": (S, s, lambda t: (t, i, r)),
        "r": (R, r, lambda t: (s, i, t)),
        "x": (X, x, lambda t: (s, i, y * X + t)),
        "y": (Y, y, lambda t: (s, i, t * X + x)),
        "i": (I, i, lambda t: (s, t, r)),
    }

    def scatter_source(stream, level):
        base, _, order, offsets = plan.streams[stream]
        if level == 0:
            return G, base
        return ref[f"sum{level - 1}"], offsets[level]

    def scatter_copies(stream, level, outgoing):
        base, size, order, offsets = plan.streams[stream]
        count, me, device = axes[order[level]]
        piece = plan.piece(stream, level)
        source, first = scatter_source(stream, level)
        for d in range(1, count):
            t = lax.rem(me + d, count)
            slot = me if outgoing else t
            copy = pltpu.make_async_remote_copy(
                src_ref=source.at[pl.ds(first + t * piece, piece)],
                dst_ref=ref[f"got{level}"].at[pl.ds(offsets[level] + slot * piece, piece)],
                send_sem=ref["rs_s"].at[stream, level, d - 1],
                recv_sem=ref["rs_r"].at[stream, level, slot],
                device_id=device(t),
                device_id_type=MESH,
            )
            if outgoing:
                copy.start()
                sent[stream].append(copy)
            else:
                copy.wait_recv()

    def add_up(stream, level):
        base, size, order, offsets = plan.streams[stream]
        count, me, _ = axes[order[level]]
        piece = plan.piece(stream, level)
        source, first = scatter_source(stream, level)
        got = ref[f"got{level}"]
        if level < len(order) - 1:
            out, at = ref[f"sum{level}"], offsets[level + 1]
        else:
            out, at = F, own_part(stream, len(order))
        step = next(k for k in (16, 12, 10, 9, 8, 7, 6, 5, 4, 3, 2, 1) if piece % k == 0)

        def run(k, carry):
            total = source[pl.ds(first + me * piece + k * step, step)].astype(f32)
            for d in range(1, count):
                t = lax.rem(me + d, count)
                total = total + got[pl.ds(offsets[level] + t * piece + k * step, step)].astype(f32)
            out[pl.ds(at + k * step, step)] = total.astype(bf16)
            return carry

        lax.fori_loop(0, piece // step, run, 0)

    def own_part(stream, depth):
        at, _, order, _ = plan.streams[stream]
        for level in range(depth):
            at = at + axes[order[level]][1] * plan.piece(stream, level)
        return at

    def gather_copies(stream, level, outgoing):
        count, me, device = axes[plan.streams[stream][2][level]]
        base = own_part(stream, level)
        piece = plan.piece(stream, level)
        for d in range(1, count):
            t = lax.rem(me + d, count)
            slot = me if outgoing else t
            there = F.at[pl.ds(base + slot * piece, piece)]
            copy = pltpu.make_async_remote_copy(
                src_ref=there,
                dst_ref=there,
                send_sem=ref["ag_s"].at[stream, level, d - 1],
                recv_sem=ref["ag_r"].at[stream, level, slot],
                device_id=device(t),
                device_id_type=MESH,
            )
            if outgoing:
                copy.start()
                sent[stream].append(copy)
            else:
                copy.wait_recv()

    done = [0] * len(plan.segments)
    started = []
    sent = [[] for _ in plan.streams]

    def pump(*which):
        for g in which or tuple(started):
            if g not in started:
                started.insert(0, g)
            k = done[g]
            depth = len(plan.streams[plan.members[g][0]][2])
            if k > 2 * depth:
                continue
            done[g] += 1
            if k == 0:
                base, size, used, _ = plan.segments[g]
                if used < base + size:
                    G[used : base + size] = jnp.zeros((base + size - used, 16, 128), bf16)
            for stream in plan.members[g]:
                if 1 <= k <= depth:
                    scatter_copies(stream, k - 1, False)
                    add_up(stream, k - 1)
                elif k > depth:
                    gather_copies(stream, 2 * depth - k, False)
                for copy in sent[stream]:
                    copy.wait_send()
                sent[stream] = []
                if k < depth:
                    scatter_copies(stream, k, True)
                elif k < 2 * depth:
                    gather_copies(stream, 2 * depth - 1 - k, True)

    vec_grads = {}

    gw = plan.gw
    span = 4 * gw
    def blocks(name, out, turned=False):
        kernels = need(name)
        shape = (span, gw) if turned else (gw, span)
        long = lax.broadcasted_iota(jnp.int32, shape, 0 if turned else 1)
        short = lax.broadcasted_iota(jnp.int32, shape, 1 if turned else 0)
        spread = (lax.rem(long, gw) == short).astype(f32).astype(bf16)
        row = lax.broadcasted_iota(jnp.int32, (span, span), 0) // gw
        col = lax.broadcasted_iota(jnp.int32, (span, span), 1) // gw
        for k, t in enumerate(ORDER):
            for h in range(width // span):
                piece = kernels[t, 4 * h : 4 * h + 4].reshape(span, gw)
                full = dot_nt(spread, piece) if turned else dot(piece, spread)
                out[h, k * span : (k + 1) * span] = jnp.where(row == col, full, 0.0).astype(bf16)

    def groups_grad(name, taps, turned):
        lane = lax.broadcasted_iota(jnp.int32, (gw, span), 1) // gw
        for t, (var, start) in enumerate(taps):
            for h in range(width // span):
                cut = slice(h * span, (h + 1) * span)
                res = dot(turned[h], flat(var[start : start + side, :, cut]))
                out = res[0:gw]
                for j in range(1, 4):
                    out = jnp.where(lane == j, res[j * gw : (j + 1) * gw], out)
                if name == "k2" and t == plan.taps - 1:
                    put(LAST_TAP, out, 0, h * span)
                else:
                    put(name, out, t * gw, h * span)

    band, bands = plan.band, plan.bands
    bhalf = band // 2
    out_id = lax.broadcasted_iota(jnp.int32, (pix, pix), 0)
    in_id = lax.broadcasted_iota(jnp.int32, (pix, pix), 1)

    def source(o):
        quarter = o // (bhalf * side)
        down = lax.rem(o, bhalf * side) // side
        return (2 * down + quarter // 2) * plan.cols + 2 * lax.rem(o, side) + lax.rem(quarter, 2)

    ref["sort"][...] = (source(out_id) == in_id).astype(f32).astype(bf16)
    ref["unsort"][...] = (source(in_id) == out_id).astype(f32).astype(bf16)

    xp, R1 = ref["xp"], ref["R1"]
    keep_vectors()

    def transpose(source, out):
        out[...] = source.astype(f32).T.astype(bf16)

    totals = [jnp.zeros((8, width), f32)] * 2
    by_band = plan.rows % band == 0
    if not by_band:
        for d in range(R):
            arrived("x", plan.rows, 0, d)
    for d in range(bands):
        if by_band:
            if d % (plan.rows // band) == 0:
                arrived("x", plan.rows, 0, d // (plan.rows // band))
            k = lax.rem(r * (plan.rows // band) + d, bands)
        else:
            k = d
        block = ref["x_in"][pl.ds(k * band, band)].reshape(pix, cin)
        block = dot(ref["sort"][...], block).astype(bf16)
        xp[k] = block.reshape(4 * bhalf, side, cin)
        full_dot(R1.at[k], block, need("w1"))
        for j in range(4 * bhalf):
            a, b = PHASES[j // bhalf]
            v = line(R1[k, j])
            mv = v * mask_row(a, b, k * bhalf + j % bhalf)
            totals = [totals[0] + fold(mv), totals[1] + fold(mv * v)]
    even = xp.at[:, 0:bhalf]

    def at_phase(ab, p):
        return p // bhalf, ab * bhalf + lax.rem(p, bhalf)

    post(0, [column(totals[0]), column(totals[1]), row_count, half_count])
    SC = ref["SC"]
    short_sums = dot_moments(SC, even[...].reshape(pix, cin), need("s1"))

    blocks("k1", ref["bd1"])

    def coefficients(first, second, inverse, gain, shift):
        mean = first * inverse
        scale = lax.rsqrt(second * inverse - mean * mean + epsilon)
        a = scale * gain
        return a, shift - mean * a, scale, -mean * scale

    tot = fetch(0, 4)
    inv_full, inv_half = 1.0 / tot[2], 1.0 / tot[3]
    n1 = coefficients(tot[0], tot[1], inv_full, vector("g1"), vector("b1"))

    va = ref["va"]
    va[3:6, 0:1] = jnp.zeros((3, 1, side, width), bf16)

    def shifted(v, edge, amount):
        return jnp.where(edge, 0.0, pltpu.roll(v, amount, 0))

    for ab, (a, b) in enumerate(PHASES):

        def step(p, ab=ab, a=a, b=b):
            v = mask_row(a, b, p) * silu(line(R1[at_phase(ab, p)]) * n1[0] + n1[1])
            v = pixels(v)
            slot = (0, 1, 3, 4)[ab]
            va[slot, p + a] = v.astype(bf16)
            if b:
                va[slot + 1, p + a] = shifted(v, first_col, 1).astype(bf16)

        over_rows(step)
    taps1 = []
    for t in range(9):
        u, v = t // 3, t % 3
        slot = (0, 1, 3, 4)[2 * (u != 1) + (v != 1)] + (v == 0)
        taps1.append((va.at[slot], 1 if u == 2 else 0))

    def convolve(taps, weights, out):
        def half(h):
            cut = slice(h * span, (h + 1) * span)
            left = [flat(taps[t][0][taps[t][1] : taps[t][1] + side, :, cut]) for t in ORDER]
            return dot(jnp.concatenate(left, axis=1), weights[h])

        return with_moments(out, (half(h) for h in range(width // span)))

    c1 = ref["c1"]
    post(1, [*convolve(taps1, ref["bd1"], c1), *short_sums])
    blocks("k2", ref["bd2"])
    tot = fetch(1, 4)
    nc1 = coefficients(tot[0], tot[1], inv_half, vector("gg1"), vector("gb1"))
    ns = coefficients(tot[2], tot[3], inv_half, vector("sg1"), vector("sb1"))

    def excite(conv, norm, hidden, gated, sq, sq_form, sqb, ex, exb):
        def step(p):
            v = mask_row(0, 0, p) * silu(line(conv[p]) * norm[0] + norm[1])
            hidden[p] = pixels(v)
            return (v,)

        (total,) = over_rows(step, 1)
        pooled = total / half_count
        pre = small_dot(pooled, sq[...], sq_form) + sqb
        inner = silu(pre)
        gate = sigmoid(small_dot(inner, ex[...], dot) + exb)
        gate_wide = wide(gate)

        def step_two(p):
            gated[p] = pixels(line(hidden[p]) * gate_wide).astype(bf16)

        over_rows(step_two)
        return pooled, pre, inner, gate

    H1, ga1 = ref["H1"], ref["ga1"]
    kept1 = excite(
        c1, nc1, H1, ga1, need("sq1"), dot_nt, vec[VEC["sqb1"], 0:1, : plan.q1], need("ex1"), vec[VEC["exb1"], 0:1]
    )
    E1 = ref["E1"]
    post(2, dot_moments(E1, lines(ga1), need("e1")))
    transpose(lines(ga1), ref["ga1t"])
    tot = fetch(2)
    ne = coefficients(tot[0], tot[1], inv_half, vector("eg1"), vector("eb1"))
    ent = ref["ent"]
    both_shifts = ne[1] + ns[1]

    def step(p):
        v = line(E1[p]) * ne[0] + line(SC[p]) * ns[0] + both_shifts
        ent[p] = pixels(mask_row(0, 0, p) * silu(v)).astype(bf16)

    over_rows(step)

    def send_out(source, out, rows, target, steps=None):
        for k in range(R // plan.copies) if steps is None else steps:
            t = lax.rem(r + plan.copies * k, R)
            there = ref[out].at[0, mine, 0] if out == "act" else ref[out].at[mine, 0]
            here = source.at[pl.ds(t * rows, rows)]
            copy = pltpu.make_async_remote_copy(
                src_ref=here,
                dst_ref=there,
                send_sem=ref[out + "_s"].at[target, k],
                recv_sem=ref[out + "_r"].at[mine],
                device_id=(target, i, t),
                device_id_type=MESH,
            )
            if k:
                copy.start()
                waits.append(copy.wait_send)
            else:
                local = pltpu.make_async_copy(here, there, ref[out + "_r"].at[mine])

                @pl.when(s == target)
                def _():
                    local.start()

                @pl.when(s != target)
                def _():
                    copy.start()

                def finish(copy=copy):
                    @pl.when(s != target)
                    def _():
                        copy.wait_send()

                waits.append(finish)

    send_out(ent, "act", plan.hrows, 0)

    R2 = ref["R2"]
    post(3, dot_moments(R2, lines(ent), need("w2")))
    transpose(lines(ent), ref["entt"])
    for k in range(bands):
        transpose(xp[k].reshape(pix, cin), ref["xpt"].at[k])
    tot = fetch(3)
    n2 = coefficients(tot[0], tot[1], inv_half, vector("g2"), vector("b2"))
    vb = ref["vb"]
    vb[:, 0:1] = jnp.zeros((3, 1, side, width), bf16)
    vb[:, side + 1 :] = jnp.zeros((3, 1, side, width), bf16)

    def three(out, p, v):
        out[0, p + 1] = shifted(v, first_col, 1).astype(bf16)
        out[1, p + 1] = v.astype(bf16)
        out[2, p + 1] = shifted(v, last_col, side - 1).astype(bf16)

    def step(p):
        three(vb, p, pixels(mask_row(0, 0, p) * silu(line(R2[p]) * n2[0] + n2[1])))

    over_rows(step)
    taps2 = [(vb.at[t % 3], t // 3) for t in range(9)]
    c2 = ref["c2"]
    post(4, convolve(taps2, ref["bd2"], c2))
    blocks("k2", ref["bd2t"], True)
    tot = fetch(4)
    nc2 = coefficients(tot[0], tot[1], inv_half, vector("gg2"), vector("gb2"))
    H2, ga2 = ref["H2"], ref["ga2"]
    kept2 = excite(
        c2, nc2, H2, ga2, need("sq2"), dot, vec[VEC["sqb2"], 0:1, : plan.q2], need("ex2"), vec[VEC["exb2"], 0:1]
    )
    E2 = ref["E2"]
    post(5, dot_moments(E2, lines(ga2), need("e2")))
    transpose(lines(ga2), ref["ga2t"])
    for d in range(R):
        arrived("og", plan.hrows, 1, d)
    tot = fetch(5)
    ne2 = coefficients(tot[0], tot[1], inv_half, vector("eg2"), vector("eb2"))
    leave, D, og = ref["leave"], ref["D"], ref["og_in"]

    def step(p):
        e = line(E2[p])
        v = e * ne2[0] + ne2[1] + line(ent[p])
        sg = sigmoid(v)
        m = mask_row(0, 0, p)
        leave[p] = pixels(m * v * sg).astype(bf16)
        g = line(og[p]) * m * (sg * (1.0 + v * (1.0 - sg)))
        D[p] = pixels(g)
        return g, g * (e * ne2[2] + ne2[3])

    parts = over_rows(step, 2)
    vec_grads["eb2"], vec_grads["eg2"] = parts
    post(6, parts)
    send_out(leave, "act", plan.hrows, 1)
    blocks("k1", ref["bd1t"], True)

    def back_rule(sums, inverse, gain, norm):
        a = gain * norm[2]
        k0 = a * (sums[0] + norm[3] * sums[1]) * inverse
        return a, k0, a * norm[2] * sums[1] * inverse

    def back_excite(dg, kept, hidden, conv, norm, sq, sq_form, ex, out):
        pooled, pre, inner, gate = kept

        def step(p):
            return (line(dg[p]) * line(hidden[p]),)

        (dgate,) = over_rows(step, 1)
        dpre = dgate * gate * (1.0 - gate)
        dsq = small_dot(dpre, ex[...], dot_nt) * slope(pre)
        dpool = wide(small_dot(dsq, sq[...], sq_form) / half_count)
        gate_wide = wide(gate)

        def step_two(p):
            v = line(conv[p])
            g = (line(dg[p]) * gate_wide + dpool) * mask_row(0, 0, p)
            g = g * slope(v * norm[0] + norm[1])
            out[p] = pixels(g)
            return g, g * (v * norm[2] + norm[3])

        return over_rows(step_two, 2), dpre, dsq

    def excite_grads(name, kept, dpre, dsq):
        pooled, pre, inner, gate = kept
        put("sq" + name, small_outer(dsq, pooled))
        put("ex" + name, small_outer(inner, dpre))
        vec_grads["exb" + name] = dpre
        count = dsq.shape[1]
        eye = (
            lax.broadcasted_iota(jnp.int32, (count, width), 0)
            == lax.broadcasted_iota(jnp.int32, (count, width), 1)
        ).astype(f32).astype(bf16)
        vec_grads["sqb" + name] = small_dot(dsq, eye, dot)

    def turn(gradient_ref, start):
        out = []
        for h in range(width // span):
            piece = flat(gradient_ref[start : start + side, :, h * span : (h + 1) * span])
            out.append(piece.astype(f32).T.astype(bf16))
        return out

    d1, dg, GR = ref["d1"], ref["dg"], ref["GR"]
    tot = fetch(6)
    rule = back_rule((tot[0], tot[1]), inv_half, vector("eg2"), ne2)

    def step(p):
        v = rule[0] * line(D[p]) - mask_row(0, 0, p) * (rule[1] + rule[2] * line(E2[p]))
        d1[p] = pixels(v).astype(bf16)

    over_rows(step)
    full_dot(dg, lines(d1), need("e2"), dot_nt)
    parts, dpre, dsq = back_excite(dg, kept2, H2, c2, nc2, need("sq2"), dot_nt, need("ex2"), GR)
    vec_grads["gb2"], vec_grads["gg2"] = parts
    post(7, parts)
    put("e2", dot(ref["ga2t"][...], lines(d1)))
    excite_grads("2", kept2, dpre, dsq)
    pump(0)
    tot = fetch(7)
    rule = back_rule((tot[0], tot[1]), inv_half, vector("gg2"), nc2)
    vd = ref["vd"]
    vd[:, 0:1] = jnp.zeros((3, 1, side, width), bf16)
    vd[:, side + 1 :] = jnp.zeros((3, 1, side, width), bf16)

    def step(p):
        v = rule[0] * line(GR[p]) - mask_row(0, 0, p) * (rule[1] + rule[2] * line(c2[p]))
        three(vd, p, pixels(v))

    over_rows(step)

    def convolve_back(taps, first, weights, out):
        for h in range(width // span):
            cut = slice(h * span, (h + 1) * span)
            left = [flat(var[start : start + side, :, cut]) for var, start in taps]
            rows = slice(first * span, (first + len(taps)) * span)
            acc = dot(jnp.concatenate(left, axis=1), weights[h, rows])
            out[:, :, cut] = acc.reshape(side, side, span)

    DA = ref["DA"]
    convolve_back(
        [(vd.at[2 - t % 3], 2 - t // 3) for t in ORDER],
        0,
        ref["bd2t"],
        DA.at[0],
    )

    def step(p):
        v = line(R2[p])
        g = line(DA[0, p]) * mask_row(0, 0, p) * slope(v * n2[0] + n2[1])
        GR[p] = pixels(g)
        return g, g * (v * n2[2] + n2[3])

    parts = over_rows(step, 2)
    vec_grads["b2"], vec_grads["g2"] = parts
    post(8, parts)
    pump(0)
    groups_grad("k2", taps2, turn(vd.at[1], 1))
    tot = fetch(8)
    rule = back_rule((tot[0], tot[1]), inv_half, vector("g2"), n2)

    def step(p):
        v = rule[0] * line(GR[p]) - mask_row(0, 0, p) * (rule[1] + rule[2] * line(R2[p]))
        d1[p] = pixels(v).astype(bf16)

    over_rows(step)
    full_dot(GR, lines(d1), need("w2"), dot_nt)
    pump(0)

    def step(p):
        e, sc = line(E1[p]), line(SC[p])
        g = line((D[p] + GR[p]).astype(bf16))
        g = g * mask_row(0, 0, p) * slope(e * ne[0] + sc * ns[0] + both_shifts)
        D[p] = pixels(g)
        return g, g * (e * ne[2] + ne[3]), g * (sc * ns[2] + ns[3])

    parts = over_rows(step, 3)
    vec_grads["eb1"], vec_grads["eg1"], vec_grads["sg1"] = parts
    vec_grads["sb1"] = parts[0]
    post(9, parts)
    put("w2", dot(ref["entt"][...], lines(d1)))
    pump(1, 0)
    tot = fetch(9, 3)
    rule_e = back_rule((tot[0], tot[1]), inv_half, vector("eg1"), ne)
    rule_s = back_rule((tot[0], tot[2]), inv_half, vector("sg1"), ns)
    d2 = ref["d2"]

    def step(p):
        g, m = line(D[p]), mask_row(0, 0, p)
        v = rule_e[0] * g - m * (rule_e[1] + rule_e[2] * line(E1[p]))
        d1[p] = pixels(v).astype(bf16)
        v = rule_s[0] * g - m * (rule_s[1] + rule_s[2] * line(SC[p]))
        d2[p] = pixels(v).astype(bf16)

    over_rows(step)
    full_dot(dg, lines(d1), need("e1"), dot_nt)
    pump(1)
    parts, dpre, dsq = back_excite(dg, kept1, H1, c1, nc1, need("sq1"), dot, need("ex1"), GR)
    vec_grads["gb1"], vec_grads["gg1"] = parts
    post(10, parts)
    put("e1", dot(ref["ga1t"][...], lines(d1)))
    put("s1", dot_tn(even[...].reshape(pix, cin), lines(d2)))
    excite_grads("1", kept1, dpre, dsq)
    pump(2, 1)
    tot = fetch(10)
    rule = back_rule((tot[0], tot[1]), inv_half, vector("gg1"), nc1)

    def step(p):
        v = rule[0] * line(GR[p]) - mask_row(0, 0, p) * (rule[1] + rule[2] * line(c1[p]))
        three(vd, p, pixels(v))

    over_rows(step)
    pump(0)
    sums = []
    for ab, (a, b) in enumerate(PHASES):
        chosen = []
        first = (0, 1, 3, 5)[ab]
        for t in ORDER[first : first + (1, 2, 2, 4)[ab]]:
            chosen.append((vd.at[2 if t % 3 == 0 else 1], 2 if t // 3 == 0 else 1))
        convolve_back(chosen, first, ref["bd1t"], DA.at[ab])

        def step(p, ab=ab, a=a, b=b):
            v = line(R1[at_phase(ab, p)])
            g = line(DA[ab, p]) * mask_row(a, b, p) * slope(v * n1[0] + n1[1])
            DA[ab, p] = pixels(g)
            return g, g * (v * n1[2] + n1[3])

        sums.append(over_rows(step, 2))
        if ab == 1:
            pump(2, 1)
        elif ab == 3:
            pump(0)
    parts = (sum(x[0] for x in sums), sum(x[1] for x in sums))
    vec_grads["b1"], vec_grads["g1"] = parts
    post(11, parts)
    pump(2)
    groups_grad("k1", taps1, turn(vd.at[1], 1))
    ids = lax.broadcasted_iota(jnp.int32, (VEC_ROWS, width), 0)
    value = jnp.zeros((VEC_ROWS, width), f32)
    for name, at in VEC.items():
        value = jnp.where(ids == at, jnp.broadcast_to(vec_grads[name], value.shape), value)
    put(VECTORS, value)
    pump(3, 2, 0)
    tot = fetch(11)
    rule = back_rule((tot[0], tot[1]), inv_full, vector("g1"), n1)
    dr = ref["dr"]
    for ab, (a, b) in enumerate(PHASES):

        def step(p, ab=ab, a=a, b=b):
            v = rule[0] * line(DA[ab, p])
            v = v - mask_row(a, b, p) * (rule[1] + rule[2] * line(R1[at_phase(ab, p)]))
            dr[at_phase(ab, p)] = pixels(v).astype(bf16)

        over_rows(step)
    total = None
    for k in range(bands):
        term = dot(ref["xpt"][k], dr[k].reshape(pix, width))
        total = term if total is None else total + term
    put("w1", total)
    pump(4, 3, 1)
    cut = cin // 2
    ref["dxo0"][...] = jnp.zeros((2 * side, plan.cols, 128), bf16)
    ref["dxo1"][...] = jnp.zeros((2 * side, plan.cols, 128), bf16)
    stepwise = plan.each == bands
    for d in [*range(1, bands), 0]:
        k = lax.rem(r + plan.copies * d, R) * plan.rows // band if stepwise else d
        for part in range(2):
            dxo = ref[f"dxo{part}"]
            rows = slice(part * cut, (part + 1) * cut)
            v = dot_nt(dr[k].reshape(pix, width), need("w1")[rows, :])
            w = dot_nt(
                d2[pl.ds(k * bhalf, bhalf)].reshape(bhalf * side, width), need("s1")[rows, :]
            )
            v = jnp.concatenate([v[: bhalf * side] + w, v[bhalf * side :]], axis=0)
            v = dot(ref["unsort"][...], v.astype(bf16)).astype(bf16)
            dxo[pl.ds(k * band, band), :, :cut] = v.reshape(band, plan.cols, cut)
            if stepwise:
                send_out(dxo, "dx", plan.rows, part, (d,))
        pump(*((4, 3, 2, 1), (4, 3, 1), (4, 3, 2), (1, 0))[(d - 1) % 4])
    if not stepwise:
        send_out(ref["dxo0"], "dx", plan.rows, 0)
        send_out(ref["dxo1"], "dx", plan.rows, 1)
    for _ in range(9):
        pump()
    for wait in waits:
        wait()
    for m in range(plan.M):
        t = (m % plan.each) * plan.copies + lax.rem(r, plan.copies)
        for out in ("act", "dx"):
            there = ref[out].at[0, m, 0] if out == "act" else ref[out].at[m, 0]
            pltpu.make_async_copy(there, there, ref[out + "_r"].at[m]).wait()


WEIGHTS = ("w1", "k1", "k2", "sq1", "ex1", "e1", "s1", "w2", "sq2", "ex2", "e2")


def run_main(plan, arrays):
    side, width, cin = plan.side, plan.width, plan.cin
    wide = 4 * plan.gw
    field = (side, side, width)
    scratch = {
        "x_in": pltpu.VMEM((2 * side, plan.cols, cin), bf16),
        "og_in": pltpu.VMEM(field, bf16),
        "st": pltpu.VMEM((EXCHANGES, plan.I, 2, 8, 128), f32),
        "hm": pltpu.VMEM((plan.pix, 128), f32),
        "cm": pltpu.VMEM((2, side, width), f32),
        **{
            name: pltpu.VMEM((width // wide, plan.taps * wide, wide), bf16)
            for name in ("bd1", "bd2", "bd1t", "bd2t")
        },
        "xpt": pltpu.VMEM((plan.bands, cin, plan.pix), bf16),
        **{name: pltpu.VMEM((width, plan.pix), bf16) for name in ("ga1t", "ga2t", "entt")},
        "sort": pltpu.VMEM((plan.pix, plan.pix), bf16),
        "unsort": pltpu.VMEM((plan.pix, plan.pix), bf16),
        "xp": pltpu.VMEM((plan.bands, 2 * plan.band, side, cin), bf16),
        "R1": pltpu.VMEM((plan.bands, 2 * plan.band, side, width), f32),
        "va": pltpu.VMEM((6, side + 1, side, width), bf16),
        "vb": pltpu.VMEM((3, side + 2, side, width), bf16),
        "vd": pltpu.VMEM((3, side + 2, side, width), bf16),
        "DA": pltpu.VMEM((4,) + field, f32),
        "dr": pltpu.VMEM((plan.bands, 2 * plan.band, side, width), bf16),
        "dxo0": pltpu.VMEM((2 * side, plan.cols, 128), bf16),
        "dxo1": pltpu.VMEM((2 * side, plan.cols, 128), bf16),
    }
    for name in ("SC", "H1", "E1", "R2", "H2", "E2", "D", "GR"):
        scratch[name] = pltpu.VMEM(field, f32)
    for name in ("c1", "ga1", "ent", "c2", "ga2", "leave", "d1", "d2", "dg"):
        scratch[name] = pltpu.VMEM(field, bf16)
    for name in ("x", "og"):
        scratch[name + "_s"] = pltpu.SemaphoreType.DMA((max(plan.R - 1, 1),))
        scratch[name + "_r"] = pltpu.SemaphoreType.DMA((plan.R,))
    scratch["st_s"] = pltpu.SemaphoreType.DMA((EXCHANGES, max(plan.I - 1, 1)))
    scratch["st_r"] = pltpu.SemaphoreType.DMA((EXCHANGES, plan.I))
    for name in ("act", "dx"):
        scratch[name + "_s"] = pltpu.SemaphoreType.DMA((2, plan.R // plan.copies))
        scratch[name + "_r"] = pltpu.SemaphoreType.DMA((plan.M,))
    for name in NAMES + WEIGHTS:
        scratch[name + "_v"] = pltpu.VMEM(arrays[name].shape, bf16)
    scratch["vec"] = pltpu.VMEM((len(NAMES), 8, width), f32)
    scratch["loads"] = pltpu.SemaphoreType.DMA((len(NAMES + WEIGHTS),))
    scratch["local"] = pltpu.VMEM((plan.blocks, 16, 128), bf16)
    for level, room in enumerate(plan.rooms):
        scratch[f"got{level}"] = pltpu.VMEM((room, 16, 128), bf16)
        if level:
            scratch[f"sum{level - 1}"] = pltpu.VMEM((room, 16, 128), bf16)
    most = max(plan.sizes.values())
    for name in ("rs", "ag"):
        scratch[name + "_s"] = pltpu.SemaphoreType.DMA((len(plan.streams), 4, most - 1))
        scratch[name + "_r"] = pltpu.SemaphoreType.DMA((len(plan.streams), 4, most))
    inputs = ("x", "og", "vr", "vc") + NAMES + WEIGHTS
    outputs = ("act", "dx", "grads")
    names = inputs + outputs + tuple(scratch)
    any_space = pl.BlockSpec(memory_space=pl.ANY)
    smem = pl.BlockSpec(memory_space=pltpu.SMEM)
    vmem = pl.BlockSpec(memory_space=pltpu.VMEM)
    return pl.pallas_call(
        functools.partial(main_kernel, plan, names),
        out_shape=(
            jax.ShapeDtypeStruct((1, plan.M, 1, plan.hrows, side, width), bf16),
            jax.ShapeDtypeStruct((plan.M, 1, plan.rows, plan.cols, 128), bf16),
            pltpu.VMEM((plan.blocks, 16, 128), bf16),
        ),
        in_specs=[any_space, any_space, smem, smem] + [any_space] * (len(NAMES) + len(WEIGHTS)),
        out_specs=(any_space, any_space, vmem),
        scratch_shapes=list(scratch.values()),
        compiler_params=pltpu.CompilerParams(
            collective_id=0, has_side_effects=True, vmem_limit_bytes=58 * 1024 * 1024
        ),
        name="blocks",
    )(*[arrays[name] for name in inputs])


OUTS = (
    "w1", "g1", "b1", "k1", "gg1", "gb1", "sq1", "sqb1", "ex1", "exb1", "e1", "eg1", "eb1",
    "s1", "sg1", "sb1", "w2", "g2", "b2", "k2", "gg2", "gb2", "sq2", "sqb2", "ex2", "exb2",
    "e2", "eg2", "eb2",
)


def unpack_kernel(plan, blocks, act_in, dx_in, *rest):
    count = len(OUTS) + 2
    outs, bufs, through, sems = rest[:count], rest[count:-2], rest[-2], rest[-1]
    copies = []
    for k, whole in enumerate((act_in, dx_in)):
        copies.append(pltpu.make_async_copy(whole, bufs[k - 2], through.at[k]))
        copies[-1].start()
    order = sorted(plan.starts, key=lambda name: plan.starts[name])
    order = [name for name in order if name not in (VECTORS, LAST_TAP)]

    def tile(name, k):
        start, per_tile = plan.starts[name]
        at = start + k * per_tile
        return blocks[at : at + per_tile].reshape(16 * per_tile, 128).astype(f32)

    tiles = plan.width // 128
    vec = None
    turn = [OUTS.index(name) for name in order]
    turn += [k for k, name in enumerate(OUTS) if name in VEC]
    for position, k in enumerate(turn):
        name, out = OUTS[k], bufs[k]
        if position < 2:
            copies[position].wait()
            copies[position] = pltpu.make_async_copy(
                bufs[position - 2], outs[position], sems.at[position]
            )
            copies[position].start()
        if name in VEC and vec is None:
            vec = jnp.concatenate([tile(VECTORS, k) for k in range(tiles)], axis=1)
        if name in VEC:
            size = out.shape[0]
            out[...] = vec[VEC[name] : VEC[name] + 1, :size].reshape(size)
        elif name[0] == "k":

            def run(t, carry, name=name, out=out, last_tap=False):
                for lane in range(tiles):
                    start, per_tile = plan.starts[name]
                    at = start + lane * per_tile + t * (plan.gw // 16)
                    if last_tap:
                        start, per_tile = plan.starts[LAST_TAP]
                        at = start + lane * per_tile
                    piece = blocks[pl.ds(at, plan.gw // 16)].reshape(plan.gw, 128)
                    piece = piece.astype(f32).T
                    for j in range(128 // plan.gw):
                        group = lane * (128 // plan.gw) + j
                        out[t, group, :, : plan.gw] = piece[j * plan.gw : (j + 1) * plan.gw]
                return carry

            if name == "k2":
                lax.fori_loop(0, plan.taps - 1, run, 0)
                run(plan.taps - 1, 0, last_tap=True)
            else:
                lax.fori_loop(0, plan.taps, run, 0)
        elif name == "sq2":
            for lane in range(tiles):
                out[128 * lane : 128 * lane + 128] = tile(name, lane).T
        else:
            for lane in range(tiles):
                out[:, 128 * lane : 128 * lane + 128] = tile(name, lane)
        copies.append(pltpu.make_async_copy(out, outs[k + 2], sems.at[k + 2]))
        copies[-1].start()
    for copy in copies:
        copy.wait()


def unpack(plan, act, dx, grads, weights):
    shapes = []
    for name, w in zip(OUTS, weights):
        shape = w.shape[:3] + (128,) if name[0] == "k" else w.shape
        shapes.append(jax.ShapeDtypeStruct(shape, f32))
    any_space = pl.BlockSpec(memory_space=pl.ANY)
    return pl.pallas_call(
        functools.partial(unpack_kernel, plan),
        out_shape=[jax.ShapeDtypeStruct(v.shape, v.dtype) for v in (act, dx)] + shapes,
        in_specs=[pl.BlockSpec(memory_space=pltpu.VMEM)]
        + [pl.BlockSpec(memory_space=pltpu.HBM)] * 2,
        out_specs=[any_space] * (len(shapes) + 2),
        scratch_shapes=[pltpu.VMEM(v.shape, v.dtype) for v in (*shapes, act, dx)]
        + [pltpu.SemaphoreType.DMA((2,))]
        + [pltpu.SemaphoreType.DMA((len(shapes) + 2,))],
        compiler_params=pltpu.CompilerParams(vmem_limit_bytes=24 * 1024 * 1024),
        name="unpack",
    )(grads, act, dx)


def body(sizes, input_maps, valid_rows, valid_cols, *rest):
    weights, output_grad = rest[:-1], rest[-1]
    (w1, g1, b1, k1, gg1, gb1, sq1, sqb1, ex1, exb1, e1, eg1, eb1, s1, sg1, sb1) = weights[:16]
    (w2, g2, b2, k2, gg2, gb2, sq2, sqb2, ex2, exb2, e2, eg2, eb2) = weights[16:]
    turned = sq1.T
    plan = Plan(sizes, [v.shape for v in (input_maps, output_grad, w1, k1, turned, sq2)])
    vectors = (
        g1, b1, gg1, gb1, exb1, eg1, eb1, sg1, sb1, sqb1, g2, b2, gg2, gb2, exb2, eg2, eb2, sqb2,
    )
    arrays = dict(
        x=input_maps, og=output_grad, vr=valid_rows.T, vc=valid_cols.T, w1=w1,
        k1=k1, k2=k2,
        sq1=turned, ex1=ex1, e1=e1, s1=s1, w2=w2, sq2=sq2, ex2=ex2, e2=e2,
        **dict(zip(NAMES, vectors)),
    )
    act, dx, grads = run_main(plan, arrays)
    act, dx, *out = unpack(plan, act, dx, grads, weights[:6] + (turned,) + weights[7:])
    out[6] = out[6].T
    for at in (3, 19):
        out[at] = out[at][..., : plan.gw]
    dx = dx[..., : plan.cin // 2]
    return (act, dx, *out)


def solution(mesh):
    tiled = P(None, "img", "row", None, None)
    image = P(None, "img")
    sizes = tuple(mesh.shape[name] for name in ("section", "img", "row"))
    return jax.shard_map(
        functools.partial(body, sizes),
        mesh=mesh,
        in_specs=(tiled, image, image) + (P(),) * 29 + (tiled,),
        out_specs=(
            P("section", None, "img", "row", None, None),
            P(None, "img", "row", None, "section"),
        )
        + (P(),) * 29,
        check_vma=False,
    )
```

```python
import functools

import jax
import jax.numpy as jnp
from jax import lax
from jax.experimental import pallas as pl
from jax.experimental.pallas import tpu as pltpu
from jax.sharding import PartitionSpec as P

epsilon = 1e-05
f32 = jnp.float32
bf16 = jnp.bfloat16
MESH = pl.DeviceIdType.MESH
PHASES = ((0, 0), (0, 1), (1, 0), (1, 1))
ORDER = (4, 3, 5, 1, 7, 0, 2, 6, 8)
EXCHANGES = 12
NAMES = (
    "g1", "b1", "gg1", "gb1", "exb1", "eg1", "eb1", "sg1", "sb1", "sqb1",
    "g2", "b2", "gg2", "gb2", "exb2", "eg2", "eb2", "sqb2",
)
VEC = {name: k for k, name in enumerate(NAMES)}
VEC_ROWS = 32
VECTORS = "vec"
LAST_TAP = "k9"


def segments_of(cin, width, taps, group, sq1, sq2, devices):
    layout = (
        (("e2", width), ("sq2", sq2), ("ex2", sq2)),
        (("k2", (taps - 1) * group), ("w2", width)),
        (("e1", width), ("s1", cin), ("sq1", sq1), ("ex1", sq1), (LAST_TAP, group)),
        (("k1", taps * group), (VECTORS, VEC_ROWS)),
        (("w1", cin),),
    )
    starts, segments, at = {}, [], 0
    for parts in layout:
        base = at
        for name, rows in parts:
            starts[name] = (at, rows // 16)
            at += rows // 16 * (width // 128)
        units = -(-(at - base) // devices)
        first = units // 2 * devices if len(segments) < len(layout) - 1 else 0
        segments.append((base, units * devices, at, first))
        at = base + units * devices
    return starts, tuple(segments), at


def sigmoid(v):
    return 0.5 * jnp.tanh(0.5 * v) + 0.5


def silu(v):
    return v * sigmoid(v)


def slope(v):
    s = sigmoid(v)
    return s * (1.0 + v * (1.0 - s))


def dot(left, right):
    return jnp.dot(left, right, preferred_element_type=f32)


def dot_nt(left, right):
    return lax.dot_general(left, right, (((1,), (1,)), ((), ())), preferred_element_type=f32)


def dot_tn(left, right):
    return lax.dot_general(left, right, (((0,), (0,)), ((), ())), preferred_element_type=f32)


def parts_of(v):
    high = v.astype(bf16).astype(f32)
    return high, v - high


def stacked(rows, width):
    ids = lax.broadcasted_iota(jnp.int32, (16, width), 0)
    total = jnp.zeros((16, width), f32)
    for k, row in enumerate(rows):
        total = jnp.where(ids == k, jnp.broadcast_to(row, (16, width)), total)
    return total.astype(bf16)


def small_dot(row, weight, form):
    out = form(stacked(parts_of(row), row.shape[1]), weight)
    return out[0:1] + out[1:2]


def small_outer(left, right):
    lh, ll = parts_of(left)
    rh, rl = parts_of(right)
    return dot_tn(
        stacked((lh, ll, lh, ll), left.shape[1]), stacked((rh, rh, rl, rl), right.shape[1])
    )


def fold(v):
    return v[0] + v[1]


def column(acc):
    return jnp.sum(acc, axis=0, keepdims=True)


class Plan:
    def __init__(self, mesh_sizes, args):
        self.S, self.I, self.R = mesh_sizes
        x, og, w1, k1, sq1, sq2 = args
        self.M, _, self.rows, self.cols, self.cin = x
        _, _, self.hrows, self.side, self.width = og
        self.taps, self.groups, self.gw, _ = k1
        self.q1, self.q2 = sq1[0], sq2[1]
        self.each = self.M // self.S
        self.copies = self.R // self.each
        self.pix = self.side * self.side
        self.band = self.pix // self.cols
        self.bands = 2 * self.side // self.band
        self.starts, self.segments, self.blocks = segments_of(
            self.cin, self.width, self.taps, self.gw, self.q1, self.q2, self.S * self.I * self.R
        )
        self.X = 1
        while self.X * self.X < self.R:
            self.X *= 2
        self.Y = self.R // self.X
        self.sizes = {"s": self.S, "x": self.X, "y": self.Y, "r": self.R, "i": self.I}
        self.streams = []
        self.members = []
        self.rooms = [0] * 4
        for base, size, _, first in self.segments:
            halves = [(base, first, "sxyi"), (base + first, size - first, "syxi")]
            if not first:
                halves = [(base, size, "sri")]
            self.members.append(range(len(self.streams), len(self.streams) + len(halves)))
            for start, count, order in halves:
                self.streams.append((start, count, order, tuple(self.rooms)))
                for level, axis in enumerate(order):
                    self.rooms[level] += count
                    count //= self.sizes[axis]

    def piece(self, stream, level):
        _, size, order, _ = self.streams[stream]
        for axis in order[: level + 1]:
            size //= self.sizes[axis]
        return size


def main_kernel(plan, names, *refs):
    ref = dict(zip(names, refs))
    S, I, R = plan.S, plan.I, plan.R
    side, width, pix, cin = plan.side, plan.width, plan.pix, plan.cin
    half_width = width // 2
    s, i, r = lax.axis_index("section"), lax.axis_index("img"), lax.axis_index("row")
    mine = s * plan.each + r // plan.copies
    waits = []

    barrier = pltpu.get_barrier_semaphore()
    peers = []
    for ds in range(S):
        for dr in range(R):
            if ds or dr:
                peers.append((lax.rem(s + ds, S), i, lax.rem(r + dr, R)))
    for di in range(1, I):
        peers.append((s, lax.rem(i + di, I), r))
    for peer in peers:
        pl.semaphore_signal(barrier, inc=1, device_id=peer, device_id_type=MESH)

    own = []
    loads = {}

    def load(*which):
        for name in which:
            at = (NAMES + WEIGHTS).index(name)
            loads[name] = pltpu.make_async_copy(ref[name], ref[name + "_v"], ref["loads"].at[at])
            loads[name].start(priority=int(name[0] == "k"))

    def need(name):
        if name in loads:
            loads.pop(name).wait()
        return ref[name + "_v"]

    load("w1", "g1", "b1", "k1", "k2")
    for name, rows in (("x", plan.rows), ("og", plan.hrows)):
        copy = pltpu.make_async_copy(
            ref[name].at[mine, 0],
            ref[name + "_in"].at[pl.ds(r * rows, rows)],
            ref[name + "_r"].at[r],
        )
        copy.start()
        own.append(copy)
    pl.semaphore_wait(barrier, len(peers))
    for name, rows in (("x", plan.rows), ("og", plan.hrows)):
        for d in range(1, R):
            t = lax.rem(r + d, R)
            copy = pltpu.make_async_remote_copy(
                src_ref=ref[name].at[s * plan.each + t // plan.copies, 0],
                dst_ref=ref[name + "_in"].at[pl.ds(r * rows, rows)],
                send_sem=ref[name + "_s"].at[d - 1],
                recv_sem=ref[name + "_r"].at[r],
                device_id=(s, i, t),
                device_id_type=MESH,
            )
            copy.start()
            waits.append(copy.wait_send)

    load("s1", *NAMES[2:], "sq1", "ex1", "e1", "w2", "sq2", "ex2", "e2")

    def arrived(name, rows, position, d):
        if d == 0:
            own[position].wait()
        else:
            t = lax.rem(r + d, R)
            there = ref[name + "_in"].at[pl.ds(t * rows, rows)]
            pltpu.make_async_remote_copy(
                src_ref=there,
                dst_ref=there,
                send_sem=ref[name + "_s"].at[d - 1],
                recv_sem=ref[name + "_r"].at[t],
                device_id=(s, i, t),
                device_id_type=MESH,
            ).wait_recv()

    st = ref["st"]

    def pairs_of(k):
        return 2 if k in (0, 1, 9) else 1

    def stats_copy(k, d, slot):
        return pltpu.make_async_remote_copy(
            src_ref=st.at[k, slot, pl.ds(0, pairs_of(k))],
            dst_ref=st.at[k, slot, pl.ds(0, pairs_of(k))],
            send_sem=ref["st_s"].at[k, d - 1],
            recv_sem=ref["st_r"].at[k, slot],
            device_id=(s, lax.rem(i + d, I), r),
            device_id_type=MESH,
        )

    def post(k, rows):
        ids = lax.broadcasted_iota(jnp.int32, (8, 128), 0)
        rows = [*rows, *([None] * (len(rows) % 2))]
        for pair in range(len(rows) // 2):
            value = jnp.zeros((8, 128), f32)
            for j in range(8):
                row = rows[2 * pair + j // 4]
                if row is not None:
                    piece = row[:, 128 * (j % 4) : 128 * (j % 4) + 128]
                    value = jnp.where(ids == j, jnp.broadcast_to(piece, (8, 128)), value)
            st[k, i, pair] = value
        for d in range(1, I):
            stats_copy(k, d, i).start()
        for d in range(1, I):
            if k:
                stats_copy(k - 1, d, i).wait_send()
            if k == EXCHANGES - 1:
                waits.append(stats_copy(k, d, i).wait_send)

    def fetch(k, count=2):
        for d in range(1, I):
            stats_copy(k, d, lax.rem(i + d, I)).wait_recv()
        out = []
        for pair in range((count + 1) // 2):
            value = st[k, 0, pair]
            for j in range(1, I):
                value = value + st[k, j, pair]
            for half in range(2):
                out.append(
                    jnp.concatenate(
                        [
                            jnp.broadcast_to(value[4 * half + j : 4 * half + j + 1], (8, 128))
                            for j in range(4)
                        ],
                        axis=1,
                    )
                )
        return out

    vec = ref["vec"]

    def keep_vectors():
        for name in NAMES:
            row = need(name)[...].astype(f32)
            size = row.shape[0]
            vec[VEC[name], :, :size] = jnp.broadcast_to(row.reshape(1, size), (8, size))

    def vector(name):
        return vec[VEC[name]]

    vr, vc = ref["vr"][0, mine], ref["vc"][0, mine]
    q_ids = lax.broadcasted_iota(jnp.int32, (side, width), 0)
    first_col, last_col = q_ids == 0, q_ids == side - 1
    cm = ref["cm"]
    for b in range(2):
        cm[b] = (2 * q_ids + b < vc).astype(f32)

    def line(value):
        return value.astype(f32).reshape(2, 8, width)

    def pixels(value):
        return value.reshape(side, width)

    def mask_row(a, b, p):
        return line(cm[b]) * (2 * p + a < vr).astype(f32)

    def wide(row):
        return jnp.broadcast_to(row, (8, width))

    row_count = jnp.full((1, width), vr * vc, jnp.int32).astype(f32)
    half_count = jnp.full((1, width), ((vr + 1) // 2) * ((vc + 1) // 2), jnp.int32).astype(f32)

    def over_rows(step, *accs):
        init = tuple(jnp.zeros((8, width), f32) for _ in range(accs[0] if accs else 0))

        def run(p, carry):
            out = step(p)
            if not carry:
                return carry
            return tuple(c + fold(o) for c, o in zip(carry, out))

        return tuple(column(c) for c in lax.fori_loop(0, side, run, init, unroll=16))

    def full_dot(out, left, weight, form=dot):
        wide = out.shape[-1]
        step = min(256, wide)
        for h in range(wide // step):
            cut = slice(h * step, h * step + step)
            w = weight[:, cut] if form is dot else weight[cut, :]
            out[:, :, cut] = form(left, w).reshape(side, side, step).astype(out.dtype)

    hm = ref["hm"]
    for p in range(side):
        hm[p * side : (p + 1) * side] = cm[0][:, :128] * (2 * p < vr).astype(f32)

    def with_moments(out, products):
        sums = []
        for h, product in enumerate(products):
            span = product.shape[1]
            value = product.astype(out.dtype)
            out[:, :, h * span : (h + 1) * span] = value.reshape(side, side, span)
            value = value.astype(f32)
            valid = value * jnp.concatenate([hm[...]] * (span // 128), axis=1)
            sums.append(
                [
                    jnp.sum(x.reshape(pix // 8, 8, span), axis=0)
                    for x in (valid, valid * value)
                ]
            )
        return [column(jnp.concatenate(x, axis=1)) for x in zip(*sums)]

    def dot_moments(out, left, weight):
        return with_moments(
            out, (dot(left, weight[:, cut : cut + 256]) for cut in range(0, width, 256))
        )

    def flat(value):
        return value.reshape(pix, value.shape[-1])

    def lines(ref_, start=0):
        return flat(ref_[start : start + side])

    G, F = ref["local"], ref["grads"]
    lead = None if plan.copies == 1 else (lax.rem(r, plan.copies) == 0).astype(f32)

    def put(name, value, row=0, lane=0):
        if lead is not None:
            value = value * lead
        start, per_tile = plan.starts[name]
        count = value.shape[0] // 16
        for k in range(value.shape[1] // 128):
            piece = value[:, 128 * k : 128 * k + 128].astype(bf16).reshape(count, 16, 128)
            at = start + (lane // 128 + k) * per_tile + row // 16
            G[at : at + count] = piece

    X, Y = plan.X, plan.Y
    x, y = lax.rem(r, X), r // X
    axes = {
        "s": (S, s, lambda t: (t, i, r)),
        "r": (R, r, lambda t: (s, i, t)),
        "x": (X, x, lambda t: (s, i, y * X + t)),
        "y": (Y, y, lambda t: (s, i, t * X + x)),
        "i": (I, i, lambda t: (s, t, r)),
    }

    def scatter_source(stream, level):
        base, _, order, offsets = plan.streams[stream]
        if level == 0:
            return G, base
        return ref[f"sum{level - 1}"], offsets[level]

    def scatter_copies(stream, level, outgoing):
        base, size, order, offsets = plan.streams[stream]
        count, me, device = axes[order[level]]
        piece = plan.piece(stream, level)
        source, first = scatter_source(stream, level)
        for d in range(1, count):
            t = lax.rem(me + d, count)
            slot = me if outgoing else t
            copy = pltpu.make_async_remote_copy(
                src_ref=source.at[pl.ds(first + t * piece, piece)],
                dst_ref=ref[f"got{level}"].at[pl.ds(offsets[level] + slot * piece, piece)],
                send_sem=ref["rs_s"].at[stream, level, d - 1],
                recv_sem=ref["rs_r"].at[stream, level, slot],
                device_id=device(t),
                device_id_type=MESH,
            )
            if outgoing:
                copy.start()
                sent[stream].append(copy)
            else:
                copy.wait_recv()

    def add_up(stream, level):
        base, size, order, offsets = plan.streams[stream]
        count, me, _ = axes[order[level]]
        piece = plan.piece(stream, level)
        source, first = scatter_source(stream, level)
        got = ref[f"got{level}"]
        if level < len(order) - 1:
            out, at = ref[f"sum{level}"], offsets[level + 1]
        else:
            out, at = F, own_part(stream, len(order))
        step = next(k for k in (16, 12, 10, 9, 8, 7, 6, 5, 4, 3, 2, 1) if piece % k == 0)

        def run(k, carry):
            total = source[pl.ds(first + me * piece + k * step, step)].astype(f32)
            for d in range(1, count):
                t = lax.rem(me + d, count)
                total = total + got[pl.ds(offsets[level] + t * piece + k * step, step)].astype(f32)
            out[pl.ds(at + k * step, step)] = total.astype(bf16)
            return carry

        lax.fori_loop(0, piece // step, run, 0)

    def own_part(stream, depth):
        at, _, order, _ = plan.streams[stream]
        for level in range(depth):
            at = at + axes[order[level]][1] * plan.piece(stream, level)
        return at

    def gather_copies(stream, level, outgoing):
        count, me, device = axes[plan.streams[stream][2][level]]
        base = own_part(stream, level)
        piece = plan.piece(stream, level)
        for d in range(1, count):
            t = lax.rem(me + d, count)
            slot = me if outgoing else t
            there = F.at[pl.ds(base + slot * piece, piece)]
            copy = pltpu.make_async_remote_copy(
                src_ref=there,
                dst_ref=there,
                send_sem=ref["ag_s"].at[stream, level, d - 1],
                recv_sem=ref["ag_r"].at[stream, level, slot],
                device_id=device(t),
                device_id_type=MESH,
            )
            if outgoing:
                copy.start()
                sent[stream].append(copy)
            else:
                copy.wait_recv()

    done = [0] * len(plan.segments)
    started = []
    sent = [[] for _ in plan.streams]

    def pump(*which):
        for g in which or tuple(started):
            if g not in started:
                started.insert(0, g)
            k = done[g]
            depth = len(plan.streams[plan.members[g][0]][2])
            if k > 2 * depth:
                continue
            done[g] += 1
            if k == 0:
                base, size, used, _ = plan.segments[g]
                if used < base + size:
                    G[used : base + size] = jnp.zeros((base + size - used, 16, 128), bf16)
            for stream in plan.members[g]:
                if 1 <= k <= depth:
                    scatter_copies(stream, k - 1, False)
                    add_up(stream, k - 1)
                elif k > depth:
                    gather_copies(stream, 2 * depth - k, False)
                for copy in sent[stream]:
                    copy.wait_send()
                sent[stream] = []
                if k < depth:
                    scatter_copies(stream, k, True)
                elif k < 2 * depth:
                    gather_copies(stream, 2 * depth - 1 - k, True)

    vec_grads = {}

    gw = plan.gw
    span = 4 * gw
    def blocks(name, out, turned=False):
        kernels = need(name)
        shape = (span, gw) if turned else (gw, span)
        long = lax.broadcasted_iota(jnp.int32, shape, 0 if turned else 1)
        short = lax.broadcasted_iota(jnp.int32, shape, 1 if turned else 0)
        spread = (lax.rem(long, gw) == short).astype(f32).astype(bf16)
        row = lax.broadcasted_iota(jnp.int32, (span, span), 0) // gw
        col = lax.broadcasted_iota(jnp.int32, (span, span), 1) // gw
        for k, t in enumerate(ORDER):
            for h in range(width // span):
                piece = kernels[t, 4 * h : 4 * h + 4].reshape(span, gw)
                full = dot_nt(spread, piece) if turned else dot(piece, spread)
                out[h, k * span : (k + 1) * span] = jnp.where(row == col, full, 0.0).astype(bf16)

    def groups_grad(name, taps, turned):
        lane = lax.broadcasted_iota(jnp.int32, (gw, span), 1) // gw
        for t, (var, start) in enumerate(taps):
            for h in range(width // span):
                cut = slice(h * span, (h + 1) * span)
                res = dot(turned[h], flat(var[start : start + side, :, cut]))
                out = res[0:gw]
                for j in range(1, 4):
                    out = jnp.where(lane == j, res[j * gw : (j + 1) * gw], out)
                if name == "k2" and t == plan.taps - 1:
                    put(LAST_TAP, out, 0, h * span)
                else:
                    put(name, out, t * gw, h * span)

    band, bands = plan.band, plan.bands
    bhalf = band // 2
    out_id = lax.broadcasted_iota(jnp.int32, (pix, pix), 0)
    in_id = lax.broadcasted_iota(jnp.int32, (pix, pix), 1)

    def source(o):
        quarter = o // (bhalf * side)
        down = lax.rem(o, bhalf * side) // side
        return (2 * down + quarter // 2) * plan.cols + 2 * lax.rem(o, side) + lax.rem(quarter, 2)

    ref["sort"][...] = (source(out_id) == in_id).astype(f32).astype(bf16)
    ref["unsort"][...] = (source(in_id) == out_id).astype(f32).astype(bf16)

    xp, R1 = ref["xp"], ref["R1"]
    keep_vectors()

    def transpose(source, out):
        out[...] = source.astype(f32).T.astype(bf16)

    totals = [jnp.zeros((8, width), f32)] * 2
    by_band = plan.rows % band == 0
    if not by_band:
        for d in range(R):
            arrived("x", plan.rows, 0, d)
    for d in range(bands):
        if by_band:
            if d % (plan.rows // band) == 0:
                arrived("x", plan.rows, 0, d // (plan.rows // band))
            k = lax.rem(r * (plan.rows // band) + d, bands)
        else:
            k = d
        block = ref["x_in"][pl.ds(k * band, band)].reshape(pix, cin)
        block = dot(ref["sort"][...], block).astype(bf16)
        xp[k] = block.reshape(4 * bhalf, side, cin)
        full_dot(R1.at[k], block, need("w1"))
        for j in range(4 * bhalf):
            a, b = PHASES[j // bhalf]
            v = line(R1[k, j])
            mv = v * mask_row(a, b, k * bhalf + j % bhalf)
            totals = [totals[0] + fold(mv), totals[1] + fold(mv * v)]
    even = xp.at[:, 0:bhalf]

    def at_phase(ab, p):
        return p // bhalf, ab * bhalf + lax.rem(p, bhalf)

    post(0, [column(totals[0]), column(totals[1]), row_count, half_count])
    SC = ref["SC"]
    short_sums = dot_moments(SC, even[...].reshape(pix, cin), need("s1"))

    blocks("k1", ref["bd1"])

    def coefficients(first, second, inverse, gain, shift):
        mean = first * inverse
        scale = lax.rsqrt(second * inverse - mean * mean + epsilon)
        a = scale * gain
        return a, shift - mean * a, scale, -mean * scale

    tot = fetch(0, 4)
    inv_full, inv_half = 1.0 / tot[2], 1.0 / tot[3]
    n1 = coefficients(tot[0], tot[1], inv_full, vector("g1"), vector("b1"))

    va = ref["va"]
    va[3:6, 0:1] = jnp.zeros((3, 1, side, width), bf16)

    def shifted(v, edge, amount):
        return jnp.where(edge, 0.0, pltpu.roll(v, amount, 0))

    for ab, (a, b) in enumerate(PHASES):

        def step(p, ab=ab, a=a, b=b):
            v = mask_row(a, b, p) * silu(line(R1[at_phase(ab, p)]) * n1[0] + n1[1])
            v = pixels(v)
            slot = (0, 1, 3, 4)[ab]
            va[slot, p + a] = v.astype(bf16)
            if b:
                va[slot + 1, p + a] = shifted(v, first_col, 1).astype(bf16)

        over_rows(step)
    taps1 = []
    for t in range(9):
        u, v = t // 3, t % 3
        slot = (0, 1, 3, 4)[2 * (u != 1) + (v != 1)] + (v == 0)
        taps1.append((va.at[slot], 1 if u == 2 else 0))

    def convolve(taps, weights, out):
        def half(h):
            cut = slice(h * span, (h + 1) * span)
            left = [flat(taps[t][0][taps[t][1] : taps[t][1] + side, :, cut]) for t in ORDER]
            return dot(jnp.concatenate(left, axis=1), weights[h])

        return with_moments(out, (half(h) for h in range(width // span)))

    c1 = ref["c1"]
    post(1, [*convolve(taps1, ref["bd1"], c1), *short_sums])
    blocks("k2", ref["bd2"])
    tot = fetch(1, 4)
    nc1 = coefficients(tot[0], tot[1], inv_half, vector("gg1"), vector("gb1"))
    ns = coefficients(tot[2], tot[3], inv_half, vector("sg1"), vector("sb1"))

    def excite(conv, norm, hidden, gated, sq, sq_form, sqb, ex, exb):
        def step(p):
            v = mask_row(0, 0, p) * silu(line(conv[p]) * norm[0] + norm[1])
            hidden[p] = pixels(v)
            return (v,)

        (total,) = over_rows(step, 1)
        pooled = total / half_count
        pre = small_dot(pooled, sq[...], sq_form) + sqb
        inner = silu(pre)
        gate = sigmoid(small_dot(inner, ex[...], dot) + exb)
        gate_wide = wide(gate)

        def step_two(p):
            gated[p] = pixels(line(hidden[p]) * gate_wide).astype(bf16)

        over_rows(step_two)
        return pooled, pre, inner, gate

    H1, ga1 = ref["H1"], ref["ga1"]
    kept1 = excite(
        c1, nc1, H1, ga1, need("sq1"), dot_nt, vec[VEC["sqb1"], 0:1, : plan.q1], need("ex1"), vec[VEC["exb1"], 0:1]
    )
    E1 = ref["E1"]
    post(2, dot_moments(E1, lines(ga1), need("e1")))
    transpose(lines(ga1), ref["ga1t"])
    tot = fetch(2)
    ne = coefficients(tot[0], tot[1], inv_half, vector("eg1"), vector("eb1"))
    ent = ref["ent"]
    both_shifts = ne[1] + ns[1]

    def step(p):
        v = line(E1[p]) * ne[0] + line(SC[p]) * ns[0] + both_shifts
        ent[p] = pixels(mask_row(0, 0, p) * silu(v)).astype(bf16)

    over_rows(step)

    def send_out(source, out, rows, target, steps=None):
        for k in range(R // plan.copies) if steps is None else steps:
            t = lax.rem(r + plan.copies * k, R)
            there = ref[out].at[0, mine, 0] if out == "act" else ref[out].at[mine, 0]
            here = source.at[pl.ds(t * rows, rows)]
            copy = pltpu.make_async_remote_copy(
                src_ref=here,
                dst_ref=there,
                send_sem=ref[out + "_s"].at[target, k],
                recv_sem=ref[out + "_r"].at[mine],
                device_id=(target, i, t),
                device_id_type=MESH,
            )
            if k:
                copy.start()
                waits.append(copy.wait_send)
            else:
                local = pltpu.make_async_copy(here, there, ref[out + "_r"].at[mine])

                @pl.when(s == target)
                def _():
                    local.start()

                @pl.when(s != target)
                def _():
                    copy.start()

                def finish(copy=copy):
                    @pl.when(s != target)
                    def _():
                        copy.wait_send()

                waits.append(finish)

    send_out(ent, "act", plan.hrows, 0)

    R2 = ref["R2"]
    post(3, dot_moments(R2, lines(ent), need("w2")))
    transpose(lines(ent), ref["entt"])
    for k in range(bands):
        transpose(xp[k].reshape(pix, cin), ref["xpt"].at[k])
    tot = fetch(3)
    n2 = coefficients(tot[0], tot[1], inv_half, vector("g2"), vector("b2"))
    vb = ref["vb"]
    vb[:, 0:1] = jnp.zeros((3, 1, side, width), bf16)
    vb[:, side + 1 :] = jnp.zeros((3, 1, side, width), bf16)

    def three(out, p, v):
        out[0, p + 1] = shifted(v, first_col, 1).astype(bf16)
        out[1, p + 1] = v.astype(bf16)
        out[2, p + 1] = shifted(v, last_col, side - 1).astype(bf16)

    def step(p):
        three(vb, p, pixels(mask_row(0, 0, p) * silu(line(R2[p]) * n2[0] + n2[1])))

    over_rows(step)
    taps2 = [(vb.at[t % 3], t // 3) for t in range(9)]
    c2 = ref["c2"]
    post(4, convolve(taps2, ref["bd2"], c2))
    blocks("k2", ref["bd2t"], True)
    tot = fetch(4)
    nc2 = coefficients(tot[0], tot[1], inv_half, vector("gg2"), vector("gb2"))
    H2, ga2 = ref["H2"], ref["ga2"]
    kept2 = excite(
        c2, nc2, H2, ga2, need("sq2"), dot, vec[VEC["sqb2"], 0:1, : plan.q2], need("ex2"), vec[VEC["exb2"], 0:1]
    )
    E2 = ref["E2"]
    post(5, dot_moments(E2, lines(ga2), need("e2")))
    transpose(lines(ga2), ref["ga2t"])
    for d in range(R):
        arrived("og", plan.hrows, 1, d)
    tot = fetch(5)
    ne2 = coefficients(tot[0], tot[1], inv_half, vector("eg2"), vector("eb2"))
    leave, D, og = ref["leave"], ref["D"], ref["og_in"]

    def step(p):
        e = line(E2[p])
        v = e * ne2[0] + ne2[1] + line(ent[p])
        sg = sigmoid(v)
        m = mask_row(0, 0, p)
        leave[p] = pixels(m * v * sg).astype(bf16)
        g = line(og[p]) * m * (sg * (1.0 + v * (1.0 - sg)))
        D[p] = pixels(g)
        return g, g * (e * ne2[2] + ne2[3])

    parts = over_rows(step, 2)
    vec_grads["eb2"], vec_grads["eg2"] = parts
    post(6, parts)
    send_out(leave, "act", plan.hrows, 1)
    blocks("k1", ref["bd1t"], True)

    def back_rule(sums, inverse, gain, norm):
        a = gain * norm[2]
        k0 = a * (sums[0] + norm[3] * sums[1]) * inverse
        return a, k0, a * norm[2] * sums[1] * inverse

    def back_excite(dg, kept, hidden, conv, norm, sq, sq_form, ex, out):
        pooled, pre, inner, gate = kept

        def step(p):
            return (line(dg[p]) * line(hidden[p]),)

        (dgate,) = over_rows(step, 1)
        dpre = dgate * gate * (1.0 - gate)
        dsq = small_dot(dpre, ex[...], dot_nt) * slope(pre)
        dpool = wide(small_dot(dsq, sq[...], sq_form) / half_count)
        gate_wide = wide(gate)

        def step_two(p):
            v = line(conv[p])
            g = (line(dg[p]) * gate_wide + dpool) * mask_row(0, 0, p)
            g = g * slope(v * norm[0] + norm[1])
            out[p] = pixels(g)
            return g, g * (v * norm[2] + norm[3])

        return over_rows(step_two, 2), dpre, dsq

    def excite_grads(name, kept, dpre, dsq):
        pooled, pre, inner, gate = kept
        put("sq" + name, small_outer(dsq, pooled))
        put("ex" + name, small_outer(inner, dpre))
        vec_grads["exb" + name] = dpre
        count = dsq.shape[1]
        eye = (
            lax.broadcasted_iota(jnp.int32, (count, width), 0)
            == lax.broadcasted_iota(jnp.int32, (count, width), 1)
        ).astype(f32).astype(bf16)
        vec_grads["sqb" + name] = small_dot(dsq, eye, dot)

    def turn(gradient_ref, start):
        out = []
        for h in range(width // span):
            piece = flat(gradient_ref[start : start + side, :, h * span : (h + 1) * span])
            out.append(piece.astype(f32).T.astype(bf16))
        return out

    d1, dg, GR = ref["d1"], ref["dg"], ref["GR"]
    tot = fetch(6)
    rule = back_rule((tot[0], tot[1]), inv_half, vector("eg2"), ne2)

    def step(p):
        v = rule[0] * line(D[p]) - mask_row(0, 0, p) * (rule[1] + rule[2] * line(E2[p]))
        d1[p] = pixels(v).astype(bf16)

    over_rows(step)
    full_dot(dg, lines(d1), need("e2"), dot_nt)
    parts, dpre, dsq = back_excite(dg, kept2, H2, c2, nc2, need("sq2"), dot_nt, need("ex2"), GR)
    vec_grads["gb2"], vec_grads["gg2"] = parts
    post(7, parts)
    put("e2", dot(ref["ga2t"][...], lines(d1)))
    excite_grads("2", kept2, dpre, dsq)
    pump(0)
    tot = fetch(7)
    rule = back_rule((tot[0], tot[1]), inv_half, vector("gg2"), nc2)
    vd = ref["vd"]
    vd[:, 0:1] = jnp.zeros((3, 1, side, width), bf16)
    vd[:, side + 1 :] = jnp.zeros((3, 1, side, width), bf16)

    def step(p):
        v = rule[0] * line(GR[p]) - mask_row(0, 0, p) * (rule[1] + rule[2] * line(c2[p]))
        three(vd, p, pixels(v))

    over_rows(step)

    def convolve_back(taps, first, weights, out):
        for h in range(width // span):
            cut = slice(h * span, (h + 1) * span)
            left = [flat(var[start : start + side, :, cut]) for var, start in taps]
            rows = slice(first * span, (first + len(taps)) * span)
            acc = dot(jnp.concatenate(left, axis=1), weights[h, rows])
            out[:, :, cut] = acc.reshape(side, side, span)

    DA = ref["DA"]
    convolve_back(
        [(vd.at[2 - t % 3], 2 - t // 3) for t in ORDER],
        0,
        ref["bd2t"],
        DA.at[0],
    )

    def step(p):
        v = line(R2[p])
        g = line(DA[0, p]) * mask_row(0, 0, p) * slope(v * n2[0] + n2[1])
        GR[p] = pixels(g)
        return g, g * (v * n2[2] + n2[3])

    parts = over_rows(step, 2)
    vec_grads["b2"], vec_grads["g2"] = parts
    post(8, parts)
    pump(0)
    groups_grad("k2", taps2, turn(vd.at[1], 1))
    tot = fetch(8)
    rule = back_rule((tot[0], tot[1]), inv_half, vector("g2"), n2)

    def step(p):
        v = rule[0] * line(GR[p]) - mask_row(0, 0, p) * (rule[1] + rule[2] * line(R2[p]))
        d1[p] = pixels(v).astype(bf16)

    over_rows(step)
    full_dot(GR, lines(d1), need("w2"), dot_nt)
    pump(0)

    def step(p):
        e, sc = line(E1[p]), line(SC[p])
        g = line((D[p] + GR[p]).astype(bf16))
        g = g * mask_row(0, 0, p) * slope(e * ne[0] + sc * ns[0] + both_shifts)
        D[p] = pixels(g)
        return g, g * (e * ne[2] + ne[3]), g * (sc * ns[2] + ns[3])

    parts = over_rows(step, 3)
    vec_grads["eb1"], vec_grads["eg1"], vec_grads["sg1"] = parts
    vec_grads["sb1"] = parts[0]
    post(9, parts)
    put("w2", dot(ref["entt"][...], lines(d1)))
    pump(1, 0)
    tot = fetch(9, 3)
    rule_e = back_rule((tot[0], tot[1]), inv_half, vector("eg1"), ne)
    rule_s = back_rule((tot[0], tot[2]), inv_half, vector("sg1"), ns)
    d2 = ref["d2"]

    def step(p):
        g, m = line(D[p]), mask_row(0, 0, p)
        v = rule_e[0] * g - m * (rule_e[1] + rule_e[2] * line(E1[p]))
        d1[p] = pixels(v).astype(bf16)
        v = rule_s[0] * g - m * (rule_s[1] + rule_s[2] * line(SC[p]))
        d2[p] = pixels(v).astype(bf16)

    over_rows(step)
    full_dot(dg, lines(d1), need("e1"), dot_nt)
    pump(1)
    parts, dpre, dsq = back_excite(dg, kept1, H1, c1, nc1, need("sq1"), dot, need("ex1"), GR)
    vec_grads["gb1"], vec_grads["gg1"] = parts
    post(10, parts)
    put("e1", dot(ref["ga1t"][...], lines(d1)))
    put("s1", dot_tn(even[...].reshape(pix, cin), lines(d2)))
    excite_grads("1", kept1, dpre, dsq)
    pump(2, 1)
    tot = fetch(10)
    rule = back_rule((tot[0], tot[1]), inv_half, vector("gg1"), nc1)

    def step(p):
        v = rule[0] * line(GR[p]) - mask_row(0, 0, p) * (rule[1] + rule[2] * line(c1[p]))
        three(vd, p, pixels(v))

    over_rows(step)
    pump(0)
    sums = []
    for ab, (a, b) in enumerate(PHASES):
        chosen = []
        first = (0, 1, 3, 5)[ab]
        for t in ORDER[first : first + (1, 2, 2, 4)[ab]]:
            chosen.append((vd.at[2 if t % 3 == 0 else 1], 2 if t // 3 == 0 else 1))
        convolve_back(chosen, first, ref["bd1t"], DA.at[ab])

        def step(p, ab=ab, a=a, b=b):
            v = line(R1[at_phase(ab, p)])
            g = line(DA[ab, p]) * mask_row(a, b, p) * slope(v * n1[0] + n1[1])
            DA[ab, p] = pixels(g)
            return g, g * (v * n1[2] + n1[3])

        sums.append(over_rows(step, 2))
        if ab == 1:
            pump(2, 1)
        elif ab == 3:
            pump(0)
    parts = (sum(x[0] for x in sums), sum(x[1] for x in sums))
    vec_grads["b1"], vec_grads["g1"] = parts
    post(11, parts)
    pump(2)
    groups_grad("k1", taps1, turn(vd.at[1], 1))
    ids = lax.broadcasted_iota(jnp.int32, (VEC_ROWS, width), 0)
    value = jnp.zeros((VEC_ROWS, width), f32)
    for name, at in VEC.items():
        value = jnp.where(ids == at, jnp.broadcast_to(vec_grads[name], value.shape), value)
    put(VECTORS, value)
    pump(3, 2, 0)
    tot = fetch(11)
    rule = back_rule((tot[0], tot[1]), inv_full, vector("g1"), n1)
    dr = ref["dr"]
    for ab, (a, b) in enumerate(PHASES):

        def step(p, ab=ab, a=a, b=b):
            v = rule[0] * line(DA[ab, p])
            v = v - mask_row(a, b, p) * (rule[1] + rule[2] * line(R1[at_phase(ab, p)]))
            dr[at_phase(ab, p)] = pixels(v).astype(bf16)

        over_rows(step)
    total = None
    for k in range(bands):
        term = dot(ref["xpt"][k], dr[k].reshape(pix, width))
        total = term if total is None else total + term
    put("w1", total)
    pump(4, 3, 1)
    cut = cin // 2
    ref["dxo0"][...] = jnp.zeros((2 * side, plan.cols, 128), bf16)
    ref["dxo1"][...] = jnp.zeros((2 * side, plan.cols, 128), bf16)
    stepwise = plan.each == bands
    for d in [*range(1, bands), 0]:
        k = lax.rem(r + plan.copies * d, R) * plan.rows // band if stepwise else d
        for part in range(2):
            dxo = ref[f"dxo{part}"]
            rows = slice(part * cut, (part + 1) * cut)
            v = dot_nt(dr[k].reshape(pix, width), need("w1")[rows, :])
            w = dot_nt(
                d2[pl.ds(k * bhalf, bhalf)].reshape(bhalf * side, width), need("s1")[rows, :]
            )
            v = jnp.concatenate([v[: bhalf * side] + w, v[bhalf * side :]], axis=0)
            v = dot(ref["unsort"][...], v.astype(bf16)).astype(bf16)
            dxo[pl.ds(k * band, band), :, :cut] = v.reshape(band, plan.cols, cut)
            if stepwise:
                send_out(dxo, "dx", plan.rows, part, (d,))
        pump(*((4, 3, 2, 1), (4, 3, 1), (4, 3, 2), (1, 0))[(d - 1) % 4])
    if not stepwise:
        send_out(ref["dxo0"], "dx", plan.rows, 0)
        send_out(ref["dxo1"], "dx", plan.rows, 1)
    for _ in range(9):
        pump()
    for wait in waits:
        wait()
    for m in range(plan.M):
        t = (m % plan.each) * plan.copies + lax.rem(r, plan.copies)
        for out in ("act", "dx"):
            there = ref[out].at[0, m, 0] if out == "act" else ref[out].at[m, 0]
            pltpu.make_async_copy(there, there, ref[out + "_r"].at[m]).wait()


WEIGHTS = ("w1", "k1", "k2", "sq1", "ex1", "e1", "s1", "w2", "sq2", "ex2", "e2")


def run_main(plan, arrays):
    side, width, cin = plan.side, plan.width, plan.cin
    wide = 4 * plan.gw
    field = (side, side, width)
    scratch = {
        "x_in": pltpu.VMEM((2 * side, plan.cols, cin), bf16),
        "og_in": pltpu.VMEM(field, bf16),
        "st": pltpu.VMEM((EXCHANGES, plan.I, 2, 8, 128), f32),
        "hm": pltpu.VMEM((plan.pix, 128), f32),
        "cm": pltpu.VMEM((2, side, width), f32),
        **{
            name: pltpu.VMEM((width // wide, plan.taps * wide, wide), bf16)
            for name in ("bd1", "bd2", "bd1t", "bd2t")
        },
        "xpt": pltpu.VMEM((plan.bands, cin, plan.pix), bf16),
        **{name: pltpu.VMEM((width, plan.pix), bf16) for name in ("ga1t", "ga2t", "entt")},
        "sort": pltpu.VMEM((plan.pix, plan.pix), bf16),
        "unsort": pltpu.VMEM((plan.pix, plan.pix), bf16),
        "xp": pltpu.VMEM((plan.bands, 2 * plan.band, side, cin), bf16),
        "R1": pltpu.VMEM((plan.bands, 2 * plan.band, side, width), f32),
        "va": pltpu.VMEM((6, side + 1, side, width), bf16),
        "vb": pltpu.VMEM((3, side + 2, side, width), bf16),
        "vd": pltpu.VMEM((3, side + 2, side, width), bf16),
        "DA": pltpu.VMEM((4,) + field, f32),
        "dr": pltpu.VMEM((plan.bands, 2 * plan.band, side, width), bf16),
        "dxo0": pltpu.VMEM((2 * side, plan.cols, 128), bf16),
        "dxo1": pltpu.VMEM((2 * side, plan.cols, 128), bf16),
    }
    for name in ("SC", "H1", "E1", "R2", "H2", "E2", "D", "GR"):
        scratch[name] = pltpu.VMEM(field, f32)
    for name in ("c1", "ga1", "ent", "c2", "ga2", "leave", "d1", "d2", "dg"):
        scratch[name] = pltpu.VMEM(field, bf16)
    for name in ("x", "og"):
        scratch[name + "_s"] = pltpu.SemaphoreType.DMA((max(plan.R - 1, 1),))
        scratch[name + "_r"] = pltpu.SemaphoreType.DMA((plan.R,))
    scratch["st_s"] = pltpu.SemaphoreType.DMA((EXCHANGES, max(plan.I - 1, 1)))
    scratch["st_r"] = pltpu.SemaphoreType.DMA((EXCHANGES, plan.I))
    for name in ("act", "dx"):
        scratch[name + "_s"] = pltpu.SemaphoreType.DMA((2, plan.R // plan.copies))
        scratch[name + "_r"] = pltpu.SemaphoreType.DMA((plan.M,))
    for name in NAMES + WEIGHTS:
        scratch[name + "_v"] = pltpu.VMEM(arrays[name].shape, bf16)
    scratch["vec"] = pltpu.VMEM((len(NAMES), 8, width), f32)
    scratch["loads"] = pltpu.SemaphoreType.DMA((len(NAMES + WEIGHTS),))
    scratch["local"] = pltpu.VMEM((plan.blocks, 16, 128), bf16)
    for level, room in enumerate(plan.rooms):
        scratch[f"got{level}"] = pltpu.VMEM((room, 16, 128), bf16)
        if level:
            scratch[f"sum{level - 1}"] = pltpu.VMEM((room, 16, 128), bf16)
    most = max(plan.sizes.values())
    for name in ("rs", "ag"):
        scratch[name + "_s"] = pltpu.SemaphoreType.DMA((len(plan.streams), 4, most - 1))
        scratch[name + "_r"] = pltpu.SemaphoreType.DMA((len(plan.streams), 4, most))
    inputs = ("x", "og", "vr", "vc") + NAMES + WEIGHTS
    outputs = ("act", "dx", "grads")
    names = inputs + outputs + tuple(scratch)
    any_space = pl.BlockSpec(memory_space=pl.ANY)
    smem = pl.BlockSpec(memory_space=pltpu.SMEM)
    vmem = pl.BlockSpec(memory_space=pltpu.VMEM)
    return pl.pallas_call(
        functools.partial(main_kernel, plan, names),
        out_shape=(
            pltpu.VMEM((1, plan.M, 1, plan.hrows, side, width), bf16),
            pltpu.VMEM((plan.M, 1, plan.rows, plan.cols, 128), bf16),
            pltpu.VMEM((plan.blocks, 16, 128), bf16),
        ),
        in_specs=[any_space, any_space, smem, smem] + [any_space] * (len(NAMES) + len(WEIGHTS)),
        out_specs=(vmem, vmem, vmem),
        scratch_shapes=list(scratch.values()),
        compiler_params=pltpu.CompilerParams(
            collective_id=0, has_side_effects=True, vmem_limit_bytes=58 * 1024 * 1024
        ),
        name="blocks",
    )(*[arrays[name] for name in inputs])


OUTS = (
    "w1", "g1", "b1", "k1", "gg1", "gb1", "sq1", "sqb1", "ex1", "exb1", "e1", "eg1", "eb1",
    "s1", "sg1", "sb1", "w2", "g2", "b2", "k2", "gg2", "gb2", "sq2", "sqb2", "ex2", "exb2",
    "e2", "eg2", "eb2",
)


def unpack_kernel(plan, blocks, act_in, dx_in, *rest):
    count = len(OUTS) + 2
    outs, bufs, sems = rest[:count], rest[count:-1], rest[-1]
    copies = []
    for k, whole in enumerate((act_in, dx_in)):
        copies.append(pltpu.make_async_copy(whole, outs[k], sems.at[k]))
        copies[-1].start()
    order = sorted(plan.starts, key=lambda name: plan.starts[name])
    order = [name for name in order if name not in (VECTORS, LAST_TAP)]

    def tile(name, k):
        start, per_tile = plan.starts[name]
        at = start + k * per_tile
        return blocks[at : at + per_tile].reshape(16 * per_tile, 128).astype(f32)

    tiles = plan.width // 128
    vec = None
    turn = [OUTS.index(name) for name in order]
    turn += [k for k, name in enumerate(OUTS) if name in VEC]
    for k in turn:
        name, out = OUTS[k], bufs[k]
        if name in VEC and vec is None:
            vec = jnp.concatenate([tile(VECTORS, k) for k in range(tiles)], axis=1)
        if name in VEC:
            size = out.shape[0]
            out[...] = vec[VEC[name] : VEC[name] + 1, :size].reshape(size)
        elif name[0] == "k":

            def run(t, carry, name=name, out=out, last_tap=False):
                for lane in range(tiles):
                    start, per_tile = plan.starts[name]
                    at = start + lane * per_tile + t * (plan.gw // 16)
                    if last_tap:
                        start, per_tile = plan.starts[LAST_TAP]
                        at = start + lane * per_tile
                    piece = blocks[pl.ds(at, plan.gw // 16)].reshape(plan.gw, 128)
                    piece = piece.astype(f32).T
                    for j in range(128 // plan.gw):
                        group = lane * (128 // plan.gw) + j
                        out[t, group, :, : plan.gw] = piece[j * plan.gw : (j + 1) * plan.gw]
                return carry

            if name == "k2":
                lax.fori_loop(0, plan.taps - 1, run, 0)
                run(plan.taps - 1, 0, last_tap=True)
            else:
                lax.fori_loop(0, plan.taps, run, 0)
        elif name == "sq2":
            for lane in range(tiles):
                out[128 * lane : 128 * lane + 128] = tile(name, lane).T
        else:
            for lane in range(tiles):
                out[:, 128 * lane : 128 * lane + 128] = tile(name, lane)
        copies.append(pltpu.make_async_copy(out, outs[k + 2], sems.at[k + 2]))
        copies[-1].start()
    for copy in copies:
        copy.wait()


def unpack(plan, act, dx, grads, weights):
    shapes = []
    for name, w in zip(OUTS, weights):
        shape = w.shape[:3] + (128,) if name[0] == "k" else w.shape
        shapes.append(jax.ShapeDtypeStruct(shape, f32))
    any_space = pl.BlockSpec(memory_space=pl.ANY)
    return pl.pallas_call(
        functools.partial(unpack_kernel, plan),
        out_shape=[jax.ShapeDtypeStruct(v.shape, v.dtype) for v in (act, dx)] + shapes,
        in_specs=[pl.BlockSpec(memory_space=pltpu.VMEM)] * 3,
        out_specs=[any_space] * (len(shapes) + 2),
        scratch_shapes=[pltpu.VMEM(v.shape, v.dtype) for v in shapes]
        + [pltpu.SemaphoreType.DMA((len(shapes) + 2,))],
        compiler_params=pltpu.CompilerParams(vmem_limit_bytes=24 * 1024 * 1024),
        name="unpack",
    )(grads, act, dx)


def body(sizes, input_maps, valid_rows, valid_cols, *rest):
    weights, output_grad = rest[:-1], rest[-1]
    (w1, g1, b1, k1, gg1, gb1, sq1, sqb1, ex1, exb1, e1, eg1, eb1, s1, sg1, sb1) = weights[:16]
    (w2, g2, b2, k2, gg2, gb2, sq2, sqb2, ex2, exb2, e2, eg2, eb2) = weights[16:]
    turned = sq1.T
    plan = Plan(sizes, [v.shape for v in (input_maps, output_grad, w1, k1, turned, sq2)])
    vectors = (
        g1, b1, gg1, gb1, exb1, eg1, eb1, sg1, sb1, sqb1, g2, b2, gg2, gb2, exb2, eg2, eb2, sqb2,
    )
    arrays = dict(
        x=input_maps, og=output_grad, vr=valid_rows.T, vc=valid_cols.T, w1=w1,
        k1=k1, k2=k2,
        sq1=turned, ex1=ex1, e1=e1, s1=s1, w2=w2, sq2=sq2, ex2=ex2, e2=e2,
        **dict(zip(NAMES, vectors)),
    )
    act, dx, grads = run_main(plan, arrays)
    act, dx, *out = unpack(plan, act, dx, grads, weights[:6] + (turned,) + weights[7:])
    out[6] = out[6].T
    for at in (3, 19):
        out[at] = out[at][..., : plan.gw]
    dx = dx[..., : plan.cin // 2]
    return (act, dx, *out)


def solution(mesh):
    tiled = P(None, "img", "row", None, None)
    image = P(None, "img")
    sizes = tuple(mesh.shape[name] for name in ("section", "img", "row"))
    return jax.shard_map(
        functools.partial(body, sizes),
        mesh=mesh,
        in_specs=(tiled, image, image) + (P(),) * 29 + (tiled,),
        out_specs=(
            P("section", None, "img", "row", None, None),
            P(None, "img", "row", None, "section"),
        )
        + (P(),) * 29,
        check_vma=False,
    )
```

```python
import functools

import jax
import jax.numpy as jnp
from jax import lax
from jax.experimental import pallas as pl
from jax.experimental.pallas import tpu as pltpu
from jax.sharding import PartitionSpec as P

epsilon = 1e-05
f32 = jnp.float32
bf16 = jnp.bfloat16
MESH = pl.DeviceIdType.MESH
PHASES = ((0, 0), (0, 1), (1, 0), (1, 1))
ORDER = (4, 3, 5, 1, 7, 0, 2, 6, 8)
EXCHANGES = 12
NAMES = (
    "g1", "b1", "gg1", "gb1", "exb1", "eg1", "eb1", "sg1", "sb1", "sqb1",
    "g2", "b2", "gg2", "gb2", "exb2", "eg2", "eb2", "sqb2",
)
VEC = {name: k for k, name in enumerate(NAMES)}
VEC_ROWS = 32
VECTORS = "vec"
LAST_TAP = "k9"


def segments_of(cin, width, taps, group, sq1, sq2, devices):
    layout = (
        (("e2", width), ("sq2", sq2), ("ex2", sq2)),
        (("k2", (taps - 1) * group), ("w2", width)),
        (("e1", width), ("s1", cin), ("sq1", sq1), ("ex1", sq1), (LAST_TAP, group)),
        (("k1", taps * group), (VECTORS, VEC_ROWS)),
        (("w1", cin),),
    )
    starts, segments, at = {}, [], 0
    for parts in layout:
        base = at
        for name, rows in parts:
            starts[name] = (at, rows // 16)
            at += rows // 16 * (width // 128)
        units = -(-(at - base) // devices)
        first = units // 2 * devices if len(segments) < len(layout) - 1 else 0
        segments.append((base, units * devices, at, first))
        at = base + units * devices
    return starts, tuple(segments), at


def sigmoid(v):
    return 0.5 * jnp.tanh(0.5 * v) + 0.5


def silu(v):
    return v * sigmoid(v)


def slope(v):
    s = sigmoid(v)
    return s * (1.0 + v * (1.0 - s))


def dot(left, right):
    return jnp.dot(left, right, preferred_element_type=f32)


def dot_nt(left, right):
    return lax.dot_general(left, right, (((1,), (1,)), ((), ())), preferred_element_type=f32)


def dot_tn(left, right):
    return lax.dot_general(left, right, (((0,), (0,)), ((), ())), preferred_element_type=f32)


def parts_of(v):
    high = v.astype(bf16).astype(f32)
    return high, v - high


def stacked(rows, width):
    ids = lax.broadcasted_iota(jnp.int32, (16, width), 0)
    total = jnp.zeros((16, width), f32)
    for k, row in enumerate(rows):
        total = jnp.where(ids == k, jnp.broadcast_to(row, (16, width)), total)
    return total.astype(bf16)


def small_dot(row, weight, form):
    out = form(stacked(parts_of(row), row.shape[1]), weight)
    return out[0:1] + out[1:2]


def small_outer(left, right):
    lh, ll = parts_of(left)
    rh, rl = parts_of(right)
    return dot_tn(
        stacked((lh, ll, lh, ll), left.shape[1]), stacked((rh, rh, rl, rl), right.shape[1])
    )


def fold(v):
    return v[0] + v[1]


def column(acc):
    return jnp.sum(acc, axis=0, keepdims=True)


class Plan:
    def __init__(self, mesh_sizes, args):
        self.S, self.I, self.R = mesh_sizes
        x, og, w1, k1, sq1, sq2 = args
        self.M, _, self.rows, self.cols, self.cin = x
        _, _, self.hrows, self.side, self.width = og
        self.taps, self.groups, self.gw, _ = k1
        self.q1, self.q2 = sq1[0], sq2[1]
        self.each = self.M // self.S
        self.copies = self.R // self.each
        self.pix = self.side * self.side
        self.band = self.pix // self.cols
        self.bands = 2 * self.side // self.band
        self.starts, self.segments, self.blocks = segments_of(
            self.cin, self.width, self.taps, self.gw, self.q1, self.q2, self.S * self.I * self.R
        )
        self.X = 1
        while self.X * self.X < self.R:
            self.X *= 2
        self.Y = self.R // self.X
        self.sizes = {"s": self.S, "x": self.X, "y": self.Y, "r": self.R, "i": self.I}
        self.streams = []
        self.members = []
        self.rooms = [0] * 4
        for base, size, _, first in self.segments:
            halves = [(base, first, "sxyi"), (base + first, size - first, "syxi")]
            if not first:
                halves = [(base, size, "sri")]
            self.members.append(range(len(self.streams), len(self.streams) + len(halves)))
            for start, count, order in halves:
                self.streams.append((start, count, order, tuple(self.rooms)))
                for level, axis in enumerate(order):
                    self.rooms[level] += count
                    count //= self.sizes[axis]

    def piece(self, stream, level):
        _, size, order, _ = self.streams[stream]
        for axis in order[: level + 1]:
            size //= self.sizes[axis]
        return size


def main_kernel(plan, names, *refs):
    ref = dict(zip(names, refs))
    S, I, R = plan.S, plan.I, plan.R
    side, width, pix, cin = plan.side, plan.width, plan.pix, plan.cin
    half_width = width // 2
    s, i, r = lax.axis_index("section"), lax.axis_index("img"), lax.axis_index("row")
    mine = s * plan.each + r // plan.copies
    waits = []

    barrier = pltpu.get_barrier_semaphore()
    peers = []
    for ds in range(S):
        for dr in range(R):
            if ds or dr:
                peers.append((lax.rem(s + ds, S), i, lax.rem(r + dr, R)))
    for di in range(1, I):
        peers.append((s, lax.rem(i + di, I), r))
    for peer in peers:
        pl.semaphore_signal(barrier, inc=1, device_id=peer, device_id_type=MESH)

    own = []
    loads = {}

    def load(*which):
        for name in which:
            at = (NAMES + WEIGHTS).index(name)
            loads[name] = pltpu.make_async_copy(ref[name], ref[name + "_v"], ref["loads"].at[at])
            loads[name].start(priority=int(name[0] == "k"))

    def need(name):
        if name in loads:
            loads.pop(name).wait()
        return ref[name + "_v"]

    load("w1", "g1", "b1", "k1")
    for name, rows in (("x", plan.rows), ("og", plan.hrows)):
        copy = pltpu.make_async_copy(
            ref[name].at[mine, 0],
            ref[name + "_in"].at[pl.ds(r * rows, rows)],
            ref[name + "_r"].at[r],
        )
        copy.start()
        own.append(copy)
    pl.semaphore_wait(barrier, len(peers))
    for name, rows in (("x", plan.rows), ("og", plan.hrows)):
        for d in range(1, R):
            t = lax.rem(r + d, R)
            copy = pltpu.make_async_remote_copy(
                src_ref=ref[name].at[s * plan.each + t // plan.copies, 0],
                dst_ref=ref[name + "_in"].at[pl.ds(r * rows, rows)],
                send_sem=ref[name + "_s"].at[d - 1],
                recv_sem=ref[name + "_r"].at[r],
                device_id=(s, i, t),
                device_id_type=MESH,
            )
            copy.start()
            waits.append(copy.wait_send)

    load("s1", "k2", *NAMES[2:], "sq1", "ex1", "e1", "w2", "sq2", "ex2", "e2")

    def arrived(name, rows, position, d):
        if d == 0:
            own[position].wait()
        else:
            t = lax.rem(r + d, R)
            there = ref[name + "_in"].at[pl.ds(t * rows, rows)]
            pltpu.make_async_remote_copy(
                src_ref=there,
                dst_ref=there,
                send_sem=ref[name + "_s"].at[d - 1],
                recv_sem=ref[name + "_r"].at[t],
                device_id=(s, i, t),
                device_id_type=MESH,
            ).wait_recv()

    st = ref["st"]

    def pairs_of(k):
        return 2 if k in (0, 1, 9) else 1

    def stats_copy(k, d, slot):
        return pltpu.make_async_remote_copy(
            src_ref=st.at[k, slot, pl.ds(0, pairs_of(k))],
            dst_ref=st.at[k, slot, pl.ds(0, pairs_of(k))],
            send_sem=ref["st_s"].at[k, d - 1],
            recv_sem=ref["st_r"].at[k, slot],
            device_id=(s, lax.rem(i + d, I), r),
            device_id_type=MESH,
        )

    def post(k, rows):
        ids = lax.broadcasted_iota(jnp.int32, (8, 128), 0)
        rows = [*rows, *([None] * (len(rows) % 2))]
        for pair in range(len(rows) // 2):
            value = jnp.zeros((8, 128), f32)
            for j in range(8):
                row = rows[2 * pair + j // 4]
                if row is not None:
                    piece = row[:, 128 * (j % 4) : 128 * (j % 4) + 128]
                    value = jnp.where(ids == j, jnp.broadcast_to(piece, (8, 128)), value)
            st[k, i, pair] = value
        for d in range(1, I):
            stats_copy(k, d, i).start()
        for d in range(1, I):
            if k:
                stats_copy(k - 1, d, i).wait_send()
            if k == EXCHANGES - 1:
                waits.append(stats_copy(k, d, i).wait_send)

    def fetch(k, count=2):
        for d in range(1, I):
            stats_copy(k, d, lax.rem(i + d, I)).wait_recv()
        out = []
        for pair in range((count + 1) // 2):
            value = st[k, 0, pair]
            for j in range(1, I):
                value = value + st[k, j, pair]
            for half in range(2):
                out.append(
                    jnp.concatenate(
                        [
                            jnp.broadcast_to(value[4 * half + j : 4 * half + j + 1], (8, 128))
                            for j in range(4)
                        ],
                        axis=1,
                    )
                )
        return out

    vec = ref["vec"]

    def keep_vectors():
        for name in NAMES:
            row = need(name)[...].astype(f32)
            size = row.shape[0]
            vec[VEC[name], :, :size] = jnp.broadcast_to(row.reshape(1, size), (8, size))

    def vector(name):
        return vec[VEC[name]]

    vr, vc = ref["vr"][0, mine], ref["vc"][0, mine]
    q_ids = lax.broadcasted_iota(jnp.int32, (side, width), 0)
    first_col, last_col = q_ids == 0, q_ids == side - 1
    cm = ref["cm"]
    for b in range(2):
        cm[b] = (2 * q_ids + b < vc).astype(f32)

    def line(value):
        return value.astype(f32).reshape(2, 8, width)

    def pixels(value):
        return value.reshape(side, width)

    def mask_row(a, b, p):
        return line(cm[b]) * (2 * p + a < vr).astype(f32)

    def wide(row):
        return jnp.broadcast_to(row, (8, width))

    row_count = jnp.full((1, width), vr * vc, jnp.int32).astype(f32)
    half_count = jnp.full((1, width), ((vr + 1) // 2) * ((vc + 1) // 2), jnp.int32).astype(f32)

    def over_rows(step, *accs):
        init = tuple(jnp.zeros((8, width), f32) for _ in range(accs[0] if accs else 0))

        def run(p, carry):
            out = step(p)
            if not carry:
                return carry
            return tuple(c + fold(o) for c, o in zip(carry, out))

        return tuple(column(c) for c in lax.fori_loop(0, side, run, init, unroll=16))

    def full_dot(out, left, weight, form=dot):
        wide = out.shape[-1]
        step = min(256, wide)
        for h in range(wide // step):
            cut = slice(h * step, h * step + step)
            w = weight[:, cut] if form is dot else weight[cut, :]
            out[:, :, cut] = form(left, w).reshape(side, side, step).astype(out.dtype)

    hm = ref["hm"]
    for p in range(side):
        hm[p * side : (p + 1) * side] = cm[0][:, :128] * (2 * p < vr).astype(f32)

    def with_moments(out, products):
        sums = []
        for h, product in enumerate(products):
            span = product.shape[1]
            value = product.astype(out.dtype)
            out[:, :, h * span : (h + 1) * span] = value.reshape(side, side, span)
            value = value.astype(f32)
            valid = value * jnp.concatenate([hm[...]] * (span // 128), axis=1)
            sums.append(
                [
                    jnp.sum(x.reshape(pix // 8, 8, span), axis=0)
                    for x in (valid, valid * value)
                ]
            )
        return [column(jnp.concatenate(x, axis=1)) for x in zip(*sums)]

    def dot_moments(out, left, weight):
        return with_moments(
            out, (dot(left, weight[:, cut : cut + 256]) for cut in range(0, width, 256))
        )

    def flat(value):
        return value.reshape(pix, value.shape[-1])

    def lines(ref_, start=0):
        return flat(ref_[start : start + side])

    G, F = ref["local"], ref["grads"]
    lead = None if plan.copies == 1 else (lax.rem(r, plan.copies) == 0).astype(f32)

    def put(name, value, row=0, lane=0):
        if lead is not None:
            value = value * lead
        start, per_tile = plan.starts[name]
        count = value.shape[0] // 16
        for k in range(value.shape[1] // 128):
            piece = value[:, 128 * k : 128 * k + 128].astype(bf16).reshape(count, 16, 128)
            at = start + (lane // 128 + k) * per_tile + row // 16
            G[at : at + count] = piece

    X, Y = plan.X, plan.Y
    x, y = lax.rem(r, X), r // X
    axes = {
        "s": (S, s, lambda t: (t, i, r)),
        "r": (R, r, lambda t: (s, i, t)),
        "x": (X, x, lambda t: (s, i, y * X + t)),
        "y": (Y, y, lambda t: (s, i, t * X + x)),
        "i": (I, i, lambda t: (s, t, r)),
    }

    def scatter_source(stream, level):
        base, _, order, offsets = plan.streams[stream]
        if level == 0:
            return G, base
        return ref[f"sum{level - 1}"], offsets[level]

    def scatter_copies(stream, level, outgoing):
        base, size, order, offsets = plan.streams[stream]
        count, me, device = axes[order[level]]
        piece = plan.piece(stream, level)
        source, first = scatter_source(stream, level)
        for d in range(1, count):
            t = lax.rem(me + d, count)
            slot = me if outgoing else t
            copy = pltpu.make_async_remote_copy(
                src_ref=source.at[pl.ds(first + t * piece, piece)],
                dst_ref=ref[f"got{level}"].at[pl.ds(offsets[level] + slot * piece, piece)],
                send_sem=ref["rs_s"].at[stream, level, d - 1],
                recv_sem=ref["rs_r"].at[stream, level, slot],
                device_id=device(t),
                device_id_type=MESH,
            )
            if outgoing:
                copy.start()
                sent[stream].append(copy)
            else:
                copy.wait_recv()

    def add_up(stream, level):
        base, size, order, offsets = plan.streams[stream]
        count, me, _ = axes[order[level]]
        piece = plan.piece(stream, level)
        source, first = scatter_source(stream, level)
        got = ref[f"got{level}"]
        if level < len(order) - 1:
            out, at = ref[f"sum{level}"], offsets[level + 1]
        else:
            out, at = F, own_part(stream, len(order))
        step = next(k for k in (16, 12, 10, 9, 8, 7, 6, 5, 4, 3, 2, 1) if piece % k == 0)

        def run(k, carry):
            total = source[pl.ds(first + me * piece + k * step, step)].astype(f32)
            for d in range(1, count):
                t = lax.rem(me + d, count)
                total = total + got[pl.ds(offsets[level] + t * piece + k * step, step)].astype(f32)
            out[pl.ds(at + k * step, step)] = total.astype(bf16)
            return carry

        lax.fori_loop(0, piece // step, run, 0)

    def own_part(stream, depth):
        at, _, order, _ = plan.streams[stream]
        for level in range(depth):
            at = at + axes[order[level]][1] * plan.piece(stream, level)
        return at

    def gather_copies(stream, level, outgoing):
        count, me, device = axes[plan.streams[stream][2][level]]
        base = own_part(stream, level)
        piece = plan.piece(stream, level)
        for d in range(1, count):
            t = lax.rem(me + d, count)
            slot = me if outgoing else t
            there = F.at[pl.ds(base + slot * piece, piece)]
            copy = pltpu.make_async_remote_copy(
                src_ref=there,
                dst_ref=there,
                send_sem=ref["ag_s"].at[stream, level, d - 1],
                recv_sem=ref["ag_r"].at[stream, level, slot],
                device_id=device(t),
                device_id_type=MESH,
            )
            if outgoing:
                copy.start()
                sent[stream].append(copy)
            else:
                copy.wait_recv()

    done = [0] * len(plan.segments)
    started = []
    sent = [[] for _ in plan.streams]

    def pump(*which):
        for g in which or tuple(started):
            if g not in started:
                started.insert(0, g)
            k = done[g]
            depth = len(plan.streams[plan.members[g][0]][2])
            if k > 2 * depth:
                continue
            done[g] += 1
            if k == 0:
                base, size, used, _ = plan.segments[g]
                if used < base + size:
                    G[used : base + size] = jnp.zeros((base + size - used, 16, 128), bf16)
            for stream in plan.members[g]:
                if 1 <= k <= depth:
                    scatter_copies(stream, k - 1, False)
                    add_up(stream, k - 1)
                elif k > depth:
                    gather_copies(stream, 2 * depth - k, False)
                for copy in sent[stream]:
                    copy.wait_send()
                sent[stream] = []
                if k < depth:
                    scatter_copies(stream, k, True)
                elif k < 2 * depth:
                    gather_copies(stream, 2 * depth - 1 - k, True)

    vec_grads = {}

    gw = plan.gw
    span = 4 * gw
    def blocks(name, out, turned=False):
        kernels = need(name)
        shape = (span, gw) if turned else (gw, span)
        long = lax.broadcasted_iota(jnp.int32, shape, 0 if turned else 1)
        short = lax.broadcasted_iota(jnp.int32, shape, 1 if turned else 0)
        spread = (lax.rem(long, gw) == short).astype(f32).astype(bf16)
        row = lax.broadcasted_iota(jnp.int32, (span, span), 0) // gw
        col = lax.broadcasted_iota(jnp.int32, (span, span), 1) // gw
        for k, t in enumerate(ORDER):
            for h in range(width // span):
                piece = kernels[t, 4 * h : 4 * h + 4].reshape(span, gw)
                full = dot_nt(spread, piece) if turned else dot(piece, spread)
                out[h, k * span : (k + 1) * span] = jnp.where(row == col, full, 0.0).astype(bf16)

    def groups_grad(name, taps, turned):
        lane = lax.broadcasted_iota(jnp.int32, (gw, span), 1) // gw
        for t, (var, start) in enumerate(taps):
            for h in range(width // span):
                cut = slice(h * span, (h + 1) * span)
                res = dot(turned[h], flat(var[start : start + side, :, cut]))
                out = res[0:gw]
                for j in range(1, 4):
                    out = jnp.where(lane == j, res[j * gw : (j + 1) * gw], out)
                if name == "k2" and t == plan.taps - 1:
                    put(LAST_TAP, out, 0, h * span)
                else:
                    put(name, out, t * gw, h * span)

    band, bands = plan.band, plan.bands
    bhalf = band // 2
    out_id = lax.broadcasted_iota(jnp.int32, (pix, pix), 0)
    in_id = lax.broadcasted_iota(jnp.int32, (pix, pix), 1)

    def source(o):
        quarter = o // (bhalf * side)
        down = lax.rem(o, bhalf * side) // side
        return (2 * down + quarter // 2) * plan.cols + 2 * lax.rem(o, side) + lax.rem(quarter, 2)

    ref["sort"][...] = (source(out_id) == in_id).astype(f32).astype(bf16)
    ref["unsort"][...] = (source(in_id) == out_id).astype(f32).astype(bf16)

    xp, R1 = ref["xp"], ref["R1"]
    keep_vectors()

    def transpose(source, out):
        out[...] = source.astype(f32).T.astype(bf16)

    totals = [jnp.zeros((8, width), f32)] * 2
    by_band = plan.rows % band == 0
    if not by_band:
        for d in range(R):
            arrived("x", plan.rows, 0, d)
    for d in range(bands):
        if by_band:
            if d % (plan.rows // band) == 0:
                arrived("x", plan.rows, 0, d // (plan.rows // band))
            k = lax.rem(r * (plan.rows // band) + d, bands)
        else:
            k = d
        block = ref["x_in"][pl.ds(k * band, band)].reshape(pix, cin)
        block = dot(ref["sort"][...], block).astype(bf16)
        xp[k] = block.reshape(4 * bhalf, side, cin)
        full_dot(R1.at[k], block, need("w1"))
        for j in range(4 * bhalf):
            a, b = PHASES[j // bhalf]
            v = line(R1[k, j])
            mv = v * mask_row(a, b, k * bhalf + j % bhalf)
            totals = [totals[0] + fold(mv), totals[1] + fold(mv * v)]
    even = xp.at[:, 0:bhalf]

    def at_phase(ab, p):
        return p // bhalf, ab * bhalf + lax.rem(p, bhalf)

    post(0, [column(totals[0]), column(totals[1]), row_count, half_count])
    SC = ref["SC"]
    short_sums = dot_moments(SC, even[...].reshape(pix, cin), need("s1"))

    blocks("k1", ref["bd1"])

    def coefficients(first, second, inverse, gain, shift):
        mean = first * inverse
        scale = lax.rsqrt(second * inverse - mean * mean + epsilon)
        a = scale * gain
        return a, shift - mean * a, scale, -mean * scale

    tot = fetch(0, 4)
    inv_full, inv_half = 1.0 / tot[2], 1.0 / tot[3]
    n1 = coefficients(tot[0], tot[1], inv_full, vector("g1"), vector("b1"))

    va = ref["va"]
    va[3:6, 0:1] = jnp.zeros((3, 1, side, width), bf16)

    def shifted(v, edge, amount):
        return jnp.where(edge, 0.0, pltpu.roll(v, amount, 0))

    for ab, (a, b) in enumerate(PHASES):

        def step(p, ab=ab, a=a, b=b):
            v = mask_row(a, b, p) * silu(line(R1[at_phase(ab, p)]) * n1[0] + n1[1])
            v = pixels(v)
            slot = (0, 1, 3, 4)[ab]
            va[slot, p + a] = v.astype(bf16)
            if b:
                va[slot + 1, p + a] = shifted(v, first_col, 1).astype(bf16)

        over_rows(step)
    taps1 = []
    for t in range(9):
        u, v = t // 3, t % 3
        slot = (0, 1, 3, 4)[2 * (u != 1) + (v != 1)] + (v == 0)
        taps1.append((va.at[slot], 1 if u == 2 else 0))

    def convolve(taps, weights, out):
        def half(h):
            cut = slice(h * span, (h + 1) * span)
            left = [flat(taps[t][0][taps[t][1] : taps[t][1] + side, :, cut]) for t in ORDER]
            return dot(jnp.concatenate(left, axis=1), weights[h])

        return with_moments(out, (half(h) for h in range(width // span)))

    c1 = ref["c1"]
    post(1, [*convolve(taps1, ref["bd1"], c1), *short_sums])
    for k in range(bands):
        transpose(xp[k].reshape(pix, cin), ref["xpt"].at[k])
    tot = fetch(1, 4)
    nc1 = coefficients(tot[0], tot[1], inv_half, vector("gg1"), vector("gb1"))
    ns = coefficients(tot[2], tot[3], inv_half, vector("sg1"), vector("sb1"))

    def excite(conv, norm, hidden, gated, sq, sq_form, sqb, ex, exb):
        def step(p):
            v = mask_row(0, 0, p) * silu(line(conv[p]) * norm[0] + norm[1])
            hidden[p] = pixels(v)
            return (v,)

        (total,) = over_rows(step, 1)
        pooled = total / half_count
        pre = small_dot(pooled, sq[...], sq_form) + sqb
        inner = silu(pre)
        gate = sigmoid(small_dot(inner, ex[...], dot) + exb)
        gate_wide = wide(gate)

        def step_two(p):
            gated[p] = pixels(line(hidden[p]) * gate_wide).astype(bf16)

        over_rows(step_two)
        return pooled, pre, inner, gate

    H1, ga1 = ref["H1"], ref["ga1"]
    kept1 = excite(
        c1, nc1, H1, ga1, need("sq1"), dot_nt, vec[VEC["sqb1"], 0:1, : plan.q1], need("ex1"), vec[VEC["exb1"], 0:1]
    )
    E1 = ref["E1"]
    post(2, dot_moments(E1, lines(ga1), need("e1")))
    transpose(lines(ga1), ref["ga1t"])
    blocks("k2", ref["bd2"])
    tot = fetch(2)
    ne = coefficients(tot[0], tot[1], inv_half, vector("eg1"), vector("eb1"))
    ent = ref["ent"]
    both_shifts = ne[1] + ns[1]

    def step(p):
        v = line(E1[p]) * ne[0] + line(SC[p]) * ns[0] + both_shifts
        ent[p] = pixels(mask_row(0, 0, p) * silu(v)).astype(bf16)

    over_rows(step)

    def send_out(source, out, rows, target, steps=None):
        for k in range(R // plan.copies) if steps is None else steps:
            t = lax.rem(r + plan.copies * k, R)
            there = ref[out].at[0, mine, 0] if out == "act" else ref[out].at[mine, 0]
            here = source.at[pl.ds(t * rows, rows)]
            copy = pltpu.make_async_remote_copy(
                src_ref=here,
                dst_ref=there,
                send_sem=ref[out + "_s"].at[target, k],
                recv_sem=ref[out + "_r"].at[mine],
                device_id=(target, i, t),
                device_id_type=MESH,
            )
            if k:
                copy.start()
                waits.append(copy.wait_send)
            else:
                local = pltpu.make_async_copy(here, there, ref[out + "_r"].at[mine])

                @pl.when(s == target)
                def _():
                    local.start()

                @pl.when(s != target)
                def _():
                    copy.start()

                def finish(copy=copy):
                    @pl.when(s != target)
                    def _():
                        copy.wait_send()

                waits.append(finish)

    send_out(ent, "act", plan.hrows, 0)

    R2 = ref["R2"]
    post(3, dot_moments(R2, lines(ent), need("w2")))
    transpose(lines(ent), ref["entt"])
    tot = fetch(3)
    n2 = coefficients(tot[0], tot[1], inv_half, vector("g2"), vector("b2"))
    vb = ref["vb"]
    vb[:, 0:1] = jnp.zeros((3, 1, side, width), bf16)
    vb[:, side + 1 :] = jnp.zeros((3, 1, side, width), bf16)

    def three(out, p, v, both=True):
        if both:
            out[0, p + 1] = shifted(v, first_col, 1).astype(bf16)
        out[1, p + 1] = v.astype(bf16)
        out[2, p + 1] = shifted(v, last_col, side - 1).astype(bf16)

    def step(p):
        three(vb, p, pixels(mask_row(0, 0, p) * silu(line(R2[p]) * n2[0] + n2[1])))

    over_rows(step)
    taps2 = [(vb.at[t % 3], t // 3) for t in range(9)]
    c2 = ref["c2"]
    post(4, convolve(taps2, ref["bd2"], c2))
    blocks("k2", ref["bd2t"], True)
    tot = fetch(4)
    nc2 = coefficients(tot[0], tot[1], inv_half, vector("gg2"), vector("gb2"))
    H2, ga2 = ref["H2"], ref["ga2"]
    kept2 = excite(
        c2, nc2, H2, ga2, need("sq2"), dot, vec[VEC["sqb2"], 0:1, : plan.q2], need("ex2"), vec[VEC["exb2"], 0:1]
    )
    E2 = ref["E2"]
    post(5, dot_moments(E2, lines(ga2), need("e2")))
    transpose(lines(ga2), ref["ga2t"])
    for d in range(R):
        arrived("og", plan.hrows, 1, d)
    tot = fetch(5)
    ne2 = coefficients(tot[0], tot[1], inv_half, vector("eg2"), vector("eb2"))
    leave, D, og = ref["leave"], ref["D"], ref["og_in"]

    def step(p):
        e = line(E2[p])
        v = e * ne2[0] + ne2[1] + line(ent[p])
        sg = sigmoid(v)
        m = mask_row(0, 0, p)
        leave[p] = pixels(m * v * sg).astype(bf16)
        g = line(og[p]) * m * (sg * (1.0 + v * (1.0 - sg)))
        D[p] = pixels(g)
        return g, g * (e * ne2[2] + ne2[3])

    parts = over_rows(step, 2)
    vec_grads["eb2"], vec_grads["eg2"] = parts
    post(6, parts)
    send_out(leave, "act", plan.hrows, 1)
    blocks("k1", ref["bd1t"], True)

    def back_rule(sums, inverse, gain, norm):
        a = gain * norm[2]
        k0 = a * (sums[0] + norm[3] * sums[1]) * inverse
        return a, k0, a * norm[2] * sums[1] * inverse

    def back_excite(dg, kept, hidden, conv, norm, sq, sq_form, ex, out):
        pooled, pre, inner, gate = kept

        def step(p):
            return (line(dg[p]) * line(hidden[p]),)

        (dgate,) = over_rows(step, 1)
        dpre = dgate * gate * (1.0 - gate)
        dsq = small_dot(dpre, ex[...], dot_nt) * slope(pre)
        dpool = wide(small_dot(dsq, sq[...], sq_form) / half_count)
        gate_wide = wide(gate)

        def step_two(p):
            v = line(conv[p])
            g = (line(dg[p]) * gate_wide + dpool) * mask_row(0, 0, p)
            g = g * slope(v * norm[0] + norm[1])
            out[p] = pixels(g)
            return g, g * (v * norm[2] + norm[3])

        return over_rows(step_two, 2), dpre, dsq

    def excite_grads(name, kept, dpre, dsq):
        pooled, pre, inner, gate = kept
        put("sq" + name, small_outer(dsq, pooled))
        put("ex" + name, small_outer(inner, dpre))
        vec_grads["exb" + name] = dpre
        count = dsq.shape[1]
        eye = (
            lax.broadcasted_iota(jnp.int32, (count, width), 0)
            == lax.broadcasted_iota(jnp.int32, (count, width), 1)
        ).astype(f32).astype(bf16)
        vec_grads["sqb" + name] = small_dot(dsq, eye, dot)

    def turn(gradient_ref, start):
        out = []
        for h in range(width // span):
            piece = flat(gradient_ref[start : start + side, :, h * span : (h + 1) * span])
            out.append(piece.astype(f32).T.astype(bf16))
        return out

    d1, dg, GR = ref["d1"], ref["dg"], ref["GR"]
    tot = fetch(6)
    rule = back_rule((tot[0], tot[1]), inv_half, vector("eg2"), ne2)

    def step(p):
        v = rule[0] * line(D[p]) - mask_row(0, 0, p) * (rule[1] + rule[2] * line(E2[p]))
        d1[p] = pixels(v).astype(bf16)

    over_rows(step)
    full_dot(dg, lines(d1), need("e2"), dot_nt)
    parts, dpre, dsq = back_excite(dg, kept2, H2, c2, nc2, need("sq2"), dot_nt, need("ex2"), GR)
    vec_grads["gb2"], vec_grads["gg2"] = parts
    post(7, parts)
    put("e2", dot(ref["ga2t"][...], lines(d1)))
    excite_grads("2", kept2, dpre, dsq)
    pump(0)
    tot = fetch(7)
    rule = back_rule((tot[0], tot[1]), inv_half, vector("gg2"), nc2)
    vd = ref["vd"]
    vd[:, 0:1] = jnp.zeros((3, 1, side, width), bf16)
    vd[:, side + 1 :] = jnp.zeros((3, 1, side, width), bf16)

    def step(p):
        v = rule[0] * line(GR[p]) - mask_row(0, 0, p) * (rule[1] + rule[2] * line(c2[p]))
        three(vd, p, pixels(v))

    over_rows(step)

    def convolve_back(taps, first, weights, out):
        for h in range(width // span):
            cut = slice(h * span, (h + 1) * span)
            left = [flat(var[start : start + side, :, cut]) for var, start in taps]
            rows = slice(first * span, (first + len(taps)) * span)
            acc = dot(jnp.concatenate(left, axis=1), weights[h, rows])
            out[:, :, cut] = acc.reshape(side, side, span)

    DA = ref["DA"]
    convolve_back(
        [(vd.at[2 - t % 3], 2 - t // 3) for t in ORDER],
        0,
        ref["bd2t"],
        DA.at[0],
    )

    def step(p):
        v = line(R2[p])
        g = line(DA[0, p]) * mask_row(0, 0, p) * slope(v * n2[0] + n2[1])
        GR[p] = pixels(g)
        return g, g * (v * n2[2] + n2[3])

    parts = over_rows(step, 2)
    vec_grads["b2"], vec_grads["g2"] = parts
    post(8, parts)
    pump(0)
    groups_grad("k2", taps2, turn(vd.at[1], 1))
    tot = fetch(8)
    rule = back_rule((tot[0], tot[1]), inv_half, vector("g2"), n2)

    def step(p):
        v = rule[0] * line(GR[p]) - mask_row(0, 0, p) * (rule[1] + rule[2] * line(R2[p]))
        d1[p] = pixels(v).astype(bf16)

    over_rows(step)
    full_dot(GR, lines(d1), need("w2"), dot_nt)
    pump(0)

    def step(p):
        e, sc = line(E1[p]), line(SC[p])
        g = line((D[p] + GR[p]).astype(bf16))
        g = g * mask_row(0, 0, p) * slope(e * ne[0] + sc * ns[0] + both_shifts)
        D[p] = pixels(g)
        return g, g * (e * ne[2] + ne[3]), g * (sc * ns[2] + ns[3])

    parts = over_rows(step, 3)
    vec_grads["eb1"], vec_grads["eg1"], vec_grads["sg1"] = parts
    vec_grads["sb1"] = parts[0]
    post(9, parts)
    put("w2", dot(ref["entt"][...], lines(d1)))
    pump(1, 0)
    tot = fetch(9, 3)
    rule_e = back_rule((tot[0], tot[1]), inv_half, vector("eg1"), ne)
    rule_s = back_rule((tot[0], tot[2]), inv_half, vector("sg1"), ns)
    d2 = ref["d2"]

    def step(p):
        g, m = line(D[p]), mask_row(0, 0, p)
        v = rule_e[0] * g - m * (rule_e[1] + rule_e[2] * line(E1[p]))
        d1[p] = pixels(v).astype(bf16)
        v = rule_s[0] * g - m * (rule_s[1] + rule_s[2] * line(SC[p]))
        d2[p] = pixels(v).astype(bf16)

    over_rows(step)
    full_dot(dg, lines(d1), need("e1"), dot_nt)
    pump(1)
    parts, dpre, dsq = back_excite(dg, kept1, H1, c1, nc1, need("sq1"), dot, need("ex1"), GR)
    vec_grads["gb1"], vec_grads["gg1"] = parts
    post(10, parts)
    put("e1", dot(ref["ga1t"][...], lines(d1)))
    put("s1", dot_tn(even[...].reshape(pix, cin), lines(d2)))
    excite_grads("1", kept1, dpre, dsq)
    pump(2, 1)
    tot = fetch(10)
    rule = back_rule((tot[0], tot[1]), inv_half, vector("gg1"), nc1)

    def step(p):
        v = rule[0] * line(GR[p]) - mask_row(0, 0, p) * (rule[1] + rule[2] * line(c1[p]))
        three(vd, p, pixels(v), both=False)

    over_rows(step)
    pump(0)
    sums = []
    for ab, (a, b) in enumerate(PHASES):
        chosen = []
        first = (0, 1, 3, 5)[ab]
        for t in ORDER[first : first + (1, 2, 2, 4)[ab]]:
            chosen.append((vd.at[2 if t % 3 == 0 else 1], 2 if t // 3 == 0 else 1))
        convolve_back(chosen, first, ref["bd1t"], DA.at[ab])

        def step(p, ab=ab, a=a, b=b):
            v = line(R1[at_phase(ab, p)])
            g = line(DA[ab, p]) * mask_row(a, b, p) * slope(v * n1[0] + n1[1])
            DA[ab, p] = pixels(g)
            return g, g * (v * n1[2] + n1[3])

        sums.append(over_rows(step, 2))
        if ab == 1:
            pump(2, 1)
        elif ab == 3:
            pump(0)
    parts = (sum(x[0] for x in sums), sum(x[1] for x in sums))
    vec_grads["b1"], vec_grads["g1"] = parts
    post(11, parts)
    pump(2)
    groups_grad("k1", taps1, turn(vd.at[1], 1))
    ids = lax.broadcasted_iota(jnp.int32, (VEC_ROWS, width), 0)
    value = jnp.zeros((VEC_ROWS, width), f32)
    for name, at in VEC.items():
        value = jnp.where(ids == at, jnp.broadcast_to(vec_grads[name], value.shape), value)
    put(VECTORS, value)
    pump(3, 2, 0)
    tot = fetch(11)
    rule = back_rule((tot[0], tot[1]), inv_full, vector("g1"), n1)
    dr = ref["dr"]
    for ab, (a, b) in enumerate(PHASES):

        def step(p, ab=ab, a=a, b=b):
            v = rule[0] * line(DA[ab, p])
            v = v - mask_row(a, b, p) * (rule[1] + rule[2] * line(R1[at_phase(ab, p)]))
            dr[at_phase(ab, p)] = pixels(v).astype(bf16)

        over_rows(step)
    total = None
    for k in range(bands):
        term = dot(ref["xpt"][k], dr[k].reshape(pix, width))
        total = term if total is None else total + term
    put("w1", total)
    pump(4, 3, 1)
    cut = cin // 2
    ref["dxo0"][...] = jnp.zeros((2 * side, plan.cols, 128), bf16)
    ref["dxo1"][...] = jnp.zeros((2 * side, plan.cols, 128), bf16)
    stepwise = plan.each == bands
    for d in [*range(1, bands), 0]:
        k = lax.rem(r + plan.copies * d, R) * plan.rows // band if stepwise else d
        for part in range(2):
            dxo = ref[f"dxo{part}"]
            rows = slice(part * cut, (part + 1) * cut)
            v = dot_nt(dr[k].reshape(pix, width), need("w1")[rows, :])
            w = dot_nt(
                d2[pl.ds(k * bhalf, bhalf)].reshape(bhalf * side, width), need("s1")[rows, :]
            )
            v = jnp.concatenate([v[: bhalf * side] + w, v[bhalf * side :]], axis=0)
            v = dot(ref["unsort"][...], v.astype(bf16)).astype(bf16)
            dxo[pl.ds(k * band, band), :, :cut] = v.reshape(band, plan.cols, cut)
            if stepwise:
                send_out(dxo, "dx", plan.rows, part, (d,))
        pump(*((4, 3, 2, 1), (4, 3, 1), (4, 3, 2), (1, 0))[(d - 1) % 4])
    if not stepwise:
        send_out(ref["dxo0"], "dx", plan.rows, 0)
        send_out(ref["dxo1"], "dx", plan.rows, 1)
    for _ in range(9):
        pump()
    for wait in waits:
        wait()
    for m in range(plan.M):
        t = (m % plan.each) * plan.copies + lax.rem(r, plan.copies)
        for out in ("act", "dx"):
            there = ref[out].at[0, m, 0] if out == "act" else ref[out].at[m, 0]
            pltpu.make_async_copy(there, there, ref[out + "_r"].at[m]).wait()


WEIGHTS = ("w1", "k1", "k2", "sq1", "ex1", "e1", "s1", "w2", "sq2", "ex2", "e2")


def run_main(plan, arrays):
    side, width, cin = plan.side, plan.width, plan.cin
    wide = 4 * plan.gw
    field = (side, side, width)
    scratch = {
        "x_in": pltpu.VMEM((2 * side, plan.cols, cin), bf16),
        "og_in": pltpu.VMEM(field, bf16),
        "st": pltpu.VMEM((EXCHANGES, plan.I, 2, 8, 128), f32),
        "hm": pltpu.VMEM((plan.pix, 128), f32),
        "cm": pltpu.VMEM((2, side, width), f32),
        **{
            name: pltpu.VMEM((width // wide, plan.taps * wide, wide), bf16)
            for name in ("bd1", "bd2", "bd1t", "bd2t")
        },
        "xpt": pltpu.VMEM((plan.bands, cin, plan.pix), bf16),
        **{name: pltpu.VMEM((width, plan.pix), bf16) for name in ("ga1t", "ga2t", "entt")},
        "sort": pltpu.VMEM((plan.pix, plan.pix), bf16),
        "unsort": pltpu.VMEM((plan.pix, plan.pix), bf16),
        "xp": pltpu.VMEM((plan.bands, 2 * plan.band, side, cin), bf16),
        "R1": pltpu.VMEM((plan.bands, 2 * plan.band, side, width), f32),
        "va": pltpu.VMEM((6, side + 1, side, width), bf16),
        "vb": pltpu.VMEM((3, side + 2, side, width), bf16),
        "vd": pltpu.VMEM((3, side + 2, side, width), bf16),
        "DA": pltpu.VMEM((4,) + field, f32),
        "dr": pltpu.VMEM((plan.bands, 2 * plan.band, side, width), bf16),
        "dxo0": pltpu.VMEM((2 * side, plan.cols, 128), bf16),
        "dxo1": pltpu.VMEM((2 * side, plan.cols, 128), bf16),
    }
    for name in ("SC", "H1", "E1", "R2", "H2", "E2", "D", "GR"):
        scratch[name] = pltpu.VMEM(field, f32)
    for name in ("c1", "ga1", "ent", "c2", "ga2", "leave", "d1", "d2", "dg"):
        scratch[name] = pltpu.VMEM(field, bf16)
    for name in ("x", "og"):
        scratch[name + "_s"] = pltpu.SemaphoreType.DMA((max(plan.R - 1, 1),))
        scratch[name + "_r"] = pltpu.SemaphoreType.DMA((plan.R,))
    scratch["st_s"] = pltpu.SemaphoreType.DMA((EXCHANGES, max(plan.I - 1, 1)))
    scratch["st_r"] = pltpu.SemaphoreType.DMA((EXCHANGES, plan.I))
    for name in ("act", "dx"):
        scratch[name + "_s"] = pltpu.SemaphoreType.DMA((2, plan.R // plan.copies))
        scratch[name + "_r"] = pltpu.SemaphoreType.DMA((plan.M,))
    for name in NAMES + WEIGHTS:
        scratch[name + "_v"] = pltpu.VMEM(arrays[name].shape, bf16)
    scratch["vec"] = pltpu.VMEM((len(NAMES), 8, width), f32)
    scratch["loads"] = pltpu.SemaphoreType.DMA((len(NAMES + WEIGHTS),))
    scratch["local"] = pltpu.VMEM((plan.blocks, 16, 128), bf16)
    for level, room in enumerate(plan.rooms):
        scratch[f"got{level}"] = pltpu.VMEM((room, 16, 128), bf16)
        if level:
            scratch[f"sum{level - 1}"] = pltpu.VMEM((room, 16, 128), bf16)
    most = max(plan.sizes.values())
    for name in ("rs", "ag"):
        scratch[name + "_s"] = pltpu.SemaphoreType.DMA((len(plan.streams), 4, most - 1))
        scratch[name + "_r"] = pltpu.SemaphoreType.DMA((len(plan.streams), 4, most))
    inputs = ("x", "og", "vr", "vc") + NAMES + WEIGHTS
    outputs = ("act", "dx", "grads")
    names = inputs + outputs + tuple(scratch)
    any_space = pl.BlockSpec(memory_space=pl.ANY)
    smem = pl.BlockSpec(memory_space=pltpu.SMEM)
    vmem = pl.BlockSpec(memory_space=pltpu.VMEM)
    return pl.pallas_call(
        functools.partial(main_kernel, plan, names),
        out_shape=(
            pltpu.VMEM((1, plan.M, 1, plan.hrows, side, width), bf16),
            pltpu.VMEM((plan.M, 1, plan.rows, plan.cols, 128), bf16),
            pltpu.VMEM((plan.blocks, 16, 128), bf16),
        ),
        in_specs=[any_space, any_space, smem, smem] + [any_space] * (len(NAMES) + len(WEIGHTS)),
        out_specs=(vmem, vmem, vmem),
        scratch_shapes=list(scratch.values()),
        compiler_params=pltpu.CompilerParams(
            collective_id=0, has_side_effects=True, vmem_limit_bytes=58 * 1024 * 1024
        ),
        name="blocks",
    )(*[arrays[name] for name in inputs])


OUTS = (
    "w1", "g1", "b1", "k1", "gg1", "gb1", "sq1", "sqb1", "ex1", "exb1", "e1", "eg1", "eb1",
    "s1", "sg1", "sb1", "w2", "g2", "b2", "k2", "gg2", "gb2", "sq2", "sqb2", "ex2", "exb2",
    "e2", "eg2", "eb2",
)


def unpack_kernel(plan, blocks, act_in, dx_in, *rest):
    count = len(OUTS) + 2
    outs, bufs, sems = rest[:count], rest[count:-1], rest[-1]
    copies = []
    for k, whole in enumerate((act_in, dx_in)):
        copies.append(pltpu.make_async_copy(whole, outs[k], sems.at[k]))
        copies[-1].start()
    order = sorted(plan.starts, key=lambda name: plan.starts[name])
    order = [name for name in order if name not in (VECTORS, LAST_TAP)]
    order.sort(key=lambda name: -16 * plan.starts[name][1])

    def tile(name, k):
        start, per_tile = plan.starts[name]
        at = start + k * per_tile
        return blocks[at : at + per_tile].reshape(16 * per_tile, 128).astype(f32)

    tiles = plan.width // 128
    vec = None
    turn = [OUTS.index(name) for name in order]
    turn += [k for k, name in enumerate(OUTS) if name in VEC]
    for k in turn:
        name, out = OUTS[k], bufs[k]
        if name in VEC and vec is None:
            vec = jnp.concatenate([tile(VECTORS, k) for k in range(tiles)], axis=1)
        if name in VEC:
            size = out.shape[0]
            out[...] = vec[VEC[name] : VEC[name] + 1, :size].reshape(size)
        elif name[0] == "k":

            def run(t, carry, name=name, out=out, last_tap=False):
                for lane in range(tiles):
                    start, per_tile = plan.starts[name]
                    at = start + lane * per_tile + t * (plan.gw // 16)
                    if last_tap:
                        start, per_tile = plan.starts[LAST_TAP]
                        at = start + lane * per_tile
                    piece = blocks[pl.ds(at, plan.gw // 16)].reshape(plan.gw, 128)
                    piece = piece.astype(f32).T
                    for j in range(128 // plan.gw):
                        group = lane * (128 // plan.gw) + j
                        out[t, group, :, : plan.gw] = piece[j * plan.gw : (j + 1) * plan.gw]
                return carry

            if name == "k2":
                lax.fori_loop(0, plan.taps - 1, run, 0)
                run(plan.taps - 1, 0, last_tap=True)
            else:
                lax.fori_loop(0, plan.taps, run, 0)
        elif name == "sq2":
            for lane in range(tiles):
                out[128 * lane : 128 * lane + 128] = tile(name, lane).T
        else:
            for lane in range(tiles):
                out[:, 128 * lane : 128 * lane + 128] = tile(name, lane)
        copies.append(pltpu.make_async_copy(out, outs[k + 2], sems.at[k + 2]))
        copies[-1].start()
    for copy in copies:
        copy.wait()


def unpack(plan, act, dx, grads, weights):
    shapes = []
    for name, w in zip(OUTS, weights):
        shape = w.shape[:3] + (128,) if name[0] == "k" else w.shape
        shapes.append(jax.ShapeDtypeStruct(shape, f32))
    any_space = pl.BlockSpec(memory_space=pl.ANY)
    return pl.pallas_call(
        functools.partial(unpack_kernel, plan),
        out_shape=[jax.ShapeDtypeStruct(v.shape, v.dtype) for v in (act, dx)] + shapes,
        in_specs=[pl.BlockSpec(memory_space=pltpu.VMEM)] * 3,
        out_specs=[any_space] * (len(shapes) + 2),
        scratch_shapes=[pltpu.VMEM(v.shape, v.dtype) for v in shapes]
        + [pltpu.SemaphoreType.DMA((len(shapes) + 2,))],
        compiler_params=pltpu.CompilerParams(vmem_limit_bytes=24 * 1024 * 1024),
        name="unpack",
    )(grads, act, dx)


def body(sizes, input_maps, valid_rows, valid_cols, *rest):
    weights, output_grad = rest[:-1], rest[-1]
    (w1, g1, b1, k1, gg1, gb1, sq1, sqb1, ex1, exb1, e1, eg1, eb1, s1, sg1, sb1) = weights[:16]
    (w2, g2, b2, k2, gg2, gb2, sq2, sqb2, ex2, exb2, e2, eg2, eb2) = weights[16:]
    turned = sq1.T
    plan = Plan(sizes, [v.shape for v in (input_maps, output_grad, w1, k1, turned, sq2)])
    vectors = (
        g1, b1, gg1, gb1, exb1, eg1, eb1, sg1, sb1, sqb1, g2, b2, gg2, gb2, exb2, eg2, eb2, sqb2,
    )
    arrays = dict(
        x=input_maps, og=output_grad, vr=valid_rows.T, vc=valid_cols.T, w1=w1,
        k1=k1, k2=k2,
        sq1=turned, ex1=ex1, e1=e1, s1=s1, w2=w2, sq2=sq2, ex2=ex2, e2=e2,
        **dict(zip(NAMES, vectors)),
    )
    act, dx, grads = run_main(plan, arrays)
    act, dx, *out = unpack(plan, act, dx, grads, weights[:6] + (turned,) + weights[7:])
    out[6] = out[6].T
    for at in (3, 19):
        out[at] = out[at][..., : plan.gw]
    dx = dx[..., : plan.cin // 2]
    return (act, dx, *out)


def solution(mesh):
    tiled = P(None, "img", "row", None, None)
    image = P(None, "img")
    sizes = tuple(mesh.shape[name] for name in ("section", "img", "row"))
    return jax.shard_map(
        functools.partial(body, sizes),
        mesh=mesh,
        in_specs=(tiled, image, image) + (P(),) * 29 + (tiled,),
        out_specs=(
            P("section", None, "img", "row", None, None),
            P(None, "img", "row", None, "section"),
        )
        + (P(),) * 29,
        check_vma=False,
    )
```

```python
import functools

import jax
import jax.numpy as jnp
from jax import lax
from jax.experimental import pallas as pl
from jax.experimental.pallas import tpu as pltpu
from jax.sharding import PartitionSpec as P

epsilon = 1e-05
f32 = jnp.float32
bf16 = jnp.bfloat16
MESH = pl.DeviceIdType.MESH
PHASES = ((0, 0), (0, 1), (1, 0), (1, 1))
ORDER = (4, 3, 5, 1, 7, 0, 2, 6, 8)
EXCHANGES = 12
NAMES = (
    "g1", "b1", "gg1", "gb1", "exb1", "eg1", "eb1", "sg1", "sb1", "sqb1",
    "g2", "b2", "gg2", "gb2", "exb2", "eg2", "eb2", "sqb2",
)
VEC = {name: k for k, name in enumerate(NAMES)}
VEC_ROWS = 32
VECTORS = "vec"
LAST_TAP = "k9"


def segments_of(cin, width, taps, group, sq1, sq2, devices):
    layout = (
        (("e2", width), ("sq2", sq2), ("ex2", sq2)),
        (("k2", (taps - 1) * group), ("w2", width)),
        (("e1", width), ("s1", cin), ("sq1", sq1), ("ex1", sq1), (LAST_TAP, group)),
        (("k1", taps * group), (VECTORS, VEC_ROWS)),
        (("w1", cin),),
    )
    starts, segments, at = {}, [], 0
    for parts in layout:
        base = at
        for name, rows in parts:
            starts[name] = (at, rows // 16)
            at += rows // 16 * (width // 128)
        units = -(-(at - base) // devices)
        first = units // 2 * devices if 0 < len(segments) < len(layout) - 1 else 0
        segments.append((base, units * devices, at, first))
        at = base + units * devices
    return starts, tuple(segments), at


def sigmoid(v):
    return 0.5 * jnp.tanh(0.5 * v) + 0.5


def silu(v):
    return v * sigmoid(v)


def slope(v):
    s = sigmoid(v)
    return s * (1.0 + v * (1.0 - s))


def dot(left, right):
    return jnp.dot(left, right, preferred_element_type=f32)


def dot_nt(left, right):
    return lax.dot_general(left, right, (((1,), (1,)), ((), ())), preferred_element_type=f32)


def dot_tn(left, right):
    return lax.dot_general(left, right, (((0,), (0,)), ((), ())), preferred_element_type=f32)


def parts_of(v):
    high = v.astype(bf16).astype(f32)
    return high, v - high


def stacked(rows, width):
    ids = lax.broadcasted_iota(jnp.int32, (16, width), 0)
    total = jnp.zeros((16, width), f32)
    for k, row in enumerate(rows):
        total = jnp.where(ids == k, jnp.broadcast_to(row, (16, width)), total)
    return total.astype(bf16)


def small_dot(row, weight, form):
    out = form(stacked(parts_of(row), row.shape[1]), weight)
    return out[0:1] + out[1:2]


def small_outer(left, right):
    lh, ll = parts_of(left)
    rh, rl = parts_of(right)
    return dot_tn(
        stacked((lh, ll, lh, ll), left.shape[1]), stacked((rh, rh, rl, rl), right.shape[1])
    )


def fold(v):
    return v[0] + v[1]


def column(acc):
    return jnp.sum(acc, axis=0, keepdims=True)


class Plan:
    def __init__(self, mesh_sizes, args):
        self.S, self.I, self.R = mesh_sizes
        x, og, w1, k1, sq1, sq2 = args
        self.M, _, self.rows, self.cols, self.cin = x
        _, _, self.hrows, self.side, self.width = og
        self.taps, self.groups, self.gw, _ = k1
        self.q1, self.q2 = sq1[0], sq2[1]
        self.each = self.M // self.S
        self.copies = self.R // self.each
        self.pix = self.side * self.side
        self.band = self.pix // self.cols
        self.bands = 2 * self.side // self.band
        self.starts, self.segments, self.blocks = segments_of(
            self.cin, self.width, self.taps, self.gw, self.q1, self.q2, self.S * self.I * self.R
        )
        self.X = 1
        while self.X * self.X < self.R:
            self.X *= 2
        self.Y = self.R // self.X
        self.sizes = {"s": self.S, "x": self.X, "y": self.Y, "r": self.R, "i": self.I}
        self.streams = []
        self.members = []
        self.rooms = [0] * 4
        for base, size, _, first in self.segments:
            halves = [(base, first, "sxyi"), (base + first, size - first, "syxi")]
            if not first:
                halves = [(base, size, "sri")]
            self.members.append(range(len(self.streams), len(self.streams) + len(halves)))
            for start, count, order in halves:
                self.streams.append((start, count, order, tuple(self.rooms)))
                for level, axis in enumerate(order):
                    self.rooms[level] += count
                    count //= self.sizes[axis]

    def piece(self, stream, level):
        _, size, order, _ = self.streams[stream]
        for axis in order[: level + 1]:
            size //= self.sizes[axis]
        return size


def main_kernel(plan, names, *refs):
    ref = dict(zip(names, refs))
    S, I, R = plan.S, plan.I, plan.R
    side, width, pix, cin = plan.side, plan.width, plan.pix, plan.cin
    half_width = width // 2
    s, i, r = lax.axis_index("section"), lax.axis_index("img"), lax.axis_index("row")
    mine = s * plan.each + r // plan.copies
    waits = []

    barrier = pltpu.get_barrier_semaphore()
    peers = []
    for ds in range(S):
        for dr in range(R):
            if ds or dr:
                peers.append((lax.rem(s + ds, S), i, lax.rem(r + dr, R)))
    for di in range(1, I):
        peers.append((s, lax.rem(i + di, I), r))
    for peer in peers:
        pl.semaphore_signal(barrier, inc=1, device_id=peer, device_id_type=MESH)

    own = []
    loads = {}

    def load(*which):
        for name in which:
            at = (NAMES + WEIGHTS).index(name)
            loads[name] = pltpu.make_async_copy(ref[name], ref[name + "_v"], ref["loads"].at[at])
            loads[name].start(priority=int(name[0] == "k"))

    def need(name):
        if name in loads:
            loads.pop(name).wait()
        return ref[name + "_v"]

    load("w1", "g1", "b1", "k1", "k2")
    for name, rows in (("x", plan.rows), ("og", plan.hrows)):
        copy = pltpu.make_async_copy(
            ref[name].at[mine, 0],
            ref[name + "_in"].at[pl.ds(r * rows, rows)],
            ref[name + "_r"].at[r],
        )
        copy.start()
        own.append(copy)
    pl.semaphore_wait(barrier, len(peers))
    for name, rows in (("x", plan.rows), ("og", plan.hrows)):
        for d in range(1, R):
            t = lax.rem(r + d, R)
            copy = pltpu.make_async_remote_copy(
                src_ref=ref[name].at[s * plan.each + t // plan.copies, 0],
                dst_ref=ref[name + "_in"].at[pl.ds(r * rows, rows)],
                send_sem=ref[name + "_s"].at[d - 1],
                recv_sem=ref[name + "_r"].at[r],
                device_id=(s, i, t),
                device_id_type=MESH,
            )
            copy.start()
            waits.append(copy.wait_send)

    load("s1", *NAMES[2:], "sq1", "ex1", "e1", "w2", "sq2", "ex2", "e2")

    def arrived(name, rows, position, d):
        if d == 0:
            own[position].wait()
        else:
            t = lax.rem(r + d, R)
            there = ref[name + "_in"].at[pl.ds(t * rows, rows)]
            pltpu.make_async_remote_copy(
                src_ref=there,
                dst_ref=there,
                send_sem=ref[name + "_s"].at[d - 1],
                recv_sem=ref[name + "_r"].at[t],
                device_id=(s, i, t),
                device_id_type=MESH,
            ).wait_recv()

    st = ref["st"]

    def pairs_of(k):
        return 2 if k in (0, 1, 9) else 1

    def stats_copy(k, d, slot):
        return pltpu.make_async_remote_copy(
            src_ref=st.at[k, slot, pl.ds(0, pairs_of(k))],
            dst_ref=st.at[k, slot, pl.ds(0, pairs_of(k))],
            send_sem=ref["st_s"].at[k, d - 1],
            recv_sem=ref["st_r"].at[k, slot],
            device_id=(s, lax.rem(i + d, I), r),
            device_id_type=MESH,
        )

    def post(k, rows):
        ids = lax.broadcasted_iota(jnp.int32, (8, 128), 0)
        rows = [*rows, *([None] * (len(rows) % 2))]
        for pair in range(len(rows) // 2):
            value = jnp.zeros((8, 128), f32)
            for j in range(8):
                row = rows[2 * pair + j // 4]
                if row is not None:
                    piece = row[:, 128 * (j % 4) : 128 * (j % 4) + 128]
                    value = jnp.where(ids == j, jnp.broadcast_to(piece, (8, 128)), value)
            st[k, i, pair] = value
        for d in range(1, I):
            stats_copy(k, d, i).start()
        for d in range(1, I):
            if k:
                stats_copy(k - 1, d, i).wait_send()
            if k == EXCHANGES - 1:
                waits.append(stats_copy(k, d, i).wait_send)

    def fetch(k, count=2):
        for d in range(1, I):
            stats_copy(k, d, lax.rem(i + d, I)).wait_recv()
        out = []
        for pair in range((count + 1) // 2):
            value = st[k, 0, pair]
            for j in range(1, I):
                value = value + st[k, j, pair]
            for half in range(2):
                out.append(
                    jnp.concatenate(
                        [
                            jnp.broadcast_to(value[4 * half + j : 4 * half + j + 1], (8, 128))
                            for j in range(4)
                        ],
                        axis=1,
                    )
                )
        return out

    vec = ref["vec"]

    def keep_vectors():
        for name in NAMES:
            row = need(name)[...].astype(f32)
            size = row.shape[0]
            vec[VEC[name], :, :size] = jnp.broadcast_to(row.reshape(1, size), (8, size))

    def vector(name):
        return vec[VEC[name]]

    vr, vc = ref["vr"][0, mine], ref["vc"][0, mine]
    q_ids = lax.broadcasted_iota(jnp.int32, (side, width), 0)
    first_col, last_col = q_ids == 0, q_ids == side - 1
    cm = ref["cm"]
    for b in range(2):
        cm[b] = (2 * q_ids + b < vc).astype(f32)

    def line(value):
        return value.astype(f32).reshape(2, 8, width)

    def pixels(value):
        return value.reshape(side, width)

    def mask_row(a, b, p):
        return line(cm[b]) * (2 * p + a < vr).astype(f32)

    def wide(row):
        return jnp.broadcast_to(row, (8, width))

    row_count = jnp.full((1, width), vr * vc, jnp.int32).astype(f32)
    half_count = jnp.full((1, width), ((vr + 1) // 2) * ((vc + 1) // 2), jnp.int32).astype(f32)

    def over_rows(step, *accs):
        init = tuple(jnp.zeros((8, width), f32) for _ in range(accs[0] if accs else 0))

        def run(p, carry):
            out = step(p)
            if not carry:
                return carry
            return tuple(c + fold(o) for c, o in zip(carry, out))

        return tuple(column(c) for c in lax.fori_loop(0, side, run, init, unroll=16))

    def full_dot(out, left, weight, form=dot):
        wide = out.shape[-1]
        step = min(256, wide)
        for h in range(wide // step):
            cut = slice(h * step, h * step + step)
            w = weight[:, cut] if form is dot else weight[cut, :]
            out[:, :, cut] = form(left, w).reshape(side, side, step).astype(out.dtype)

    hm = ref["hm"]
    for p in range(side):
        hm[p * side : (p + 1) * side] = cm[0][:, :128] * (2 * p < vr).astype(f32)

    def with_moments(out, products):
        sums = []
        for h, product in enumerate(products):
            span = product.shape[1]
            value = product.astype(out.dtype)
            out[:, :, h * span : (h + 1) * span] = value.reshape(side, side, span)
            value = value.astype(f32)
            valid = value * jnp.concatenate([hm[...]] * (span // 128), axis=1)
            sums.append(
                [
                    jnp.sum(x.reshape(pix // 8, 8, span), axis=0)
                    for x in (valid, valid * value)
                ]
            )
        return [column(jnp.concatenate(x, axis=1)) for x in zip(*sums)]

    def dot_moments(out, left, weight):
        return with_moments(
            out, (dot(left, weight[:, cut : cut + 256]) for cut in range(0, width, 256))
        )

    def flat(value):
        return value.reshape(pix, value.shape[-1])

    def lines(ref_, start=0):
        return flat(ref_[start : start + side])

    G, F = ref["local"], ref["grads"]
    lead = None if plan.copies == 1 else (lax.rem(r, plan.copies) == 0).astype(f32)

    def put(name, value, row=0, lane=0):
        if lead is not None:
            value = value * lead
        start, per_tile = plan.starts[name]
        count = value.shape[0] // 16
        for k in range(value.shape[1] // 128):
            piece = value[:, 128 * k : 128 * k + 128].astype(bf16).reshape(count, 16, 128)
            at = start + (lane // 128 + k) * per_tile + row // 16
            G[at : at + count] = piece

    X, Y = plan.X, plan.Y
    x, y = lax.rem(r, X), r // X
    axes = {
        "s": (S, s, lambda t: (t, i, r)),
        "r": (R, r, lambda t: (s, i, t)),
        "x": (X, x, lambda t: (s, i, y * X + t)),
        "y": (Y, y, lambda t: (s, i, t * X + x)),
        "i": (I, i, lambda t: (s, t, r)),
    }

    def scatter_source(stream, level):
        base, _, order, offsets = plan.streams[stream]
        if level == 0:
            return G, base
        return ref[f"sum{level - 1}"], offsets[level]

    def scatter_copies(stream, level, outgoing):
        base, size, order, offsets = plan.streams[stream]
        count, me, device = axes[order[level]]
        piece = plan.piece(stream, level)
        source, first = scatter_source(stream, level)
        for d in range(1, count):
            t = lax.rem(me + d, count)
            slot = me if outgoing else t
            copy = pltpu.make_async_remote_copy(
                src_ref=source.at[pl.ds(first + t * piece, piece)],
                dst_ref=ref[f"got{level}"].at[pl.ds(offsets[level] + slot * piece, piece)],
                send_sem=ref["rs_s"].at[stream, level, d - 1],
                recv_sem=ref["rs_r"].at[stream, level, slot],
                device_id=device(t),
                device_id_type=MESH,
            )
            if outgoing:
                copy.start()
                sent[stream].append(copy)
            else:
                copy.wait_recv()

    def add_up(stream, level):
        base, size, order, offsets = plan.streams[stream]
        count, me, _ = axes[order[level]]
        piece = plan.piece(stream, level)
        source, first = scatter_source(stream, level)
        got = ref[f"got{level}"]
        if level < len(order) - 1:
            out, at = ref[f"sum{level}"], offsets[level + 1]
        else:
            out, at = F, own_part(stream, len(order))
        step = next(k for k in (16, 12, 10, 9, 8, 7, 6, 5, 4, 3, 2, 1) if piece % k == 0)

        def run(k, carry):
            total = source[pl.ds(first + me * piece + k * step, step)].astype(f32)
            for d in range(1, count):
                t = lax.rem(me + d, count)
                total = total + got[pl.ds(offsets[level] + t * piece + k * step, step)].astype(f32)
            out[pl.ds(at + k * step, step)] = total.astype(bf16)
            return carry

        lax.fori_loop(0, piece // step, run, 0)

    def own_part(stream, depth):
        at, _, order, _ = plan.streams[stream]
        for level in range(depth):
            at = at + axes[order[level]][1] * plan.piece(stream, level)
        return at

    def gather_copies(stream, level, outgoing):
        count, me, device = axes[plan.streams[stream][2][level]]
        base = own_part(stream, level)
        piece = plan.piece(stream, level)
        for d in range(1, count):
            t = lax.rem(me + d, count)
            slot = me if outgoing else t
            there = F.at[pl.ds(base + slot * piece, piece)]
            copy = pltpu.make_async_remote_copy(
                src_ref=there,
                dst_ref=there,
                send_sem=ref["ag_s"].at[stream, level, d - 1],
                recv_sem=ref["ag_r"].at[stream, level, slot],
                device_id=device(t),
                device_id_type=MESH,
            )
            if outgoing:
                copy.start()
                sent[stream].append(copy)
            else:
                copy.wait_recv()

    done = [0] * len(plan.segments)
    started = []
    sent = [[] for _ in plan.streams]

    def pump(*which):
        for g in which or tuple(started):
            if g not in started:
                started.insert(0, g)
            k = done[g]
            depth = len(plan.streams[plan.members[g][0]][2])
            if k > 2 * depth:
                continue
            done[g] += 1
            if k == 0:
                base, size, used, _ = plan.segments[g]
                if used < base + size:
                    G[used : base + size] = jnp.zeros((base + size - used, 16, 128), bf16)
            for stream in plan.members[g]:
                if 1 <= k <= depth:
                    scatter_copies(stream, k - 1, False)
                    add_up(stream, k - 1)
                elif k > depth:
                    gather_copies(stream, 2 * depth - k, False)
                for copy in sent[stream]:
                    copy.wait_send()
                sent[stream] = []
                if k < depth:
                    scatter_copies(stream, k, True)
                elif k < 2 * depth:
                    gather_copies(stream, 2 * depth - 1 - k, True)

    vec_grads = {}

    gw = plan.gw
    span = 4 * gw
    def blocks(name, out, turned=False):
        kernels = need(name)
        shape = (span, gw) if turned else (gw, span)
        long = lax.broadcasted_iota(jnp.int32, shape, 0 if turned else 1)
        short = lax.broadcasted_iota(jnp.int32, shape, 1 if turned else 0)
        spread = (lax.rem(long, gw) == short).astype(f32).astype(bf16)
        row = lax.broadcasted_iota(jnp.int32, (span, span), 0) // gw
        col = lax.broadcasted_iota(jnp.int32, (span, span), 1) // gw
        for k, t in enumerate(ORDER):
            for h in range(width // span):
                piece = kernels[t, 4 * h : 4 * h + 4].reshape(span, gw)
                full = dot_nt(spread, piece) if turned else dot(piece, spread)
                out[h, k * span : (k + 1) * span] = jnp.where(row == col, full, 0.0).astype(bf16)

    def groups_grad(name, taps, turned):
        lane = lax.broadcasted_iota(jnp.int32, (gw, span), 1) // gw
        for t, (var, start) in enumerate(taps):
            for h in range(width // span):
                cut = slice(h * span, (h + 1) * span)
                res = dot(turned[h], flat(var[start : start + side, :, cut]))
                out = res[0:gw]
                for j in range(1, 4):
                    out = jnp.where(lane == j, res[j * gw : (j + 1) * gw], out)
                if name == "k2" and t == plan.taps - 1:
                    put(LAST_TAP, out, 0, h * span)
                else:
                    put(name, out, t * gw, h * span)

    band, bands = plan.band, plan.bands
    bhalf = band // 2
    out_id = lax.broadcasted_iota(jnp.int32, (pix, pix), 0)
    in_id = lax.broadcasted_iota(jnp.int32, (pix, pix), 1)

    def source(o):
        quarter = o // (bhalf * side)
        down = lax.rem(o, bhalf * side) // side
        return (2 * down + quarter // 2) * plan.cols + 2 * lax.rem(o, side) + lax.rem(quarter, 2)

    ref["sort"][...] = (source(out_id) == in_id).astype(f32).astype(bf16)
    ref["unsort"][...] = (source(in_id) == out_id).astype(f32).astype(bf16)

    xp, R1 = ref["xp"], ref["R1"]
    keep_vectors()

    def transpose(source, out):
        out[...] = source.astype(f32).T.astype(bf16)

    totals = [jnp.zeros((8, width), f32)] * 2
    by_band = plan.rows % band == 0
    if not by_band:
        for d in range(R):
            arrived("x", plan.rows, 0, d)
    for d in range(bands):
        if by_band:
            if d % (plan.rows // band) == 0:
                arrived("x", plan.rows, 0, d // (plan.rows // band))
            k = lax.rem(r * (plan.rows // band) + d, bands)
        else:
            k = d
        block = ref["x_in"][pl.ds(k * band, band)].reshape(pix, cin)
        block = dot(ref["sort"][...], block).astype(bf16)
        xp[k] = block.reshape(4 * bhalf, side, cin)
        full_dot(R1.at[k], block, need("w1"))
        for j in range(4 * bhalf):
            a, b = PHASES[j // bhalf]
            v = line(R1[k, j])
            mv = v * mask_row(a, b, k * bhalf + j % bhalf)
            totals = [totals[0] + fold(mv), totals[1] + fold(mv * v)]
    even = xp.at[:, 0:bhalf]

    def at_phase(ab, p):
        return p // bhalf, ab * bhalf + lax.rem(p, bhalf)

    post(0, [column(totals[0]), column(totals[1]), row_count, half_count])
    SC = ref["SC"]
    short_sums = dot_moments(SC, even[...].reshape(pix, cin), need("s1"))

    blocks("k1", ref["bd1"])

    def coefficients(first, second, inverse, gain, shift):
        mean = first * inverse
        scale = lax.rsqrt(second * inverse - mean * mean + epsilon)
        a = scale * gain
        return a, shift - mean * a, scale, -mean * scale

    tot = fetch(0, 4)
    inv_full, inv_half = 1.0 / tot[2], 1.0 / tot[3]
    n1 = coefficients(tot[0], tot[1], inv_full, vector("g1"), vector("b1"))

    va = ref["va"]
    va[3:6, 0:1] = jnp.zeros((3, 1, side, width), bf16)

    def shifted(v, edge, amount):
        return jnp.where(edge, 0.0, pltpu.roll(v, amount, 0))

    for ab, (a, b) in enumerate(PHASES):

        def step(p, ab=ab, a=a, b=b):
            v = mask_row(a, b, p) * silu(line(R1[at_phase(ab, p)]) * n1[0] + n1[1])
            v = pixels(v)
            slot = (0, 1, 3, 4)[ab]
            va[slot, p + a] = v.astype(bf16)
            if b:
                va[slot + 1, p + a] = shifted(v, first_col, 1).astype(bf16)

        over_rows(step)
    taps1 = []
    for t in range(9):
        u, v = t // 3, t % 3
        slot = (0, 1, 3, 4)[2 * (u != 1) + (v != 1)] + (v == 0)
        taps1.append((va.at[slot], 1 if u == 2 else 0))

    def convolve(taps, weights, out):
        def half(h):
            cut = slice(h * span, (h + 1) * span)
            left = [flat(taps[t][0][taps[t][1] : taps[t][1] + side, :, cut]) for t in ORDER]
            return dot(jnp.concatenate(left, axis=1), weights[h])

        return with_moments(out, (half(h) for h in range(width // span)))

    c1 = ref["c1"]
    post(1, [*convolve(taps1, ref["bd1"], c1), *short_sums])
    blocks("k2", ref["bd2"])
    tot = fetch(1, 4)
    nc1 = coefficients(tot[0], tot[1], inv_half, vector("gg1"), vector("gb1"))
    ns = coefficients(tot[2], tot[3], inv_half, vector("sg1"), vector("sb1"))

    def excite(conv, norm, hidden, gated, sq, sq_form, sqb, ex, exb):
        def step(p):
            v = mask_row(0, 0, p) * silu(line(conv[p]) * norm[0] + norm[1])
            hidden[p] = pixels(v)
            return (v,)

        (total,) = over_rows(step, 1)
        pooled = total / half_count
        pre = small_dot(pooled, sq[...], sq_form) + sqb
        inner = silu(pre)
        gate = sigmoid(small_dot(inner, ex[...], dot) + exb)
        gate_wide = wide(gate)

        def step_two(p):
            gated[p] = pixels(line(hidden[p]) * gate_wide).astype(bf16)

        over_rows(step_two)
        return pooled, pre, inner, gate

    H1, ga1 = ref["H1"], ref["ga1"]
    kept1 = excite(
        c1, nc1, H1, ga1, need("sq1"), dot_nt, vec[VEC["sqb1"], 0:1, : plan.q1], need("ex1"), vec[VEC["exb1"], 0:1]
    )
    E1 = ref["E1"]
    post(2, dot_moments(E1, lines(ga1), need("e1")))
    transpose(lines(ga1), ref["ga1t"])
    tot = fetch(2)
    ne = coefficients(tot[0], tot[1], inv_half, vector("eg1"), vector("eb1"))
    ent = ref["ent"]
    both_shifts = ne[1] + ns[1]

    def step(p):
        v = line(E1[p]) * ne[0] + line(SC[p]) * ns[0] + both_shifts
        ent[p] = pixels(mask_row(0, 0, p) * silu(v)).astype(bf16)

    over_rows(step)

    def send_out(source, out, rows, target, steps=None):
        for k in range(R // plan.copies) if steps is None else steps:
            t = lax.rem(r + plan.copies * k, R)
            there = ref[out].at[0, mine, 0] if out == "act" else ref[out].at[mine, 0]
            here = source.at[pl.ds(t * rows, rows)]
            copy = pltpu.make_async_remote_copy(
                src_ref=here,
                dst_ref=there,
                send_sem=ref[out + "_s"].at[target, k],
                recv_sem=ref[out + "_r"].at[mine],
                device_id=(target, i, t),
                device_id_type=MESH,
            )
            if k:
                copy.start()
                waits.append(copy.wait_send)
            else:
                local = pltpu.make_async_copy(here, there, ref[out + "_r"].at[mine])

                @pl.when(s == target)
                def _():
                    local.start()

                @pl.when(s != target)
                def _():
                    copy.start()

                def finish(copy=copy):
                    @pl.when(s != target)
                    def _():
                        copy.wait_send()

                waits.append(finish)

    send_out(ent, "act", plan.hrows, 0)

    R2 = ref["R2"]
    post(3, dot_moments(R2, lines(ent), need("w2")))
    transpose(lines(ent), ref["entt"])
    for k in range(bands):
        transpose(xp[k].reshape(pix, cin), ref["xpt"].at[k])
    tot = fetch(3)
    n2 = coefficients(tot[0], tot[1], inv_half, vector("g2"), vector("b2"))
    vb = ref["vb"]
    vb[:, 0:1] = jnp.zeros((3, 1, side, width), bf16)
    vb[:, side + 1 :] = jnp.zeros((3, 1, side, width), bf16)

    def three(out, p, v):
        out[0, p + 1] = shifted(v, first_col, 1).astype(bf16)
        out[1, p + 1] = v.astype(bf16)
        out[2, p + 1] = shifted(v, last_col, side - 1).astype(bf16)

    def step(p):
        three(vb, p, pixels(mask_row(0, 0, p) * silu(line(R2[p]) * n2[0] + n2[1])))

    over_rows(step)
    taps2 = [(vb.at[t % 3], t // 3) for t in range(9)]
    c2 = ref["c2"]
    post(4, convolve(taps2, ref["bd2"], c2))
    blocks("k2", ref["bd2t"], True)
    tot = fetch(4)
    nc2 = coefficients(tot[0], tot[1], inv_half, vector("gg2"), vector("gb2"))
    H2, ga2 = ref["H2"], ref["ga2"]
    kept2 = excite(
        c2, nc2, H2, ga2, need("sq2"), dot, vec[VEC["sqb2"], 0:1, : plan.q2], need("ex2"), vec[VEC["exb2"], 0:1]
    )
    E2 = ref["E2"]
    post(5, dot_moments(E2, lines(ga2), need("e2")))
    transpose(lines(ga2), ref["ga2t"])
    for d in range(R):
        arrived("og", plan.hrows, 1, d)
    tot = fetch(5)
    ne2 = coefficients(tot[0], tot[1], inv_half, vector("eg2"), vector("eb2"))
    leave, D, og = ref["leave"], ref["D"], ref["og_in"]

    def step(p):
        e = line(E2[p])
        v = e * ne2[0] + ne2[1] + line(ent[p])
        sg = sigmoid(v)
        m = mask_row(0, 0, p)
        leave[p] = pixels(m * v * sg).astype(bf16)
        g = line(og[p]) * m * (sg * (1.0 + v * (1.0 - sg)))
        D[p] = pixels(g)
        return g, g * (e * ne2[2] + ne2[3])

    parts = over_rows(step, 2)
    vec_grads["eb2"], vec_grads["eg2"] = parts
    post(6, parts)
    send_out(leave, "act", plan.hrows, 1)
    blocks("k1", ref["bd1t"], True)

    def back_rule(sums, inverse, gain, norm):
        a = gain * norm[2]
        k0 = a * (sums[0] + norm[3] * sums[1]) * inverse
        return a, k0, a * norm[2] * sums[1] * inverse

    def back_excite(dg, kept, hidden, conv, norm, sq, sq_form, ex, out):
        pooled, pre, inner, gate = kept

        def step(p):
            return (line(dg[p]) * line(hidden[p]),)

        (dgate,) = over_rows(step, 1)
        dpre = dgate * gate * (1.0 - gate)
        dsq = small_dot(dpre, ex[...], dot_nt) * slope(pre)
        dpool = wide(small_dot(dsq, sq[...], sq_form) / half_count)
        gate_wide = wide(gate)

        def step_two(p):
            v = line(conv[p])
            g = (line(dg[p]) * gate_wide + dpool) * mask_row(0, 0, p)
            g = g * slope(v * norm[0] + norm[1])
            out[p] = pixels(g)
            return g, g * (v * norm[2] + norm[3])

        return over_rows(step_two, 2), dpre, dsq

    def excite_grads(name, kept, dpre, dsq):
        pooled, pre, inner, gate = kept
        put("sq" + name, small_outer(dsq, pooled))
        put("ex" + name, small_outer(inner, dpre))
        vec_grads["exb" + name] = dpre
        count = dsq.shape[1]
        eye = (
            lax.broadcasted_iota(jnp.int32, (count, width), 0)
            == lax.broadcasted_iota(jnp.int32, (count, width), 1)
        ).astype(f32).astype(bf16)
        vec_grads["sqb" + name] = small_dot(dsq, eye, dot)

    def turn(gradient_ref, start):
        out = []
        for h in range(width // span):
            piece = flat(gradient_ref[start : start + side, :, h * span : (h + 1) * span])
            out.append(piece.astype(f32).T.astype(bf16))
        return out

    d1, dg, GR = ref["d1"], ref["dg"], ref["GR"]
    tot = fetch(6)
    rule = back_rule((tot[0], tot[1]), inv_half, vector("eg2"), ne2)

    def step(p):
        v = rule[0] * line(D[p]) - mask_row(0, 0, p) * (rule[1] + rule[2] * line(E2[p]))
        d1[p] = pixels(v).astype(bf16)

    over_rows(step)
    full_dot(dg, lines(d1), need("e2"), dot_nt)
    parts, dpre, dsq = back_excite(dg, kept2, H2, c2, nc2, need("sq2"), dot_nt, need("ex2"), GR)
    vec_grads["gb2"], vec_grads["gg2"] = parts
    post(7, parts)
    put("e2", dot(ref["ga2t"][...], lines(d1)))
    excite_grads("2", kept2, dpre, dsq)
    pump(0)
    tot = fetch(7)
    rule = back_rule((tot[0], tot[1]), inv_half, vector("gg2"), nc2)
    vd = ref["vd"]
    vd[:, 0:1] = jnp.zeros((3, 1, side, width), bf16)
    vd[:, side + 1 :] = jnp.zeros((3, 1, side, width), bf16)

    def step(p):
        v = rule[0] * line(GR[p]) - mask_row(0, 0, p) * (rule[1] + rule[2] * line(c2[p]))
        three(vd, p, pixels(v))

    over_rows(step)

    def convolve_back(taps, first, weights, out):
        for h in range(width // span):
            cut = slice(h * span, (h + 1) * span)
            left = [flat(var[start : start + side, :, cut]) for var, start in taps]
            rows = slice(first * span, (first + len(taps)) * span)
            acc = dot(jnp.concatenate(left, axis=1), weights[h, rows])
            out[:, :, cut] = acc.reshape(side, side, span)

    DA = ref["DA"]
    convolve_back(
        [(vd.at[2 - t % 3], 2 - t // 3) for t in ORDER],
        0,
        ref["bd2t"],
        DA.at[0],
    )
    pump(0)

    def step(p):
        v = line(R2[p])
        g = line(DA[0, p]) * mask_row(0, 0, p) * slope(v * n2[0] + n2[1])
        GR[p] = pixels(g)
        return g, g * (v * n2[2] + n2[3])

    parts = over_rows(step, 2)
    vec_grads["b2"], vec_grads["g2"] = parts
    post(8, parts)
    groups_grad("k2", taps2, turn(vd.at[1], 1))
    tot = fetch(8)
    rule = back_rule((tot[0], tot[1]), inv_half, vector("g2"), n2)

    def step(p):
        v = rule[0] * line(GR[p]) - mask_row(0, 0, p) * (rule[1] + rule[2] * line(R2[p]))
        d1[p] = pixels(v).astype(bf16)

    over_rows(step)
    full_dot(GR, lines(d1), need("w2"), dot_nt)

    def step(p):
        e, sc = line(E1[p]), line(SC[p])
        g = line((D[p] + GR[p]).astype(bf16))
        g = g * mask_row(0, 0, p) * slope(e * ne[0] + sc * ns[0] + both_shifts)
        D[p] = pixels(g)
        return g, g * (e * ne[2] + ne[3]), g * (sc * ns[2] + ns[3])

    parts = over_rows(step, 3)
    vec_grads["eb1"], vec_grads["eg1"], vec_grads["sg1"] = parts
    vec_grads["sb1"] = parts[0]
    post(9, parts)
    put("w2", dot(ref["entt"][...], lines(d1)))
    pump(1, 0)
    tot = fetch(9, 3)
    rule_e = back_rule((tot[0], tot[1]), inv_half, vector("eg1"), ne)
    rule_s = back_rule((tot[0], tot[2]), inv_half, vector("sg1"), ns)
    d2 = ref["d2"]

    def step(p):
        g, m = line(D[p]), mask_row(0, 0, p)
        v = rule_e[0] * g - m * (rule_e[1] + rule_e[2] * line(E1[p]))
        d1[p] = pixels(v).astype(bf16)
        v = rule_s[0] * g - m * (rule_s[1] + rule_s[2] * line(SC[p]))
        d2[p] = pixels(v).astype(bf16)

    over_rows(step)
    full_dot(dg, lines(d1), need("e1"), dot_nt)
    parts, dpre, dsq = back_excite(dg, kept1, H1, c1, nc1, need("sq1"), dot, need("ex1"), GR)
    vec_grads["gb1"], vec_grads["gg1"] = parts
    post(10, parts)
    put("e1", dot(ref["ga1t"][...], lines(d1)))
    put("s1", dot_tn(even[...].reshape(pix, cin), lines(d2)))
    excite_grads("1", kept1, dpre, dsq)
    pump(2, 1, 0)
    tot = fetch(10)
    rule = back_rule((tot[0], tot[1]), inv_half, vector("gg1"), nc1)

    def step(p):
        v = rule[0] * line(GR[p]) - mask_row(0, 0, p) * (rule[1] + rule[2] * line(c1[p]))
        three(vd, p, pixels(v))

    over_rows(step)
    sums = []
    for ab, (a, b) in enumerate(PHASES):
        chosen = []
        first = (0, 1, 3, 5)[ab]
        for t in ORDER[first : first + (1, 2, 2, 4)[ab]]:
            chosen.append((vd.at[2 if t % 3 == 0 else 1], 2 if t // 3 == 0 else 1))
        convolve_back(chosen, first, ref["bd1t"], DA.at[ab])

        def step(p, ab=ab, a=a, b=b):
            v = line(R1[at_phase(ab, p)])
            g = line(DA[ab, p]) * mask_row(a, b, p) * slope(v * n1[0] + n1[1])
            DA[ab, p] = pixels(g)
            return g, g * (v * n1[2] + n1[3])

        sums.append(over_rows(step, 2))
        if ab == 1:
            pump(2)
    parts = (sum(x[0] for x in sums), sum(x[1] for x in sums))
    vec_grads["b1"], vec_grads["g1"] = parts
    post(11, parts)
    pump(1, 0)
    groups_grad("k1", taps1, turn(vd.at[1], 1))
    ids = lax.broadcasted_iota(jnp.int32, (VEC_ROWS, width), 0)
    value = jnp.zeros((VEC_ROWS, width), f32)
    for name, at in VEC.items():
        value = jnp.where(ids == at, jnp.broadcast_to(vec_grads[name], value.shape), value)
    put(VECTORS, value)
    pump(3, 1)
    tot = fetch(11)
    rule = back_rule((tot[0], tot[1]), inv_full, vector("g1"), n1)
    dr = ref["dr"]
    for ab, (a, b) in enumerate(PHASES):

        def step(p, ab=ab, a=a, b=b):
            v = rule[0] * line(DA[ab, p])
            v = v - mask_row(a, b, p) * (rule[1] + rule[2] * line(R1[at_phase(ab, p)]))
            dr[at_phase(ab, p)] = pixels(v).astype(bf16)

        over_rows(step)
    total = None
    for k in range(bands):
        term = dot(ref["xpt"][k], dr[k].reshape(pix, width))
        total = term if total is None else total + term
    put("w1", total)
    pump(4, 2)
    cut = cin // 2
    ref["dxo0"][...] = jnp.zeros((2 * side, plan.cols, 128), bf16)
    ref["dxo1"][...] = jnp.zeros((2 * side, plan.cols, 128), bf16)
    stepwise = plan.each == bands
    for d in [*range(1, bands), 0]:
        k = lax.rem(r + plan.copies * d, R) * plan.rows // band if stepwise else d
        for part in range(2):
            dxo = ref[f"dxo{part}"]
            rows = slice(part * cut, (part + 1) * cut)
            v = dot_nt(dr[k].reshape(pix, width), need("w1")[rows, :])
            w = dot_nt(
                d2[pl.ds(k * bhalf, bhalf)].reshape(bhalf * side, width), need("s1")[rows, :]
            )
            v = jnp.concatenate([v[: bhalf * side] + w, v[bhalf * side :]], axis=0)
            v = dot(ref["unsort"][...], v.astype(bf16)).astype(bf16)
            dxo[pl.ds(k * band, band), :, :cut] = v.reshape(band, plan.cols, cut)
            if stepwise:
                send_out(dxo, "dx", plan.rows, part, (d,))
        pump(*((3, 1), (4, 3, 2, 1), (4, 3, 2, 1, 0), (4, 3, 2))[(d - 1) % 4])
    if not stepwise:
        send_out(ref["dxo0"], "dx", plan.rows, 0)
        send_out(ref["dxo1"], "dx", plan.rows, 1)
    for _ in range(9):
        pump()
    for wait in waits:
        wait()
    for m in range(plan.M):
        t = (m % plan.each) * plan.copies + lax.rem(r, plan.copies)
        for out in ("act", "dx"):
            there = ref[out].at[0, m, 0] if out == "act" else ref[out].at[m, 0]
            pltpu.make_async_copy(there, there, ref[out + "_r"].at[m]).wait()


WEIGHTS = ("w1", "k1", "k2", "sq1", "ex1", "e1", "s1", "w2", "sq2", "ex2", "e2")


def run_main(plan, arrays):
    side, width, cin = plan.side, plan.width, plan.cin
    wide = 4 * plan.gw
    field = (side, side, width)
    scratch = {
        "x_in": pltpu.VMEM((2 * side, plan.cols, cin), bf16),
        "og_in": pltpu.VMEM(field, bf16),
        "st": pltpu.VMEM((EXCHANGES, plan.I, 2, 8, 128), f32),
        "hm": pltpu.VMEM((plan.pix, 128), f32),
        "cm": pltpu.VMEM((2, side, width), f32),
        **{
            name: pltpu.VMEM((width // wide, plan.taps * wide, wide), bf16)
            for name in ("bd1", "bd2", "bd1t", "bd2t")
        },
        "xpt": pltpu.VMEM((plan.bands, cin, plan.pix), bf16),
        **{name: pltpu.VMEM((width, plan.pix), bf16) for name in ("ga1t", "ga2t", "entt")},
        "sort": pltpu.VMEM((plan.pix, plan.pix), bf16),
        "unsort": pltpu.VMEM((plan.pix, plan.pix), bf16),
        "xp": pltpu.VMEM((plan.bands, 2 * plan.band, side, cin), bf16),
        "R1": pltpu.VMEM((plan.bands, 2 * plan.band, side, width), f32),
        "va": pltpu.VMEM((6, side + 1, side, width), bf16),
        "vb": pltpu.VMEM((3, side + 2, side, width), bf16),
        "vd": pltpu.VMEM((3, side + 2, side, width), bf16),
        "DA": pltpu.VMEM((4,) + field, f32),
        "dr": pltpu.VMEM((plan.bands, 2 * plan.band, side, width), bf16),
        "dxo0": pltpu.VMEM((2 * side, plan.cols, 128), bf16),
        "dxo1": pltpu.VMEM((2 * side, plan.cols, 128), bf16),
    }
    for name in ("SC", "H1", "E1", "R2", "H2", "E2", "D", "GR"):
        scratch[name] = pltpu.VMEM(field, f32)
    for name in ("c1", "ga1", "ent", "c2", "ga2", "leave", "d1", "d2", "dg"):
        scratch[name] = pltpu.VMEM(field, bf16)
    for name in ("x", "og"):
        scratch[name + "_s"] = pltpu.SemaphoreType.DMA((max(plan.R - 1, 1),))
        scratch[name + "_r"] = pltpu.SemaphoreType.DMA((plan.R,))
    scratch["st_s"] = pltpu.SemaphoreType.DMA((EXCHANGES, max(plan.I - 1, 1)))
    scratch["st_r"] = pltpu.SemaphoreType.DMA((EXCHANGES, plan.I))
    for name in ("act", "dx"):
        scratch[name + "_s"] = pltpu.SemaphoreType.DMA((2, plan.R // plan.copies))
        scratch[name + "_r"] = pltpu.SemaphoreType.DMA((plan.M,))
    for name in NAMES + WEIGHTS:
        scratch[name + "_v"] = pltpu.VMEM(arrays[name].shape, bf16)
    scratch["vec"] = pltpu.VMEM((len(NAMES), 8, width), f32)
    scratch["loads"] = pltpu.SemaphoreType.DMA((len(NAMES + WEIGHTS),))
    scratch["local"] = pltpu.VMEM((plan.blocks, 16, 128), bf16)
    for level, room in enumerate(plan.rooms):
        scratch[f"got{level}"] = pltpu.VMEM((room, 16, 128), bf16)
        if level:
            scratch[f"sum{level - 1}"] = pltpu.VMEM((room, 16, 128), bf16)
    most = max(plan.sizes.values())
    for name in ("rs", "ag"):
        scratch[name + "_s"] = pltpu.SemaphoreType.DMA((len(plan.streams), 4, most - 1))
        scratch[name + "_r"] = pltpu.SemaphoreType.DMA((len(plan.streams), 4, most))
    inputs = ("x", "og", "vr", "vc") + NAMES + WEIGHTS
    outputs = ("act", "dx", "grads")
    names = inputs + outputs + tuple(scratch)
    any_space = pl.BlockSpec(memory_space=pl.ANY)
    smem = pl.BlockSpec(memory_space=pltpu.SMEM)
    vmem = pl.BlockSpec(memory_space=pltpu.VMEM)
    return pl.pallas_call(
        functools.partial(main_kernel, plan, names),
        out_shape=(
            pltpu.VMEM((1, plan.M, 1, plan.hrows, side, width), bf16),
            pltpu.VMEM((plan.M, 1, plan.rows, plan.cols, 128), bf16),
            pltpu.VMEM((plan.blocks, 16, 128), bf16),
        ),
        in_specs=[any_space, any_space, smem, smem] + [any_space] * (len(NAMES) + len(WEIGHTS)),
        out_specs=(vmem, vmem, vmem),
        scratch_shapes=list(scratch.values()),
        compiler_params=pltpu.CompilerParams(
            collective_id=0, has_side_effects=True, vmem_limit_bytes=58 * 1024 * 1024
        ),
        name="blocks",
    )(*[arrays[name] for name in inputs])


OUTS = (
    "w1", "g1", "b1", "k1", "gg1", "gb1", "sq1", "sqb1", "ex1", "exb1", "e1", "eg1", "eb1",
    "s1", "sg1", "sb1", "w2", "g2", "b2", "k2", "gg2", "gb2", "sq2", "sqb2", "ex2", "exb2",
    "e2", "eg2", "eb2",
)


def unpack_kernel(plan, blocks, act_in, dx_in, *rest):
    count = len(OUTS) + 2
    outs, bufs, sems = rest[:count], rest[count:-1], rest[-1]
    copies = []
    for k, whole in enumerate((act_in, dx_in)):
        copies.append(pltpu.make_async_copy(whole, outs[k], sems.at[k]))
        copies[-1].start()
    order = sorted(plan.starts, key=lambda name: plan.starts[name])
    order = [name for name in order if name not in (VECTORS, LAST_TAP)]

    def tile(name, k):
        start, per_tile = plan.starts[name]
        at = start + k * per_tile
        return blocks[at : at + per_tile].reshape(16 * per_tile, 128).astype(f32)

    tiles = plan.width // 128
    vec = None
    turn = [OUTS.index(name) for name in order]
    turn += [k for k, name in enumerate(OUTS) if name in VEC]
    for k in turn:
        name, out = OUTS[k], bufs[k]
        if name in VEC and vec is None:
            vec = jnp.concatenate([tile(VECTORS, k) for k in range(tiles)], axis=1)
        if name in VEC:
            size = out.shape[0]
            out[...] = vec[VEC[name] : VEC[name] + 1, :size].reshape(size)
        elif name[0] == "k":

            def run(t, carry, name=name, out=out, last_tap=False):
                for lane in range(tiles):
                    start, per_tile = plan.starts[name]
                    at = start + lane * per_tile + t * (plan.gw // 16)
                    if last_tap:
                        start, per_tile = plan.starts[LAST_TAP]
                        at = start + lane * per_tile
                    piece = blocks[pl.ds(at, plan.gw // 16)].reshape(plan.gw, 128)
                    piece = piece.astype(f32).T
                    for j in range(128 // plan.gw):
                        group = lane * (128 // plan.gw) + j
                        out[t, group, :, : plan.gw] = piece[j * plan.gw : (j + 1) * plan.gw]
                return carry

            if name == "k2":
                lax.fori_loop(0, plan.taps - 1, run, 0)
                run(plan.taps - 1, 0, last_tap=True)
            else:
                lax.fori_loop(0, plan.taps, run, 0)
        elif name == "sq2":
            for lane in range(tiles):
                out[128 * lane : 128 * lane + 128] = tile(name, lane).T
        else:
            for lane in range(tiles):
                out[:, 128 * lane : 128 * lane + 128] = tile(name, lane)
        copies.append(pltpu.make_async_copy(out, outs[k + 2], sems.at[k + 2]))
        copies[-1].start()
    for copy in copies:
        copy.wait()


def unpack(plan, act, dx, grads, weights):
    shapes = []
    for name, w in zip(OUTS, weights):
        shape = w.shape[:3] + (128,) if name[0] == "k" else w.shape
        shapes.append(jax.ShapeDtypeStruct(shape, f32))
    any_space = pl.BlockSpec(memory_space=pl.ANY)
    return pl.pallas_call(
        functools.partial(unpack_kernel, plan),
        out_shape=[jax.ShapeDtypeStruct(v.shape, v.dtype) for v in (act, dx)] + shapes,
        in_specs=[pl.BlockSpec(memory_space=pltpu.VMEM)] * 3,
        out_specs=[any_space] * (len(shapes) + 2),
        scratch_shapes=[pltpu.VMEM(v.shape, v.dtype) for v in shapes]
        + [pltpu.SemaphoreType.DMA((len(shapes) + 2,))],
        compiler_params=pltpu.CompilerParams(vmem_limit_bytes=24 * 1024 * 1024),
        name="unpack",
    )(grads, act, dx)


def body(sizes, input_maps, valid_rows, valid_cols, *rest):
    weights, output_grad = rest[:-1], rest[-1]
    (w1, g1, b1, k1, gg1, gb1, sq1, sqb1, ex1, exb1, e1, eg1, eb1, s1, sg1, sb1) = weights[:16]
    (w2, g2, b2, k2, gg2, gb2, sq2, sqb2, ex2, exb2, e2, eg2, eb2) = weights[16:]
    turned = sq1.T
    plan = Plan(sizes, [v.shape for v in (input_maps, output_grad, w1, k1, turned, sq2)])
    vectors = (
        g1, b1, gg1, gb1, exb1, eg1, eb1, sg1, sb1, sqb1, g2, b2, gg2, gb2, exb2, eg2, eb2, sqb2,
    )
    arrays = dict(
        x=input_maps, og=output_grad, vr=valid_rows.T, vc=valid_cols.T, w1=w1,
        k1=k1, k2=k2,
        sq1=turned, ex1=ex1, e1=e1, s1=s1, w2=w2, sq2=sq2, ex2=ex2, e2=e2,
        **dict(zip(NAMES, vectors)),
    )
    act, dx, grads = run_main(plan, arrays)
    act, dx, *out = unpack(plan, act, dx, grads, weights[:6] + (turned,) + weights[7:])
    out[6] = out[6].T
    for at in (3, 19):
        out[at] = out[at][..., : plan.gw]
    dx = dx[..., : plan.cin // 2]
    return (act, dx, *out)


def solution(mesh):
    tiled = P(None, "img", "row", None, None)
    image = P(None, "img")
    sizes = tuple(mesh.shape[name] for name in ("section", "img", "row"))
    return jax.shard_map(
        functools.partial(body, sizes),
        mesh=mesh,
        in_specs=(tiled, image, image) + (P(),) * 29 + (tiled,),
        out_specs=(
            P("section", None, "img", "row", None, None),
            P(None, "img", "row", None, "section"),
        )
        + (P(),) * 29,
        check_vma=False,
    )
```
